32 devices in a mesh: seq: 4 (over x, core), chan: 8 (over z, y).
Axes of the slice: x: 2, y: 2, z: 4, core: 2. Of those that a mesh axis runs over, the one named last changes fastest.
Arguments:
- layer_entry: bfloat16 [16384, 1024], P(('seq', 'chan')), may hold values from -6 to 6
- upstream_gradient: bfloat16 [16384, 1024], P(('seq', 'chan')), may hold values from -6 to 6
- norm_alpha_factor: float32 [1024], replicated, may hold values from 0.5 to 1.5
- norm_alpha_offset: float32 [1024], replicated, may hold values from -0.5 to 0.5
- attention_lookup_share: float32 [1024], replicated, may hold values from 0 to 1
- attention_payload_share: float32 [1024], replicated, may hold values from 0 to 1
- attention_gate_share: float32 [1024], replicated, may hold values from 0 to 1
- log_fading_rate: float32 [1024], replicated, may hold values from -7.6 to -2
- present_step_boost: float32 [1024], replicated, may hold values from -1 to 1
- lookup_projection: bfloat16 [1024, 1024], replicated, may hold values from -0.1875 to 0.1875
- payload_projection: bfloat16 [1024, 1024], replicated, may hold values from -0.1875 to 0.1875
- gate_projection: bfloat16 [1024, 1024], replicated, may hold values from -0.1875 to 0.1875
- attention_exit_matrix: bfloat16 [1024, 1024], replicated, may hold values from -0.5 to 0.5
- norm_beta_factor: float32 [1024], replicated, may hold values from 0.5 to 1.5
- norm_beta_offset: float32 [1024], replicated, may hold values from -0.5 to 0.5
- feedforward_lookup_share: float32 [1024], replicated, may hold values from 0 to 1
- feedforward_gate_share: float32 [1024], replicated, may hold values from 0 to 1
- feedforward_lookup_matrix: bfloat16 [1024, 4096], replicated, may hold values from -0.1875 to 0.1875
- feedforward_payload_matrix: bfloat16 [4096, 1024], replicated, may hold values from -0.09375 to 0.09375
- feedforward_gate_matrix: bfloat16 [1024, 1024], replicated, may hold values from -0.1875 to 0.1875
- packed_spans: int32 [4, 8], P('seq'), may hold values from 256 to 1024, as said below
- filler_tallies: int32 [4, 8], P('seq'), may hold values from 0 to 128
Outputs:
- block_out: bfloat16 [16384, 1024], P(('seq', 'chan'))
- grad_in: bfloat16 [16384, 1024], P(('seq', 'chan'))
- grad_ln1_gain: float32 [1024], P('chan')
- grad_ln1_bias: float32 [1024], P('chan')
- grad_mix_key: float32 [1024], P('chan')
- grad_mix_value: float32 [1024], P('chan')
- grad_mix_recept: float32 [1024], P('chan')
- grad_time_decay: float32 [1024], P('chan')
- grad_time_first: float32 [1024], P('chan')
- grad_w_key: float32 [1024, 1024], P('seq', 'chan')
- grad_w_value: float32 [1024, 1024], P('seq', 'chan')
- grad_w_recept: float32 [1024, 1024], P('seq', 'chan')
- grad_w_output: float32 [1024, 1024], P('seq', 'chan')
- grad_ln2_gain: float32 [1024], P('chan')
- grad_ln2_bias: float32 [1024], P('chan')
- grad_cmix_key: float32 [1024], P('chan')
- grad_cmix_recept: float32 [1024], P('chan')
- grad_f_key: float32 [1024, 4096], P('seq', 'chan')
- grad_f_value: float32 [4096, 1024], P('seq', 'chan')
- grad_f_recept: float32 [1024, 1024], P('seq', 'chan')
The draws below stay inside these ranges and needn't reach their ends.
Inputs may be any that keep to these rules, and one draw needn't show every extreme that they name: `packed_spans`: each row sums to 4096, and one sequence of every group has length exactly 1024.
All inputs are finite; a program needn't handle non-finite values.
Results may differ from the reference program's by a relative error of at most 0.018.
Values may be sent and summed in bfloat16 or wider, within the bound.
A program may use at most 192 MiB of HBM per device.

```python
import jax
import jax.numpy as jnp
from jax import lax

EMBED_DIM = 1024
FF = 4096
SLOTS = 8
GROUP = 4096
MOST = 1024
GROUPS = 4
TOKENS = 16384


def draw_packed_spans(key, part):
    key = jax.random.fold_in(key, 11)
    first_key, second_key = jax.random.split(key, 2)
    base = MOST // 4
    leftover = 3 * MOST - 7 * base
    paired = 2 * (leftover // 7)
    extra = jax.random.randint(first_key, (GROUPS, 3), 0, paired + 1)
    last_extra = jnp.full((GROUPS, 1), leftover - 3 * paired, jnp.int32)
    others = base + jnp.concatenate([extra, paired - extra, last_extra], axis=1)
    longest = jnp.full((GROUPS, 1), MOST, jnp.int32)
    whole = jnp.concatenate([longest, others], axis=1).astype(jnp.int32)
    scores = jax.random.randint(second_key, (GROUPS, SLOTS), 0, 1 << 20) * SLOTS + jnp.arange(SLOTS, dtype=jnp.int32)[None, :]
    order = jnp.argsort(scores, axis=1)
    return jnp.take_along_axis(whole, order, axis=1).astype(jnp.int32)


def plant(drawn, stream_key, smallest, top_value):
    extent = drawn.shape
    index_at = [jax.random.randint(jax.random.fold_in(stream_key, axis), (), 0, extent[axis]) for axis in range(len(extent))]
    drawn = drawn.at[tuple(index_at)].set(smallest)
    longest = extent.index(max(extent))
    index_at[longest] = (index_at[longest] + 1) % extent[longest]
    return drawn.at[tuple(index_at)].set(top_value)


def level_of(key, extent, pieces, smallest, top_value):
    level, own = 1.0, jax.random.fold_in(key, 6)
    for axis_at, blocks in pieces:
        steps = jnp.exp(jax.random.uniform(jax.random.fold_in(own, axis_at), (blocks,), jnp.float32, smallest / len(pieces), top_value / len(pieces)))
        level = level * jnp.repeat(steps, extent[axis_at] // blocks).reshape([-1 if axis == axis_at else 1 for axis in range(len(extent))])
    return level


def scatter_about(own_key, extent, width, reach, cuts=(), held_as=jnp.bfloat16):
    level = level_of(own_key, extent, cuts, -0.22, 0.18) if cuts else 1.0
    array = jax.random.normal(own_key, extent, jnp.float32) * width * level
    return jnp.minimum(jnp.maximum(array, -reach), reach).astype(held_as)


def setup_inputs(seed: int = 0) -> dict:
    key_of = jax.random.split(jax.random.key(seed), 23)
    layer_entry = scatter_about(key_of[0], (TOKENS, EMBED_DIM), 1.0, 6.0, ((0, 32),))
    upstream_gradient = scatter_about(key_of[1], (TOKENS, EMBED_DIM), 1.0, 6.0, ((0, 32),))
    norm_alpha_factor = jnp.clip(1.0 + 0.1 * jax.random.normal(key_of[2], (EMBED_DIM,), jnp.float32), 0.5, 1.5)
    norm_alpha_offset = jnp.clip(jax.random.uniform(key_of[3], (EMBED_DIM,), jnp.float32, -0.5, 0.5), -0.5, 0.5)
    attention_lookup_share = jnp.clip(jax.random.uniform(key_of[4], (EMBED_DIM,), jnp.float32, 0.0, 1.0), 0.0, 1.0)
    attention_payload_share = jnp.clip(jax.random.uniform(key_of[5], (EMBED_DIM,), jnp.float32, 0.0, 1.0), 0.0, 1.0)
    attention_gate_share = jnp.clip(jax.random.uniform(key_of[6], (EMBED_DIM,), jnp.float32, 0.0, 1.0), 0.0, 1.0)
    log_fading_rate = jnp.clip(jax.random.uniform(key_of[7], (EMBED_DIM,), jnp.float32, -7.6, -2.0), -7.6, -2.0)
    present_step_boost = jnp.clip(jax.random.uniform(key_of[8], (EMBED_DIM,), jnp.float32, -1.0, 1.0), -1.0, 1.0)
    lookup_projection = scatter_about(key_of[9], (EMBED_DIM, EMBED_DIM), EMBED_DIM ** -0.5, 0.1875)
    payload_projection = scatter_about(key_of[10], (EMBED_DIM, EMBED_DIM), EMBED_DIM ** -0.5, 0.1875)
    gate_projection = scatter_about(key_of[11], (EMBED_DIM, EMBED_DIM), EMBED_DIM ** -0.5, 0.1875)
    attention_exit_matrix = scatter_about(key_of[12], (EMBED_DIM, EMBED_DIM), (EMBED_DIM // 8) ** -0.5, 0.5)
    norm_beta_factor = jnp.clip(1.0 + 0.1 * jax.random.normal(key_of[13], (EMBED_DIM,), jnp.float32), 0.5, 1.5)
    norm_beta_offset = jnp.clip(jax.random.uniform(key_of[14], (EMBED_DIM,), jnp.float32, -0.5, 0.5), -0.5, 0.5)
    feedforward_lookup_share = jnp.clip(jax.random.uniform(key_of[15], (EMBED_DIM,), jnp.float32, 0.0, 1.0), 0.0, 1.0)
    feedforward_gate_share = jnp.clip(jax.random.uniform(key_of[16], (EMBED_DIM,), jnp.float32, 0.0, 1.0), 0.0, 1.0)
    feedforward_lookup_matrix = scatter_about(key_of[17], (EMBED_DIM, FF), EMBED_DIM ** -0.5, 0.1875)
    feedforward_payload_matrix = scatter_about(key_of[18], (FF, EMBED_DIM), FF ** -0.5, 0.09375)
    feedforward_gate_matrix = scatter_about(key_of[19], (EMBED_DIM, EMBED_DIM), EMBED_DIM ** -0.5, 0.1875)
    packed_spans = draw_packed_spans(jax.random.fold_in(key_of[22], 71), 0)
    filler_tallies = plant(jax.random.randint(key_of[21], (GROUPS, SLOTS), 0, MOST // 8 + 1), jax.random.fold_in(key_of[21], 1), 0, (MOST // 8 + 1) - 1).astype(jnp.int32)
    return {"layer_entry": layer_entry, "upstream_gradient": upstream_gradient, "norm_alpha_factor": norm_alpha_factor, "norm_alpha_offset": norm_alpha_offset, "attention_lookup_share": attention_lookup_share, "attention_payload_share": attention_payload_share, "attention_gate_share": attention_gate_share, "log_fading_rate": log_fading_rate, "present_step_boost": present_step_boost, "lookup_projection": lookup_projection, "payload_projection": payload_projection, "gate_projection": gate_projection, "attention_exit_matrix": attention_exit_matrix, "norm_beta_factor": norm_beta_factor, "norm_beta_offset": norm_beta_offset, "feedforward_lookup_share": feedforward_lookup_share, "feedforward_gate_share": feedforward_gate_share, "feedforward_lookup_matrix": feedforward_lookup_matrix, "feedforward_payload_matrix": feedforward_payload_matrix, "feedforward_gate_matrix": feedforward_gate_matrix, "packed_spans": packed_spans, "filler_tallies": filler_tallies}


@jax.custom_vjp
def low(v):
    return lax.optimization_barrier(v.astype(jnp.bfloat16)).astype(jnp.float32)

@jax.custom_vjp
def low_back(v):
    return v

def low_keep(v):
    return (low(v), None)

def low_pass(kept, grad):
    return (grad,)

def back_keep(v):
    return (v, None)

def back_low(kept, grad):
    return (low(grad),)
low.defvjp(low_keep, low_pass)
low_back.defvjp(back_keep, back_low)

def layer_norm(payload_vectors, gain, bias):
    center = payload_vectors - lax.optimization_barrier(jnp.mean(payload_vectors, axis=-1, keepdims=True))
    spread = lax.optimization_barrier(jnp.mean(center * center, axis=-1, keepdims=True))
    return center * lax.rsqrt(spread + 1e-05) * gain + bias

def group_marks(lengths, pads, positions):
    offsets = jnp.cumsum(lengths) - lengths
    ends = offsets + lengths - pads
    after = positions[:, None] >= offsets[None, :]
    sequence_label = lax.optimization_barrier(jnp.sum(after.astype(jnp.int32), axis=1)) - 1
    opening_positions = jnp.any(positions[:, None] == offsets[None, :], axis=1).astype(jnp.float32)
    genuine_flag = jnp.any(after & (positions[:, None] < ends[None, :]), axis=1).astype(jnp.float32)
    return (opening_positions, sequence_label, genuine_flag)

def matmul(left, right):
    return jnp.dot(left, right, precision=lax.Precision.HIGHEST)

def attention_sweep(lookup_vectors, payload_vectors, log_fading_rate, present_step_boost, opening_positions, genuine_flag):
    keep_rate = jnp.exp(-jnp.exp(log_fading_rate))

    def step(carry, inputs):
        weighted_total, normalizer_total = carry
        lookup_line, payload_line, start_flag, real_flag = inputs
        weighted_total = weighted_total * (1.0 - start_flag)
        normalizer_total = normalizer_total * (1.0 - start_flag)
        step_boost = jnp.exp(present_step_boost + lookup_line)
        layer_outcome = (weighted_total + step_boost * payload_line) / (normalizer_total + step_boost)
        weight = jnp.exp(lookup_line) * real_flag
        return ((keep_rate * weighted_total + weight * payload_line, keep_rate * normalizer_total + weight), layer_outcome)
    zeros = jnp.zeros((EMBED_DIM,), jnp.float32)
    final_state, outputs = lax.scan(jax.checkpoint(step), (zeros, zeros), (lookup_vectors, payload_vectors, opening_positions, genuine_flag))
    return outputs

def shift_rows(normed, opening_positions):
    shifted = jnp.concatenate([jnp.zeros((1, EMBED_DIM), jnp.float32), normed[:-1]], axis=0)
    return shifted * (1.0 - opening_positions)[:, None]

def group_block(inputs, parameter_bundle):
    tokens, lengths, pads = inputs
    norm_alpha_factor, norm_alpha_offset, attention_lookup_share, attention_payload_share, attention_gate_share, log_fading_rate, present_step_boost, lookup_projection, payload_projection, gate_projection, attention_exit_matrix, norm_beta_factor, norm_beta_offset, feedforward_lookup_share, feedforward_gate_share, feedforward_lookup_matrix, feedforward_payload_matrix, feedforward_gate_matrix = parameter_bundle
    opening_positions, sequence_label, genuine_flag = group_marks(lengths, pads, jnp.arange(GROUP, dtype=jnp.int32))
    normed = layer_norm(tokens, norm_alpha_factor, norm_alpha_offset)
    shifted = shift_rows(normed, opening_positions)
    mixed_key = low(normed * attention_lookup_share + shifted * (1.0 - attention_lookup_share))
    mixed_value = low(normed * attention_payload_share + shifted * (1.0 - attention_payload_share))
    mixed_recept = low(normed * attention_gate_share + shifted * (1.0 - attention_gate_share))
    lookup_vectors = low_back(low(matmul(mixed_key, lookup_projection)))
    payload_vectors = low_back(low(matmul(mixed_value, payload_projection)))
    recept = low_back(matmul(mixed_recept, gate_projection))
    attention_average = low_back(low(attention_sweep(lookup_vectors, payload_vectors, log_fading_rate, present_step_boost, opening_positions, genuine_flag)))
    gated = low(jax.nn.sigmoid(recept) * attention_average)
    attended = low_back(matmul(gated, attention_exit_matrix))
    middle = tokens + attended
    normed_two = layer_norm(middle, norm_beta_factor, norm_beta_offset)
    shifted_two = shift_rows(normed_two, opening_positions)
    chan_key = low(normed_two * feedforward_lookup_share + shifted_two * (1.0 - feedforward_lookup_share))
    chan_recept = low(normed_two * feedforward_gate_share + shifted_two * (1.0 - feedforward_gate_share))
    pre_act = low_back(matmul(chan_key, feedforward_lookup_matrix))
    hidden = low(jnp.square(jax.nn.relu(pre_act)))
    value_out = low_back(matmul(hidden, feedforward_payload_matrix))
    gate_pre = low_back(matmul(chan_recept, feedforward_gate_matrix))
    return middle + jax.nn.sigmoid(gate_pre) * value_out

def row_mask(lengths, pads):
    return group_marks(lengths, pads, jnp.arange(GROUP, dtype=jnp.int32))[2]

def reference(layer_entry, upstream_gradient, norm_alpha_factor, norm_alpha_offset, attention_lookup_share, attention_payload_share, attention_gate_share, log_fading_rate, present_step_boost, lookup_projection, payload_projection, gate_projection, attention_exit_matrix, norm_beta_factor, norm_beta_offset, feedforward_lookup_share, feedforward_gate_share, feedforward_lookup_matrix, feedforward_payload_matrix, feedforward_gate_matrix, packed_spans, filler_tallies):
    coefficient_set = tuple((element_entry.astype(jnp.float32) for element_entry in (norm_alpha_factor, norm_alpha_offset, attention_lookup_share, attention_payload_share, attention_gate_share, log_fading_rate, present_step_boost, lookup_projection, payload_projection, gate_projection, attention_exit_matrix, norm_beta_factor, norm_beta_offset, feedforward_lookup_share, feedforward_gate_share, feedforward_lookup_matrix, feedforward_payload_matrix, feedforward_gate_matrix)))

    def forward(tokens_all, *parameter_bundle):
        grouped = tokens_all.reshape(GROUPS, GROUP, EMBED_DIM)

        def one_group(inputs):
            return group_block(inputs, parameter_bundle)
        outputs = lax.map(jax.checkpoint(one_group), (grouped, packed_spans, filler_tallies))
        return outputs.reshape(TOKENS, EMBED_DIM)
    real_rows = jax.vmap(row_mask)(packed_spans, filler_tallies).reshape(TOKENS)
    layer_outcome, pullback = jax.vjp(forward, layer_entry.astype(jnp.float32), *coefficient_set)
    grads = pullback(upstream_gradient.astype(jnp.float32) * real_rows[:, None])
    return (layer_outcome.astype(jnp.bfloat16), grads[0].astype(jnp.bfloat16), grads[1], grads[2], grads[3], grads[4], grads[5], grads[6], grads[7], grads[8], grads[9], grads[10], grads[11], grads[12], grads[13], grads[14], grads[15], grads[16], grads[17], grads[18])
```

```python
import functools

import jax
import jax.numpy as jnp
from jax import lax
from jax.experimental import pallas as pl
from jax.experimental.pallas import tpu as pltpu
from jax.sharding import PartitionSpec as P

F32, BF16 = jnp.float32, jnp.bfloat16
LANES = 128
TILE = 64
MIB = 1 << 20
VMEM = pl.BlockSpec(memory_space=pltpu.VMEM)
SMEM = pl.BlockSpec(memory_space=pltpu.SMEM)
ANY = pl.BlockSpec(memory_space=pl.ANY)
G1, B1, SK, SV, SR, G2, B2, FK, FR = range(9)


def sds(shape, dtype):
    return jax.ShapeDtypeStruct(shape, dtype)


def params(limit_mib):
    return pltpu.CompilerParams(vmem_limit_bytes=limit_mib * MIB)


def dot(a, b):
    return jnp.dot(a, b, preferred_element_type=F32)


def dot_t(a, b):
    return lax.dot_general(a, b, (((1,), (1,)), ((), ())), preferred_element_type=F32)


def t_dot(a, b):
    return lax.dot_general(a, b, (((0,), (0,)), ((), ())), preferred_element_type=F32)


def fold8(v):
    return jnp.sum(v.reshape(v.shape[0] // 8, 8, v.shape[1]), axis=0)


def normalized(v):
    center = v - jnp.mean(v, axis=-1, keepdims=True)
    inv = lax.rsqrt(jnp.mean(center * center, axis=-1, keepdims=True) + 1e-05)
    return center * inv, inv


def norm_back(d_hat, hat, inv):
    return inv * (
        d_hat
        - jnp.mean(d_hat, axis=-1, keepdims=True)
        - hat * jnp.mean(d_hat * hat, axis=-1, keepdims=True)
    )


def marks(first, rows, spans, pads):
    pos = first + lax.broadcasted_iota(jnp.int32, (rows, LANES), 0)
    begin = jnp.int32(0)
    start, real = pos < 0, pos < 0
    for i in range(spans.shape[1]):
        length = spans[0, i]
        start = start | (pos == begin)
        real = real | ((pos >= begin) & (pos < begin + length - pads[0, i]))
        begin = begin + length
    return start, real


def first_start_from(spans, at, otherwise):
    begin, best = jnp.int32(0), jnp.int32(otherwise)
    for i in range(spans.shape[1]):
        best = jnp.where((begin >= at) & (begin < best), begin, best)
        begin = begin + spans[0, i]
    return best


def last_start_before(spans, at):
    begin, best = jnp.int32(0), jnp.int32(-(1 << 20))
    for i in range(spans.shape[1]):
        best = jnp.where(begin < at, begin, best)
        begin = begin + spans[0, i]
    return best


def wide(flag, width):
    return jnp.concatenate([flag] * (width // LANES), axis=1)


def with_previous(ref, at):
    block = ref[pl.ds(at, TILE + 8)]
    return block[8:], block[7 : TILE + 7]


def columns(j):
    return slice(j * LANES, (j + 1) * LANES)


def gather_carry(hops, rows, carry_ref, counts, rate):
    a, b = carry_ref[0], carry_ref[1]
    for h in range(1, hops):
        scale = jnp.exp(-rate * float(rows * h)) * counts[h]
        a, b = a + scale * carry_ref[2 * h], b + scale * carry_ref[2 * h + 1]
    return a, b


def project_kernel(
    base, x_ref, xprev_ref, vec_ref, rate_ref, spans, pads, keep_s, wk_hbm, wv_hbm, wr_hbm,
    xk_ref, xv_ref, xr_ref, k_ref, v_ref, r_ref, at_ref, bt_ref, end_ref,
    h_scr, ek_scr, ev_scr, w_scr, sems,
):
    rows, width = x_ref.shape
    blocks = width // LANES
    copies = [
        pltpu.make_async_copy(hbm, w_scr.at[i], sems.at[i])
        for i, hbm in enumerate((wk_hbm, wv_hbm, wr_hbm))
    ]
    for copy in copies:
        copy.start()
    first = base()
    gain, bias = vec_ref[G1 : G1 + 1], vec_ref[B1 : B1 + 1]
    prev = xprev_ref[...].astype(F32)
    h_scr[0:8] = normalized(prev)[0] * gain + bias

    @pl.loop(0, rows // TILE)
    def _(i):
        at = pl.multiple_of(i * TILE, TILE)
        hat, _ = normalized(x_ref[pl.ds(at, TILE)].astype(F32))
        h_scr[pl.ds(at + 8, TILE)] = hat * gain + bias

    @pl.loop(0, rows // TILE)
    def _(i):
        at = pl.multiple_of(i * TILE, TILE)
        start, _ = marks(first + at, TILE, spans, pads)
        keep = wide(1.0 - start.astype(F32), width)
        h, p = with_previous(h_scr, at)
        p = p * keep
        for row, out in ((SK, xk_ref), (SV, xv_ref), (SR, xr_ref)):
            share = vec_ref[row : row + 1]
            out[pl.ds(at, TILE)] = (h * share + p * (1.0 - share)).astype(BF16)

    _, real = marks(first, rows, spans, pads)
    real = real.astype(F32)
    step = 256
    for i, (src, out) in enumerate(((xk_ref, k_ref), (xv_ref, v_ref), (xr_ref, r_ref))):
        copies[i].wait()
        for j in range(width // step):
            tile = dot(src[...], w_scr[i, :, j * step : (j + 1) * step])
            out[:, j * step : (j + 1) * step] = tile.astype(out.dtype)
    for j in range(blocks):
        ek = jnp.exp(k_ref[:, columns(j)].astype(F32)) * real
        ek_scr[pl.ds(j, rows, stride=blocks)] = ek
        ev_scr[pl.ds(j, rows, stride=blocks)] = ek * v_ref[:, columns(j)].astype(F32)
    decay = jnp.exp(-jnp.exp(rate_ref[0:blocks]))

    def scan(t8, carry):
        a, b = carry
        for u in range(8):
            t = t8 * 8 + u
            keep = keep_s[t]
            here = pl.ds(pl.multiple_of(t * blocks, blocks), blocks)
            at_ref[here] = a * keep
            bt_ref[here] = b * keep
            fade = decay * keep
            a = a * fade + ev_scr[here]
            b = b * fade + ek_scr[here]
        return a, b

    zero = jnp.zeros((blocks, LANES), F32)
    a, b = lax.fori_loop(0, rows // 8, scan, (zero, zero))
    end_ref[0] = a
    end_ref[1] = b


def project(base, x, xprev, vecs, rates, spans, pads, keep, wk, wv, wr):
    rows, width = x.shape
    shape = (rows, width)
    tall = (rows * (width // LANES), LANES)
    return pl.pallas_call(
        functools.partial(project_kernel, base),
        out_shape=(
            [sds(shape, BF16)] * 5 + [sds(shape, F32)] + [sds(tall, F32)] * 2 + [sds((2, width // LANES, LANES), F32)]
        ),
        in_specs=[VMEM] * 4 + [SMEM] * 3 + [ANY] * 3,
        out_specs=[VMEM] * 9,
        scratch_shapes=[
            pltpu.VMEM((rows + 8, width), F32),
            pltpu.VMEM(tall, F32),
            pltpu.VMEM(tall, F32),
            pltpu.VMEM((3, width, width), BF16),
            pltpu.SemaphoreType.DMA((3,)),
        ],
        compiler_params=params(56),
        name="project",
    )(x, xprev, vecs, rates, spans, pads, keep, wk, wv, wr)


def wkv_parts(at, j, rows, blocks, k, v, at_ref, bt_ref, a_in, b_in, rate, boost, first_start):
    here = pl.ds(at * blocks + j, rows, stride=blocks)
    pos = at + lax.broadcasted_iota(jnp.int32, (rows, LANES), 0)
    lift = jnp.where(pos < first_start, jnp.exp(-rate[j : j + 1] * pos.astype(F32)), 0.0)
    a = at_ref[here] + lift * a_in[j : j + 1]
    b = bt_ref[here] + lift * b_in[j : j + 1]
    eu = jnp.exp(boost[j : j + 1] + k)
    inv = 1.0 / (b + eu)
    return a, b, eu, inv, (a + eu * v) * inv


def carry_counts(hops, rows, first, spans):
    last = last_start_before(spans, first)
    return [jnp.where(last < first - h * rows, 1.0, 0.0) for h in range(hops)]


def exit_kernel(
    base, hops, x_ref, k_ref, v_ref, r_ref, at_ref, bt_ref, carry_ref, rate_ref, vec_ref, spans, wo_hbm,
    wkv_ref, gated_ref, middle_ref, last_ref, in_ref, wo_scr, sem,
):
    rows, width = x_ref.shape
    blocks = width // LANES
    copy = pltpu.make_async_copy(wo_hbm, wo_scr, sem)
    copy.start()
    first = base()
    rate = jnp.exp(rate_ref[0:blocks])
    boost = rate_ref[blocks : 2 * blocks]
    a_in, b_in = gather_carry(hops, rows, carry_ref, carry_counts(hops, rows, first, spans), rate)
    in_ref[0] = a_in
    in_ref[1] = b_in
    first_start = first_start_from(spans, first, 1 << 20) - first

    @pl.loop(0, rows // TILE)
    def _(i):
        at = pl.multiple_of(i * TILE, TILE)
        for j in range(blocks):
            here = (pl.ds(at, TILE), columns(j))
            k, v = k_ref[here].astype(F32), v_ref[here].astype(F32)
            wkv = wkv_parts(at, j, TILE, blocks, k, v, at_ref, bt_ref, a_in, b_in, rate, boost, first_start)[-1]
            wkv = wkv.astype(BF16)
            wkv_ref[here] = wkv
            gated_ref[here] = (jax.nn.sigmoid(r_ref[here]) * wkv.astype(F32)).astype(BF16)

    copy.wait()
    step = 256
    for j in range(width // step):
        here = (slice(None), slice(j * step, (j + 1) * step))
        middle_ref[here] = x_ref[here].astype(F32) + dot(gated_ref[...], wo_scr[here])
    hat, _ = normalized(middle_ref[rows - 8 : rows])
    last_ref[...] = hat * vec_ref[G2 : G2 + 1] + vec_ref[B2 : B2 + 1]


def exit_call(base, hops, x, k, v, r, at, bt, carry, rates, vecs, spans, wo):
    rows, width = x.shape
    blocks = width // LANES
    return pl.pallas_call(
        functools.partial(exit_kernel, base, hops),
        out_shape=[
            sds((rows, width), BF16),
            sds((rows, width), BF16),
            sds((rows, width), F32),
            sds((8, width), F32),
            sds((2, blocks, LANES), F32),
        ],
        in_specs=[VMEM] * 9 + [SMEM, ANY],
        out_specs=[VMEM] * 5,
        scratch_shapes=[pltpu.VMEM((width, width), BF16), pltpu.SemaphoreType.DMA(())],
        compiler_params=params(56),
        name="exit",
    )(x, k, v, r, at, bt, carry, rates, vecs, spans, wo)


def ffn_kernel(
    base, mid_ref, g_ref, hprev_ref, vec_ref, spans, pads, wg_ref, wk_ref, wv_ref,
    out_ref, gfk_ref, gfv_ref, gfr_ref, dh_ref, back_ref, sums_ref,
    h_scr, ck_scr, cr_scr, ckt_scr, sig_scr, dvo_scr, val_scr, dck_scr, pass_scr,
):
    rows, width = mid_ref.shape
    step = pl.program_id(0)
    first = base()
    tiles = rows // TILE

    @pl.when(step == 0)
    def _():
        gain, bias = vec_ref[G2 : G2 + 1], vec_ref[B2 : B2 + 1]
        h_scr[0:8] = hprev_ref[...]

        @pl.loop(0, tiles)
        def _(i):
            at = pl.multiple_of(i * TILE, TILE)
            hat, _ = normalized(mid_ref[pl.ds(at, TILE)])
            h_scr[pl.ds(at + 8, TILE)] = hat * gain + bias

        @pl.loop(0, tiles)
        def _(i):
            at = pl.multiple_of(i * TILE, TILE)
            start, _ = marks(first + at, TILE, spans, pads)
            keep = wide(1.0 - start.astype(F32), width)
            h, p = with_previous(h_scr, at)
            p = p * keep
            for row, out in ((FK, ck_scr), (FR, cr_scr)):
                share = vec_ref[row : row + 1]
                out[pl.ds(at, TILE)] = (h * share + p * (1.0 - share)).astype(BF16)

        ckt_scr[...] = ck_scr[...].T
        _, real = marks(first, rows, spans, pads)
        real = wide(real.astype(F32), 256)
        for j in range(width // 256):
            here = (slice(None), slice(j * 256, (j + 1) * 256))
            sig = jax.nn.sigmoid(dot(cr_scr[...], wg_ref[here]))
            sig_scr[here] = sig
            dvo_scr[here] = (g_ref[here].astype(F32) * real * sig).astype(BF16)
        val_scr[...] = jnp.zeros_like(val_scr)
        dck_scr[...] = jnp.zeros_like(dck_scr)

    act = jnp.maximum(dot(ck_scr[...], wk_ref[...]), 0.0)
    hidden = (act * act).astype(BF16)
    val_scr[...] += dot(hidden, wv_ref[...])
    gfv_ref[...] = t_dot(hidden, dvo_scr[...]).astype(BF16)
    d_pre = (dot_t(dvo_scr[...], wv_ref[...]) * (2.0 * act)).astype(BF16)
    gfk_ref[...] = dot(ckt_scr[...], d_pre).astype(BF16)
    dck_scr[...] += dot_t(d_pre, wk_ref[...])

    @pl.when(step == pl.num_programs(0) - 1)
    def _():
        dgp_scr = dvo_scr
        _, real = marks(first, rows, spans, pads)
        real = wide(real.astype(F32), 256)
        for j in range(width // 256):
            here = (slice(None), slice(j * 256, (j + 1) * 256))
            sig, value = sig_scr[here], val_scr[here]
            out_ref[here] = (mid_ref[here] + sig * value).astype(BF16)
            top = g_ref[here].astype(F32) * real
            dgp_scr[here] = (top * value * sig * (1.0 - sig)).astype(BF16)
        for j in range(width // 256):
            here = (slice(None), slice(j * 256, (j + 1) * 256))
            gfr_ref[here] = t_dot(cr_scr[...], dgp_scr[here]).astype(BF16)
        dcr_scr = val_scr
        for j in range(width // 256):
            dcr_scr[:, j * 256 : (j + 1) * 256] = dot_t(dgp_scr[...], wg_ref[j * 256 : (j + 1) * 256])
        sums_ref[...] = jnp.zeros_like(sums_ref)
        share_k, share_r = vec_ref[FK : FK + 1], vec_ref[FR : FR + 1]

        @pl.loop(0, tiles)
        def _(i):
            at = pl.multiple_of(i * TILE, TILE)
            here = pl.ds(at, TILE)
            start, _ = marks(first + at, TILE, spans, pads)
            keep = wide(1.0 - start.astype(F32), width)
            h, p = with_previous(h_scr, at)
            diff = h - p * keep
            dck, dcr = dck_scr[here], dcr_scr[here]
            sums_ref[0] += fold8(diff * dck)
            sums_ref[1] += fold8(diff * dcr)
            pass_scr[here] = (dck * (1.0 - share_k) + dcr * (1.0 - share_r)) * keep
            dh_ref[here] = dck * share_k + dcr * share_r

        back_ref[...] = pass_scr[0:8]

        pass_scr[rows : rows + 8] = jnp.zeros((8, width), F32)

        @pl.loop(0, tiles)
        def _(i):
            at = pl.multiple_of(i * TILE, TILE)
            dh_ref[pl.ds(at, TILE)] += pass_scr[pl.ds(at, TILE + 8)][1 : TILE + 1]


def ffn(base, middle, g, hprev, vecs, spans, pads, wg, wk, wv):
    rows, width = middle.shape
    hid = wk.shape[1]
    unit = 512
    full = lambda shape: pl.BlockSpec(shape, lambda j: (0,) * len(shape))
    return pl.pallas_call(
        functools.partial(ffn_kernel, base),
        grid=(hid // unit,),
        out_shape=[
            sds((rows, width), BF16),
            sds((width, hid), BF16),
            sds((hid, width), BF16),
            sds((width, width), BF16),
            sds((rows, width), F32),
            sds((8, width), F32),
            sds((2, 8, width), F32),
        ],
        in_specs=[
            full((rows, width)),
            full((rows, width)),
            full((8, width)),
            full(vecs.shape),
            SMEM,
            SMEM,
            full((width, width)),
            pl.BlockSpec((width, unit), lambda j: (0, j)),
            pl.BlockSpec((unit, width), lambda j: (j, 0)),
        ],
        out_specs=[
            full((rows, width)),
            pl.BlockSpec((width, unit), lambda j: (0, j)),
            pl.BlockSpec((unit, width), lambda j: (j, 0)),
            full((width, width)),
            full((rows, width)),
            full((8, width)),
            full((2, 8, width)),
        ],
        scratch_shapes=[
            pltpu.VMEM((rows + 8, width), F32),
            pltpu.VMEM((rows, width), BF16),
            pltpu.VMEM((rows, width), BF16),
            pltpu.VMEM((width, rows), BF16),
            pltpu.VMEM((rows, width), F32),
            pltpu.VMEM((rows, width), BF16),
            pltpu.VMEM((rows, width), F32),
            pltpu.VMEM((rows, width), F32),
            pltpu.VMEM((rows + 8, width), F32),
        ],
        compiler_params=params(60),
        name="ffn",
    )(middle, g, hprev, vecs, spans, pads, wg, wk, wv)


def exit_back_kernel(
    base, mid_ref, g_ref, dh_ref, dhnext_ref, vec_ref, rate_ref, gated_ref, wkv_ref, r_ref, k_ref, v_ref, at_ref, bt_ref,
    in_ref, spans, pads, keep_s, wo_ref,
    dmid_ref, gwo_ref, dwkv_ref, dr_ref, sums_ref, adja_ref, adjb_ref, adjend_ref,
    datt_scr, dn_scr, dd_scr,
):
    rows, width = mid_ref.shape
    blocks = width // LANES
    first = base()
    gain = vec_ref[G2 : G2 + 1]
    sums_ref[...] = jnp.zeros_like(sums_ref)
    tail = dhnext_ref[...]
    row = lax.broadcasted_iota(jnp.int32, tail.shape, 0)
    dh_ref[rows - 8 : rows] += jnp.where(row == 7, pltpu.roll(tail, 7, axis=0), 0.0)

    @pl.loop(0, rows // TILE)
    def _(i):
        at = pl.multiple_of(i * TILE, TILE)
        here = pl.ds(at, TILE)
        _, real = marks(first + at, TILE, spans, pads)
        hat, inv = normalized(mid_ref[here])
        dh = dh_ref[here]
        sums_ref[0] += fold8(dh * hat)
        sums_ref[1] += fold8(dh)
        d_mid = norm_back(dh * gain, hat, inv) + g_ref[here].astype(F32) * wide(real.astype(F32), width)
        dmid_ref[here] = d_mid
        datt_scr[here] = d_mid.astype(BF16)

    step = 256
    rate = jnp.exp(rate_ref[0:blocks])
    boost = rate_ref[blocks : 2 * blocks]
    a_in, b_in = in_ref[0], in_ref[1]
    first_start = first_start_from(spans, first, 1 << 20) - first
    for j in range(width // step):
        here = (slice(None), slice(j * step, (j + 1) * step))
        dr_ref[here] = dot_t(datt_scr[...], wo_ref[j * step : (j + 1) * step]).astype(BF16)
    d_gated = dr_ref

    @pl.loop(0, rows // TILE)
    def _(i):
        at = pl.multiple_of(i * TILE, TILE)
        for j in range(blocks):
            here = (pl.ds(at, TILE), columns(j))
            sig = jax.nn.sigmoid(r_ref[here])
            dg = d_gated[here].astype(F32)
            dwkv = (dg * sig).astype(BF16)
            dwkv_ref[here] = dwkv
            dr_ref[here] = (dg * wkv_ref[here].astype(F32) * sig * (1.0 - sig)).astype(BF16)
            k, v = k_ref[here].astype(F32), v_ref[here].astype(F32)
            _, _, _, inv, wkv = wkv_parts(
                at, j, TILE, blocks, k, v, at_ref, bt_ref, a_in, b_in, rate, boost, first_start
            )
            dn = dwkv.astype(F32) * inv
            there = pl.ds(at * blocks + j, TILE, stride=blocks)
            dn_scr[there] = dn
            dd_scr[there] = -dn * wkv

    decay = jnp.exp(-rate)

    def scan(t8, carry):
        a, b = carry
        for u in range(8):
            t = rows - 1 - (t8 * 8 + u)
            keep = keep_s[t]
            here = pl.ds(pl.multiple_of(t * blocks, blocks), blocks)
            adja_ref[here] = a
            adjb_ref[here] = b
            fade = decay * keep
            a = a * fade + dn_scr[here] * keep
            b = b * fade + dd_scr[here] * keep
        return a, b

    zero = jnp.zeros((blocks, LANES), F32)
    a, b = lax.fori_loop(0, rows // 8, scan, (zero, zero))
    adjend_ref[0] = a
    adjend_ref[1] = b
    for j in range(width // step):
        here = (slice(None), slice(j * step, (j + 1) * step))
        gwo_ref[here] = t_dot(gated_ref[...], datt_scr[here]).astype(BF16)


def exit_back(base, middle, g, dh, dhnext, vecs, rates, gated, wkv, r, k, v, at, bt, carry, spans, pads, keep, wo):
    rows, width = middle.shape
    blocks = width // LANES
    tall = (rows * blocks, LANES)
    return pl.pallas_call(
        functools.partial(exit_back_kernel, base),
        out_shape=[
            sds((rows, width), F32),
            sds((width, width), BF16),
            sds((rows, width), BF16),
            sds((rows, width), BF16),
            sds((2, 8, width), F32),
            sds(tall, F32),
            sds(tall, F32),
            sds((2, blocks, LANES), F32),
        ],
        in_specs=[VMEM] * 14 + [SMEM] * 3 + [VMEM],
        out_specs=[VMEM] * 8,
        scratch_shapes=[
            pltpu.VMEM((rows, width), BF16),
            pltpu.VMEM(tall, F32),
            pltpu.VMEM(tall, F32),
        ],
        compiler_params=params(60),
        name="exit_back",
    )(middle, g, dh, dhnext, vecs, rates, gated, wkv, r, k, v, at, bt, carry, spans, pads, keep, wo)


def project_back_kernel(
    base, hops, total, x_ref, xprev_ref, vec_ref, rate_ref, k_ref, v_ref, dwkv_ref, dr_ref, at_ref, bt_ref, in_ref,
    adja_ref, adjb_ref, adj_ref, xk_ref, xv_ref, xr_ref, spans, pads, wk_hbm, wv_hbm, wr_hbm,
    gwk_ref, gwv_ref, gwr_ref, dh_ref, back_ref, sums_ref, wsums_ref,
    h_scr, dk_scr, dv_scr, d_scr, pass_scr, w_scr, sems,
):
    rows, width = x_ref.shape
    blocks = width // LANES
    copies = [
        pltpu.make_async_copy(hbm, w_scr.at[i], sems.at[i])
        for i, hbm in enumerate((wk_hbm, wv_hbm, wr_hbm))
    ]
    for copy in copies:
        copy.start()
    first = base()
    rate = jnp.exp(rate_ref[0:blocks])
    boost = rate_ref[blocks : 2 * blocks]
    a_in, b_in = in_ref[0], in_ref[1]
    first_start = first_start_from(spans, first, 1 << 20) - first
    last_start = last_start_before(spans, first + rows) - first
    after = first_start_from(spans, first + rows, total)
    counts = [jnp.where(after >= first + (h + 1) * rows, 1.0, 0.0) for h in range(hops)]
    adj_a, adj_b = gather_carry(hops, rows, adj_ref, counts, rate)
    wsums_ref[...] = jnp.zeros_like(wsums_ref)
    sums_ref[...] = jnp.zeros_like(sums_ref)

    @pl.loop(0, rows // TILE)
    def _(i):
        at = pl.multiple_of(i * TILE, TILE)
        _, real = marks(first + at, TILE, spans, pads)
        real = real.astype(F32)
        pos = at + lax.broadcasted_iota(jnp.int32, (TILE, LANES), 0)
        for j in range(blocks):
            here = (pl.ds(at, TILE), columns(j))
            k, v = k_ref[here].astype(F32), v_ref[here].astype(F32)
            a, b, eu, inv, wkv = wkv_parts(
                at, j, TILE, blocks, k, v, at_ref, bt_ref, a_in, b_in, rate, boost, first_start
            )
            there = pl.ds(at * blocks + j, TILE, stride=blocks)
            lift = jnp.where(
                pos >= last_start, jnp.exp(-rate[j : j + 1] * (rows - 1 - pos).astype(F32)), 0.0
            )
            post_a = adja_ref[there] + lift * adj_a[j : j + 1]
            post_b = adjb_ref[there] + lift * adj_b[j : j + 1]
            dn = dwkv_ref[here].astype(F32) * inv
            own = eu * dn
            weight = jnp.exp(k) * real
            dv_scr[here] = (own + weight * post_a).astype(BF16)
            first_term = own * (v - wkv)
            dk_scr[here] = (first_term + weight * (v * post_a + post_b)).astype(BF16)
            wsums_ref[0, :, columns(j)] += fold8(a * post_a + b * post_b)
            wsums_ref[1, :, columns(j)] += fold8(first_term)

    for j in range(blocks):
        r = rate[j : j + 1]
        wsums_ref[0, :, columns(j)] *= -r * jnp.exp(-r)
    gain, bias = vec_ref[G1 : G1 + 1], vec_ref[B1 : B1 + 1]
    h_scr[0:8] = normalized(xprev_ref[...].astype(F32))[0] * gain + bias

    @pl.loop(0, rows // TILE)
    def _(i):
        at = pl.multiple_of(i * TILE, TILE)
        hat, _ = normalized(x_ref[pl.ds(at, TILE)].astype(F32))
        h_scr[pl.ds(at + 8, TILE)] = hat * gain + bias

    step = 256
    dh_ref[...] = jnp.zeros_like(dh_ref)
    groups = ((dk_scr, xk_ref, gwk_ref, SK), (dv_scr, xv_ref, gwv_ref, SV), (dr_ref, xr_ref, gwr_ref, SR))
    pass_scr[...] = jnp.zeros_like(pass_scr)
    for i, (grad, mixed, out, row) in enumerate(groups):
        copies[i].wait()
        for j in range(width // step):
            here = (slice(None), slice(j * step, (j + 1) * step))
            d_scr[:, j * step : (j + 1) * step] = dot_t(grad[...], w_scr[i, j * step : (j + 1) * step])
            out[here] = t_dot(mixed[...], grad[here]).astype(BF16)
        share = vec_ref[row : row + 1]

        @pl.loop(0, rows // TILE)
        def _(t):
            at = pl.multiple_of(t * TILE, TILE)
            here = pl.ds(at, TILE)
            start, _ = marks(first + at, TILE, spans, pads)
            keep = wide(1.0 - start.astype(F32), width)
            h, p = with_previous(h_scr, at)
            d = d_scr[here]
            sums_ref[i] += fold8((h - p * keep) * d)
            pass_scr[here] += d * (1.0 - share) * keep
            dh_ref[here] += d * share

    back_ref[...] = pass_scr[0:8]

    @pl.loop(0, rows // TILE)
    def _(i):
        at = pl.multiple_of(i * TILE, TILE)
        dh_ref[pl.ds(at, TILE)] += pass_scr[pl.ds(at, TILE + 8)][1 : TILE + 1]


def project_back(base, hops, total, x, xprev, vecs, rates, k, v, dwkv, dr, at, bt, carry, adja, adjb, adj, xk, xv, xr, spans, pads, wk, wv, wr):
    rows, width = x.shape
    return pl.pallas_call(
        functools.partial(project_back_kernel, base, hops, total),
        out_shape=[sds((width, width), BF16)] * 3
        + [
            sds((rows, width), F32),
            sds((8, width), F32),
            sds((3, 8, width), F32),
            sds((2, 8, width), F32),
        ],
        in_specs=[VMEM] * 17 + [SMEM] * 2 + [ANY] * 3,
        out_specs=[VMEM] * 7,
        scratch_shapes=[
            pltpu.VMEM((rows + 8, width), F32),
            pltpu.VMEM((rows, width), BF16),
            pltpu.VMEM((rows, width), BF16),
            pltpu.VMEM((rows, width), F32),
            pltpu.VMEM((rows + 8, width), F32),
            pltpu.VMEM((3, width, width), BF16),
            pltpu.SemaphoreType.DMA((3,)),
        ],
        compiler_params=params(60),
        name="project_back",
    )(x, xprev, vecs, rates, k, v, dwkv, dr, at, bt, carry, adja, adjb, adj, xk, xv, xr, spans, pads, wk, wv, wr)


def entry_back_kernel(x_ref, dh_ref, dhnext_ref, dmid_ref, vec_ref, out_ref, sums_ref):
    rows = x_ref.shape[0]
    gain = vec_ref[G1 : G1 + 1]
    sums_ref[...] = jnp.zeros_like(sums_ref)
    tail = dhnext_ref[...]
    row = lax.broadcasted_iota(jnp.int32, tail.shape, 0)
    dh_ref[rows - 8 : rows] += jnp.where(row == 7, pltpu.roll(tail, 7, axis=0), 0.0)

    @pl.loop(0, rows // TILE)
    def _(i):
        here = pl.ds(pl.multiple_of(i * TILE, TILE), TILE)
        hat, inv = normalized(x_ref[here].astype(F32))
        dh = dh_ref[here]
        sums_ref[0] += fold8(dh * hat)
        sums_ref[1] += fold8(dh)
        out_ref[here] = (norm_back(dh * gain, hat, inv) + dmid_ref[here]).astype(BF16)


def entry_back(x, dh, dhnext, dmid, vecs):
    rows, width = x.shape
    return pl.pallas_call(
        entry_back_kernel,
        out_shape=[sds((rows, width), BF16), sds((2, 8, width), F32)],
        in_specs=[VMEM] * 5,
        out_specs=[VMEM] * 2,
        compiler_params=params(40),
        name="entry_back",
    )(x, dh, dhnext, dmid, vecs)


X, Y, Z = "x", "y", "z"
ORDERS = {
    X: ("x", "y", "low", "high"),
    Y: ("y", "x", "low", "high"),
    Z: ("low", "high", "x", "y"),
}
AXIS_BIT = {"core": ("seq", 1), "x": ("seq", 2), "y": ("chan", 1), "low": ("chan", 2), "high": ("chan", 4)}
STEPS = 5
MESH = pl.DeviceIdType.MESH


def bit_of(index, weight):
    return index // weight % 2


def partner(axis):
    name, weight = AXIS_BIT[axis]
    where = {"seq": lax.axis_index("seq"), "chan": lax.axis_index("chan")}
    bit = bit_of(where[name], weight)
    where[name] = where[name] + weight * (1 - 2 * bit)
    return bit, (where["seq"], where["chan"])


def summing_kernel(plan, parts, *refs):
    count = len(parts)
    grads, refs = refs[:count], refs[count:]
    outs, refs = refs[:count], refs[count:]
    received, refs = refs[:count], refs[count:]
    buffers = [refs[i * 6 : i * 6 + 6] for i in range(2)]
    send_sems, recv_sems, stage_sems = refs[12:]
    sides = {axis: partner(axis) for axis in AXIS_BIT}
    core, core_mate = sides["core"]

    barrier = pltpu.get_barrier_semaphore()
    for _, mate in sides.values():
        pl.semaphore_signal(barrier, inc=1, device_id=mate, device_id_type=MESH)
    pl.semaphore_wait(barrier, len(sides))

    chunks = [chunk for tick in plan for chunk in tick]
    starts = [sum(len(t) for t in plan[:i]) for i in range(len(plan) + 1)]

    def across(number):
        part, first, rows, _ = chunks[number]
        return pltpu.make_async_remote_copy(
            src_ref=grads[part].at[:, 1 - core, first : first + rows],
            dst_ref=received[part].at[:, first : first + rows],
            send_sem=send_sems.at[number, 0],
            recv_sem=recv_sems.at[number, 0],
            device_id=core_mate,
            device_id_type=MESH,
        )

    def stages(number):
        part, first, rows, _ = chunks[number]
        stage = buffers[parts[part][0]][0].at[number % 4]
        own = pltpu.make_async_copy(
            grads[part].at[:, core, first : first + rows], stage.at[0, :, 0:rows], stage_sems.at[number % 4, 0]
        )
        other = pltpu.make_async_copy(
            received[part].at[:, first : first + rows], stage.at[1, :, 0:rows], stage_sems.at[number % 4, 1]
        )
        return own, other

    def send(number, step):
        part, first, rows, stream = chunks[number]
        which, base = parts[part]
        here = pl.ds(base + first, rows)
        bit, mate = sides[ORDERS[stream][step - 1]]
        source, target = buffers[which][step], buffers[which][step + 1]
        free = (slice(None),) * (4 - step)
        return pltpu.make_async_remote_copy(
            src_ref=source.at[(1 - bit, *free, here)],
            dst_ref=target.at[(*free, here)],
            send_sem=send_sems.at[number, step],
            recv_sem=recv_sems.at[number, step],
            device_id=mate,
            device_id_type=MESH,
        )

    def start_stage(number):
        across(number).wait_recv()
        for copy in stages(number):
            copy.start()

    def first_sum(number):
        part, first, rows, stream = chunks[number]
        which, base = parts[part]
        stage, target = buffers[which][0], buffers[which][1]
        width = target.shape[-1]
        for copy in stages(number):
            copy.wait()

        @pl.loop(0, 16)
        def _(i):
            c = i % 8
            bits = {"x": i // 8, "y": c % 2, "low": c // 2 % 2, "high": c // 4}
            cols = pl.ds(pl.multiple_of(c * width, LANES), width)
            total = stage[number % 4, 0, i // 8, 0:rows, cols].astype(F32) + stage[
                number % 4, 1, i // 8, 0:rows, cols
            ].astype(F32)
            at = tuple(bits[axis] for axis in ORDERS[stream])
            target[(*at, pl.ds(base + first, rows))] = total.astype(BF16)

        send(number, 1).start()

    def later_sum(number, step):
        part, first, rows, stream = chunks[number]
        which, base = parts[part]
        here = pl.ds(base + first, rows)
        bit, _ = sides[ORDERS[stream][step - 1]]
        source, target = buffers[which][step], buffers[which][step + 1]
        send(number, step).wait_recv()
        if step == 4:
            outs[part][first : first + rows] = source[bit, here].astype(F32) + target[here].astype(F32)
            return
        many = 1 << (4 - step)

        @pl.loop(0, many)
        def _(i):
            at = tuple(i // (1 << (3 - step - d)) % 2 for d in range(4 - step))
            total = source[(bit, *at, here)].astype(F32) + target[(*at, here)].astype(F32)
            target[(*at, here)] = total.astype(BF16)

        send(number, step + 1).start()

    ticks = len(plan)
    for number in range(starts[min(2, ticks)]):
        across(number).start()
    for number in range(starts[1]):
        start_stage(number)
    for tick in range(ticks + 4):
        if tick + 2 < ticks:
            for number in range(starts[tick + 2], starts[tick + 3]):
                across(number).start()
        if tick < ticks:
            for number in range(starts[tick], starts[tick + 1]):
                first_sum(number)
        for step in range(1, 5):
            if 0 <= tick - step < ticks:
                for number in range(starts[tick - step], starts[tick - step + 1]):
                    later_sum(number, step)
            if step == 1 and tick + 1 < ticks:
                for number in range(starts[tick + 1], starts[tick + 2]):
                    start_stage(number)
    for number in range(len(chunks)):
        across(number).wait_send()
        for step in range(1, STEPS):
            send(number, step).wait_send()


def sum_plan():
    return [
        [(0, 0, 208, X), (0, 400, 208, Y), (0, 800, 112, Z)],
        [(0, 208, 192, X), (0, 608, 192, Y), (0, 912, 112, Z)],
        [(1, 0, 48, X), (1, 96, 48, Y), (1, 192, 32, Z)],
        [(1, 48, 48, X), (1, 144, 48, Y), (1, 224, 32, Z)],
        [(3, 0, 256, X), (5, 0, 256, Y), (2, 0, 128, Z)],
        [(4, 0, 256, X), (6, 0, 256, Y), (2, 128, 128, Z), (7, 0, 16, Y)],
    ]


def sum_arrays(grads):
    blocks = [g.reshape(2, 2, g.shape[0] // 4, g.shape[1]) for g in grads]
    narrow = min(b.shape[3] for b in blocks)
    wide_ = max(b.shape[3] for b in blocks)
    parts, filled = [], [0, 0]
    for b in blocks:
        which = int(b.shape[3] != narrow)
        parts.append((which, filled[which]))
        filled[which] += b.shape[2]
    plan = sum_plan()
    most = [0, 0]
    for tick in plan:
        for part, _, rows, _ in tick:
            most[parts[part][0]] = max(most[parts[part][0]], rows)
    scratch = []
    for which, full in enumerate((narrow, wide_)):
        scratch.append(pltpu.VMEM((4, 2, 2, most[which], full), BF16))
        scratch += [pltpu.VMEM((2,) * (4 - d) + (filled[which], full // 8), BF16) for d in range(5)]
    count = sum(len(tick) for tick in plan)
    result = pl.pallas_call(
        functools.partial(summing_kernel, plan, parts),
        out_shape=[sds((b.shape[2], b.shape[3] // 8), F32) for b in blocks]
        + [sds((2,) + b.shape[2:], BF16) for b in blocks],
        in_specs=[ANY] * len(blocks),
        out_specs=[VMEM] * len(blocks) + [ANY] * len(blocks),
        scratch_shapes=scratch
        + [
            pltpu.SemaphoreType.DMA((count, STEPS)),
            pltpu.SemaphoreType.DMA((count, STEPS)),
            pltpu.SemaphoreType.DMA((4, 2)),
        ],
        compiler_params=pltpu.CompilerParams(
            vmem_limit_bytes=60 * MIB, collective_id=0, has_side_effects=True
        ),
        name="sum_weights",
    )(*blocks)
    return result[: len(blocks)]


def shift(value, steps):
    count = lax.axis_size("chan")
    pairs = [(i, i + steps) for i in range(count) if 0 <= i + steps < count]
    return lax.ppermute(value, "chan", pairs)


def scatter_sums(mats, vecs):
    seqs, chans, width = lax.axis_size("seq"), lax.axis_size("chan"), vecs.shape[1]
    if (seqs, chans) == (4, 8) and width % (chans * LANES) == 0:
        gwk, gwv, gwr, gwo, gfk, gfv, gfr = mats
        vec = jnp.pad(vecs.astype(BF16), ((0, 16 - vecs.shape[0]), (0, 0)))
        vec = jnp.broadcast_to(vec[None], (4, 16, width)).reshape(64, width)
        gfv, gfk, gfr, gwo, gwr, gwk, gwv, vec = sum_arrays([gfv, gfk, gfr, gwo, gwr, gwk, gwv, vec])
        return [gwk, gwv, gwr, gwo, gfk, gfv, gfr], vec

    def both(m):
        m = lax.psum_scatter(m, "chan", scatter_dimension=1, tiled=True)
        return lax.psum_scatter(m, "seq", scatter_dimension=0, tiled=True).astype(F32)

    v = lax.psum_scatter(vecs.astype(BF16), "chan", scatter_dimension=1, tiled=True).astype(F32)
    return [both(m) for m in mats], lax.psum(v, "seq")


def per_device(
    x, g, gain1, bias1, share_k, share_v, share_r, log_rate, boost, wk, wv, wr, wo, gain2, bias2, share_fk, share_fr,
    wfk, wfv, wfr, spans, pads,
):
    rows, width = x.shape
    chans = lax.axis_size("chan")
    total = rows * chans
    hops = max(1, min(chans - 1, total // 4 // rows))
    base = lambda: lax.axis_index("chan") * rows
    vecs = jnp.stack([gain1, bias1, share_k, share_v, share_r, gain2, bias2, share_fk, share_fr])
    rates = jnp.stack([log_rate, boost]).reshape(2 * width // LANES, LANES)
    begins = jnp.cumsum(spans[0]) - spans[0]
    pos = base() + jnp.arange(rows, dtype=jnp.int32)
    keep = 1.0 - jnp.any(pos[:, None] == begins[None, :], axis=1).astype(F32)

    xprev = shift(jnp.broadcast_to(x[rows - 1 :], (16, width)), 1)[:8]
    xk, xv, xr, k, v, r, at, bt, end = project(base, x, xprev, vecs, rates, spans, pads, keep, wk, wv, wr)
    carry = jnp.concatenate([shift(end, h + 1) for h in range(hops)], axis=0)
    wkv, gated, middle, last, carried = exit_call(base, hops, x, k, v, r, at, bt, carry, rates, vecs, spans, wo)
    hprev = jnp.broadcast_to(shift(last[7:], 1), (8, width))
    block_out, gfk, gfv, gfr, dh2, back2, sums2 = ffn(base, middle, g, hprev, vecs, spans, pads, wfr, wfk, wfv)
    dh2next = shift(back2, -1)
    dmid, gwo, dwkv, dr, sumsn2, adja, adjb, adjend = exit_back(
        base, middle, g, dh2, dh2next, vecs, rates, gated, wkv, r, k, v, at, bt, carried, spans, pads, keep, wo
    )
    adj = jnp.concatenate([shift(adjend, -h - 1) for h in range(hops)], axis=0)
    gwk, gwv, gwr, dh1, back1, sums1, wsums = project_back(
        base, hops, total, x, xprev, vecs, rates, k, v, dwkv, dr, at, bt, carried, adja, adjb, adj, xk, xv, xr, spans,
        pads, wk, wv, wr,
    )
    grad_in, sumsn1 = entry_back(x, dh1, shift(back1, -1), dmid, vecs)
    vec_parts = jnp.concatenate([sumsn1, sums1, wsums, sumsn2, sums2], axis=0).sum(axis=1)
    (gwk, gwv, gwr, gwo, gfk, gfv, gfr), vec = scatter_sums((gwk, gwv, gwr, gwo, gfk, gfv, gfr), vec_parts)
    return (block_out, grad_in, *[vec[i] for i in range(7)], gwk, gwv, gwr, gwo, *[vec[i] for i in range(7, 11)], gfk, gfv, gfr)


def solution(mesh):
    tokens, chan, both = P(("seq", "chan"), None), P("chan"), P("seq", "chan")
    placed = (tokens, tokens) + (P(),) * 18 + (P("seq", None),) * 2
    return jax.shard_map(
        per_device,
        mesh=mesh,
        in_specs=placed,
        out_specs=(tokens, tokens) + (chan,) * 7 + (both,) * 4 + (chan,) * 4 + (both,) * 3,
        check_vma=False,
    )
```

```python
import functools

import jax
import jax.numpy as jnp
from jax import lax
from jax.experimental import pallas as pl
from jax.experimental.pallas import tpu as pltpu
from jax.sharding import PartitionSpec as P

F32, BF16 = jnp.float32, jnp.bfloat16
LANES = 128
TILE = 64
MIB = 1 << 20
VMEM = pl.BlockSpec(memory_space=pltpu.VMEM)
SMEM = pl.BlockSpec(memory_space=pltpu.SMEM)
ANY = pl.BlockSpec(memory_space=pl.ANY)
G1, B1, SK, SV, SR, G2, B2, FK, FR = range(9)


def sds(shape, dtype):
    return jax.ShapeDtypeStruct(shape, dtype)


def params(limit_mib):
    return pltpu.CompilerParams(vmem_limit_bytes=limit_mib * MIB)


def dot(a, b):
    return jnp.dot(a, b, preferred_element_type=F32)


def dot_t(a, b):
    return lax.dot_general(a, b, (((1,), (1,)), ((), ())), preferred_element_type=F32)


def t_dot(a, b):
    return lax.dot_general(a, b, (((0,), (0,)), ((), ())), preferred_element_type=F32)


def fold8(v):
    return jnp.sum(v.reshape(v.shape[0] // 8, 8, v.shape[1]), axis=0)


def normalized(v):
    center = v - jnp.mean(v, axis=-1, keepdims=True)
    inv = lax.rsqrt(jnp.mean(center * center, axis=-1, keepdims=True) + 1e-05)
    return center * inv, inv


def norm_back(d_hat, hat, inv):
    return inv * (
        d_hat
        - jnp.mean(d_hat, axis=-1, keepdims=True)
        - hat * jnp.mean(d_hat * hat, axis=-1, keepdims=True)
    )


def marks(first, rows, spans, pads):
    pos = first + lax.broadcasted_iota(jnp.int32, (rows, LANES), 0)
    begin = jnp.int32(0)
    start, real = pos < 0, pos < 0
    for i in range(spans.shape[1]):
        length = spans[0, i]
        start = start | (pos == begin)
        real = real | ((pos >= begin) & (pos < begin + length - pads[0, i]))
        begin = begin + length
    return start, real


def first_start_from(spans, at, otherwise):
    begin, best = jnp.int32(0), jnp.int32(otherwise)
    for i in range(spans.shape[1]):
        best = jnp.where((begin >= at) & (begin < best), begin, best)
        begin = begin + spans[0, i]
    return best


def last_start_before(spans, at):
    begin, best = jnp.int32(0), jnp.int32(-(1 << 20))
    for i in range(spans.shape[1]):
        best = jnp.where(begin < at, begin, best)
        begin = begin + spans[0, i]
    return best


def wide(flag, width):
    return jnp.concatenate([flag] * (width // LANES), axis=1)


def with_previous(ref, at):
    block = ref[pl.ds(at, TILE + 8)]
    return block[8:], block[7 : TILE + 7]


def columns(j):
    return slice(j * LANES, (j + 1) * LANES)


def gather_carry(hops, rows, carry_ref, counts, rate):
    a, b = carry_ref[0], carry_ref[1]
    for h in range(1, hops):
        scale = jnp.exp(-rate * float(rows * h)) * counts[h]
        a, b = a + scale * carry_ref[2 * h], b + scale * carry_ref[2 * h + 1]
    return a, b


def project_kernel(
    base, x_ref, xprev_ref, vec_ref, rate_ref, spans, pads, keep_s, wk_hbm, wv_hbm, wr_hbm,
    xk_ref, xv_ref, xr_ref, k_ref, v_ref, r_ref, at_ref, bt_ref, end_ref,
    h_scr, ek_scr, ev_scr, w_scr, sems,
):
    rows, width = x_ref.shape
    blocks = width // LANES
    copies = [
        pltpu.make_async_copy(hbm, w_scr.at[i], sems.at[i])
        for i, hbm in enumerate((wk_hbm, wv_hbm, wr_hbm))
    ]
    for copy in copies:
        copy.start()
    first = base()
    gain, bias = vec_ref[G1 : G1 + 1], vec_ref[B1 : B1 + 1]
    prev = xprev_ref[...].astype(F32)
    h_scr[0:8] = normalized(prev)[0] * gain + bias

    @pl.loop(0, rows // TILE)
    def _(i):
        at = pl.multiple_of(i * TILE, TILE)
        hat, _ = normalized(x_ref[pl.ds(at, TILE)].astype(F32))
        h_scr[pl.ds(at + 8, TILE)] = hat * gain + bias

    @pl.loop(0, rows // TILE)
    def _(i):
        at = pl.multiple_of(i * TILE, TILE)
        start, _ = marks(first + at, TILE, spans, pads)
        keep = wide(1.0 - start.astype(F32), width)
        h, p = with_previous(h_scr, at)
        p = p * keep
        for row, out in ((SK, xk_ref), (SV, xv_ref), (SR, xr_ref)):
            share = vec_ref[row : row + 1]
            out[pl.ds(at, TILE)] = (h * share + p * (1.0 - share)).astype(BF16)

    _, real = marks(first, rows, spans, pads)
    real = real.astype(F32)
    step = 256
    for i, (src, out) in enumerate(((xk_ref, k_ref), (xv_ref, v_ref), (xr_ref, r_ref))):
        copies[i].wait()
        for j in range(width // step):
            tile = dot(src[...], w_scr[i, :, j * step : (j + 1) * step])
            out[:, j * step : (j + 1) * step] = tile.astype(out.dtype)
    for j in range(blocks):
        ek = jnp.exp(k_ref[:, columns(j)].astype(F32)) * real
        ek_scr[pl.ds(j, rows, stride=blocks)] = ek
        ev_scr[pl.ds(j, rows, stride=blocks)] = ek * v_ref[:, columns(j)].astype(F32)
    decay = jnp.exp(-jnp.exp(rate_ref[0:blocks]))

    def scan(t8, carry):
        a, b = carry
        for u in range(8):
            t = t8 * 8 + u
            keep = keep_s[t]
            here = pl.ds(pl.multiple_of(t * blocks, blocks), blocks)
            at_ref[here] = a * keep
            bt_ref[here] = b * keep
            fade = decay * keep
            a = a * fade + ev_scr[here]
            b = b * fade + ek_scr[here]
        return a, b

    zero = jnp.zeros((blocks, LANES), F32)
    a, b = lax.fori_loop(0, rows // 8, scan, (zero, zero))
    end_ref[0] = a
    end_ref[1] = b


def project(base, x, xprev, vecs, rates, spans, pads, keep, wk, wv, wr):
    rows, width = x.shape
    shape = (rows, width)
    tall = (rows * (width // LANES), LANES)
    return pl.pallas_call(
        functools.partial(project_kernel, base),
        out_shape=(
            [sds(shape, BF16)] * 5 + [sds(shape, F32)] + [sds(tall, F32)] * 2 + [sds((2, width // LANES, LANES), F32)]
        ),
        in_specs=[VMEM] * 4 + [SMEM] * 3 + [ANY] * 3,
        out_specs=[VMEM] * 9,
        scratch_shapes=[
            pltpu.VMEM((rows + 8, width), F32),
            pltpu.VMEM(tall, F32),
            pltpu.VMEM(tall, F32),
            pltpu.VMEM((3, width, width), BF16),
            pltpu.SemaphoreType.DMA((3,)),
        ],
        compiler_params=params(56),
        name="project",
    )(x, xprev, vecs, rates, spans, pads, keep, wk, wv, wr)


def wkv_parts(at, j, rows, blocks, k, v, at_ref, bt_ref, a_in, b_in, rate, boost, first_start):
    here = pl.ds(at * blocks + j, rows, stride=blocks)
    pos = at + lax.broadcasted_iota(jnp.int32, (rows, LANES), 0)
    lift = jnp.where(pos < first_start, jnp.exp(-rate[j : j + 1] * pos.astype(F32)), 0.0)
    a = at_ref[here] + lift * a_in[j : j + 1]
    b = bt_ref[here] + lift * b_in[j : j + 1]
    eu = jnp.exp(boost[j : j + 1] + k)
    inv = 1.0 / (b + eu)
    return a, b, eu, inv, (a + eu * v) * inv


def carry_counts(hops, rows, first, spans):
    last = last_start_before(spans, first)
    return [jnp.where(last < first - h * rows, 1.0, 0.0) for h in range(hops)]


def exit_kernel(
    base, hops, x_ref, k_ref, v_ref, r_ref, at_ref, bt_ref, carry_ref, rate_ref, vec_ref, spans, wo_hbm,
    wkv_ref, gated_ref, middle_ref, last_ref, in_ref, wo_scr, sem,
):
    rows, width = x_ref.shape
    blocks = width // LANES
    copy = pltpu.make_async_copy(wo_hbm, wo_scr, sem)
    copy.start()
    first = base()
    rate = jnp.exp(rate_ref[0:blocks])
    boost = rate_ref[blocks : 2 * blocks]
    a_in, b_in = gather_carry(hops, rows, carry_ref, carry_counts(hops, rows, first, spans), rate)
    in_ref[0] = a_in
    in_ref[1] = b_in
    first_start = first_start_from(spans, first, 1 << 20) - first

    @pl.loop(0, rows // TILE)
    def _(i):
        at = pl.multiple_of(i * TILE, TILE)
        for j in range(blocks):
            here = (pl.ds(at, TILE), columns(j))
            k, v = k_ref[here].astype(F32), v_ref[here].astype(F32)
            wkv = wkv_parts(at, j, TILE, blocks, k, v, at_ref, bt_ref, a_in, b_in, rate, boost, first_start)[-1]
            wkv = wkv.astype(BF16)
            wkv_ref[here] = wkv
            gated_ref[here] = (jax.nn.sigmoid(r_ref[here]) * wkv.astype(F32)).astype(BF16)

    copy.wait()
    step = 256
    for j in range(width // step):
        here = (slice(None), slice(j * step, (j + 1) * step))
        middle_ref[here] = x_ref[here].astype(F32) + dot(gated_ref[...], wo_scr[here])
    hat, _ = normalized(middle_ref[rows - 8 : rows])
    last_ref[...] = hat * vec_ref[G2 : G2 + 1] + vec_ref[B2 : B2 + 1]


def exit_call(base, hops, x, k, v, r, at, bt, carry, rates, vecs, spans, wo):
    rows, width = x.shape
    blocks = width // LANES
    return pl.pallas_call(
        functools.partial(exit_kernel, base, hops),
        out_shape=[
            sds((rows, width), BF16),
            sds((rows, width), BF16),
            sds((rows, width), F32),
            sds((8, width), F32),
            sds((2, blocks, LANES), F32),
        ],
        in_specs=[VMEM] * 9 + [SMEM, ANY],
        out_specs=[VMEM] * 5,
        scratch_shapes=[pltpu.VMEM((width, width), BF16), pltpu.SemaphoreType.DMA(())],
        compiler_params=params(56),
        name="exit",
    )(x, k, v, r, at, bt, carry, rates, vecs, spans, wo)


def ffn_kernel(
    base, mid_ref, g_ref, hprev_ref, vec_ref, spans, pads, wg_ref, wk_ref, wv_ref,
    out_ref, gfk_ref, gfv_ref, gfr_ref, dh_ref, back_ref, sums_ref,
    h_scr, ck_scr, cr_scr, ckt_scr, sig_scr, dvo_scr, val_scr, dck_scr, pass_scr,
):
    rows, width = mid_ref.shape
    step = pl.program_id(0)
    first = base()
    tiles = rows // TILE

    @pl.when(step == 0)
    def _():
        gain, bias = vec_ref[G2 : G2 + 1], vec_ref[B2 : B2 + 1]
        h_scr[0:8] = hprev_ref[...]

        @pl.loop(0, tiles)
        def _(i):
            at = pl.multiple_of(i * TILE, TILE)
            hat, _ = normalized(mid_ref[pl.ds(at, TILE)])
            h_scr[pl.ds(at + 8, TILE)] = hat * gain + bias

        @pl.loop(0, tiles)
        def _(i):
            at = pl.multiple_of(i * TILE, TILE)
            start, _ = marks(first + at, TILE, spans, pads)
            keep = wide(1.0 - start.astype(F32), width)
            h, p = with_previous(h_scr, at)
            p = p * keep
            for row, out in ((FK, ck_scr), (FR, cr_scr)):
                share = vec_ref[row : row + 1]
                out[pl.ds(at, TILE)] = (h * share + p * (1.0 - share)).astype(BF16)

        ckt_scr[...] = ck_scr[...].T
        _, real = marks(first, rows, spans, pads)
        real = wide(real.astype(F32), 256)
        for j in range(width // 256):
            here = (slice(None), slice(j * 256, (j + 1) * 256))
            sig = jax.nn.sigmoid(dot(cr_scr[...], wg_ref[here]))
            sig_scr[here] = sig
            dvo_scr[here] = (g_ref[here].astype(F32) * real * sig).astype(BF16)
        val_scr[...] = jnp.zeros_like(val_scr)
        dck_scr[...] = jnp.zeros_like(dck_scr)

    act = jnp.maximum(dot(ck_scr[...], wk_ref[...]), 0.0)
    hidden = (act * act).astype(BF16)
    val_scr[...] += dot(hidden, wv_ref[...])
    gfv_ref[...] = t_dot(hidden, dvo_scr[...]).astype(BF16)
    d_pre = (dot_t(dvo_scr[...], wv_ref[...]) * (2.0 * act)).astype(BF16)
    gfk = dot(ckt_scr[...], d_pre).astype(BF16)
    if len(gfk_ref.shape) == 2:
        gfk_ref[...] = gfk
    else:
        for q in range(gfk_ref.shape[0]):
            gfk_ref[q] = gfk[:, columns(q)]
    dck_scr[...] += dot_t(d_pre, wk_ref[...])

    @pl.when(step == pl.num_programs(0) - 1)
    def _():
        dgp_scr = dvo_scr
        _, real = marks(first, rows, spans, pads)
        real = wide(real.astype(F32), 256)
        for j in range(width // 256):
            here = (slice(None), slice(j * 256, (j + 1) * 256))
            sig, value = sig_scr[here], val_scr[here]
            out_ref[here] = (mid_ref[here] + sig * value).astype(BF16)
            top = g_ref[here].astype(F32) * real
            dgp_scr[here] = (top * value * sig * (1.0 - sig)).astype(BF16)
        for j in range(width // 256):
            here = (slice(None), slice(j * 256, (j + 1) * 256))
            gfr_ref[here] = t_dot(cr_scr[...], dgp_scr[here]).astype(BF16)
        dcr_scr = val_scr
        for j in range(width // 256):
            dcr_scr[:, j * 256 : (j + 1) * 256] = dot_t(dgp_scr[...], wg_ref[j * 256 : (j + 1) * 256])
        sums_ref[...] = jnp.zeros_like(sums_ref)
        share_k, share_r = vec_ref[FK : FK + 1], vec_ref[FR : FR + 1]

        @pl.loop(0, tiles)
        def _(i):
            at = pl.multiple_of(i * TILE, TILE)
            here = pl.ds(at, TILE)
            start, _ = marks(first + at, TILE, spans, pads)
            keep = wide(1.0 - start.astype(F32), width)
            h, p = with_previous(h_scr, at)
            diff = h - p * keep
            dck, dcr = dck_scr[here], dcr_scr[here]
            sums_ref[0] += fold8(diff * dck)
            sums_ref[1] += fold8(diff * dcr)
            pass_scr[here] = (dck * (1.0 - share_k) + dcr * (1.0 - share_r)) * keep
            dh_ref[here] = dck * share_k + dcr * share_r

        back_ref[...] = pass_scr[0:8]

        pass_scr[rows : rows + 8] = jnp.zeros((8, width), F32)

        @pl.loop(0, tiles)
        def _(i):
            at = pl.multiple_of(i * TILE, TILE)
            dh_ref[pl.ds(at, TILE)] += pass_scr[pl.ds(at, TILE + 8)][1 : TILE + 1]


def ffn(base, split, middle, g, hprev, vecs, spans, pads, wg, wk, wv):
    rows, width = middle.shape
    hid = wk.shape[1]
    unit = 512
    full = lambda shape: pl.BlockSpec(shape, lambda j: (0,) * len(shape))
    gfk_shape, gfk_spec = (width, hid), pl.BlockSpec((width, unit), lambda j: (0, j))
    if split:
        parts = unit // LANES
        gfk_shape = (parts, width, hid // parts)
        gfk_spec = pl.BlockSpec((parts, width, LANES), lambda j: (0, 0, j))
    return pl.pallas_call(
        functools.partial(ffn_kernel, base),
        grid=(hid // unit,),
        out_shape=[
            sds((rows, width), BF16),
            sds(gfk_shape, BF16),
            sds((hid, width), BF16),
            sds((width, width), BF16),
            sds((rows, width), F32),
            sds((8, width), F32),
            sds((2, 8, width), F32),
        ],
        in_specs=[
            full((rows, width)),
            full((rows, width)),
            full((8, width)),
            full(vecs.shape),
            SMEM,
            SMEM,
            full((width, width)),
            pl.BlockSpec((width, unit), lambda j: (0, j)),
            pl.BlockSpec((unit, width), lambda j: (j, 0)),
        ],
        out_specs=[
            full((rows, width)),
            gfk_spec,
            pl.BlockSpec((unit, width), lambda j: (j, 0)),
            full((width, width)),
            full((rows, width)),
            full((8, width)),
            full((2, 8, width)),
        ],
        scratch_shapes=[
            pltpu.VMEM((rows + 8, width), F32),
            pltpu.VMEM((rows, width), BF16),
            pltpu.VMEM((rows, width), BF16),
            pltpu.VMEM((width, rows), BF16),
            pltpu.VMEM((rows, width), F32),
            pltpu.VMEM((rows, width), BF16),
            pltpu.VMEM((rows, width), F32),
            pltpu.VMEM((rows, width), F32),
            pltpu.VMEM((rows + 8, width), F32),
        ],
        compiler_params=params(60),
        name="ffn",
    )(middle, g, hprev, vecs, spans, pads, wg, wk, wv)


def exit_back_kernel(
    base, mid_ref, g_ref, dh_ref, dhnext_ref, vec_ref, rate_ref, gated_ref, wkv_ref, r_ref, k_ref, v_ref, at_ref, bt_ref,
    in_ref, spans, pads, keep_s, wo_ref,
    dmid_ref, gwo_ref, dwkv_ref, dr_ref, sums_ref, adja_ref, adjb_ref, adjend_ref,
    datt_scr, dn_scr, dd_scr,
):
    rows, width = mid_ref.shape
    blocks = width // LANES
    first = base()
    gain = vec_ref[G2 : G2 + 1]
    sums_ref[...] = jnp.zeros_like(sums_ref)
    tail = dhnext_ref[...]
    row = lax.broadcasted_iota(jnp.int32, tail.shape, 0)
    dh_ref[rows - 8 : rows] += jnp.where(row == 7, pltpu.roll(tail, 7, axis=0), 0.0)

    @pl.loop(0, rows // TILE)
    def _(i):
        at = pl.multiple_of(i * TILE, TILE)
        here = pl.ds(at, TILE)
        _, real = marks(first + at, TILE, spans, pads)
        hat, inv = normalized(mid_ref[here])
        dh = dh_ref[here]
        sums_ref[0] += fold8(dh * hat)
        sums_ref[1] += fold8(dh)
        d_mid = norm_back(dh * gain, hat, inv) + g_ref[here].astype(F32) * wide(real.astype(F32), width)
        dmid_ref[here] = d_mid
        datt_scr[here] = d_mid.astype(BF16)

    step = 256
    rate = jnp.exp(rate_ref[0:blocks])
    boost = rate_ref[blocks : 2 * blocks]
    a_in, b_in = in_ref[0], in_ref[1]
    first_start = first_start_from(spans, first, 1 << 20) - first
    for j in range(width // step):
        here = (slice(None), slice(j * step, (j + 1) * step))
        dr_ref[here] = dot_t(datt_scr[...], wo_ref[j * step : (j + 1) * step]).astype(BF16)
    d_gated = dr_ref

    @pl.loop(0, rows // TILE)
    def _(i):
        at = pl.multiple_of(i * TILE, TILE)
        for j in range(blocks):
            here = (pl.ds(at, TILE), columns(j))
            sig = jax.nn.sigmoid(r_ref[here])
            dg = d_gated[here].astype(F32)
            dwkv = (dg * sig).astype(BF16)
            dwkv_ref[here] = dwkv
            dr_ref[here] = (dg * wkv_ref[here].astype(F32) * sig * (1.0 - sig)).astype(BF16)
            k, v = k_ref[here].astype(F32), v_ref[here].astype(F32)
            _, _, _, inv, wkv = wkv_parts(
                at, j, TILE, blocks, k, v, at_ref, bt_ref, a_in, b_in, rate, boost, first_start
            )
            dn = dwkv.astype(F32) * inv
            there = pl.ds(at * blocks + j, TILE, stride=blocks)
            dn_scr[there] = dn
            dd_scr[there] = -dn * wkv

    decay = jnp.exp(-rate)

    def scan(t8, carry):
        a, b = carry
        for u in range(8):
            t = rows - 1 - (t8 * 8 + u)
            keep = keep_s[t]
            here = pl.ds(pl.multiple_of(t * blocks, blocks), blocks)
            adja_ref[here] = a
            adjb_ref[here] = b
            fade = decay * keep
            a = a * fade + dn_scr[here] * keep
            b = b * fade + dd_scr[here] * keep
        return a, b

    zero = jnp.zeros((blocks, LANES), F32)
    a, b = lax.fori_loop(0, rows // 8, scan, (zero, zero))
    adjend_ref[0] = a
    adjend_ref[1] = b
    for j in range(width // step):
        here = (slice(None), slice(j * step, (j + 1) * step))
        gwo_ref[here] = t_dot(gated_ref[...], datt_scr[here]).astype(BF16)


def exit_back(base, middle, g, dh, dhnext, vecs, rates, gated, wkv, r, k, v, at, bt, carry, spans, pads, keep, wo):
    rows, width = middle.shape
    blocks = width // LANES
    tall = (rows * blocks, LANES)
    return pl.pallas_call(
        functools.partial(exit_back_kernel, base),
        out_shape=[
            sds((rows, width), F32),
            sds((width, width), BF16),
            sds((rows, width), BF16),
            sds((rows, width), BF16),
            sds((2, 8, width), F32),
            sds(tall, F32),
            sds(tall, F32),
            sds((2, blocks, LANES), F32),
        ],
        in_specs=[VMEM] * 14 + [SMEM] * 3 + [VMEM],
        out_specs=[VMEM] * 8,
        scratch_shapes=[
            pltpu.VMEM((rows, width), BF16),
            pltpu.VMEM(tall, F32),
            pltpu.VMEM(tall, F32),
        ],
        compiler_params=params(60),
        name="exit_back",
    )(middle, g, dh, dhnext, vecs, rates, gated, wkv, r, k, v, at, bt, carry, spans, pads, keep, wo)


def project_back_kernel(
    base, hops, total, x_ref, xprev_ref, vec_ref, rate_ref, k_ref, v_ref, dwkv_ref, dr_ref, at_ref, bt_ref, in_ref,
    adja_ref, adjb_ref, adj_ref, xk_ref, xv_ref, xr_ref, spans, pads, wk_hbm, wv_hbm, wr_hbm,
    gwk_ref, gwv_ref, gwr_ref, dh_ref, back_ref, sums_ref, wsums_ref,
    h_scr, dk_scr, dv_scr, d_scr, pass_scr, w_scr, sems,
):
    rows, width = x_ref.shape
    blocks = width // LANES
    copies = [
        pltpu.make_async_copy(hbm, w_scr.at[i], sems.at[i])
        for i, hbm in enumerate((wk_hbm, wv_hbm, wr_hbm))
    ]
    for copy in copies:
        copy.start()
    first = base()
    rate = jnp.exp(rate_ref[0:blocks])
    boost = rate_ref[blocks : 2 * blocks]
    a_in, b_in = in_ref[0], in_ref[1]
    first_start = first_start_from(spans, first, 1 << 20) - first
    last_start = last_start_before(spans, first + rows) - first
    after = first_start_from(spans, first + rows, total)
    counts = [jnp.where(after >= first + (h + 1) * rows, 1.0, 0.0) for h in range(hops)]
    adj_a, adj_b = gather_carry(hops, rows, adj_ref, counts, rate)
    wsums_ref[...] = jnp.zeros_like(wsums_ref)
    sums_ref[...] = jnp.zeros_like(sums_ref)

    @pl.loop(0, rows // TILE)
    def _(i):
        at = pl.multiple_of(i * TILE, TILE)
        _, real = marks(first + at, TILE, spans, pads)
        real = real.astype(F32)
        pos = at + lax.broadcasted_iota(jnp.int32, (TILE, LANES), 0)
        for j in range(blocks):
            here = (pl.ds(at, TILE), columns(j))
            k, v = k_ref[here].astype(F32), v_ref[here].astype(F32)
            a, b, eu, inv, wkv = wkv_parts(
                at, j, TILE, blocks, k, v, at_ref, bt_ref, a_in, b_in, rate, boost, first_start
            )
            there = pl.ds(at * blocks + j, TILE, stride=blocks)
            lift = jnp.where(
                pos >= last_start, jnp.exp(-rate[j : j + 1] * (rows - 1 - pos).astype(F32)), 0.0
            )
            post_a = adja_ref[there] + lift * adj_a[j : j + 1]
            post_b = adjb_ref[there] + lift * adj_b[j : j + 1]
            dn = dwkv_ref[here].astype(F32) * inv
            own = eu * dn
            weight = jnp.exp(k) * real
            dv_scr[here] = (own + weight * post_a).astype(BF16)
            first_term = own * (v - wkv)
            dk_scr[here] = (first_term + weight * (v * post_a + post_b)).astype(BF16)
            wsums_ref[0, :, columns(j)] += fold8(a * post_a + b * post_b)
            wsums_ref[1, :, columns(j)] += fold8(first_term)

    for j in range(blocks):
        r = rate[j : j + 1]
        wsums_ref[0, :, columns(j)] *= -r * jnp.exp(-r)
    gain, bias = vec_ref[G1 : G1 + 1], vec_ref[B1 : B1 + 1]
    h_scr[0:8] = normalized(xprev_ref[...].astype(F32))[0] * gain + bias

    @pl.loop(0, rows // TILE)
    def _(i):
        at = pl.multiple_of(i * TILE, TILE)
        hat, _ = normalized(x_ref[pl.ds(at, TILE)].astype(F32))
        h_scr[pl.ds(at + 8, TILE)] = hat * gain + bias

    step = 256
    dh_ref[...] = jnp.zeros_like(dh_ref)
    groups = ((dk_scr, xk_ref, gwk_ref, SK), (dv_scr, xv_ref, gwv_ref, SV), (dr_ref, xr_ref, gwr_ref, SR))
    pass_scr[...] = jnp.zeros_like(pass_scr)
    for i, (grad, mixed, out, row) in enumerate(groups):
        copies[i].wait()
        for j in range(width // step):
            here = (slice(None), slice(j * step, (j + 1) * step))
            d_scr[:, j * step : (j + 1) * step] = dot_t(grad[...], w_scr[i, j * step : (j + 1) * step])
            out[here] = t_dot(mixed[...], grad[here]).astype(BF16)
        share = vec_ref[row : row + 1]

        @pl.loop(0, rows // TILE)
        def _(t):
            at = pl.multiple_of(t * TILE, TILE)
            here = pl.ds(at, TILE)
            start, _ = marks(first + at, TILE, spans, pads)
            keep = wide(1.0 - start.astype(F32), width)
            h, p = with_previous(h_scr, at)
            d = d_scr[here]
            sums_ref[i] += fold8((h - p * keep) * d)
            pass_scr[here] += d * (1.0 - share) * keep
            dh_ref[here] += d * share

    back_ref[...] = pass_scr[0:8]

    @pl.loop(0, rows // TILE)
    def _(i):
        at = pl.multiple_of(i * TILE, TILE)
        dh_ref[pl.ds(at, TILE)] += pass_scr[pl.ds(at, TILE + 8)][1 : TILE + 1]


def project_back(base, hops, total, x, xprev, vecs, rates, k, v, dwkv, dr, at, bt, carry, adja, adjb, adj, xk, xv, xr, spans, pads, wk, wv, wr):
    rows, width = x.shape
    return pl.pallas_call(
        functools.partial(project_back_kernel, base, hops, total),
        out_shape=[sds((width, width), BF16)] * 3
        + [
            sds((rows, width), F32),
            sds((8, width), F32),
            sds((3, 8, width), F32),
            sds((2, 8, width), F32),
        ],
        in_specs=[VMEM] * 17 + [SMEM] * 2 + [ANY] * 3,
        out_specs=[VMEM] * 7,
        scratch_shapes=[
            pltpu.VMEM((rows + 8, width), F32),
            pltpu.VMEM((rows, width), BF16),
            pltpu.VMEM((rows, width), BF16),
            pltpu.VMEM((rows, width), F32),
            pltpu.VMEM((rows + 8, width), F32),
            pltpu.VMEM((3, width, width), BF16),
            pltpu.SemaphoreType.DMA((3,)),
        ],
        compiler_params=params(60),
        name="project_back",
    )(x, xprev, vecs, rates, k, v, dwkv, dr, at, bt, carry, adja, adjb, adj, xk, xv, xr, spans, pads, wk, wv, wr)


def entry_back_kernel(x_ref, dh_ref, dhnext_ref, dmid_ref, vec_ref, out_ref, sums_ref):
    rows = x_ref.shape[0]
    gain = vec_ref[G1 : G1 + 1]
    sums_ref[...] = jnp.zeros_like(sums_ref)
    tail = dhnext_ref[...]
    row = lax.broadcasted_iota(jnp.int32, tail.shape, 0)
    dh_ref[rows - 8 : rows] += jnp.where(row == 7, pltpu.roll(tail, 7, axis=0), 0.0)

    @pl.loop(0, rows // TILE)
    def _(i):
        here = pl.ds(pl.multiple_of(i * TILE, TILE), TILE)
        hat, inv = normalized(x_ref[here].astype(F32))
        dh = dh_ref[here]
        sums_ref[0] += fold8(dh * hat)
        sums_ref[1] += fold8(dh)
        out_ref[here] = (norm_back(dh * gain, hat, inv) + dmid_ref[here]).astype(BF16)


def entry_back(x, dh, dhnext, dmid, vecs):
    rows, width = x.shape
    return pl.pallas_call(
        entry_back_kernel,
        out_shape=[sds((rows, width), BF16), sds((2, 8, width), F32)],
        in_specs=[VMEM] * 5,
        out_specs=[VMEM] * 2,
        compiler_params=params(40),
        name="entry_back",
    )(x, dh, dhnext, dmid, vecs)


X, Y, Z = "x", "y", "z"
ORDERS = {
    X: ("x", "y", "low", "high"),
    Y: ("y", "x", "low", "high"),
    Z: ("low", "high", "x", "y"),
}
AXIS_BIT = {"core": ("seq", 1), "x": ("seq", 2), "y": ("chan", 1), "low": ("chan", 2), "high": ("chan", 4)}
STEPS = 5
RING = 3
MESH = pl.DeviceIdType.MESH
ARRAYS = ("fv", "fk0", "fk1", "fk2", "fk3", "fr", "wo", "wr", "wv", "wk", "vec")
PLAN = (
    (("fv", 0, 192, X), ("fv", 384, 192, Y), ("fv", 768, 128, Z)),
    (("fv", 192, 192, X), ("fv", 576, 192, Y), ("fv", 896, 128, Z)),
    (("fk0", 0, 128, X), ("fk1", 128, 128, Y), ("fk3", 0, 128, Z)),
    (("fk0", 128, 128, X), ("fk2", 0, 128, Y), ("fk3", 128, 128, Z)),
    (("fk1", 0, 128, X), ("fk2", 128, 128, Y)),
    (("fr", 0, 128, X), ("fr", 128, 128, Y)),
    (("wo", 0, 128, X), ("wo", 128, 128, Y)),
    (("wr", 0, 128, X), ("wr", 128, 128, Y)),
    (("wv", 0, 128, X), ("wv", 128, 64, Y), ("wv", 192, 64, Z)),
    (("wk", 0, 64, X), ("wk", 64, 128, Y), ("wk", 192, 64, Z), ("vec", 0, 16, Y)),
)
SLOT = {X: (0, 192), Y: (1, 192), Z: (2, 128), "vec": (3, 16)}


def bit_of(index, weight):
    return index // weight % 2


def partner(axis):
    name, weight = AXIS_BIT[axis]
    where = {"seq": lax.axis_index("seq"), "chan": lax.axis_index("chan")}
    bit = bit_of(where[name], weight)
    where[name] = where[name] + weight * (1 - 2 * bit)
    return bit, (where["seq"], where["chan"])


class Summing:
    def __init__(self, grads, bases, received, outs, stages, rings, levels, sems):
        self.grads, self.bases, self.received, self.outs = grads, bases, received, outs
        self.stages, self.rings, self.levels = stages, rings, levels
        self.send_sems, self.recv_sems, self.stage_sems = sems
        self.sides = {axis: partner(axis) for axis in AXIS_BIT}
        self.chunks = [chunk for tick in PLAN for chunk in tick]
        self.tick_of = [t for t, tick in enumerate(PLAN) for _ in tick]
        self.ticks = [[n for n, t in enumerate(self.tick_of) if t == tick] for tick in range(len(PLAN))]

    def place(self, number):
        array, first, rows, stream = self.chunks[number]
        lane = SLOT["vec" if array == "vec" else stream][0]
        return array, first, rows, stream, lane, pl.ds(self.bases[array] + first, rows)

    def across(self, number):
        array, first, rows, _, _, there = self.place(number)
        core, mate = self.sides["core"]
        return pltpu.make_async_remote_copy(
            src_ref=self.grads[array].at[:, 1 - core, pl.ds(first, rows)],
            dst_ref=self.received.at[:, there],
            send_sem=self.send_sems.at[number, 0],
            recv_sem=self.recv_sems.at[number, 0],
            device_id=mate,
            device_id_type=MESH,
        )

    def staged(self, number):
        array, first, rows, _, lane, there = self.place(number)
        core, _ = self.sides["core"]
        stage = self.stages[lane]
        return (
            pltpu.make_async_copy(
                self.grads[array].at[:, core, pl.ds(first, rows)], stage.at[0, :, 0:rows], self.stage_sems.at[lane, 0]
            ),
            pltpu.make_async_copy(self.received.at[:, there], stage.at[1, :, 0:rows], self.stage_sems.at[lane, 1]),
        )

    def send(self, number, step):
        _, _, rows, stream, lane, there = self.place(number)
        bit, mate = self.sides[ORDERS[stream][step - 1]]
        free = (slice(None),) * (4 - step)
        if step == 1:
            source = self.rings[lane].at[(self.tick_of[number] % RING, 1 - bit, *free, slice(0, rows))]
        else:
            source = self.levels[step - 2].at[(1 - bit, *free, there)]
        return pltpu.make_async_remote_copy(
            src_ref=source,
            dst_ref=self.levels[step - 1].at[(*free, there)],
            send_sem=self.send_sems.at[number, step],
            recv_sem=self.recv_sems.at[number, step],
            device_id=mate,
            device_id_type=MESH,
        )

    def start_stage(self, number):
        self.across(number).wait_recv()
        for copy in self.staged(number):
            copy.start()

    def first_sum(self, number):
        _, _, rows, stream, lane, _ = self.place(number)
        tick = self.tick_of[number]
        stage, ring = self.stages[lane], self.rings[lane]
        other = self.before(number)
        if other is not None:
            self.send(other, 1).wait_send()
        for copy in self.staged(number):
            copy.wait()

        @pl.loop(0, 16)
        def _(i):
            c = i % 8
            bits = {"x": i // 8, "y": c % 2, "low": c // 2 % 2, "high": c // 4}
            cols = pl.ds(pl.multiple_of(c * LANES, LANES), LANES)
            total = stage[0, i // 8, 0:rows, cols].astype(F32) + stage[1, i // 8, 0:rows, cols].astype(F32)
            at = tuple(bits[axis] for axis in ORDERS[stream])
            ring[(tick % RING, *at, slice(0, rows))] = total.astype(BF16)

        self.send(number, 1).start()

    def later_sum(self, number, step):
        array, first, rows, stream, lane, there = self.place(number)
        bit, _ = self.sides[ORDERS[stream][step - 1]]
        target = self.levels[step - 1]
        self.send(number, step).wait_recv()
        if step == 1:
            source, lead, here = self.rings[lane], (self.tick_of[number] % RING, bit), slice(0, rows)
        else:
            source, lead, here = self.levels[step - 2], (bit,), there
        if step == 4:
            out, cols = self.outs[array]
            out[first : first + rows, cols] = source[(*lead, here)].astype(F32) + target[there].astype(F32)
            return

        @pl.loop(0, 1 << (4 - step))
        def _(i):
            at = tuple(i // (1 << (3 - step - d)) % 2 for d in range(4 - step))
            total = source[(*lead, *at, here)].astype(F32) + target[(*at, there)].astype(F32)
            target[(*at, there)] = total.astype(BF16)

        self.send(number, step + 1).start()

    def actions(self):
        ticks = self.ticks
        for tick in range(len(ticks) + 4):
            if tick == 0:
                for t in range(min(2, len(ticks))):
                    for n in ticks[t]:
                        yield self.chunks[n][0], functools.partial(lambda n: self.across(n).start(), n)
                for n in ticks[0]:
                    yield None, functools.partial(self.start_stage, n)
            if tick + 2 < len(ticks):
                for n in ticks[tick + 2]:
                    yield self.chunks[n][0], functools.partial(lambda n: self.across(n).start(), n)
            if tick < len(ticks):
                for n in ticks[tick]:
                    yield None, functools.partial(self.first_sum, n)
            for step in range(1, 5):
                if 0 <= tick - step < len(ticks):
                    for n in ticks[tick - step]:
                        yield None, functools.partial(self.later_sum, n, step)
                if step == 1 and tick + 1 < len(ticks):
                    for n in ticks[tick + 1]:
                        yield None, functools.partial(self.start_stage, n)

    def before(self, number):
        same = lambda o: (self.place(o)[4], self.tick_of[o] % RING)
        earlier = [o for o in range(number) if same(o) == same(number)]
        return earlier[-1] if earlier else None

    def finish(self):
        count = len(self.chunks)
        waited = {self.before(n) for n in range(count)}
        for n in range(count):
            self.across(n).wait_send()
            for step in range(1, STEPS):
                if step > 1 or n not in waited:
                    self.send(n, step).wait_send()


def back_kernel(*refs):
    (
        mid_h, g_h, dh_h, gated_h, wkv_h, r_h, k_h, v_h, at_h, bt_h, x_h, xk_h, xv_h, xr_h, wo_h, wk_h, wv_h, wr_h,
        fv_h, fk_h, fr_h,
        vec_ref, rate_ref, in_ref, xprev_ref, back2_ref, sums2_ref, spans, pads, keep_s,
        gin_ref, ofv, ofk, ofr, owo, owr, owv, owk, ovec, received, gw_h, gvec_h,
        mid, dh, h_scr, d_scr, pass_scr, at_scr, bt_scr, dn_scr, dd_scr,
        b0, b1, b2, b3, b4, b5, b6, b7, w_scr, tile_scr, vec_scr, halo2, halo1, mine1, adj_mine, adj_in,
        sums, wsums, s0, s1, s2, s3, g0, g1, g2, g3, l1, l2, l3, l4,
        load_sems, tile_sems, halo_send, halo_recv, send_sems, recv_sems, stage_sems,
    ) = refs
    rows, width = x_h.shape
    blocks = width // LANES
    chans = lax.axis_size("chan")
    seq, chan = lax.axis_index("seq"), lax.axis_index("chan")
    first = chan * rows
    total = rows * chans
    hops = adj_in.shape[0]
    tiles = rows // TILE
    step = 256
    around = [(seq, (chan + chans + d) % chans) for h in range(hops) for d in (h + 1, -h - 1)]

    grads = {"fv": fv_h, "fr": fr_h, "vec": gvec_h}
    outs = {"fv": (ofv, slice(None)), "fr": (ofr, slice(None)), "vec": (ovec, slice(None))}
    for i in range(4):
        grads[f"fk{i}"], outs[f"fk{i}"] = fk_h.at[i], (ofk, columns(i))
    for i, (name, out) in enumerate((("wo", owo), ("wr", owr), ("wv", owv), ("wk", owk))):
        grads[name], outs[name] = gw_h.at[i], (out, slice(None))
    bases, filled = {}, 0
    for name in ARRAYS:
        bases[name] = filled
        filled += grads[name].shape[2]
    summing = Summing(
        grads, bases, received, outs, (s0, s1, s2, s3), (g0, g1, g2, g3), (l1, l2, l3, l4),
        (send_sems, recv_sems, stage_sems),
    )

    loads = {}

    def load(name, source, target):
        loads[name] = pltpu.make_async_copy(source, target, load_sems.at[len(loads)])
        loads[name].start()

    gated, wkv, k, v, datt, dwkv, dr = b1, b2, b3, b4, b5, b6, b7
    g, r = b0, h_scr.at[0:rows]
    load("mid", mid_h, mid)
    load("g", g_h, g)
    load("dh", dh_h, dh)
    load("wo", wo_h, w_scr.at[0])
    load("r", r_h, r)
    load("wkv", wkv_h, wkv)
    load("k", k_h, k)
    load("v", v_h, v)
    load("at", at_h, at_scr)
    load("bt", bt_h, bt_scr)
    load("gated", gated_h, gated)
    load("wr", wr_h, w_scr.at[1])

    barrier = pltpu.get_barrier_semaphore()
    mates = [mate for _, mate in summing.sides.values()] + around
    for mate in mates:
        pl.semaphore_signal(barrier, inc=1, device_id=mate, device_id_type=MESH)
    pl.semaphore_wait(barrier, len(mates))

    def hand(source, target, number, offset):
        return pltpu.make_async_remote_copy(
            src_ref=source,
            dst_ref=target,
            send_sem=halo_send.at[number],
            recv_sem=halo_recv.at[number],
            device_id=(seq, (chan + chans + offset) % chans),
            device_id_type=MESH,
        )

    hand2 = hand(back2_ref, halo2, 0, -1)
    hand1 = hand(mine1, halo1, 1, -1)
    hand_adj = [hand(adj_mine, adj_in.at[h], 2 + h, -h - 1) for h in range(hops)]
    hand2.start()

    done = set(("fv", "fk0", "fk1", "fk2", "fk3", "fr"))
    pending = list(summing.actions())

    def pump(count):
        while count and pending and (pending[0][0] is None or pending[0][0] in done):
            pending.pop(0)[1]()
            count -= 1

    def col(j):
        return slice(j * step, (j + 1) * step)

    written = []

    def write_grad(index, name, left, right):
        for j in range(width // step):
            if len(written) >= 2:
                for copy in written[-2]:
                    copy.wait()
            slot = len(written) % 2
            tile_scr[slot] = t_dot(left[...], right[:, col(j)]).astype(BF16).reshape(4, width // 4, step)
            copies = []
            for s in range(4):
                copy = pltpu.make_async_copy(
                    tile_scr.at[slot, s], gw_h.at[index, s // 2, s % 2, :, col(j)], tile_sems.at[slot, s]
                )
                copy.start()
                copies.append(copy)
            written.append(copies)
            pump(1)
        for copies in written[-2:]:
            for copy in copies:
                copy.wait()
        written.clear()
        done.add(name)
        pump(1)

    pump(9)
    gain2, gain1, bias1 = vec_ref[G2 : G2 + 1], vec_ref[G1 : G1 + 1], vec_ref[B1 : B1 + 1]
    rate = jnp.exp(rate_ref[0:blocks])
    boost = rate_ref[blocks : 2 * blocks]
    a_in, b_in = in_ref[0], in_ref[1]
    first_start = first_start_from(spans, first, 1 << 20) - first
    last_start = last_start_before(spans, first + rows) - first
    after = first_start_from(spans, first + rows, total)
    sums[...] = jnp.zeros_like(sums)
    wsums[...] = jnp.zeros_like(wsums)

    for name in ("mid", "g", "dh"):
        loads[name].wait()

    def norm2_tile(i):
        at = pl.multiple_of(i * TILE, TILE)
        here = pl.ds(at, TILE)
        _, real = marks(first + at, TILE, spans, pads)
        hat, inv = normalized(mid[here])
        d = dh[here]
        sums[0] += fold8(d * hat)
        sums[1] += fold8(d)
        d_mid = norm_back(d * gain2, hat, inv) + g[here].astype(F32) * wide(real.astype(F32), width)
        mid[here] = d_mid
        datt[here] = d_mid.astype(BF16)

    def last_row(halo):
        row = lax.broadcasted_iota(jnp.int32, halo.shape, 0)
        return jnp.where(row == 7, pltpu.roll(halo[...], 7, axis=0), 0.0)

    half = tiles // 2
    pl.loop(0, half)(norm2_tile)
    pump(4)
    pl.loop(half, tiles - 1)(norm2_tile)
    pump(2)
    hand2.wait_recv()
    dh[rows - 8 : rows] += last_row(halo2)
    norm2_tile(tiles - 1)
    dmid = mid
    load("x", x_h, b0)

    loads["wo"].wait()
    for j in range(width // step):
        d_scr[:, col(j)] = dot_t(datt[...], w_scr[0, col(j)])
    load("wv", wv_h, w_scr.at[0])
    pump(4)
    for name in ("r", "wkv", "k", "v", "at", "bt"):
        loads[name].wait()

    def gate_tile(i):
        at = pl.multiple_of(i * TILE, TILE)
        for j in range(blocks):
            here = (pl.ds(at, TILE), columns(j))
            sig = jax.nn.sigmoid(r[here])
            dg = d_scr[here]
            dw = (dg * sig).astype(BF16)
            dwkv[here] = dw
            dr[here] = (dg * wkv[here].astype(F32) * sig * (1.0 - sig)).astype(BF16)
            kk, vv = k[here].astype(F32), v[here].astype(F32)
            _, _, _, inv, out = wkv_parts(
                at, j, TILE, blocks, kk, vv, at_scr, bt_scr, a_in, b_in, rate, boost, first_start
            )
            dn = dw.astype(F32) * inv
            there = pl.ds(at * blocks + j, TILE, stride=blocks)
            dn_scr[there] = dn
            dd_scr[there] = -dn * out

    for part in range(4):
        pl.loop(part * tiles // 4, (part + 1) * tiles // 4)(gate_tile)
        pump(3)
    load("xv", xv_h, wkv)

    decay = jnp.exp(-rate)

    def scan(t8, carry):
        a, b = carry
        for u in range(8):
            t = rows - 1 - (t8 * 8 + u)
            keep = keep_s[t]
            here = pl.ds(pl.multiple_of(t * blocks, blocks), blocks)
            dn, dd = dn_scr[here], dd_scr[here]
            dn_scr[here] = a
            dd_scr[here] = b
            fade = decay * keep
            a = a * fade + dn * keep
            b = b * fade + dd * keep
        return a, b

    zero = jnp.zeros((blocks, LANES), F32)
    carry = lax.fori_loop(0, rows // 16, scan, (zero, zero))
    pump(3)
    a, b = lax.fori_loop(rows // 16, rows // 8, scan, carry)
    adj_mine[0] = a
    adj_mine[1] = b
    for copy in hand_adj:
        copy.start()
    pump(2)

    loads["gated"].wait()
    write_grad(0, "wo", gated, datt)
    load("xk", xk_h, gated)
    load("xr", xr_h, datt)
    xk, xv, xr = gated, wkv, datt

    h_scr[0:8] = normalized(xprev_ref[...].astype(F32))[0] * gain1 + bias1
    loads["x"].wait()
    x = b0

    @pl.loop(0, tiles)
    def _(i):
        at = pl.multiple_of(i * TILE, TILE)
        hat, _ = normalized(x[pl.ds(at, TILE)].astype(F32))
        h_scr[pl.ds(at + 8, TILE)] = hat * gain1 + bias1

    pump(3)
    loads["xr"].wait()
    write_grad(1, "wr", xr, dr)

    for copy in hand_adj:
        copy.wait_recv()
    adj_a, adj_b = adj_in[0, 0], adj_in[0, 1]
    for h in range(1, hops):
        scale = jnp.exp(-rate * float(rows * h)) * jnp.where(after >= first + (h + 1) * rows, 1.0, 0.0)
        adj_a, adj_b = adj_a + scale * adj_in[h, 0], adj_b + scale * adj_in[h, 1]

    def recur_tile(i):
        at = pl.multiple_of(i * TILE, TILE)
        _, real = marks(first + at, TILE, spans, pads)
        real = real.astype(F32)
        pos = at + lax.broadcasted_iota(jnp.int32, (TILE, LANES), 0)
        for j in range(blocks):
            here = (pl.ds(at, TILE), columns(j))
            kk, vv = k[here].astype(F32), v[here].astype(F32)
            a, b, eu, inv, out = wkv_parts(
                at, j, TILE, blocks, kk, vv, at_scr, bt_scr, a_in, b_in, rate, boost, first_start
            )
            there = pl.ds(at * blocks + j, TILE, stride=blocks)
            lift = jnp.where(pos >= last_start, jnp.exp(-rate[j : j + 1] * (rows - 1 - pos).astype(F32)), 0.0)
            post_a = dn_scr[there] + lift * adj_a[j : j + 1]
            post_b = dd_scr[there] + lift * adj_b[j : j + 1]
            dn = dwkv[here].astype(F32) * inv
            own = eu * dn
            weight = jnp.exp(kk) * real
            v[here] = (own + weight * post_a).astype(BF16)
            first_term = own * (vv - out)
            k[here] = (first_term + weight * (vv * post_a + post_b)).astype(BF16)
            wsums[0, :, columns(j)] += fold8(a * post_a + b * post_b)
            wsums[1, :, columns(j)] += fold8(first_term)

    for part in range(4):
        pl.loop(part * tiles // 4, (part + 1) * tiles // 4)(recur_tile)
        pump(3)
    for j in range(blocks):
        rr = rate[j : j + 1]
        wsums[0, :, columns(j)] *= -rr * jnp.exp(-rr)
    dk, dv = k, v
    loads["xv"].wait()
    write_grad(2, "wv", xv, dv)
    loads["xk"].wait()
    write_grad(3, "wk", xk, dk)

    def mix_back(grad, weight, share_row, index, fresh):
        for j in range(width // step):
            d_scr[:, col(j)] = dot_t(grad[...], weight[col(j)])
        pump(1)
        share = vec_ref[share_row : share_row + 1]

        @pl.loop(0, tiles)
        def _(t):
            at = pl.multiple_of(t * TILE, TILE)
            here = pl.ds(at, TILE)
            start, _ = marks(first + at, TILE, spans, pads)
            keep = wide(1.0 - start.astype(F32), width)
            h, p = with_previous(h_scr, at)
            d = d_scr[here]
            sums[index] += fold8((h - p * keep) * d)
            passed = d * (1.0 - share) * keep
            if fresh:
                pass_scr[here] = passed
                dh[here] = d * share
            else:
                pass_scr[here] += passed
                dh[here] += d * share

        pump(2)

    loads["wr"].wait()
    mix_back(dr, w_scr.at[1], SR, 4, True)
    load("wk", wk_h, w_scr.at[1])
    loads["wv"].wait()
    mix_back(dv, w_scr.at[0], SV, 3, False)
    loads["wk"].wait()
    mix_back(dk, w_scr.at[1], SK, 2, False)
    mine1[...] = pass_scr[0:8]
    hand1.start()
    pass_scr[rows : rows + 8] = jnp.zeros((8, width), F32)

    def norm1_tile(i, extra=None):
        at = pl.multiple_of(i * TILE, TILE)
        here = pl.ds(at, TILE)
        d = dh[here] + pass_scr[pl.ds(at, TILE + 8)][1 : TILE + 1]
        if extra is not None:
            d = d + extra
        hat, inv = normalized(x[here].astype(F32))
        sums[5] += fold8(d * hat)
        sums[6] += fold8(d)
        gin_ref[here] = (norm_back(d * gain1, hat, inv) + dmid[here]).astype(BF16)

    pl.loop(0, tiles - 1)(norm1_tile)
    pump(2)
    hand1.wait_recv()
    tail = jnp.concatenate([jnp.zeros((TILE - 8, width), F32), last_row(halo1)], axis=0)
    norm1_tile(tiles - 1, tail)

    parts = [sums[5], sums[6], sums[2], sums[3], sums[4], wsums[0], wsums[1], sums[0], sums[1], sums2_ref[0], sums2_ref[1]]
    lines = [jnp.sum(p, axis=0, keepdims=True) for p in parts]
    lines.append(jnp.zeros((16 - len(lines), width), F32))
    vec_scr[...] = jnp.concatenate(lines, axis=0).astype(BF16)
    copies = [
        pltpu.make_async_copy(vec_scr, gvec_h.at[s // 2, s % 2], tile_sems.at[0, s]) for s in range(4)
    ]
    for copy in copies:
        copy.start()
    for copy in copies:
        copy.wait()
    done.add("vec")
    pump(len(pending))
    summing.finish()
    for copy in (hand2, hand1, *hand_adj):
        copy.wait_send()


def back(mid, g, dh, gated, wkv, r, k, v, at, bt, x, xk, xv, xr, wo, wk, wv, wr, fv, fk, fr, vecs, rates, carried, xprev, back2, sums2, spans, pads, keep, hops):
    rows, width = x.shape
    blocks = width // LANES
    quarter = width // 4
    fv = fv.reshape(2, 2, fv.shape[0] // 4, width)
    fk = fk.reshape(4, 2, 2, quarter, width)
    fr = fr.reshape(2, 2, quarter, width)
    block_rows = fv.shape[2] + 4 * quarter + 5 * quarter + 16
    chunks = sum(len(tick) for tick in PLAN)
    half = pltpu.VMEM((rows, width), BF16)
    tall = pltpu.VMEM((rows * blocks, LANES), F32)
    flat, flat8 = pltpu.VMEM((rows, width), F32), pltpu.VMEM((rows + 8, width), F32)
    eight = pltpu.VMEM((8, width), F32)
    lanes = [most for _, most in sorted(SLOT.values())]
    outs = [(fv.shape[2], LANES), (quarter, 4 * LANES)] + [(quarter, LANES)] * 5 + [(16, LANES)]
    result = pl.pallas_call(
        back_kernel,
        out_shape=[sds((rows, width), BF16)]
        + [sds(shape, F32) for shape in outs]
        + [sds((2, block_rows, width), BF16), sds((4, 2, 2, quarter, width), BF16), sds((2, 2, 16, width), BF16)],
        in_specs=[ANY] * 21 + [VMEM] * 6 + [SMEM] * 3,
        out_specs=[VMEM] * 9 + [ANY] * 3,
        scratch_shapes=[flat, flat, flat8, flat, flat8, tall, tall, tall, tall]
        + [half] * 8
        + [
            pltpu.VMEM((2, width, width), BF16),
            pltpu.VMEM((2, 4, quarter, 256), BF16),
            pltpu.VMEM((16, width), BF16),
            eight,
            eight,
            eight,
            pltpu.VMEM((2, blocks, LANES), F32),
            pltpu.VMEM((hops, 2, blocks, LANES), F32),
            pltpu.VMEM((7, 8, width), F32),
            pltpu.VMEM((2, 8, width), F32),
        ]
        + [pltpu.VMEM((2, 2, most, width), BF16) for most in lanes]
        + [pltpu.VMEM((RING, 2, 2, 2, 2, most, LANES), BF16) for most in lanes]
        + [pltpu.VMEM((2,) * (3 - d) + (block_rows, LANES), BF16) for d in range(4)]
        + [
            pltpu.SemaphoreType.DMA((20,)),
            pltpu.SemaphoreType.DMA((2, 4)),
            pltpu.SemaphoreType.DMA((2 + hops,)),
            pltpu.SemaphoreType.DMA((2 + hops,)),
            pltpu.SemaphoreType.DMA((chunks, STEPS)),
            pltpu.SemaphoreType.DMA((chunks, STEPS)),
            pltpu.SemaphoreType.DMA((len(lanes), 2)),
        ],
        compiler_params=pltpu.CompilerParams(
            vmem_limit_bytes=62 * MIB, collective_id=0, has_side_effects=True
        ),
        name="back",
    )(mid, g, dh, gated, wkv, r, k, v, at, bt, x, xk, xv, xr, wo, wk, wv, wr, fv, fk, fr, vecs, rates, carried, xprev, back2, sums2, spans, pads, keep)
    return result[:9]


def finish_kernel(*refs):
    count = len(refs) // 2
    sems = refs[-1]
    copies = [
        pltpu.make_async_copy(source, target, sems.at[i])
        for i, (source, target) in enumerate(zip(refs[:count], refs[count:-1]))
    ]
    for copy in copies:
        copy.start()
    for copy in copies:
        copy.wait()


def finish(arrays):
    return pl.pallas_call(
        finish_kernel,
        out_shape=[sds(a.shape, a.dtype) for a in arrays],
        in_specs=[ANY] * len(arrays),
        out_specs=[VMEM] * len(arrays),
        scratch_shapes=[pltpu.SemaphoreType.DMA((len(arrays),))],
        compiler_params=params(16),
        name="finish",
    )(*arrays)


def shift(value, steps):
    count = lax.axis_size("chan")
    pairs = [(i, i + steps) for i in range(count) if 0 <= i + steps < count]
    return lax.ppermute(value, "chan", pairs)


def scatter_sums(mats, vecs):
    def both(m):
        m = lax.psum_scatter(m, "chan", scatter_dimension=1, tiled=True)
        return lax.psum_scatter(m, "seq", scatter_dimension=0, tiled=True).astype(F32)

    v = lax.psum_scatter(vecs.astype(BF16), "chan", scatter_dimension=1, tiled=True).astype(F32)
    return [both(m) for m in mats], lax.psum(v, "seq")


def per_device(
    x, g, gain1, bias1, share_k, share_v, share_r, log_rate, boost, wk, wv, wr, wo, gain2, bias2, share_fk, share_fr,
    wfk, wfv, wfr, spans, pads,
):
    rows, width = x.shape
    chans = lax.axis_size("chan")
    total = rows * chans
    hops = max(1, min(chans - 1, total // 4 // rows))
    base = lambda: lax.axis_index("chan") * rows
    vecs = jnp.stack([gain1, bias1, share_k, share_v, share_r, gain2, bias2, share_fk, share_fr])
    rates = jnp.stack([log_rate, boost]).reshape(2 * width // LANES, LANES)
    begins = jnp.cumsum(spans[0]) - spans[0]
    pos = base() + jnp.arange(rows, dtype=jnp.int32)
    keep = 1.0 - jnp.any(pos[:, None] == begins[None, :], axis=1).astype(F32)

    xprev = shift(jnp.broadcast_to(x[rows - 1 :], (16, width)), 1)[:8]
    xk, xv, xr, k, v, r, at, bt, end = project(base, x, xprev, vecs, rates, spans, pads, keep, wk, wv, wr)
    carry = jnp.concatenate([shift(end, h + 1) for h in range(hops)], axis=0)
    wkv, gated, middle, last, carried = exit_call(base, hops, x, k, v, r, at, bt, carry, rates, vecs, spans, wo)
    hprev = jnp.broadcast_to(shift(last[7:], 1), (8, width))
    together = (lax.axis_size("seq"), chans, wfk.shape[1] // chans, width) == (4, 8, 4 * LANES, 8 * LANES)
    block_out, gfk, gfv, gfr, dh2, back2, sums2 = ffn(base, together, middle, g, hprev, vecs, spans, pads, wfr, wfk, wfv)
    if together:
        grad_in, *sums = back(
            middle, g, dh2, gated, wkv, r, k, v, at, bt, x, xk, xv, xr, wo, wk, wv, wr, gfv, gfk, gfr, vecs, rates,
            carried, xprev, back2, sums2, spans, pads, keep, hops,
        )
        gfv, gfk, gfr, gwo, gwr, gwv, gwk, vec = sums
        grad_in, gfv, gfk, gfr, gwo, gwr, gwv, gwk = finish([grad_in, gfv, gfk, gfr, gwo, gwr, gwv, gwk])
        return (block_out, grad_in, *[vec[i] for i in range(7)], gwk, gwv, gwr, gwo, *[vec[i] for i in range(7, 11)], gfk, gfv, gfr)
    dh2next = shift(back2, -1)
    dmid, gwo, dwkv, dr, sumsn2, adja, adjb, adjend = exit_back(
        base, middle, g, dh2, dh2next, vecs, rates, gated, wkv, r, k, v, at, bt, carried, spans, pads, keep, wo
    )
    adj = jnp.concatenate([shift(adjend, -h - 1) for h in range(hops)], axis=0)
    gwk, gwv, gwr, dh1, back1, sums1, wsums = project_back(
        base, hops, total, x, xprev, vecs, rates, k, v, dwkv, dr, at, bt, carried, adja, adjb, adj, xk, xv, xr, spans,
        pads, wk, wv, wr,
    )
    grad_in, sumsn1 = entry_back(x, dh1, shift(back1, -1), dmid, vecs)
    vec_parts = jnp.concatenate([sumsn1, sums1, wsums, sumsn2, sums2], axis=0).sum(axis=1)
    (gwk, gwv, gwr, gwo, gfk, gfv, gfr), vec = scatter_sums((gwk, gwv, gwr, gwo, gfk, gfv, gfr), vec_parts)
    return (block_out, grad_in, *[vec[i] for i in range(7)], gwk, gwv, gwr, gwo, *[vec[i] for i in range(7, 11)], gfk, gfv, gfr)


def solution(mesh):
    tokens, chan, both = P(("seq", "chan"), None), P("chan"), P("seq", "chan")
    placed = (tokens, tokens) + (P(),) * 18 + (P("seq", None),) * 2
    return jax.shard_map(
        per_device,
        mesh=mesh,
        in_specs=placed,
        out_specs=(tokens, tokens) + (chan,) * 7 + (both,) * 4 + (chan,) * 4 + (both,) * 3,
        check_vma=False,
    )
```

```python
import functools

import jax
import jax.numpy as jnp
from jax import lax
from jax.experimental import pallas as pl
from jax.experimental.pallas import tpu as pltpu
from jax.sharding import PartitionSpec as P

F32, BF16 = jnp.float32, jnp.bfloat16
LANES = 128
TILE = 64
MIB = 1 << 20
VMEM = pl.BlockSpec(memory_space=pltpu.VMEM)
SMEM = pl.BlockSpec(memory_space=pltpu.SMEM)
ANY = pl.BlockSpec(memory_space=pl.ANY)
G1, B1, SK, SV, SR, G2, B2, FK, FR = range(9)


def sds(shape, dtype):
    return jax.ShapeDtypeStruct(shape, dtype)


def params(limit_mib):
    return pltpu.CompilerParams(vmem_limit_bytes=limit_mib * MIB)


def dot(a, b):
    return jnp.dot(a, b, preferred_element_type=F32)


def dot_t(a, b):
    return lax.dot_general(a, b, (((1,), (1,)), ((), ())), preferred_element_type=F32)


def t_dot(a, b):
    return lax.dot_general(a, b, (((0,), (0,)), ((), ())), preferred_element_type=F32)


def fold8(v):
    return jnp.sum(v.reshape(v.shape[0] // 8, 8, v.shape[1]), axis=0)


def normalized(v):
    center = v - jnp.mean(v, axis=-1, keepdims=True)
    inv = lax.rsqrt(jnp.mean(center * center, axis=-1, keepdims=True) + 1e-05)
    return center * inv, inv


def norm_back(d_hat, hat, inv):
    return inv * (
        d_hat
        - jnp.mean(d_hat, axis=-1, keepdims=True)
        - hat * jnp.mean(d_hat * hat, axis=-1, keepdims=True)
    )


def marks(first, rows, spans, pads):
    pos = first + lax.broadcasted_iota(jnp.int32, (rows, LANES), 0)
    begin = 0
    start, real = pos < 0, pos < 0
    for i in range(spans.shape[1]):
        length = spans[0, i]
        start = start | (pos == begin)
        real = real | ((pos >= begin) & (pos < begin + length - pads[0, i]))
        begin = begin + length
    return start, real


def first_start_from(spans, at, otherwise):
    begin, best = 0, otherwise
    for i in range(spans.shape[1]):
        best = jnp.where((begin >= at) & (begin < best), begin, best)
        begin = begin + spans[0, i]
    return best


def last_start_before(spans, at):
    begin, best = 0, -(1 << 20)
    for i in range(spans.shape[1]):
        best = jnp.where(begin < at, begin, best)
        begin = begin + spans[0, i]
    return best


def wide(flag, width):
    return jnp.concatenate([flag] * (width // LANES), axis=1)


def with_previous(ref, at):
    block = ref[pl.ds(at, TILE + 8)]
    return block[8:], block[7 : TILE + 7]


def columns(j):
    return slice(j * LANES, (j + 1) * LANES)


def gather_carry(hops, rows, carry_ref, counts, rate):
    a, b = carry_ref[0], carry_ref[1]
    for h in range(1, hops):
        scale = jnp.exp(-rate * float(rows * h)) * counts[h]
        a, b = a + scale * carry_ref[2 * h], b + scale * carry_ref[2 * h + 1]
    return a, b


def project_kernel(
    base, x_ref, xprev_ref, vec_ref, rate_ref, spans, pads, keep_s, wk_hbm, wv_hbm, wr_hbm,
    xk_ref, xv_ref, xr_ref, k_ref, v_ref, r_ref, at_ref, bt_ref, end_ref,
    h_scr, ek_scr, ev_scr, w_scr, sems,
):
    rows, width = x_ref.shape
    blocks = width // LANES
    copies = [
        pltpu.make_async_copy(hbm, w_scr.at[i], sems.at[i])
        for i, hbm in enumerate((wk_hbm, wv_hbm, wr_hbm))
    ]
    for copy in copies:
        copy.start()
    first = base()
    gain, bias = vec_ref[G1 : G1 + 1], vec_ref[B1 : B1 + 1]
    prev = xprev_ref[...].astype(F32)
    h_scr[0:8] = normalized(prev)[0] * gain + bias

    @pl.loop(0, rows // TILE)
    def _(i):
        at = pl.multiple_of(i * TILE, TILE)
        hat, _ = normalized(x_ref[pl.ds(at, TILE)].astype(F32))
        h_scr[pl.ds(at + 8, TILE)] = hat * gain + bias

    @pl.loop(0, rows // TILE)
    def _(i):
        at = pl.multiple_of(i * TILE, TILE)
        start, _ = marks(first + at, TILE, spans, pads)
        keep = wide(1.0 - start.astype(F32), width)
        h, p = with_previous(h_scr, at)
        p = p * keep
        for row, out in ((SK, xk_ref), (SV, xv_ref), (SR, xr_ref)):
            share = vec_ref[row : row + 1]
            out[pl.ds(at, TILE)] = (h * share + p * (1.0 - share)).astype(BF16)

    _, real = marks(first, rows, spans, pads)
    real = real.astype(F32)
    step = 256
    for i, (src, out) in enumerate(((xk_ref, k_ref), (xv_ref, v_ref), (xr_ref, r_ref))):
        copies[i].wait()
        for j in range(width // step):
            tile = dot(src[...], w_scr[i, :, j * step : (j + 1) * step])
            out[:, j * step : (j + 1) * step] = tile.astype(out.dtype)
    for j in range(blocks):
        ek = jnp.exp(k_ref[:, columns(j)].astype(F32)) * real
        ek_scr[pl.ds(j, rows, stride=blocks)] = ek
        ev_scr[pl.ds(j, rows, stride=blocks)] = ek * v_ref[:, columns(j)].astype(F32)
    decay = jnp.exp(-jnp.exp(rate_ref[0:blocks]))

    def scan(t8, carry):
        a, b = carry
        for u in range(8):
            t = t8 * 8 + u
            keep = keep_s[t]
            here = pl.ds(pl.multiple_of(t * blocks, blocks), blocks)
            at_ref[here] = a * keep
            bt_ref[here] = b * keep
            fade = decay * keep
            a = a * fade + ev_scr[here]
            b = b * fade + ek_scr[here]
        return a, b

    zero = jnp.zeros((blocks, LANES), F32)
    a, b = lax.fori_loop(0, rows // 8, scan, (zero, zero))
    end_ref[0] = a
    end_ref[1] = b


def project(base, x, xprev, vecs, rates, spans, pads, keep, wk, wv, wr):
    rows, width = x.shape
    shape = (rows, width)
    tall = (rows * (width // LANES), LANES)
    return pl.pallas_call(
        functools.partial(project_kernel, base),
        out_shape=(
            [sds(shape, BF16)] * 5 + [sds(shape, F32)] + [sds(tall, F32)] * 2 + [sds((2, width // LANES, LANES), F32)]
        ),
        in_specs=[VMEM] * 4 + [SMEM] * 3 + [ANY] * 3,
        out_specs=[VMEM] * 9,
        scratch_shapes=[
            pltpu.VMEM((rows + 8, width), F32),
            pltpu.VMEM(tall, F32),
            pltpu.VMEM(tall, F32),
            pltpu.VMEM((3, width, width), BF16),
            pltpu.SemaphoreType.DMA((3,)),
        ],
        compiler_params=params(56),
        name="project",
    )(x, xprev, vecs, rates, spans, pads, keep, wk, wv, wr)


def wkv_parts(at, j, rows, blocks, k, v, at_ref, bt_ref, a_in, b_in, rate, boost, first_start):
    here = pl.ds(at * blocks + j, rows, stride=blocks)
    pos = at + lax.broadcasted_iota(jnp.int32, (rows, LANES), 0)
    lift = jnp.where(pos < first_start, jnp.exp(-rate[j : j + 1] * pos.astype(F32)), 0.0)
    a = at_ref[here] + lift * a_in[j : j + 1]
    b = bt_ref[here] + lift * b_in[j : j + 1]
    eu = jnp.exp(boost[j : j + 1] + k)
    inv = 1.0 / (b + eu)
    return a, b, eu, inv, (a + eu * v) * inv


def carry_counts(hops, rows, first, spans):
    last = last_start_before(spans, first)
    return [jnp.where(last < first - h * rows, 1.0, 0.0) for h in range(hops)]


def exit_kernel(
    base, hops, x_ref, k_ref, v_ref, r_ref, at_ref, bt_ref, carry_ref, rate_ref, vec_ref, spans, wo_hbm,
    wkv_ref, gated_ref, middle_ref, last_ref, in_ref, wo_scr, sem,
):
    rows, width = x_ref.shape
    blocks = width // LANES
    copy = pltpu.make_async_copy(wo_hbm, wo_scr, sem)
    copy.start()
    first = base()
    rate = jnp.exp(rate_ref[0:blocks])
    boost = rate_ref[blocks : 2 * blocks]
    a_in, b_in = gather_carry(hops, rows, carry_ref, carry_counts(hops, rows, first, spans), rate)
    in_ref[0] = a_in
    in_ref[1] = b_in
    first_start = first_start_from(spans, first, 1 << 20) - first

    @pl.loop(0, rows // TILE)
    def _(i):
        at = pl.multiple_of(i * TILE, TILE)
        for j in range(blocks):
            here = (pl.ds(at, TILE), columns(j))
            k, v = k_ref[here].astype(F32), v_ref[here].astype(F32)
            wkv = wkv_parts(at, j, TILE, blocks, k, v, at_ref, bt_ref, a_in, b_in, rate, boost, first_start)[-1]
            wkv = wkv.astype(BF16)
            wkv_ref[here] = wkv
            gated_ref[here] = (jax.nn.sigmoid(r_ref[here]) * wkv.astype(F32)).astype(BF16)

    copy.wait()
    step = 256
    for j in range(width // step):
        here = (slice(None), slice(j * step, (j + 1) * step))
        middle_ref[here] = x_ref[here].astype(F32) + dot(gated_ref[...], wo_scr[here])
    hat, _ = normalized(middle_ref[rows - 8 : rows])
    last_ref[...] = hat * vec_ref[G2 : G2 + 1] + vec_ref[B2 : B2 + 1]


def exit_call(base, hops, x, k, v, r, at, bt, carry, rates, vecs, spans, wo):
    rows, width = x.shape
    blocks = width // LANES
    return pl.pallas_call(
        functools.partial(exit_kernel, base, hops),
        out_shape=[
            sds((rows, width), BF16),
            sds((rows, width), BF16),
            sds((rows, width), F32),
            sds((8, width), F32),
            sds((2, blocks, LANES), F32),
        ],
        in_specs=[VMEM] * 9 + [SMEM, ANY],
        out_specs=[VMEM] * 5,
        scratch_shapes=[pltpu.VMEM((width, width), BF16), pltpu.SemaphoreType.DMA(())],
        compiler_params=params(56),
        name="exit",
    )(x, k, v, r, at, bt, carry, rates, vecs, spans, wo)


def ffn_kernel(
    base, mid_ref, g_ref, hprev_ref, vec_ref, spans, pads, wg_ref, wk_ref, wv_ref,
    out_ref, gfk_ref, gfv_ref, gfr_ref, dh_ref, back_ref, sums_ref,
    h_scr, ck_scr, cr_scr, ckt_scr, sig_scr, dvo_scr, val_scr, dck_scr, pass_scr,
):
    rows, width = mid_ref.shape
    step = pl.program_id(0)
    first = base()
    tiles = rows // TILE

    @pl.when(step == 0)
    def _():
        gain, bias = vec_ref[G2 : G2 + 1], vec_ref[B2 : B2 + 1]
        h_scr[0:8] = hprev_ref[...]

        @pl.loop(0, tiles)
        def _(i):
            at = pl.multiple_of(i * TILE, TILE)
            hat, _ = normalized(mid_ref[pl.ds(at, TILE)])
            h_scr[pl.ds(at + 8, TILE)] = hat * gain + bias

        @pl.loop(0, tiles)
        def _(i):
            at = pl.multiple_of(i * TILE, TILE)
            start, _ = marks(first + at, TILE, spans, pads)
            keep = wide(1.0 - start.astype(F32), width)
            h, p = with_previous(h_scr, at)
            p = p * keep
            for row, out in ((FK, ck_scr), (FR, cr_scr)):
                share = vec_ref[row : row + 1]
                out[pl.ds(at, TILE)] = (h * share + p * (1.0 - share)).astype(BF16)

        ckt_scr[...] = ck_scr[...].T
        _, real = marks(first, rows, spans, pads)
        real = wide(real.astype(F32), 256)
        for j in range(width // 256):
            here = (slice(None), slice(j * 256, (j + 1) * 256))
            sig = jax.nn.sigmoid(dot(cr_scr[...], wg_ref[here]))
            sig_scr[here] = sig
            dvo_scr[here] = (g_ref[here].astype(F32) * real * sig).astype(BF16)
        val_scr[...] = jnp.zeros_like(val_scr)
        dck_scr[...] = jnp.zeros_like(dck_scr)

    act = jnp.maximum(dot(ck_scr[...], wk_ref[...]), 0.0)
    hidden = (act * act).astype(BF16)
    val_scr[...] += dot(hidden, wv_ref[...])
    gfv_ref[...] = t_dot(hidden, dvo_scr[...]).astype(BF16)
    d_pre = (dot_t(dvo_scr[...], wv_ref[...]) * (2.0 * act)).astype(BF16)
    gfk_ref[...] = dot(ckt_scr[...], d_pre).astype(BF16)
    dck_scr[...] += dot_t(d_pre, wk_ref[...])

    @pl.when(step == pl.num_programs(0) - 1)
    def _():
        dgp_scr = dvo_scr
        _, real = marks(first, rows, spans, pads)
        real = wide(real.astype(F32), 256)
        for j in range(width // 256):
            here = (slice(None), slice(j * 256, (j + 1) * 256))
            sig, value = sig_scr[here], val_scr[here]
            out_ref[here] = (mid_ref[here] + sig * value).astype(BF16)
            top = g_ref[here].astype(F32) * real
            dgp_scr[here] = (top * value * sig * (1.0 - sig)).astype(BF16)
        for j in range(width // 256):
            here = (slice(None), slice(j * 256, (j + 1) * 256))
            gfr_ref[here] = t_dot(cr_scr[...], dgp_scr[here]).astype(BF16)
        dcr_scr = val_scr
        for j in range(width // 256):
            dcr_scr[:, j * 256 : (j + 1) * 256] = dot_t(dgp_scr[...], wg_ref[j * 256 : (j + 1) * 256])
        sums_ref[...] = jnp.zeros_like(sums_ref)
        share_k, share_r = vec_ref[FK : FK + 1], vec_ref[FR : FR + 1]

        @pl.loop(0, tiles)
        def _(i):
            at = pl.multiple_of(i * TILE, TILE)
            here = pl.ds(at, TILE)
            start, _ = marks(first + at, TILE, spans, pads)
            keep = wide(1.0 - start.astype(F32), width)
            h, p = with_previous(h_scr, at)
            diff = h - p * keep
            dck, dcr = dck_scr[here], dcr_scr[here]
            sums_ref[0] += fold8(diff * dck)
            sums_ref[1] += fold8(diff * dcr)
            pass_scr[here] = (dck * (1.0 - share_k) + dcr * (1.0 - share_r)) * keep
            dh_ref[here] = dck * share_k + dcr * share_r

        back_ref[...] = pass_scr[0:8]

        pass_scr[rows : rows + 8] = jnp.zeros((8, width), F32)

        @pl.loop(0, tiles)
        def _(i):
            at = pl.multiple_of(i * TILE, TILE)
            dh_ref[pl.ds(at, TILE)] += pass_scr[pl.ds(at, TILE + 8)][1 : TILE + 1]


def ffn(base, middle, g, hprev, vecs, spans, pads, wg, wk, wv):
    rows, width = middle.shape
    hid = wk.shape[1]
    unit = 512
    full = lambda shape: pl.BlockSpec(shape, lambda j: (0,) * len(shape))
    return pl.pallas_call(
        functools.partial(ffn_kernel, base),
        grid=(hid // unit,),
        out_shape=[
            sds((rows, width), BF16),
            sds((width, hid), BF16),
            sds((hid, width), BF16),
            sds((width, width), BF16),
            sds((rows, width), F32),
            sds((8, width), F32),
            sds((2, 8, width), F32),
        ],
        in_specs=[
            full((rows, width)),
            full((rows, width)),
            full((8, width)),
            full(vecs.shape),
            SMEM,
            SMEM,
            full((width, width)),
            pl.BlockSpec((width, unit), lambda j: (0, j)),
            pl.BlockSpec((unit, width), lambda j: (j, 0)),
        ],
        out_specs=[
            full((rows, width)),
            pl.BlockSpec((width, unit), lambda j: (0, j)),
            pl.BlockSpec((unit, width), lambda j: (j, 0)),
            full((width, width)),
            full((rows, width)),
            full((8, width)),
            full((2, 8, width)),
        ],
        scratch_shapes=[
            pltpu.VMEM((rows + 8, width), F32),
            pltpu.VMEM((rows, width), BF16),
            pltpu.VMEM((rows, width), BF16),
            pltpu.VMEM((width, rows), BF16),
            pltpu.VMEM((rows, width), F32),
            pltpu.VMEM((rows, width), BF16),
            pltpu.VMEM((rows, width), F32),
            pltpu.VMEM((rows, width), F32),
            pltpu.VMEM((rows + 8, width), F32),
        ],
        compiler_params=params(60),
        name="ffn",
    )(middle, g, hprev, vecs, spans, pads, wg, wk, wv)


def exit_back_kernel(
    base, mid_ref, g_ref, dh_ref, dhnext_ref, vec_ref, rate_ref, gated_ref, wkv_ref, r_ref, k_ref, v_ref, at_ref, bt_ref,
    in_ref, spans, pads, keep_s, wo_ref,
    dmid_ref, gwo_ref, dwkv_ref, dr_ref, sums_ref, adja_ref, adjb_ref, adjend_ref,
    datt_scr, dn_scr, dd_scr,
):
    rows, width = mid_ref.shape
    blocks = width // LANES
    first = base()
    gain = vec_ref[G2 : G2 + 1]
    sums_ref[...] = jnp.zeros_like(sums_ref)
    tail = dhnext_ref[...]
    row = lax.broadcasted_iota(jnp.int32, tail.shape, 0)
    dh_ref[rows - 8 : rows] += jnp.where(row == 7, pltpu.roll(tail, 7, axis=0), 0.0)

    @pl.loop(0, rows // TILE)
    def _(i):
        at = pl.multiple_of(i * TILE, TILE)
        here = pl.ds(at, TILE)
        _, real = marks(first + at, TILE, spans, pads)
        hat, inv = normalized(mid_ref[here])
        dh = dh_ref[here]
        sums_ref[0] += fold8(dh * hat)
        sums_ref[1] += fold8(dh)
        d_mid = norm_back(dh * gain, hat, inv) + g_ref[here].astype(F32) * wide(real.astype(F32), width)
        dmid_ref[here] = d_mid
        datt_scr[here] = d_mid.astype(BF16)

    step = 256
    rate = jnp.exp(rate_ref[0:blocks])
    boost = rate_ref[blocks : 2 * blocks]
    a_in, b_in = in_ref[0], in_ref[1]
    first_start = first_start_from(spans, first, 1 << 20) - first
    for j in range(width // step):
        here = (slice(None), slice(j * step, (j + 1) * step))
        dr_ref[here] = dot_t(datt_scr[...], wo_ref[j * step : (j + 1) * step]).astype(BF16)
    d_gated = dr_ref

    @pl.loop(0, rows // TILE)
    def _(i):
        at = pl.multiple_of(i * TILE, TILE)
        for j in range(blocks):
            here = (pl.ds(at, TILE), columns(j))
            sig = jax.nn.sigmoid(r_ref[here])
            dg = d_gated[here].astype(F32)
            dwkv = (dg * sig).astype(BF16)
            dwkv_ref[here] = dwkv
            dr_ref[here] = (dg * wkv_ref[here].astype(F32) * sig * (1.0 - sig)).astype(BF16)
            k, v = k_ref[here].astype(F32), v_ref[here].astype(F32)
            _, _, _, inv, wkv = wkv_parts(
                at, j, TILE, blocks, k, v, at_ref, bt_ref, a_in, b_in, rate, boost, first_start
            )
            dn = dwkv.astype(F32) * inv
            there = pl.ds(at * blocks + j, TILE, stride=blocks)
            dn_scr[there] = dn
            dd_scr[there] = -dn * wkv

    decay = jnp.exp(-rate)

    def scan(t8, carry):
        a, b = carry
        for u in range(8):
            t = rows - 1 - (t8 * 8 + u)
            keep = keep_s[t]
            here = pl.ds(pl.multiple_of(t * blocks, blocks), blocks)
            adja_ref[here] = a
            adjb_ref[here] = b
            fade = decay * keep
            a = a * fade + dn_scr[here] * keep
            b = b * fade + dd_scr[here] * keep
        return a, b

    zero = jnp.zeros((blocks, LANES), F32)
    a, b = lax.fori_loop(0, rows // 8, scan, (zero, zero))
    adjend_ref[0] = a
    adjend_ref[1] = b
    for j in range(width // step):
        here = (slice(None), slice(j * step, (j + 1) * step))
        gwo_ref[here] = t_dot(gated_ref[...], datt_scr[here]).astype(BF16)


def exit_back(base, middle, g, dh, dhnext, vecs, rates, gated, wkv, r, k, v, at, bt, carry, spans, pads, keep, wo):
    rows, width = middle.shape
    blocks = width // LANES
    tall = (rows * blocks, LANES)
    return pl.pallas_call(
        functools.partial(exit_back_kernel, base),
        out_shape=[
            sds((rows, width), F32),
            sds((width, width), BF16),
            sds((rows, width), BF16),
            sds((rows, width), BF16),
            sds((2, 8, width), F32),
            sds(tall, F32),
            sds(tall, F32),
            sds((2, blocks, LANES), F32),
        ],
        in_specs=[VMEM] * 14 + [SMEM] * 3 + [VMEM],
        out_specs=[VMEM] * 8,
        scratch_shapes=[
            pltpu.VMEM((rows, width), BF16),
            pltpu.VMEM(tall, F32),
            pltpu.VMEM(tall, F32),
        ],
        compiler_params=params(60),
        name="exit_back",
    )(middle, g, dh, dhnext, vecs, rates, gated, wkv, r, k, v, at, bt, carry, spans, pads, keep, wo)


def project_back_kernel(
    base, hops, total, x_ref, xprev_ref, vec_ref, rate_ref, k_ref, v_ref, dwkv_ref, dr_ref, at_ref, bt_ref, in_ref,
    adja_ref, adjb_ref, adj_ref, xk_ref, xv_ref, xr_ref, spans, pads, wk_hbm, wv_hbm, wr_hbm,
    gwk_ref, gwv_ref, gwr_ref, dh_ref, back_ref, sums_ref, wsums_ref,
    h_scr, dk_scr, dv_scr, d_scr, pass_scr, w_scr, sems,
):
    rows, width = x_ref.shape
    blocks = width // LANES
    copies = [
        pltpu.make_async_copy(hbm, w_scr.at[i], sems.at[i])
        for i, hbm in enumerate((wk_hbm, wv_hbm, wr_hbm))
    ]
    for copy in copies:
        copy.start()
    first = base()
    rate = jnp.exp(rate_ref[0:blocks])
    boost = rate_ref[blocks : 2 * blocks]
    a_in, b_in = in_ref[0], in_ref[1]
    first_start = first_start_from(spans, first, 1 << 20) - first
    last_start = last_start_before(spans, first + rows) - first
    after = first_start_from(spans, first + rows, total)
    counts = [jnp.where(after >= first + (h + 1) * rows, 1.0, 0.0) for h in range(hops)]
    adj_a, adj_b = gather_carry(hops, rows, adj_ref, counts, rate)
    wsums_ref[...] = jnp.zeros_like(wsums_ref)
    sums_ref[...] = jnp.zeros_like(sums_ref)

    @pl.loop(0, rows // TILE)
    def _(i):
        at = pl.multiple_of(i * TILE, TILE)
        _, real = marks(first + at, TILE, spans, pads)
        real = real.astype(F32)
        pos = at + lax.broadcasted_iota(jnp.int32, (TILE, LANES), 0)
        for j in range(blocks):
            here = (pl.ds(at, TILE), columns(j))
            k, v = k_ref[here].astype(F32), v_ref[here].astype(F32)
            a, b, eu, inv, wkv = wkv_parts(
                at, j, TILE, blocks, k, v, at_ref, bt_ref, a_in, b_in, rate, boost, first_start
            )
            there = pl.ds(at * blocks + j, TILE, stride=blocks)
            lift = jnp.where(
                pos >= last_start, jnp.exp(-rate[j : j + 1] * (rows - 1 - pos).astype(F32)), 0.0
            )
            post_a = adja_ref[there] + lift * adj_a[j : j + 1]
            post_b = adjb_ref[there] + lift * adj_b[j : j + 1]
            dn = dwkv_ref[here].astype(F32) * inv
            own = eu * dn
            weight = jnp.exp(k) * real
            dv_scr[here] = (own + weight * post_a).astype(BF16)
            first_term = own * (v - wkv)
            dk_scr[here] = (first_term + weight * (v * post_a + post_b)).astype(BF16)
            wsums_ref[0, :, columns(j)] += fold8(a * post_a + b * post_b)
            wsums_ref[1, :, columns(j)] += fold8(first_term)

    for j in range(blocks):
        r = rate[j : j + 1]
        wsums_ref[0, :, columns(j)] *= -r * jnp.exp(-r)
    gain, bias = vec_ref[G1 : G1 + 1], vec_ref[B1 : B1 + 1]
    h_scr[0:8] = normalized(xprev_ref[...].astype(F32))[0] * gain + bias

    @pl.loop(0, rows // TILE)
    def _(i):
        at = pl.multiple_of(i * TILE, TILE)
        hat, _ = normalized(x_ref[pl.ds(at, TILE)].astype(F32))
        h_scr[pl.ds(at + 8, TILE)] = hat * gain + bias

    step = 256
    dh_ref[...] = jnp.zeros_like(dh_ref)
    groups = ((dk_scr, xk_ref, gwk_ref, SK), (dv_scr, xv_ref, gwv_ref, SV), (dr_ref, xr_ref, gwr_ref, SR))
    pass_scr[...] = jnp.zeros_like(pass_scr)
    for i, (grad, mixed, out, row) in enumerate(groups):
        copies[i].wait()
        for j in range(width // step):
            here = (slice(None), slice(j * step, (j + 1) * step))
            d_scr[:, j * step : (j + 1) * step] = dot_t(grad[...], w_scr[i, j * step : (j + 1) * step])
            out[here] = t_dot(mixed[...], grad[here]).astype(BF16)
        share = vec_ref[row : row + 1]

        @pl.loop(0, rows // TILE)
        def _(t):
            at = pl.multiple_of(t * TILE, TILE)
            here = pl.ds(at, TILE)
            start, _ = marks(first + at, TILE, spans, pads)
            keep = wide(1.0 - start.astype(F32), width)
            h, p = with_previous(h_scr, at)
            d = d_scr[here]
            sums_ref[i] += fold8((h - p * keep) * d)
            pass_scr[here] += d * (1.0 - share) * keep
            dh_ref[here] += d * share

    back_ref[...] = pass_scr[0:8]

    @pl.loop(0, rows // TILE)
    def _(i):
        at = pl.multiple_of(i * TILE, TILE)
        dh_ref[pl.ds(at, TILE)] += pass_scr[pl.ds(at, TILE + 8)][1 : TILE + 1]


def project_back(base, hops, total, x, xprev, vecs, rates, k, v, dwkv, dr, at, bt, carry, adja, adjb, adj, xk, xv, xr, spans, pads, wk, wv, wr):
    rows, width = x.shape
    return pl.pallas_call(
        functools.partial(project_back_kernel, base, hops, total),
        out_shape=[sds((width, width), BF16)] * 3
        + [
            sds((rows, width), F32),
            sds((8, width), F32),
            sds((3, 8, width), F32),
            sds((2, 8, width), F32),
        ],
        in_specs=[VMEM] * 17 + [SMEM] * 2 + [ANY] * 3,
        out_specs=[VMEM] * 7,
        scratch_shapes=[
            pltpu.VMEM((rows + 8, width), F32),
            pltpu.VMEM((rows, width), BF16),
            pltpu.VMEM((rows, width), BF16),
            pltpu.VMEM((rows, width), F32),
            pltpu.VMEM((rows + 8, width), F32),
            pltpu.VMEM((3, width, width), BF16),
            pltpu.SemaphoreType.DMA((3,)),
        ],
        compiler_params=params(60),
        name="project_back",
    )(x, xprev, vecs, rates, k, v, dwkv, dr, at, bt, carry, adja, adjb, adj, xk, xv, xr, spans, pads, wk, wv, wr)


def entry_back_kernel(x_ref, dh_ref, dhnext_ref, dmid_ref, vec_ref, out_ref, sums_ref):
    rows = x_ref.shape[0]
    gain = vec_ref[G1 : G1 + 1]
    sums_ref[...] = jnp.zeros_like(sums_ref)
    tail = dhnext_ref[...]
    row = lax.broadcasted_iota(jnp.int32, tail.shape, 0)
    dh_ref[rows - 8 : rows] += jnp.where(row == 7, pltpu.roll(tail, 7, axis=0), 0.0)

    @pl.loop(0, rows // TILE)
    def _(i):
        here = pl.ds(pl.multiple_of(i * TILE, TILE), TILE)
        hat, inv = normalized(x_ref[here].astype(F32))
        dh = dh_ref[here]
        sums_ref[0] += fold8(dh * hat)
        sums_ref[1] += fold8(dh)
        out_ref[here] = (norm_back(dh * gain, hat, inv) + dmid_ref[here]).astype(BF16)


def entry_back(x, dh, dhnext, dmid, vecs):
    rows, width = x.shape
    return pl.pallas_call(
        entry_back_kernel,
        out_shape=[sds((rows, width), BF16), sds((2, 8, width), F32)],
        in_specs=[VMEM] * 5,
        out_specs=[VMEM] * 2,
        compiler_params=params(40),
        name="entry_back",
    )(x, dh, dhnext, dmid, vecs)


X, Y, Z = "x", "y", "z"
ORDERS = {
    X: ("x", "y", "low", "high"),
    Y: ("y", "x", "low", "high"),
    Z: ("low", "high", "x", "y"),
}
AXIS_BIT = {"core": ("seq", 1), "x": ("seq", 2), "y": ("chan", 1), "low": ("chan", 2), "high": ("chan", 4)}
STEPS = 5
RING = 3
MESH = pl.DeviceIdType.MESH
ARRAYS = ("fv", "fk0", "fk1", "fk2", "fk3", "fr", "wo", "wr", "wv", "wk", "vec")
UNITS = (0, 4, 1, 5, 2, 6, 3, 7)


def third(name):
    return ((name, 0, 96, X), (name, 96, 96, Y), (name, 192, 64, Z))


PLAN = tuple(
    tick
    for q in range(4)
    for tick in (
        (("fv", q * 128, 128, X), ("fv", (q + 4) * 128, 128, Y)),
        ((f"fk{q}", 0, 64, X), (f"fk{q}", 64, 64, Y), (f"fk{q}", 128, 128, Z)),
    )
) + (third("fr"), third("wo"), third("wr"), third("wv"), third("wk") + (("vec", 0, 16, Y),))
SLOT = {X: (0, 128), Y: (1, 128), Z: (2, 128), "vec": (3, 16)}


def bit_of(index, weight):
    return index // weight % 2


def partner(axis):
    name, weight = AXIS_BIT[axis]
    where = {"seq": lax.axis_index("seq"), "chan": lax.axis_index("chan")}
    bit = bit_of(where[name], weight)
    where[name] = where[name] + weight * (1 - 2 * bit)
    return bit, (where["seq"], where["chan"])


class Summing:
    def __init__(self, grads, received, outs, stages, rings, levels, sems):
        self.grads, self.received, self.outs = grads, received, outs
        self.stages, self.rings, self.levels = stages, rings, levels
        self.send_sems, self.recv_sems, self.stage_sems = sems
        self.sides = {axis: partner(axis) for axis in AXIS_BIT}
        self.chunks = [chunk for tick in PLAN for chunk in tick]
        self.tick_of = [t for t, tick in enumerate(PLAN) for _ in tick]
        self.ticks = [[n for n, t in enumerate(self.tick_of) if t == tick] for tick in range(len(PLAN))]
        self.bases, filled = {}, 0
        for name in ARRAYS:
            self.bases[name] = filled
            filled += grads[name]().shape[2]
        self.done = set()
        self.pending = list(self.actions())

    def place(self, number):
        array, first, rows, stream = self.chunks[number]
        lane = SLOT["vec" if array == "vec" else stream][0]
        return array, first, rows, stream, lane, pl.ds(self.bases[array] + first, rows)

    def key(self, number):
        array, first, _, _ = self.chunks[number]
        return f"fv{first // 128}" if array == "fv" else array

    def across(self, number):
        array, first, rows, _, _, there = self.place(number)
        core, mate = self.sides["core"]
        return pltpu.make_async_remote_copy(
            src_ref=self.grads[array]().at[:, 1 - core, pl.ds(first, rows)],
            dst_ref=self.received.at[:, there],
            send_sem=self.send_sems.at[number, 0],
            recv_sem=self.recv_sems.at[number, 0],
            device_id=mate,
            device_id_type=MESH,
        )

    def staged(self, number):
        array, first, rows, _, lane, there = self.place(number)
        core, _ = self.sides["core"]
        stage = self.stages[lane]
        return (
            pltpu.make_async_copy(
                self.grads[array]().at[:, core, pl.ds(first, rows)], stage.at[0, :, 0:rows], self.stage_sems.at[lane, 0]
            ),
            pltpu.make_async_copy(self.received.at[:, there], stage.at[1, :, 0:rows], self.stage_sems.at[lane, 1]),
        )

    def send(self, number, step):
        _, _, rows, stream, lane, there = self.place(number)
        bit, mate = self.sides[ORDERS[stream][step - 1]]
        free = (slice(None),) * (4 - step)
        if step == 1:
            source = self.rings[lane].at[(self.tick_of[number] % RING, 1 - bit, *free, slice(0, rows))]
        else:
            source = self.levels[step - 2].at[(1 - bit, *free, there)]
        return pltpu.make_async_remote_copy(
            src_ref=source,
            dst_ref=self.levels[step - 1].at[(*free, there)],
            send_sem=self.send_sems.at[number, step],
            recv_sem=self.recv_sems.at[number, step],
            device_id=mate,
            device_id_type=MESH,
        )

    def start_stage(self, number):
        self.across(number).wait_recv()
        for copy in self.staged(number):
            copy.start()

    def first_sum(self, number):
        _, _, rows, stream, lane, _ = self.place(number)
        tick = self.tick_of[number]
        stage, ring = self.stages[lane], self.rings[lane]
        other = self.before(number)
        if other is not None:
            self.send(other, 1).wait_send()
        for copy in self.staged(number):
            copy.wait()

        @pl.loop(0, 16)
        def _(i):
            c = i % 8
            bits = {"x": i // 8, "y": c % 2, "low": c // 2 % 2, "high": c // 4}
            cols = pl.ds(pl.multiple_of(c * LANES, LANES), LANES)
            total = stage[0, i // 8, 0:rows, cols].astype(F32) + stage[1, i // 8, 0:rows, cols].astype(F32)
            at = tuple(bits[axis] for axis in ORDERS[stream])
            ring[(tick % RING, *at, slice(0, rows))] = total.astype(BF16)

        self.send(number, 1).start()

    def later_sum(self, number, step):
        array, first, rows, stream, lane, there = self.place(number)
        bit, _ = self.sides[ORDERS[stream][step - 1]]
        target = self.levels[step - 1]
        self.send(number, step).wait_recv()
        if step == 1:
            source, lead, here = self.rings[lane], (self.tick_of[number] % RING, bit), slice(0, rows)
        else:
            source, lead, here = self.levels[step - 2], (bit,), there
        if step == 4:
            out, cols = self.outs[array]
            out[first : first + rows, cols] = source[(*lead, here)].astype(F32) + target[there].astype(F32)
            return

        @pl.loop(0, 1 << (4 - step))
        def _(i):
            at = tuple(i // (1 << (3 - step - d)) % 2 for d in range(4 - step))
            total = source[(*lead, *at, here)].astype(F32) + target[(*at, there)].astype(F32)
            target[(*at, there)] = total.astype(BF16)

        self.send(number, step + 1).start()

    def actions(self):
        ticks = self.ticks
        for tick in range(len(ticks) + 4):
            if tick == 0:
                for n in ticks[0]:
                    yield self.key(n), functools.partial(self.start_stage, n)
            if tick < len(ticks):
                for n in ticks[tick]:
                    yield None, functools.partial(self.first_sum, n)
            for step in range(1, 5):
                if 0 <= tick - step < len(ticks):
                    for n in ticks[tick - step]:
                        yield None, functools.partial(self.later_sum, n, step)
                if step == 1 and tick + 1 < len(ticks):
                    for n in ticks[tick + 1]:
                        yield self.key(n), functools.partial(self.start_stage, n)

    def complete(self, key):
        self.done.add(key)
        for n in range(len(self.chunks)):
            if self.key(n) == key:
                self.across(n).start()

    def pump(self, count):
        while count and self.pending and (self.pending[0][0] is None or self.pending[0][0] in self.done):
            self.pending.pop(0)[1]()
            count -= 1

    def before(self, number):
        same = lambda o: (self.place(o)[4], self.tick_of[o] % RING)
        earlier = [o for o in range(number) if same(o) == same(number)]
        return earlier[-1] if earlier else None

    def finish(self):
        count = len(self.chunks)
        waited = {self.before(n) for n in range(count)}
        for n in range(count):
            self.across(n).wait_send()
            for step in range(1, STEPS):
                if step > 1 or n not in waited:
                    self.send(n, step).wait_send()


def view(ref, *index):
    return lambda: ref.at[index]


class Copies:
    def __init__(self, sems):
        self.sems, self.all, self.waited = sems, {}, set()

    def start(self, name, source, target):
        assert name not in self.all
        self.all[name] = (source, target, len(self.all))
        self.copy(name).start()

    def copy(self, name):
        source, target, number = self.all[name]
        source, target = (r() if callable(r) else r for r in (source, target))
        return pltpu.make_async_copy(source, target, self.sems.at[number])

    def wait(self, *names):
        for name in names:
            if name not in self.waited:
                self.copy(name).wait()
                self.waited.add(name)

    def finish(self):
        self.wait(*self.all)


def block_kernel(*refs):
    (
        x_h, g_h, wk_h, wv_h, wr_h, wo_h, wfk_h, wfv_h, wfr_h,
        gain1_ref, bias1_ref, sk_ref, sv_ref, sr_ref, gain2_ref, bias2_ref, fk_ref, fr_ref, rate_ref, boost_ref,
        spans, pads,
        out_h, gin_h, ofv, ofk, ofr, owo, owr, owv, owk, ovec,
        received, gw_h, gfv_h, gfk_h, gvec_h, spill_b, spill_r, spill_t,
        mid, dh, h_scr, d_scr, pass_scr, b0, b1, b2, b3, b4, b5, b6, b7, w_scr, tile_scr, vec_scr,
        keep_scr, real_scr, xlast, halo2, halob2, halo1, mine2, mine1, mineb2, st_mine, st_in, adj_mine, adj_in, in_scr,
        sums, wsums, s0, s1, s2, s3, g0, g1, g2, g3, l1, l2, l3, l4,
        copy_sems, halo_send, halo_recv, send_sems, recv_sems, stage_sems,
    ) = refs
    rows, width = x_h.shape
    blocks = width // LANES
    chans = lax.axis_size("chan")
    seq, chan = lax.axis_index("seq"), lax.axis_index("chan")
    first = chan * rows
    total = rows * chans
    hops = adj_in.shape[0]
    tiles = rows // TILE
    step = 256
    quarter = width // 4

    grads = {"fv": lambda: gfv_h, "vec": lambda: gvec_h}
    outs = {"fv": (ofv, slice(None)), "vec": (ovec, slice(None))}
    for i in range(4):
        grads[f"fk{i}"], outs[f"fk{i}"] = view(gfk_h, i), (ofk, columns(i))
    names = ("fr", "wo", "wr", "wv", "wk")
    for i, (name, out) in enumerate(zip(names, (ofr, owo, owr, owv, owk))):
        grads[name], outs[name] = view(gw_h, i), (out, slice(None))
    summing = Summing(
        grads, received, outs, (s0, s1, s2, s3), (g0, g1, g2, g3), (l1, l2, l3, l4), (send_sems, recv_sems, stage_sems)
    )
    pump = summing.pump
    copies = Copies(copy_sems)
    start, wait = copies.start, copies.wait

    def row_tiles(body, lo=0, hi=tiles):
        @pl.loop(lo, hi)
        def _(i):
            at = pl.multiple_of(i * TILE, TILE)
            body(at, pl.ds(at, TILE))

    def col(j):
        return slice(j * step, (j + 1) * step)

    def spread(ref, here, to=width):
        return wide(ref[here], to)

    def hand(source, target, number, offset):
        return lambda: pltpu.make_async_remote_copy(
            src_ref=source() if callable(source) else source,
            dst_ref=target() if callable(target) else target,
            send_sem=halo_send.at[number],
            recv_sem=halo_recv.at[number],
            device_id=(seq, (chan + chans + offset) % chans),
            device_id_type=MESH,
        )

    hand_x = hand(view(x_h, pl.ds(rows - 16, 16)), xlast, 0, 1)
    hand_h2 = hand(mine2, halo2, 1, 1)
    hand_b2 = hand(mineb2, halob2, 2, -1)
    hand_b1 = hand(mine1, halo1, 3, -1)
    hand_st = [hand(st_mine, view(st_in, h), 4 + h, h + 1) for h in range(hops)]
    hand_adj = [hand(adj_mine, view(adj_in, h), 4 + hops + h, -h - 1) for h in range(hops)]

    x, xk, xv, xr, k, v = b0, b1, b2, b3, b4, b5
    start("x", x_h, x)
    start("wk", wk_h, view(w_scr, 0))
    start("wv", wv_h, view(w_scr, 1))
    around = [(seq, (chan + chans + d) % chans) for h in range(hops) for d in (h + 1, -h - 1)]
    barrier = pltpu.get_barrier_semaphore()
    mates = [mate for _, mate in summing.sides.values()] + around
    for mate in mates:
        pl.semaphore_signal(barrier, inc=1, device_id=mate, device_id_type=MESH)

    rate = jnp.exp(rate_ref[...])
    decay = jnp.exp(-rate)
    boost = boost_ref[...]
    gain1, bias1, gain2, bias2 = gain1_ref[...], bias1_ref[...], gain2_ref[...], bias2_ref[...]
    sums[...] = jnp.zeros_like(sums)
    wsums[...] = jnp.zeros_like(wsums)
    first_start = first_start_from(spans, first, 1 << 20) - first
    last_start = last_start_before(spans, first + rows) - first
    before = last_start_before(spans, first)
    after = first_start_from(spans, first + rows, total)

    def marks_tile(at, here):
        begins, real = marks(first + at, TILE, spans, pads)
        keep_scr[here] = 1.0 - begins.astype(F32)
        real_scr[here] = real.astype(F32)

    row_tiles(marks_tile)
    wait("x")

    def norm1_of(at, here):
        hat, _ = normalized(x[here].astype(F32))
        h_scr[pl.ds(at + 8, TILE)] = hat * gain1 + bias1

    row_tiles(norm1_of)
    pl.semaphore_wait(barrier, len(mates))
    hand_x().start()

    def halo1_rows():
        h_scr[0:8] = normalized(xlast[8:16].astype(F32))[0] * gain1 + bias1

    def mixed(at, here, shares):
        keep = spread(keep_scr, here)
        h, p = with_previous(h_scr, at)
        p = p * keep
        for share_ref, out in shares:
            share = share_ref[...]
            out[here] = (h * share + p * (1.0 - share)).astype(BF16)

    mix1 = functools.partial(mixed, shares=((sk_ref, xk), (sv_ref, xv), (sr_ref, xr)))
    row_tiles(mix1, 1)
    hand_x().wait_recv()
    halo1_rows()
    row_tiles(mix1, 0, 1)

    def wkv_at(at, j, at_scr, bt_scr):
        here = (pl.ds(at, TILE), columns(j))
        return wkv_parts(
            at, j, TILE, blocks, k[here].astype(F32), v[here].astype(F32), at_scr, bt_scr, in_scr[0], in_scr[1],
            rate, boost, first_start,
        )

    def forward(at_scr, bt_scr, ev_scr, ek_scr):
        wait("wk")
        for j in range(width // step):
            k[:, col(j)] = dot(xk[...], w_scr[0, :, col(j)]).astype(BF16)
        start("wr", wr_h, view(w_scr, 0))
        wait("wv")
        for j in range(width // step):
            v[:, col(j)] = dot(xv[...], w_scr[1, :, col(j)]).astype(BF16)
        start("wo", wo_h, view(w_scr, 1))

        def weights_tile(at, here):
            real = real_scr[here]
            for j in range(blocks):
                there = pl.ds(at * blocks + j, TILE, stride=blocks)
                ek = jnp.exp(k[here, columns(j)].astype(F32)) * real
                ek_scr[there] = ek
                ev_scr[there] = ek * v[here, columns(j)].astype(F32)

        row_tiles(weights_tile)

        def scan(t8, carry):
            a, b = carry
            for u in range(8):
                t = t8 * 8 + u
                keep = keep_scr[pl.ds(t, 1)]
                here = pl.ds(pl.multiple_of(t * blocks, blocks), blocks)
                a = a * keep
                b = b * keep
                at_scr[here] = a
                bt_scr[here] = b
                a = a * decay + ev_scr[here]
                b = b * decay + ek_scr[here]
            return a, b

        zero = jnp.zeros((blocks, LANES), F32)
        st_mine[0], st_mine[1] = lax.fori_loop(0, rows // 8, scan, (zero, zero))
        for copy in hand_st:
            copy().start()
        start("xk out", xk, view(spill_b, 0))
        start("xv out", xv, view(spill_b, 1))
        start("xr out", xr, view(spill_b, 2))
        start("at out", at_scr, view(spill_t, 0))
        start("bt out", bt_scr, view(spill_t, 1))
        r = d_scr
        wait("wr")
        for j in range(width // step):
            r[:, col(j)] = dot(xr[...], w_scr[0, :, col(j)])
        start("wfr", wfr_h, view(w_scr, 0))
        start("r out", r, spill_r)
        for copy in hand_st:
            copy().wait_recv()
        a_in, b_in = st_in[0, 0], st_in[0, 1]
        for h in range(1, hops):
            scale = jnp.exp(-rate * float(rows * h)) * jnp.where(before < first - h * rows, 1.0, 0.0)
            a_in, b_in = a_in + scale * st_in[h, 0], b_in + scale * st_in[h, 1]
        in_scr[0], in_scr[1] = a_in, b_in
        wkv, gated = b6, b7

        def outputs_tile(at, here):
            for j in range(blocks):
                out = wkv_at(at, j, at_scr, bt_scr)[-1].astype(BF16)
                wkv[here, columns(j)] = out
                gated[here, columns(j)] = (jax.nn.sigmoid(r[here, columns(j)]) * out.astype(F32)).astype(BF16)

        row_tiles(outputs_tile)
        start("k out", k, view(spill_b, 3))
        start("v out", v, view(spill_b, 4))
        start("wkv out", wkv, view(spill_b, 5))
        start("gated out", gated, view(spill_b, 6))
        wait("at out", "bt out")

    tall = pltpu.VMEM((rows * blocks, LANES), F32)
    pl.run_scoped(forward, tall, tall, tall, tall)

    def ffn(wk_scr, wv_scr, ckt_scr, fv_tile, fk_tile):
        def load_unit(index):
            unit, slot = UNITS[index], index % 2
            for s in range(4):
                at = s * (wfk_h.shape[1] // 4) + unit * LANES
                start(f"wfk{index} {s}", view(wfk_h, slice(None), pl.ds(at, LANES)), view(wk_scr, slot, slice(None), columns(s)))
                start(f"wfv{index} {s}", view(wfv_h, pl.ds(at, LANES)), view(wv_scr, slot, columns(s)))

        load_unit(0)
        load_unit(1)
        gated, g, ck, cr, dvo = b7, b0, b1, b2, b3
        wait("wo")
        for j in range(width // step):
            mid[:, col(j)] = x[:, col(j)].astype(F32) + dot(gated[...], w_scr[1, :, col(j)])
        start("g", g_h, g)
        mine2[...] = normalized(mid[rows - 8 : rows])[0] * gain2 + bias2
        hand_h2().start()

        def norm2_of(at, here):
            hat, _ = normalized(mid[here])
            h_scr[pl.ds(at + 8, TILE)] = hat * gain2 + bias2

        row_tiles(norm2_of)
        wait("xk out", "xv out", "xr out")
        mix2 = functools.partial(mixed, shares=((fk_ref, ck), (fr_ref, cr)))
        row_tiles(mix2, 1)
        hand_h2().wait_recv()
        h_scr[0:8] = halo2[...]
        row_tiles(mix2, 0, 1)
        ckt_scr[...] = ck[...].T
        sig, dck = d_scr, dh
        wait("wfr", "r out", "g")
        real = spread(real_scr, slice(None), step)
        for j in range(width // step):
            s = jax.nn.sigmoid(dot(cr[...], w_scr[0, :, col(j)]))
            sig[:, col(j)] = s
            dvo[:, col(j)] = (g[:, col(j)].astype(F32) * real * s).astype(BF16)
        for index, unit in enumerate(UNITS):
            slot = index % 2
            for s in range(4):
                wait(f"wfk{index} {s}", f"wfv{index} {s}")
            act = jnp.maximum(dot(ck[...], wk_scr[slot]), 0.0)
            hidden = (act * act).astype(BF16)
            fv = t_dot(hidden, dvo[...]).astype(BF16)
            if index:
                for s in range(4):
                    wait(f"fv{index - 1} {s}")
            fv_tile[...] = fv.reshape(4, LANES, width)
            for s in range(4):
                start(f"fv{index} {s}", view(fv_tile, s), view(gfv_h, s // 2, s % 2, pl.ds(unit * LANES, LANES)))
            pump(PUMPS["ffn"][0])
            d_pre = (dot_t(dvo[...], wv_scr[slot]) * (2.0 * act)).astype(BF16)
            fk = dot(ckt_scr[...], d_pre).astype(BF16)
            for s in range(4):
                wait(f"fv{index} {s}")
            summing.complete(f"fv{unit}")
            if index:
                for s in range(4):
                    wait(f"fk{index - 1} {s}")
            fk_tile[...] = fk.reshape(2, 2, quarter, 4 * LANES)
            for s in range(4):
                at = columns(2 * s + unit // 4)
                start(f"fk{index} {s}", view(fk_tile, slice(None), slice(None), slice(None), columns(s)), view(gfk_h, unit % 4, slice(None), slice(None), slice(None), at))
            pump(PUMPS["ffn"][1])
            if index:
                pass_scr[0:rows] += dot(hidden, wv_scr[slot])
                dck[...] += dot_t(d_pre, wk_scr[slot])
            else:
                pass_scr[0:rows] = dot(hidden, wv_scr[slot])
                dck[...] = dot_t(d_pre, wk_scr[slot])
            if index + 2 < len(UNITS):
                load_unit(index + 2)
            if index % 2:
                for s in range(4):
                    wait(f"fk{index} {s}")
                summing.complete(f"fk{unit % 4}")
            pump(PUMPS["ffn"][2])
        dgp = dvo
        wait("k out")
        block_out = b4
        for j in range(width // step):
            s, value = sig[:, col(j)], pass_scr[0:rows, col(j)]
            block_out[:, col(j)] = (mid[:, col(j)] + s * value).astype(BF16)
            top = g[:, col(j)].astype(F32) * real
            dgp[:, col(j)] = (top * value * s * (1.0 - s)).astype(BF16)
        start("block out", block_out, out_h)
        pump(PUMPS["mid"][0])
        write_grad(0, "fr", cr, dgp, 1)
        dcr = pass_scr
        for j in range(width // step):
            dcr[0:rows, col(j)] = dot_t(dgp[...], w_scr[0, col(j)])
        start("wo again", wo_h, view(w_scr, 0))
        pump(PUMPS["mid"][1])

    written = []

    def write_grad(index, name, left, right, pumps):
        for j in range(width // step):
            slot = j % 2
            if j >= 2:
                wait(*written[-2])
            tile_scr[slot] = t_dot(left[...], right[:, col(j)]).astype(BF16).reshape(2, 2, quarter, step)
            written.append((f"{name} tile {j}",))
            start(written[-1][0], view(tile_scr, slot), view(gw_h, index, slice(None), slice(None), slice(None), col(j)))
            pump(pumps)
        wait(*written[-1], *written[-2])
        summing.complete(name)

    half = pltpu.VMEM((rows, width), BF16)
    pl.run_scoped(
        ffn,
        pltpu.VMEM((2, width, 4 * LANES), BF16),
        pltpu.VMEM((2, 4 * LANES, width), BF16),
        pltpu.VMEM((width, rows), BF16),
        pltpu.VMEM((4, LANES, width), BF16),
        pltpu.VMEM((2, 2, quarter, 4 * LANES), BF16),
    )

    def last_row(halo):
        row = lax.broadcasted_iota(jnp.int32, halo.shape, 0)
        return jnp.where(row == 7, pltpu.roll(halo[...], 7, axis=0), 0.0)

    def attention_back(at_scr, bt_scr, dn_scr, dd_scr):
        g, gated, wkv, datt, dwkv, dr = b0, b1, b2, b5, b6, b7
        wait("block out", "v out", "gated out", "wkv out")
        start("at", view(spill_t, 0), at_scr)
        start("bt", view(spill_t, 1), bt_scr)
        start("gated", view(spill_b, 6), gated)
        start("wkv", view(spill_b, 5), wkv)
        start("k", view(spill_b, 3), b3)
        start("wr again", wr_h, view(w_scr, 1))
        start("v", view(spill_b, 4), b4)
        k, v = b3, b4
        share_k, share_r = fk_ref[...], fr_ref[...]

        def mix2_back(at, here):
            keep = spread(keep_scr, here)
            h, p = with_previous(h_scr, at)
            diff = h - p * keep
            dck, dcr = dh[here], pass_scr[here]
            sums[7] += fold8(diff * dck)
            sums[8] += fold8(diff * dcr)
            pass_scr[here] = (dck * (1.0 - share_k) + dcr * (1.0 - share_r)) * keep
            dh[here] = dck * share_k + dcr * share_r

        row_tiles(mix2_back, 0, 1)
        mineb2[...] = pass_scr[0:8]
        hand_b2().start()
        row_tiles(mix2_back, 1)
        pass_scr[rows : rows + 8] = jnp.zeros((8, width), F32)
        start("r", spill_r, view(h_scr, slice(0, rows)))
        pump(PUMPS["back"][0])

        def norm2_back(at, here, extra=None):
            hat, inv = normalized(mid[here])
            d = dh[here] + pass_scr[pl.ds(at, TILE + 8)][1 : TILE + 1]
            if extra is not None:
                d = d + extra
            sums[0] += fold8(d * hat)
            sums[1] += fold8(d)
            d_mid = norm_back(d * gain2, hat, inv) + g[here].astype(F32) * spread(real_scr, here)
            mid[here] = d_mid
            datt[here] = d_mid.astype(BF16)

        def tail_of(halo):
            return jnp.concatenate([jnp.zeros((TILE - 8, width), F32), last_row(halo)], axis=0)

        row_tiles(norm2_back, 0, tiles - 1)
        pump(PUMPS["back"][1])
        hand_b2().wait_recv()
        norm2_back(rows - TILE, slice(rows - TILE, rows), tail_of(halob2))
        dmid = mid
        start("x again", x_h, b0)

        wait("wo again")
        for j in range(width // step):
            d_scr[:, col(j)] = dot_t(datt[...], w_scr[0, col(j)])
        start("wv again", wv_h, view(w_scr, 0))
        pump(PUMPS["back"][2])
        wait("r", "wkv", "k", "v", "at", "bt")

        def wkv_at(at, j):
            here = (pl.ds(at, TILE), columns(j))
            kk, vv = k[here].astype(F32), v[here].astype(F32)
            return kk, vv, *wkv_parts(
                at, j, TILE, blocks, kk, vv, at_scr, bt_scr, in_scr[0], in_scr[1], rate, boost, first_start
            )

        def gate_tile(at, rows_here):
            for j in range(blocks):
                here = (rows_here, columns(j))
                sig = jax.nn.sigmoid(h_scr[here])
                dg = d_scr[here]
                dw = (dg * sig).astype(BF16)
                dwkv[here] = dw
                dr[here] = (dg * wkv[here].astype(F32) * sig * (1.0 - sig)).astype(BF16)
                *_, inv, out = wkv_at(at, j)
                dn = dw.astype(F32) * inv
                there = pl.ds(at * blocks + j, TILE, stride=blocks)
                dn_scr[there] = dn
                dd_scr[there] = -dn * out

        for part in range(4):
            row_tiles(gate_tile, part * tiles // 4, (part + 1) * tiles // 4)
            pump(PUMPS["back"][3])
        start("xv", view(spill_b, 1), wkv)

        def scan(t8, carry):
            a, b = carry
            for u in range(8):
                t = rows - 1 - (t8 * 8 + u)
                keep = keep_scr[pl.ds(t, 1)]
                here = pl.ds(pl.multiple_of(t * blocks, blocks), blocks)
                dn, dd = dn_scr[here], dd_scr[here]
                dn_scr[here] = a
                dd_scr[here] = b
                a = (a * decay + dn) * keep
                b = (b * decay + dd) * keep
            return a, b

        zero = jnp.zeros((blocks, LANES), F32)
        carry = lax.fori_loop(0, rows // 16, scan, (zero, zero))
        pump(PUMPS["back"][4])
        adj_mine[0], adj_mine[1] = lax.fori_loop(rows // 16, rows // 8, scan, carry)
        for copy in hand_adj:
            copy().start()
        pump(PUMPS["back"][5])

        wait("gated")
        write_grad(1, "wo", gated, datt, PUMPS["grad"])
        start("xk", view(spill_b, 0), gated)
        start("xr", view(spill_b, 2), datt)
        xk, xv, xr = gated, wkv, datt

        halo1_rows()
        wait("x again")
        row_tiles(norm1_of)
        pump(PUMPS["back"][6])
        wait("xr")
        write_grad(2, "wr", xr, dr, PUMPS["grad"])

        for copy in hand_adj:
            copy().wait_recv()
        adj_a, adj_b = adj_in[0, 0], adj_in[0, 1]
        for h in range(1, hops):
            scale = jnp.exp(-rate * float(rows * h)) * jnp.where(after >= first + (h + 1) * rows, 1.0, 0.0)
            adj_a, adj_b = adj_a + scale * adj_in[h, 0], adj_b + scale * adj_in[h, 1]

        def recur_tile(at, rows_here):
            real = real_scr[rows_here]
            pos = at + lax.broadcasted_iota(jnp.int32, (TILE, LANES), 0)
            for j in range(blocks):
                here = (rows_here, columns(j))
                kk, vv, a, b, eu, inv, out = wkv_at(at, j)
                there = pl.ds(at * blocks + j, TILE, stride=blocks)
                lift = jnp.where(pos >= last_start, jnp.exp(-rate[j : j + 1] * (rows - 1 - pos).astype(F32)), 0.0)
                post_a = dn_scr[there] + lift * adj_a[j : j + 1]
                post_b = dd_scr[there] + lift * adj_b[j : j + 1]
                dn = dwkv[here].astype(F32) * inv
                own = eu * dn
                weight = jnp.exp(kk) * real
                v[here] = (own + weight * post_a).astype(BF16)
                first_term = own * (vv - out)
                k[here] = (first_term + weight * (vv * post_a + post_b)).astype(BF16)
                wsums[0, :, columns(j)] += fold8(a * post_a + b * post_b)
                wsums[1, :, columns(j)] += fold8(first_term)

        for part in range(4):
            row_tiles(recur_tile, part * tiles // 4, (part + 1) * tiles // 4)
            pump(PUMPS["back"][7])
        for j in range(blocks):
            rr = rate[j : j + 1]
            wsums[0, :, columns(j)] *= -rr * jnp.exp(-rr)
        dk, dv = k, v
        wait("xv")
        write_grad(3, "wv", xv, dv, PUMPS["grad"])
        wait("xk")
        write_grad(4, "wk", xk, dk, PUMPS["grad"])

        def mix1_back(grad, weight, share_ref, index, fresh):
            for j in range(width // step):
                d_scr[:, col(j)] = dot_t(grad[...], weight[col(j)])
            pump(PUMPS["back"][8])
            share = share_ref[...]

            def tile(at, here):
                h, p = with_previous(h_scr, at)
                d = d_scr[here]
                keep = spread(keep_scr, here)
                sums[index] += fold8((h - p * keep) * d)
                passed = d * (1.0 - share) * keep
                if fresh:
                    pass_scr[here] = passed
                    dh[here] = d * share
                else:
                    pass_scr[here] += passed
                    dh[here] += d * share

            row_tiles(tile)
            pump(PUMPS["back"][9])

        wait("wr again")
        mix1_back(dr, w_scr.at[1], sr_ref, 4, True)
        start("wk again", wk_h, view(w_scr, 1))
        wait("wv again")
        mix1_back(dv, w_scr.at[0], sv_ref, 3, False)
        wait("wk again")
        mix1_back(dk, w_scr.at[1], sk_ref, 2, False)
        mine1[...] = pass_scr[0:8]
        hand_b1().start()
        x, grad_in = b0, dwkv

        def norm1_back(at, here, extra=None):
            d = dh[here] + pass_scr[pl.ds(at, TILE + 8)][1 : TILE + 1]
            if extra is not None:
                d = d + extra
            hat, inv = normalized(x[here].astype(F32))
            sums[5] += fold8(d * hat)
            sums[6] += fold8(d)
            grad_in[here] = (norm_back(d * gain1, hat, inv) + dmid[here]).astype(BF16)

        row_tiles(norm1_back, 0, tiles - 1)
        pump(PUMPS["back"][10])
        hand_b1().wait_recv()
        norm1_back(rows - TILE, slice(rows - TILE, rows), tail_of(halo1))
        start("grad in", grad_in, gin_h)

    pl.run_scoped(attention_back, tall, tall, tall, tall)
    parts = [sums[i] for i in (5, 6, 2, 3, 4)] + [wsums[0], wsums[1]] + [sums[i] for i in (0, 1, 7, 8)]
    lines = [jnp.sum(p, axis=0, keepdims=True) for p in parts]
    lines.append(jnp.zeros((16 - len(lines), width), F32))
    vec_scr[...] = jnp.concatenate(lines, axis=0).astype(BF16)
    for s in range(4):
        start(f"vec {s}", vec_scr, view(gvec_h, s // 2, s % 2))
    for s in range(4):
        wait(f"vec {s}")
    summing.complete("vec")
    pump(len(summing.pending))
    summing.finish()
    copies.finish()
    for copy in (hand_x, hand_h2, hand_b2, hand_b1, *hand_st, *hand_adj):
        copy().wait_send()


PUMPS = {"ffn": (3, 2, 3), "mid": (3, 3), "grad": 2, "back": (3, 3, 3, 2, 2, 2, 3, 2, 2, 2, 3)}


def block(x, g, weights, vectors, rates, spans, pads, hops):
    rows, width = x.shape
    blocks = width // LANES
    quarter = width // 4
    hid = weights[4].shape[1]
    fv_rows = hid // 4
    block_rows = fv_rows + 4 * quarter + 5 * quarter + 16
    chunks = sum(len(tick) for tick in PLAN)
    half = pltpu.VMEM((rows, width), BF16)
    flat, flat8 = pltpu.VMEM((rows, width), F32), pltpu.VMEM((rows + 8, width), F32)
    eight = pltpu.VMEM((8, width), F32)
    state = pltpu.VMEM((2, blocks, LANES), F32)
    states = pltpu.VMEM((hops, 2, blocks, LANES), F32)
    lanes = [most for _, most in sorted(SLOT.values())]
    outs = [(fv_rows, LANES), (quarter, 4 * LANES)] + [(quarter, LANES)] * 5 + [(16, LANES)]
    result = pl.pallas_call(
        block_kernel,
        out_shape=[sds((rows, width), BF16)] * 2
        + [sds(shape, F32) for shape in outs]
        + [
            sds((2, block_rows, width), BF16),
            sds((5, 2, 2, quarter, width), BF16),
            sds((2, 2, fv_rows, width), BF16),
            sds((4, 2, 2, quarter, width), BF16),
            sds((2, 2, 16, width), BF16),
            sds((7, rows, width), BF16),
            sds((rows, width), F32),
            sds((2, rows * blocks, LANES), F32),
        ],
        in_specs=[ANY] * 9 + [VMEM] * 11 + [SMEM] * 2,
        out_specs=[ANY] * 2 + [VMEM] * 8 + [ANY] * 8,
        scratch_shapes=[flat, flat, flat8, flat, flat8]
        + [half] * 8
        + [
            pltpu.VMEM((2, width, width), BF16),
            pltpu.VMEM((2, 2, 2, quarter, 256), BF16),
            pltpu.VMEM((16, width), BF16),
            pltpu.VMEM((rows, LANES), F32),
            pltpu.VMEM((rows, LANES), F32),
            pltpu.VMEM((16, width), BF16),
        ]
        + [eight] * 6
        + [state, states, state, states, state]
        + [pltpu.VMEM((9, 8, width), F32), pltpu.VMEM((2, 8, width), F32)]
        + [pltpu.VMEM((2, 2, most, width), BF16) for most in lanes]
        + [pltpu.VMEM((RING, 2, 2, 2, 2, most, LANES), BF16) for most in lanes]
        + [pltpu.VMEM((2,) * (3 - d) + (block_rows, LANES), BF16) for d in range(4)]
        + [
            pltpu.SemaphoreType.DMA((192,)),
            pltpu.SemaphoreType.DMA((4 + 2 * hops,)),
            pltpu.SemaphoreType.DMA((4 + 2 * hops,)),
            pltpu.SemaphoreType.DMA((chunks, STEPS)),
            pltpu.SemaphoreType.DMA((chunks, STEPS)),
            pltpu.SemaphoreType.DMA((len(lanes), 2)),
        ],
        compiler_params=pltpu.CompilerParams(
            vmem_limit_bytes=63 * MIB, collective_id=0, has_side_effects=True
        ),
        name="block",
    )(x, g, *weights, *vectors, *rates, spans, pads)
    return result[:10]


def finish_kernel(*refs):
    count = (len(refs) - 1) // 2
    sems = refs[-1]
    copies = [
        pltpu.make_async_copy(source, target, sems.at[i])
        for i, (source, target) in enumerate(zip(refs[:count], refs[count:-1]))
    ]
    for copy in copies:
        copy.start()
    for copy in copies:
        copy.wait()


def finish(arrays):
    return pl.pallas_call(
        finish_kernel,
        out_shape=[sds(a.shape, a.dtype) for a in arrays],
        in_specs=[ANY] * len(arrays),
        out_specs=[VMEM] * len(arrays),
        scratch_shapes=[pltpu.SemaphoreType.DMA((len(arrays),))],
        compiler_params=params(62),
        name="finish",
    )(*arrays)


def shift(value, steps):
    count = lax.axis_size("chan")
    pairs = [(i, i + steps) for i in range(count) if 0 <= i + steps < count]
    return lax.ppermute(value, "chan", pairs)


def scatter_sums(mats, vecs):
    def both(m):
        m = lax.psum_scatter(m, "chan", scatter_dimension=1, tiled=True)
        return lax.psum_scatter(m, "seq", scatter_dimension=0, tiled=True).astype(F32)

    v = lax.psum_scatter(vecs.astype(BF16), "chan", scatter_dimension=1, tiled=True).astype(F32)
    return [both(m) for m in mats], lax.psum(v, "seq")


def per_device(
    x, g, gain1, bias1, share_k, share_v, share_r, log_rate, boost, wk, wv, wr, wo, gain2, bias2, share_fk, share_fr,
    wfk, wfv, wfr, spans, pads,
):
    rows, width = x.shape
    chans = lax.axis_size("chan")
    total = rows * chans
    hops = max(1, min(chans - 1, total // 4 // rows))
    if (lax.axis_size("seq"), chans, wfk.shape[1] // chans, width) == (4, 8, 4 * LANES, 8 * LANES):
        line = lambda v: v.reshape(1, width)
        tall = lambda v: v.reshape(width // LANES, LANES)
        vectors = [line(v) for v in (gain1, bias1, share_k, share_v, share_r, gain2, bias2, share_fk, share_fr)]
        weights = (wk, wv, wr, wo, wfk, wfv, wfr)
        results = block(x, g, weights, vectors, (tall(log_rate), tall(boost)), spans, pads, hops)
        vec = results[-1]
        block_out, grad_in, gfv, gfk, gfr, gwo, gwr, gwv, gwk = finish(results[:-1])
        return (block_out, grad_in, *[vec[i] for i in range(7)], gwk, gwv, gwr, gwo, *[vec[i] for i in range(7, 11)], gfk, gfv, gfr)
    base = lambda: lax.axis_index("chan") * rows
    vecs = jnp.stack([gain1, bias1, share_k, share_v, share_r, gain2, bias2, share_fk, share_fr])
    rates = jnp.stack([log_rate, boost]).reshape(2 * width // LANES, LANES)
    begins = jnp.cumsum(spans[0]) - spans[0]
    pos = base() + jnp.arange(rows, dtype=jnp.int32)
    keep = 1.0 - jnp.any(pos[:, None] == begins[None, :], axis=1).astype(F32)

    xprev = shift(jnp.broadcast_to(x[rows - 1 :], (16, width)), 1)[:8]
    xk, xv, xr, k, v, r, at, bt, end = project(base, x, xprev, vecs, rates, spans, pads, keep, wk, wv, wr)
    carry = jnp.concatenate([shift(end, h + 1) for h in range(hops)], axis=0)
    wkv, gated, middle, last, carried = exit_call(base, hops, x, k, v, r, at, bt, carry, rates, vecs, spans, wo)
    hprev = jnp.broadcast_to(shift(last[7:], 1), (8, width))
    block_out, gfk, gfv, gfr, dh2, back2, sums2 = ffn(base, middle, g, hprev, vecs, spans, pads, wfr, wfk, wfv)
    dh2next = shift(back2, -1)
    dmid, gwo, dwkv, dr, sumsn2, adja, adjb, adjend = exit_back(
        base, middle, g, dh2, dh2next, vecs, rates, gated, wkv, r, k, v, at, bt, carried, spans, pads, keep, wo
    )
    adj = jnp.concatenate([shift(adjend, -h - 1) for h in range(hops)], axis=0)
    gwk, gwv, gwr, dh1, back1, sums1, wsums = project_back(
        base, hops, total, x, xprev, vecs, rates, k, v, dwkv, dr, at, bt, carried, adja, adjb, adj, xk, xv, xr, spans,
        pads, wk, wv, wr,
    )
    grad_in, sumsn1 = entry_back(x, dh1, shift(back1, -1), dmid, vecs)
    vec_parts = jnp.concatenate([sumsn1, sums1, wsums, sumsn2, sums2], axis=0).sum(axis=1)
    (gwk, gwv, gwr, gwo, gfk, gfv, gfr), vec = scatter_sums((gwk, gwv, gwr, gwo, gfk, gfv, gfr), vec_parts)
    return (block_out, grad_in, *[vec[i] for i in range(7)], gwk, gwv, gwr, gwo, *[vec[i] for i in range(7, 11)], gfk, gfv, gfr)


def solution(mesh):
    tokens, chan, both = P(("seq", "chan"), None), P("chan"), P("seq", "chan")
    placed = (tokens, tokens) + (P(),) * 18 + (P("seq", None),) * 2
    return jax.shard_map(
        per_device,
        mesh=mesh,
        in_specs=placed,
        out_specs=(tokens, tokens) + (chan,) * 7 + (both,) * 4 + (chan,) * 4 + (both,) * 3,
        check_vma=False,
    )
```

```python
import functools

import jax
import jax.numpy as jnp
from jax import lax
from jax.experimental import pallas as pl
from jax.experimental.pallas import tpu as pltpu
from jax.sharding import PartitionSpec as P

F32, BF16 = jnp.float32, jnp.bfloat16
LANES = 128
TILE = 64
MIB = 1 << 20
VMEM = pl.BlockSpec(memory_space=pltpu.VMEM)
SMEM = pl.BlockSpec(memory_space=pltpu.SMEM)
ANY = pl.BlockSpec(memory_space=pl.ANY)
G1, B1, SK, SV, SR, G2, B2, FK, FR = range(9)


def sds(shape, dtype):
    return jax.ShapeDtypeStruct(shape, dtype)


def params(limit_mib):
    return pltpu.CompilerParams(vmem_limit_bytes=limit_mib * MIB)


def dot(a, b):
    return jnp.dot(a, b, preferred_element_type=F32)


def dot_t(a, b):
    return lax.dot_general(a, b, (((1,), (1,)), ((), ())), preferred_element_type=F32)


def t_dot(a, b):
    return lax.dot_general(a, b, (((0,), (0,)), ((), ())), preferred_element_type=F32)


def fold8(v):
    return jnp.sum(v.reshape(v.shape[0] // 8, 8, v.shape[1]), axis=0)


def normalized(v):
    center = v - jnp.mean(v, axis=-1, keepdims=True)
    inv = lax.rsqrt(jnp.mean(center * center, axis=-1, keepdims=True) + 1e-05)
    return center * inv, inv


def norm_back(d_hat, hat, inv):
    return inv * (
        d_hat
        - jnp.mean(d_hat, axis=-1, keepdims=True)
        - hat * jnp.mean(d_hat * hat, axis=-1, keepdims=True)
    )


def marks(first, rows, spans, pads):
    pos = first + lax.broadcasted_iota(jnp.int32, (rows, LANES), 0)
    begin = 0
    start, real = pos < 0, pos < 0
    for i in range(spans.shape[1]):
        length = spans[0, i]
        start = start | (pos == begin)
        real = real | ((pos >= begin) & (pos < begin + length - pads[0, i]))
        begin = begin + length
    return start, real


def first_start_from(spans, at, otherwise):
    begin, best = 0, otherwise
    for i in range(spans.shape[1]):
        best = jnp.where((begin >= at) & (begin < best), begin, best)
        begin = begin + spans[0, i]
    return best


def last_start_before(spans, at):
    begin, best = 0, -(1 << 20)
    for i in range(spans.shape[1]):
        best = jnp.where(begin < at, begin, best)
        begin = begin + spans[0, i]
    return best


def wide(flag, width):
    return jnp.concatenate([flag] * (width // LANES), axis=1)


def with_previous(ref, at):
    block = ref[pl.ds(at, TILE + 8)]
    return block[8:], block[7 : TILE + 7]


def columns(j):
    return slice(j * LANES, (j + 1) * LANES)


def gather_carry(hops, rows, carry_ref, counts, rate):
    a, b = carry_ref[0], carry_ref[1]
    for h in range(1, hops):
        scale = jnp.exp(-rate * float(rows * h)) * counts[h]
        a, b = a + scale * carry_ref[2 * h], b + scale * carry_ref[2 * h + 1]
    return a, b


def project_kernel(
    base, x_ref, xprev_ref, vec_ref, rate_ref, spans, pads, keep_s, wk_hbm, wv_hbm, wr_hbm,
    xk_ref, xv_ref, xr_ref, k_ref, v_ref, r_ref, at_ref, bt_ref, end_ref,
    h_scr, ek_scr, ev_scr, w_scr, sems,
):
    rows, width = x_ref.shape
    blocks = width // LANES
    copies = [
        pltpu.make_async_copy(hbm, w_scr.at[i], sems.at[i])
        for i, hbm in enumerate((wk_hbm, wv_hbm, wr_hbm))
    ]
    for copy in copies:
        copy.start()
    first = base()
    gain, bias = vec_ref[G1 : G1 + 1], vec_ref[B1 : B1 + 1]
    prev = xprev_ref[...].astype(F32)
    h_scr[0:8] = normalized(prev)[0] * gain + bias

    @pl.loop(0, rows // TILE)
    def _(i):
        at = pl.multiple_of(i * TILE, TILE)
        hat, _ = normalized(x_ref[pl.ds(at, TILE)].astype(F32))
        h_scr[pl.ds(at + 8, TILE)] = hat * gain + bias

    @pl.loop(0, rows // TILE)
    def _(i):
        at = pl.multiple_of(i * TILE, TILE)
        start, _ = marks(first + at, TILE, spans, pads)
        keep = wide(1.0 - start.astype(F32), width)
        h, p = with_previous(h_scr, at)
        p = p * keep
        for row, out in ((SK, xk_ref), (SV, xv_ref), (SR, xr_ref)):
            share = vec_ref[row : row + 1]
            out[pl.ds(at, TILE)] = (h * share + p * (1.0 - share)).astype(BF16)

    _, real = marks(first, rows, spans, pads)
    real = real.astype(F32)
    step = 256
    for i, (src, out) in enumerate(((xk_ref, k_ref), (xv_ref, v_ref), (xr_ref, r_ref))):
        copies[i].wait()
        for j in range(width // step):
            tile = dot(src[...], w_scr[i, :, j * step : (j + 1) * step])
            out[:, j * step : (j + 1) * step] = tile.astype(out.dtype)
    for j in range(blocks):
        ek = jnp.exp(k_ref[:, columns(j)].astype(F32)) * real
        ek_scr[pl.ds(j, rows, stride=blocks)] = ek
        ev_scr[pl.ds(j, rows, stride=blocks)] = ek * v_ref[:, columns(j)].astype(F32)
    decay = jnp.exp(-jnp.exp(rate_ref[0:blocks]))

    def scan(t8, carry):
        a, b = carry
        for u in range(8):
            t = t8 * 8 + u
            keep = keep_s[t]
            here = pl.ds(pl.multiple_of(t * blocks, blocks), blocks)
            at_ref[here] = a * keep
            bt_ref[here] = b * keep
            fade = decay * keep
            a = a * fade + ev_scr[here]
            b = b * fade + ek_scr[here]
        return a, b

    zero = jnp.zeros((blocks, LANES), F32)
    a, b = lax.fori_loop(0, rows // 8, scan, (zero, zero))
    end_ref[0] = a
    end_ref[1] = b


def project(base, x, xprev, vecs, rates, spans, pads, keep, wk, wv, wr):
    rows, width = x.shape
    shape = (rows, width)
    tall = (rows * (width // LANES), LANES)
    return pl.pallas_call(
        functools.partial(project_kernel, base),
        out_shape=(
            [sds(shape, BF16)] * 5 + [sds(shape, F32)] + [sds(tall, F32)] * 2 + [sds((2, width // LANES, LANES), F32)]
        ),
        in_specs=[VMEM] * 4 + [SMEM] * 3 + [ANY] * 3,
        out_specs=[VMEM] * 9,
        scratch_shapes=[
            pltpu.VMEM((rows + 8, width), F32),
            pltpu.VMEM(tall, F32),
            pltpu.VMEM(tall, F32),
            pltpu.VMEM((3, width, width), BF16),
            pltpu.SemaphoreType.DMA((3,)),
        ],
        compiler_params=params(56),
        name="project",
    )(x, xprev, vecs, rates, spans, pads, keep, wk, wv, wr)


def wkv_parts(at, j, rows, blocks, k, v, at_ref, bt_ref, a_in, b_in, rate, boost, first_start):
    here = pl.ds(at * blocks + j, rows, stride=blocks)
    pos = at + lax.broadcasted_iota(jnp.int32, (rows, LANES), 0)
    lift = jnp.where(pos < first_start, jnp.exp(-rate[j : j + 1] * pos.astype(F32)), 0.0)
    a = at_ref[here] + lift * a_in[j : j + 1]
    b = bt_ref[here] + lift * b_in[j : j + 1]
    eu = jnp.exp(boost[j : j + 1] + k)
    inv = 1.0 / (b + eu)
    return a, b, eu, inv, (a + eu * v) * inv


def carry_counts(hops, rows, first, spans):
    last = last_start_before(spans, first)
    return [jnp.where(last < first - h * rows, 1.0, 0.0) for h in range(hops)]


def exit_kernel(
    base, hops, x_ref, k_ref, v_ref, r_ref, at_ref, bt_ref, carry_ref, rate_ref, vec_ref, spans, wo_hbm,
    wkv_ref, gated_ref, middle_ref, last_ref, in_ref, wo_scr, sem,
):
    rows, width = x_ref.shape
    blocks = width // LANES
    copy = pltpu.make_async_copy(wo_hbm, wo_scr, sem)
    copy.start()
    first = base()
    rate = jnp.exp(rate_ref[0:blocks])
    boost = rate_ref[blocks : 2 * blocks]
    a_in, b_in = gather_carry(hops, rows, carry_ref, carry_counts(hops, rows, first, spans), rate)
    in_ref[0] = a_in
    in_ref[1] = b_in
    first_start = first_start_from(spans, first, 1 << 20) - first

    @pl.loop(0, rows // TILE)
    def _(i):
        at = pl.multiple_of(i * TILE, TILE)
        for j in range(blocks):
            here = (pl.ds(at, TILE), columns(j))
            k, v = k_ref[here].astype(F32), v_ref[here].astype(F32)
            wkv = wkv_parts(at, j, TILE, blocks, k, v, at_ref, bt_ref, a_in, b_in, rate, boost, first_start)[-1]
            wkv = wkv.astype(BF16)
            wkv_ref[here] = wkv
            gated_ref[here] = (jax.nn.sigmoid(r_ref[here]) * wkv.astype(F32)).astype(BF16)

    copy.wait()
    step = 256
    for j in range(width // step):
        here = (slice(None), slice(j * step, (j + 1) * step))
        middle_ref[here] = x_ref[here].astype(F32) + dot(gated_ref[...], wo_scr[here])
    hat, _ = normalized(middle_ref[rows - 8 : rows])
    last_ref[...] = hat * vec_ref[G2 : G2 + 1] + vec_ref[B2 : B2 + 1]


def exit_call(base, hops, x, k, v, r, at, bt, carry, rates, vecs, spans, wo):
    rows, width = x.shape
    blocks = width // LANES
    return pl.pallas_call(
        functools.partial(exit_kernel, base, hops),
        out_shape=[
            sds((rows, width), BF16),
            sds((rows, width), BF16),
            sds((rows, width), F32),
            sds((8, width), F32),
            sds((2, blocks, LANES), F32),
        ],
        in_specs=[VMEM] * 9 + [SMEM, ANY],
        out_specs=[VMEM] * 5,
        scratch_shapes=[pltpu.VMEM((width, width), BF16), pltpu.SemaphoreType.DMA(())],
        compiler_params=params(56),
        name="exit",
    )(x, k, v, r, at, bt, carry, rates, vecs, spans, wo)


def ffn_kernel(
    base, mid_ref, g_ref, hprev_ref, vec_ref, spans, pads, wg_ref, wk_ref, wv_ref,
    out_ref, gfk_ref, gfv_ref, gfr_ref, dh_ref, back_ref, sums_ref,
    h_scr, ck_scr, cr_scr, ckt_scr, sig_scr, dvo_scr, val_scr, dck_scr, pass_scr,
):
    rows, width = mid_ref.shape
    step = pl.program_id(0)
    first = base()
    tiles = rows // TILE

    @pl.when(step == 0)
    def _():
        gain, bias = vec_ref[G2 : G2 + 1], vec_ref[B2 : B2 + 1]
        h_scr[0:8] = hprev_ref[...]

        @pl.loop(0, tiles)
        def _(i):
            at = pl.multiple_of(i * TILE, TILE)
            hat, _ = normalized(mid_ref[pl.ds(at, TILE)])
            h_scr[pl.ds(at + 8, TILE)] = hat * gain + bias

        @pl.loop(0, tiles)
        def _(i):
            at = pl.multiple_of(i * TILE, TILE)
            start, _ = marks(first + at, TILE, spans, pads)
            keep = wide(1.0 - start.astype(F32), width)
            h, p = with_previous(h_scr, at)
            p = p * keep
            for row, out in ((FK, ck_scr), (FR, cr_scr)):
                share = vec_ref[row : row + 1]
                out[pl.ds(at, TILE)] = (h * share + p * (1.0 - share)).astype(BF16)

        ckt_scr[...] = ck_scr[...].T
        _, real = marks(first, rows, spans, pads)
        real = wide(real.astype(F32), 256)
        for j in range(width // 256):
            here = (slice(None), slice(j * 256, (j + 1) * 256))
            sig = jax.nn.sigmoid(dot(cr_scr[...], wg_ref[here]))
            sig_scr[here] = sig
            dvo_scr[here] = (g_ref[here].astype(F32) * real * sig).astype(BF16)
        val_scr[...] = jnp.zeros_like(val_scr)
        dck_scr[...] = jnp.zeros_like(dck_scr)

    act = jnp.maximum(dot(ck_scr[...], wk_ref[...]), 0.0)
    hidden = (act * act).astype(BF16)
    val_scr[...] += dot(hidden, wv_ref[...])
    gfv_ref[...] = t_dot(hidden, dvo_scr[...]).astype(BF16)
    d_pre = (dot_t(dvo_scr[...], wv_ref[...]) * (2.0 * act)).astype(BF16)
    gfk_ref[...] = dot(ckt_scr[...], d_pre).astype(BF16)
    dck_scr[...] += dot_t(d_pre, wk_ref[...])

    @pl.when(step == pl.num_programs(0) - 1)
    def _():
        dgp_scr = dvo_scr
        _, real = marks(first, rows, spans, pads)
        real = wide(real.astype(F32), 256)
        for j in range(width // 256):
            here = (slice(None), slice(j * 256, (j + 1) * 256))
            sig, value = sig_scr[here], val_scr[here]
            out_ref[here] = (mid_ref[here] + sig * value).astype(BF16)
            top = g_ref[here].astype(F32) * real
            dgp_scr[here] = (top * value * sig * (1.0 - sig)).astype(BF16)
        for j in range(width // 256):
            here = (slice(None), slice(j * 256, (j + 1) * 256))
            gfr_ref[here] = t_dot(cr_scr[...], dgp_scr[here]).astype(BF16)
        dcr_scr = val_scr
        for j in range(width // 256):
            dcr_scr[:, j * 256 : (j + 1) * 256] = dot_t(dgp_scr[...], wg_ref[j * 256 : (j + 1) * 256])
        sums_ref[...] = jnp.zeros_like(sums_ref)
        share_k, share_r = vec_ref[FK : FK + 1], vec_ref[FR : FR + 1]

        @pl.loop(0, tiles)
        def _(i):
            at = pl.multiple_of(i * TILE, TILE)
            here = pl.ds(at, TILE)
            start, _ = marks(first + at, TILE, spans, pads)
            keep = wide(1.0 - start.astype(F32), width)
            h, p = with_previous(h_scr, at)
            diff = h - p * keep
            dck, dcr = dck_scr[here], dcr_scr[here]
            sums_ref[0] += fold8(diff * dck)
            sums_ref[1] += fold8(diff * dcr)
            pass_scr[here] = (dck * (1.0 - share_k) + dcr * (1.0 - share_r)) * keep
            dh_ref[here] = dck * share_k + dcr * share_r

        back_ref[...] = pass_scr[0:8]

        pass_scr[rows : rows + 8] = jnp.zeros((8, width), F32)

        @pl.loop(0, tiles)
        def _(i):
            at = pl.multiple_of(i * TILE, TILE)
            dh_ref[pl.ds(at, TILE)] += pass_scr[pl.ds(at, TILE + 8)][1 : TILE + 1]


def ffn(base, middle, g, hprev, vecs, spans, pads, wg, wk, wv):
    rows, width = middle.shape
    hid = wk.shape[1]
    unit = 512
    full = lambda shape: pl.BlockSpec(shape, lambda j: (0,) * len(shape))
    return pl.pallas_call(
        functools.partial(ffn_kernel, base),
        grid=(hid // unit,),
        out_shape=[
            sds((rows, width), BF16),
            sds((width, hid), BF16),
            sds((hid, width), BF16),
            sds((width, width), BF16),
            sds((rows, width), F32),
            sds((8, width), F32),
            sds((2, 8, width), F32),
        ],
        in_specs=[
            full((rows, width)),
            full((rows, width)),
            full((8, width)),
            full(vecs.shape),
            SMEM,
            SMEM,
            full((width, width)),
            pl.BlockSpec((width, unit), lambda j: (0, j)),
            pl.BlockSpec((unit, width), lambda j: (j, 0)),
        ],
        out_specs=[
            full((rows, width)),
            pl.BlockSpec((width, unit), lambda j: (0, j)),
            pl.BlockSpec((unit, width), lambda j: (j, 0)),
            full((width, width)),
            full((rows, width)),
            full((8, width)),
            full((2, 8, width)),
        ],
        scratch_shapes=[
            pltpu.VMEM((rows + 8, width), F32),
            pltpu.VMEM((rows, width), BF16),
            pltpu.VMEM((rows, width), BF16),
            pltpu.VMEM((width, rows), BF16),
            pltpu.VMEM((rows, width), F32),
            pltpu.VMEM((rows, width), BF16),
            pltpu.VMEM((rows, width), F32),
            pltpu.VMEM((rows, width), F32),
            pltpu.VMEM((rows + 8, width), F32),
        ],
        compiler_params=params(60),
        name="ffn",
    )(middle, g, hprev, vecs, spans, pads, wg, wk, wv)


def exit_back_kernel(
    base, mid_ref, g_ref, dh_ref, dhnext_ref, vec_ref, rate_ref, gated_ref, wkv_ref, r_ref, k_ref, v_ref, at_ref, bt_ref,
    in_ref, spans, pads, keep_s, wo_ref,
    dmid_ref, gwo_ref, dwkv_ref, dr_ref, sums_ref, adja_ref, adjb_ref, adjend_ref,
    datt_scr, dn_scr, dd_scr,
):
    rows, width = mid_ref.shape
    blocks = width // LANES
    first = base()
    gain = vec_ref[G2 : G2 + 1]
    sums_ref[...] = jnp.zeros_like(sums_ref)
    tail = dhnext_ref[...]
    row = lax.broadcasted_iota(jnp.int32, tail.shape, 0)
    dh_ref[rows - 8 : rows] += jnp.where(row == 7, pltpu.roll(tail, 7, axis=0), 0.0)

    @pl.loop(0, rows // TILE)
    def _(i):
        at = pl.multiple_of(i * TILE, TILE)
        here = pl.ds(at, TILE)
        _, real = marks(first + at, TILE, spans, pads)
        hat, inv = normalized(mid_ref[here])
        dh = dh_ref[here]
        sums_ref[0] += fold8(dh * hat)
        sums_ref[1] += fold8(dh)
        d_mid = norm_back(dh * gain, hat, inv) + g_ref[here].astype(F32) * wide(real.astype(F32), width)
        dmid_ref[here] = d_mid
        datt_scr[here] = d_mid.astype(BF16)

    step = 256
    rate = jnp.exp(rate_ref[0:blocks])
    boost = rate_ref[blocks : 2 * blocks]
    a_in, b_in = in_ref[0], in_ref[1]
    first_start = first_start_from(spans, first, 1 << 20) - first
    for j in range(width // step):
        here = (slice(None), slice(j * step, (j + 1) * step))
        dr_ref[here] = dot_t(datt_scr[...], wo_ref[j * step : (j + 1) * step]).astype(BF16)
    d_gated = dr_ref

    @pl.loop(0, rows // TILE)
    def _(i):
        at = pl.multiple_of(i * TILE, TILE)
        for j in range(blocks):
            here = (pl.ds(at, TILE), columns(j))
            sig = jax.nn.sigmoid(r_ref[here])
            dg = d_gated[here].astype(F32)
            dwkv = (dg * sig).astype(BF16)
            dwkv_ref[here] = dwkv
            dr_ref[here] = (dg * wkv_ref[here].astype(F32) * sig * (1.0 - sig)).astype(BF16)
            k, v = k_ref[here].astype(F32), v_ref[here].astype(F32)
            _, _, _, inv, wkv = wkv_parts(
                at, j, TILE, blocks, k, v, at_ref, bt_ref, a_in, b_in, rate, boost, first_start
            )
            dn = dwkv.astype(F32) * inv
            there = pl.ds(at * blocks + j, TILE, stride=blocks)
            dn_scr[there] = dn
            dd_scr[there] = -dn * wkv

    decay = jnp.exp(-rate)

    def scan(t8, carry):
        a, b = carry
        for u in range(8):
            t = rows - 1 - (t8 * 8 + u)
            keep = keep_s[t]
            here = pl.ds(pl.multiple_of(t * blocks, blocks), blocks)
            adja_ref[here] = a
            adjb_ref[here] = b
            fade = decay * keep
            a = a * fade + dn_scr[here] * keep
            b = b * fade + dd_scr[here] * keep
        return a, b

    zero = jnp.zeros((blocks, LANES), F32)
    a, b = lax.fori_loop(0, rows // 8, scan, (zero, zero))
    adjend_ref[0] = a
    adjend_ref[1] = b
    for j in range(width // step):
        here = (slice(None), slice(j * step, (j + 1) * step))
        gwo_ref[here] = t_dot(gated_ref[...], datt_scr[here]).astype(BF16)


def exit_back(base, middle, g, dh, dhnext, vecs, rates, gated, wkv, r, k, v, at, bt, carry, spans, pads, keep, wo):
    rows, width = middle.shape
    blocks = width // LANES
    tall = (rows * blocks, LANES)
    return pl.pallas_call(
        functools.partial(exit_back_kernel, base),
        out_shape=[
            sds((rows, width), F32),
            sds((width, width), BF16),
            sds((rows, width), BF16),
            sds((rows, width), BF16),
            sds((2, 8, width), F32),
            sds(tall, F32),
            sds(tall, F32),
            sds((2, blocks, LANES), F32),
        ],
        in_specs=[VMEM] * 14 + [SMEM] * 3 + [VMEM],
        out_specs=[VMEM] * 8,
        scratch_shapes=[
            pltpu.VMEM((rows, width), BF16),
            pltpu.VMEM(tall, F32),
            pltpu.VMEM(tall, F32),
        ],
        compiler_params=params(60),
        name="exit_back",
    )(middle, g, dh, dhnext, vecs, rates, gated, wkv, r, k, v, at, bt, carry, spans, pads, keep, wo)


def project_back_kernel(
    base, hops, total, x_ref, xprev_ref, vec_ref, rate_ref, k_ref, v_ref, dwkv_ref, dr_ref, at_ref, bt_ref, in_ref,
    adja_ref, adjb_ref, adj_ref, xk_ref, xv_ref, xr_ref, spans, pads, wk_hbm, wv_hbm, wr_hbm,
    gwk_ref, gwv_ref, gwr_ref, dh_ref, back_ref, sums_ref, wsums_ref,
    h_scr, dk_scr, dv_scr, d_scr, pass_scr, w_scr, sems,
):
    rows, width = x_ref.shape
    blocks = width // LANES
    copies = [
        pltpu.make_async_copy(hbm, w_scr.at[i], sems.at[i])
        for i, hbm in enumerate((wk_hbm, wv_hbm, wr_hbm))
    ]
    for copy in copies:
        copy.start()
    first = base()
    rate = jnp.exp(rate_ref[0:blocks])
    boost = rate_ref[blocks : 2 * blocks]
    a_in, b_in = in_ref[0], in_ref[1]
    first_start = first_start_from(spans, first, 1 << 20) - first
    last_start = last_start_before(spans, first + rows) - first
    after = first_start_from(spans, first + rows, total)
    counts = [jnp.where(after >= first + (h + 1) * rows, 1.0, 0.0) for h in range(hops)]
    adj_a, adj_b = gather_carry(hops, rows, adj_ref, counts, rate)
    wsums_ref[...] = jnp.zeros_like(wsums_ref)
    sums_ref[...] = jnp.zeros_like(sums_ref)

    @pl.loop(0, rows // TILE)
    def _(i):
        at = pl.multiple_of(i * TILE, TILE)
        _, real = marks(first + at, TILE, spans, pads)
        real = real.astype(F32)
        pos = at + lax.broadcasted_iota(jnp.int32, (TILE, LANES), 0)
        for j in range(blocks):
            here = (pl.ds(at, TILE), columns(j))
            k, v = k_ref[here].astype(F32), v_ref[here].astype(F32)
            a, b, eu, inv, wkv = wkv_parts(
                at, j, TILE, blocks, k, v, at_ref, bt_ref, a_in, b_in, rate, boost, first_start
            )
            there = pl.ds(at * blocks + j, TILE, stride=blocks)
            lift = jnp.where(
                pos >= last_start, jnp.exp(-rate[j : j + 1] * (rows - 1 - pos).astype(F32)), 0.0
            )
            post_a = adja_ref[there] + lift * adj_a[j : j + 1]
            post_b = adjb_ref[there] + lift * adj_b[j : j + 1]
            dn = dwkv_ref[here].astype(F32) * inv
            own = eu * dn
            weight = jnp.exp(k) * real
            dv_scr[here] = (own + weight * post_a).astype(BF16)
            first_term = own * (v - wkv)
            dk_scr[here] = (first_term + weight * (v * post_a + post_b)).astype(BF16)
            wsums_ref[0, :, columns(j)] += fold8(a * post_a + b * post_b)
            wsums_ref[1, :, columns(j)] += fold8(first_term)

    for j in range(blocks):
        r = rate[j : j + 1]
        wsums_ref[0, :, columns(j)] *= -r * jnp.exp(-r)
    gain, bias = vec_ref[G1 : G1 + 1], vec_ref[B1 : B1 + 1]
    h_scr[0:8] = normalized(xprev_ref[...].astype(F32))[0] * gain + bias

    @pl.loop(0, rows // TILE)
    def _(i):
        at = pl.multiple_of(i * TILE, TILE)
        hat, _ = normalized(x_ref[pl.ds(at, TILE)].astype(F32))
        h_scr[pl.ds(at + 8, TILE)] = hat * gain + bias

    step = 256
    dh_ref[...] = jnp.zeros_like(dh_ref)
    groups = ((dk_scr, xk_ref, gwk_ref, SK), (dv_scr, xv_ref, gwv_ref, SV), (dr_ref, xr_ref, gwr_ref, SR))
    pass_scr[...] = jnp.zeros_like(pass_scr)
    for i, (grad, mixed, out, row) in enumerate(groups):
        copies[i].wait()
        for j in range(width // step):
            here = (slice(None), slice(j * step, (j + 1) * step))
            d_scr[:, j * step : (j + 1) * step] = dot_t(grad[...], w_scr[i, j * step : (j + 1) * step])
            out[here] = t_dot(mixed[...], grad[here]).astype(BF16)
        share = vec_ref[row : row + 1]

        @pl.loop(0, rows // TILE)
        def _(t):
            at = pl.multiple_of(t * TILE, TILE)
            here = pl.ds(at, TILE)
            start, _ = marks(first + at, TILE, spans, pads)
            keep = wide(1.0 - start.astype(F32), width)
            h, p = with_previous(h_scr, at)
            d = d_scr[here]
            sums_ref[i] += fold8((h - p * keep) * d)
            pass_scr[here] += d * (1.0 - share) * keep
            dh_ref[here] += d * share

    back_ref[...] = pass_scr[0:8]

    @pl.loop(0, rows // TILE)
    def _(i):
        at = pl.multiple_of(i * TILE, TILE)
        dh_ref[pl.ds(at, TILE)] += pass_scr[pl.ds(at, TILE + 8)][1 : TILE + 1]


def project_back(base, hops, total, x, xprev, vecs, rates, k, v, dwkv, dr, at, bt, carry, adja, adjb, adj, xk, xv, xr, spans, pads, wk, wv, wr):
    rows, width = x.shape
    return pl.pallas_call(
        functools.partial(project_back_kernel, base, hops, total),
        out_shape=[sds((width, width), BF16)] * 3
        + [
            sds((rows, width), F32),
            sds((8, width), F32),
            sds((3, 8, width), F32),
            sds((2, 8, width), F32),
        ],
        in_specs=[VMEM] * 17 + [SMEM] * 2 + [ANY] * 3,
        out_specs=[VMEM] * 7,
        scratch_shapes=[
            pltpu.VMEM((rows + 8, width), F32),
            pltpu.VMEM((rows, width), BF16),
            pltpu.VMEM((rows, width), BF16),
            pltpu.VMEM((rows, width), F32),
            pltpu.VMEM((rows + 8, width), F32),
            pltpu.VMEM((3, width, width), BF16),
            pltpu.SemaphoreType.DMA((3,)),
        ],
        compiler_params=params(60),
        name="project_back",
    )(x, xprev, vecs, rates, k, v, dwkv, dr, at, bt, carry, adja, adjb, adj, xk, xv, xr, spans, pads, wk, wv, wr)


def entry_back_kernel(x_ref, dh_ref, dhnext_ref, dmid_ref, vec_ref, out_ref, sums_ref):
    rows = x_ref.shape[0]
    gain = vec_ref[G1 : G1 + 1]
    sums_ref[...] = jnp.zeros_like(sums_ref)
    tail = dhnext_ref[...]
    row = lax.broadcasted_iota(jnp.int32, tail.shape, 0)
    dh_ref[rows - 8 : rows] += jnp.where(row == 7, pltpu.roll(tail, 7, axis=0), 0.0)

    @pl.loop(0, rows // TILE)
    def _(i):
        here = pl.ds(pl.multiple_of(i * TILE, TILE), TILE)
        hat, inv = normalized(x_ref[here].astype(F32))
        dh = dh_ref[here]
        sums_ref[0] += fold8(dh * hat)
        sums_ref[1] += fold8(dh)
        out_ref[here] = (norm_back(dh * gain, hat, inv) + dmid_ref[here]).astype(BF16)


def entry_back(x, dh, dhnext, dmid, vecs):
    rows, width = x.shape
    return pl.pallas_call(
        entry_back_kernel,
        out_shape=[sds((rows, width), BF16), sds((2, 8, width), F32)],
        in_specs=[VMEM] * 5,
        out_specs=[VMEM] * 2,
        compiler_params=params(40),
        name="entry_back",
    )(x, dh, dhnext, dmid, vecs)


X, Y, Z = "x", "y", "z"
ORDERS = {
    X: ("x", "y", "low", "high"),
    Y: ("y", "x", "low", "high"),
    Z: ("low", "high", "x", "y"),
    "vec": ("x", "y", "low", "high"),
}
AXIS_BIT = {"core": ("seq", 1), "x": ("seq", 2), "y": ("chan", 1), "low": ("chan", 2), "high": ("chan", 4)}
STEPS = 5
RING = 3
MESH = pl.DeviceIdType.MESH
ARRAYS = ("fv", "fk0", "fk1", "fk2", "fk3", "fr", "wo", "wr", "wv", "wk", "vec")
UNITS = (0, 4, 1, 5, 2, 6, 3, 7)


def third(name, even):
    more, less = (X, Y) if even else (Y, X)
    return ((name, 0, 112, more), (name, 112, 96, less), (name, 208, 48, Z))


CHUNKS = tuple(
    chunk
    for q in range(4)
    for chunk in (
        ("fv", q * 128, 128, X),
        ("fv", (q + 4) * 128, 128, Y),
        (f"fk{q}", 128, 128, Z),
        (f"fk{q}", 0, 64, X),
        (f"fk{q}", 64, 64, Y),
    )
) + third("fr", 0) + third("wo", 1) + third("wr", 0) + third("wv", 1) + third("wk", 0) + (("vec", 0, 16, "vec"),)
MOST = {X: 128, Y: 128, Z: 128, "vec": 16}
LANES_OF = (X, Y, Z, "vec")
TURNS = 6
LINK, CORE, HOP, FETCH, ACTION = 46000.0, 570000.0, 1.7, 1.4, 0.12
BACKLOG = 9.0


def bit_of(index, weight):
    return index // weight % 2


def partner(axis):
    name, weight = AXIS_BIT[axis]
    where = {"seq": lax.axis_index("seq"), "chan": lax.axis_index("chan")}
    bit = bit_of(where[name], weight)
    where[name] = where[name] + weight * (1 - 2 * bit)
    return bit, (where["seq"], where["chan"])


class Summing:
    def __init__(self, grads, received, outs, stages, rings, levels, sems):
        self.grads, self.received, self.outs = grads, received, outs
        self.stages, self.rings, self.levels = stages, rings, levels
        self.across_sem, self.ring_sems, self.level_sems, self.across_recv, self.recv_sems, self.stage_sems = sems
        self.sides = {axis: partner(axis) for axis in AXIS_BIT}
        self.bases, filled = {}, 0
        for name in ARRAYS:
            self.bases[name] = filled
            filled += grads[name]().shape[2]
        count = len(CHUNKS)
        self.queue = {lane: [n for n in range(count) if CHUNKS[n][3] == lane] for lane in LANES_OF}
        self.turn = {n: i for queue in self.queue.values() for i, n in enumerate(queue)}
        self.now, self.waited = 0.0, 0.0
        self.free = dict.fromkeys(("core", "x", "y", "end", "middle"), 0.0)
        self.ready = {}
        self.did = set()


    def place(self, number):
        array, first, rows, stream = CHUNKS[number]
        return array, first, rows, stream, LANES_OF.index(stream), pl.ds(self.bases[array] + first, rows)

    def key(self, number):
        array, first, _, _ = CHUNKS[number]
        return f"fv{first // 128}" if array == "fv" else array

    def across(self, number):
        array, first, rows, _, _, there = self.place(number)
        core, mate = self.sides["core"]
        return pltpu.make_async_remote_copy(
            src_ref=self.grads[array]().at[:, 1 - core, pl.ds(first, rows)],
            dst_ref=self.received.at[:, there],
            send_sem=self.across_sem,
            recv_sem=self.across_recv.at[number],
            device_id=mate,
            device_id_type=MESH,
        )

    def staged(self, number):
        array, first, rows, _, lane, there = self.place(number)
        core, _ = self.sides["core"]
        stage = self.stages[lane]
        return (
            pltpu.make_async_copy(
                self.grads[array]().at[:, core, pl.ds(first, rows)], stage.at[0, :, 0:rows], self.stage_sems.at[lane, 0]
            ),
            pltpu.make_async_copy(self.received.at[:, there], stage.at[1, :, 0:rows], self.stage_sems.at[lane, 1]),
        )

    def send(self, number, step):
        _, _, rows, stream, lane, there = self.place(number)
        bit, mate = self.sides[ORDERS[stream][step - 1]]
        free = (slice(None),) * (4 - step)
        slot = self.turn[number] % RING
        if step == 1:
            source = self.rings[lane].at[(slot, 1 - bit, *free, slice(0, rows))]
            send_sem = self.ring_sems.at[lane, slot]
        else:
            source = self.levels[step - 2].at[(1 - bit, *free, there)]
            send_sem = self.level_sems.at[step - 2]
        return pltpu.make_async_remote_copy(
            src_ref=source,
            dst_ref=self.levels[step - 1].at[(*free, there)],
            send_sem=send_sem,
            recv_sem=self.recv_sems.at[lane, self.turn[number] % TURNS, step - 1],
            device_id=mate,
            device_id_type=MESH,
        )


    def transfer(self, number, step):
        rows = CHUNKS[number][2]
        if step == 0:
            hops = (("core", rows * 4096 / CORE),)
        else:
            took = rows * (16 >> step) * 256 / LINK
            axis = ORDERS[CHUNKS[number][3]][step - 1]
            hops = {"low": (("end", took),), "high": (("end", took), ("middle", 2 * took))}.get(axis, ((axis, took),))
        arrived = 0.0
        for link, took in hops:
            self.free[link] = max(self.now, self.free[link]) + took
            arrived = max(arrived, self.free[link])
        self.ready[number, step] = arrived + HOP

    def link_of(self, number, step):
        axis = ORDERS[CHUNKS[number][3]][step - 1]
        return {"low": "end", "high": "end"}.get(axis, axis)

    def possible(self):
        found = []
        for queue in self.queue.values():
            for n in queue:
                if (n, 0) not in self.ready:
                    break
                turn = self.turn[n]
                if (n, "fetch") not in self.did:
                    if turn == 0 or (queue[turn - 1], 0) in self.did:
                        found.append((self.ready[n, 0], None, n, "fetch"))
                    break
                if (n, 0) not in self.did:
                    old = queue[turn - RING] if turn >= RING else None
                    if old is None or (old, 1) in self.did:
                        when = max(self.ready[n, "fetch"], 0.0 if old is None else self.ready[old, 1])
                        found.append((when, self.link_of(n, 1), n, 0))
                    continue
                step = next((s for s in range(1, STEPS) if (n, s) not in self.did), None)
                if step:
                    found.append((self.ready[n, step], self.link_of(n, step + 1) if step < 4 else None, n, step))
        return found

    def act(self, when, number, step):
        self.waited += max(0.0, when - self.now)
        self.now = max(self.now, when) + ACTION
        rows = CHUNKS[number][2]
        self.did.add((number, step))
        if step == "fetch":
            self.start_stage(number)
            self.ready[number, "fetch"] = self.now + FETCH
        elif step == 0:
            self.now += rows * 0.002
            self.first_sum(number)
            self.transfer(number, 1)
        else:
            self.now += rows * 0.003 / (1 << step)
            self.later_sum(number, step)
            if step < 4:
                self.transfer(number, step + 1)

    def pump(self, took):
        self.now += took
        while True:
            able = [
                (self.free.get(link, 0.0), n, step, when)
                for when, link, n, step in self.possible()
                if when <= self.now and self.free.get(link, 0.0) < self.now + BACKLOG
            ]
            if not able:
                return
            _, number, step, when = min(able, key=lambda a: a[:2])
            self.act(when, number, step)

    def drain(self):
        while found := self.possible():
            when, _, number, step = min(found, key=lambda a: (max(a[0], self.now), a[2]))
            self.act(when, number, step)

    def complete(self, key):
        for n in range(len(CHUNKS)):
            if self.key(n) == key:
                self.across(n).start()
                self.now += 0.05
                self.transfer(n, 0)


    def start_stage(self, number):
        self.across(number).wait_recv()
        for copy in self.staged(number):
            copy.start()

    def first_sum(self, number):
        _, _, rows, stream, lane, _ = self.place(number)
        turn = self.turn[number]
        stage, ring = self.stages[lane], self.rings[lane]
        if turn >= RING:
            self.send(self.queue[stream][turn - RING], 1).wait_send()
        for copy in self.staged(number):
            copy.wait()
        for i in range(16):
            c = i % 8
            bits = {"x": i // 8, "y": c % 2, "low": c // 2 % 2, "high": c // 4}
            at = tuple(bits[axis] for axis in ORDERS[stream])
            ring[(turn % RING, *at, slice(0, rows))] = stage[0, i // 8, 0:rows, columns(c)] + stage[1, i // 8, 0:rows, columns(c)]
        self.send(number, 1).start()

    def later_sum(self, number, step):
        array, first, rows, stream, lane, there = self.place(number)
        bit, _ = self.sides[ORDERS[stream][step - 1]]
        target = self.levels[step - 1]
        self.send(number, step).wait_recv()
        if step == 1:
            source, lead, here = self.rings[lane], (self.turn[number] % RING, bit), slice(0, rows)
        else:
            source, lead, here = self.levels[step - 2], (bit,), there
        if step == 4:
            out, cols = self.outs[array]
            out[first : first + rows, cols] = source[(*lead, here)].astype(F32) + target[there].astype(F32)
            return
        for i in range(1 << (4 - step)):
            at = tuple(i // (1 << (3 - step - d)) % 2 for d in range(4 - step))
            target[(*at, there)] = source[(*lead, *at, here)] + target[(*at, there)]
        self.send(number, step + 1).start()

    def finish(self):
        pltpu.make_async_copy(self.received, self.received, self.across_sem).wait()
        for i, level in enumerate(self.levels[1:]):
            pltpu.make_async_copy(level, level, self.level_sems.at[i]).wait()
        for queue in self.queue.values():
            for n in queue[-RING:]:
                self.send(n, 1).wait_send()


def view(ref, *index):
    return lambda: ref.at[index]


class Copies:
    def __init__(self, sems):
        self.sems, self.all, self.waited = sems, {}, set()
        self.idle = list(range(sems.shape[0]))

    def start(self, name, source, target):
        assert name not in self.all
        self.all[name] = (source, target, self.idle.pop(0))
        self.copy(name).start()

    def copy(self, name):
        source, target, number = self.all[name]
        source, target = (r() if callable(r) else r for r in (source, target))
        return pltpu.make_async_copy(source, target, self.sems.at[number])

    def wait(self, *names):
        for name in names:
            if name not in self.waited:
                self.copy(name).wait()
                self.waited.add(name)
                self.idle.append(self.all[name][2])

    def finish(self):
        self.wait(*self.all)


def block_kernel(*refs):
    (
        spans, pads,
        out_h, gin_h, ofv_h, ofk_h, ofr_h, owo_h, owr_h, owv_h, owk_h, ovec_h,
        received, gw_h, gfv_h, gfk_h, gvec_h, spill_b, spill_r, spill_t,
        mid, dh, h_scr, d_scr, pass_scr, b0, b1, b2, b3, b4, b5, b6, b7, w_scr, tile_scr, vec_scr,
        keep_scr, real_scr, xlast, halo2, halob2, halo1, mine2, mine1, mineb2, st_mine, st_in, adj_mine, adj_in, in_scr,
        line, tall_line, ofv, ofk, ofr, owo, owr, owv, owk, ovec,
        sums, wsums, s0, s1, s2, s3, g0, g1, g2, g3, l1, l2, l3, l4,
        copy_sems, halo_send, halo_recv, *sum_sems,
    ) = refs[9 + 11 :]
    small_h, refs = refs[9 : 9 + 11], refs[:9]
    x_h, g_h, wk_h, wv_h, wr_h, wo_h, wfk_h, wfv_h, wfr_h = refs
    gain1_ref, bias1_ref, sk_ref, sv_ref, sr_ref, gain2_ref, bias2_ref, fk_ref, fr_ref = [line.at[i] for i in range(9)]
    rows, width = x_h.shape
    blocks = width // LANES
    chans = lax.axis_size("chan")
    seq, chan = lax.axis_index("seq"), lax.axis_index("chan")
    first = chan * rows
    total = rows * chans
    hops = adj_in.shape[0]
    tiles = rows // TILE
    step = 256
    quarter = width // 4

    grads = {"fv": lambda: gfv_h, "vec": lambda: gvec_h}
    outs = {"fv": (ofv, slice(None)), "vec": (ovec, slice(None))}
    for i in range(4):
        grads[f"fk{i}"], outs[f"fk{i}"] = view(gfk_h, i), (ofk, columns(i))
    names = ("fr", "wo", "wr", "wv", "wk")
    for i, (name, out) in enumerate(zip(names, (ofr, owo, owr, owv, owk))):
        grads[name], outs[name] = view(gw_h, i), (out, slice(None))
    summing = Summing(
        grads, received, outs, (s0, s1, s2, s3), (g0, g1, g2, g3), (l1, l2, l3, l4), sum_sems
    )
    pump = summing.pump
    copies = Copies(copy_sems)
    start, wait = copies.start, copies.wait

    def row_tiles(body, lo=0, hi=tiles):
        @pl.loop(lo, hi)
        def _(i):
            at = pl.multiple_of(i * TILE, TILE)
            body(at, pl.ds(at, TILE))

    def col(j):
        return slice(j * step, (j + 1) * step)

    def spread(ref, here, to=width):
        return wide(ref[here], to)

    def hand(source, target, number, offset):
        return lambda: pltpu.make_async_remote_copy(
            src_ref=source() if callable(source) else source,
            dst_ref=target() if callable(target) else target,
            send_sem=halo_send.at[number],
            recv_sem=halo_recv.at[number],
            device_id=(seq, (chan + chans + offset) % chans),
            device_id_type=MESH,
        )

    hand_x = hand(view(x_h, pl.ds(rows - 16, 16)), xlast, 0, 1)
    hand_h2 = hand(mine2, halo2, 1, 1)
    hand_b2 = hand(mineb2, halob2, 2, -1)
    hand_b1 = hand(mine1, halo1, 3, -1)
    hand_st = [hand(st_mine, view(st_in, h), 4 + h, h + 1) for h in range(hops)]
    hand_adj = [hand(adj_mine, view(adj_in, h), 4 + hops + h, -h - 1) for h in range(hops)]

    x, xk, xv, xr, k, v = b0, b1, b2, b3, b4, b5
    start("x", x_h, x)
    for i, small in enumerate(small_h):
        start(f"small {i}", small, view(line, i) if i < 9 else view(tall_line, i - 9))
    start("wk", wk_h, view(w_scr, 0))
    start("wv", wv_h, view(w_scr, 1))
    around = [(seq, (chan + chans + d) % chans) for h in range(hops) for d in (h + 1, -h - 1)]
    barrier = pltpu.get_barrier_semaphore()
    mates = [mate for _, mate in summing.sides.values()] + around
    for mate in mates:
        pl.semaphore_signal(barrier, inc=1, device_id=mate, device_id_type=MESH)

    wait(*(f"small {i}" for i in range(len(small_h))))
    rate = jnp.exp(tall_line[0])
    decay = jnp.exp(-rate)
    boost = tall_line[1]
    gain1, bias1, gain2, bias2 = gain1_ref[...], bias1_ref[...], gain2_ref[...], bias2_ref[...]
    sums[...] = jnp.zeros_like(sums)
    wsums[...] = jnp.zeros_like(wsums)
    first_start = first_start_from(spans, first, 1 << 20) - first
    last_start = last_start_before(spans, first + rows) - first
    before = last_start_before(spans, first)
    after = first_start_from(spans, first + rows, total)

    def marks_tile(at, here):
        begins, real = marks(first + at, TILE, spans, pads)
        keep_scr[here] = 1.0 - begins.astype(F32)
        real_scr[here] = real.astype(F32)

    row_tiles(marks_tile)
    wait("x")

    def norm1_of(at, here):
        hat, _ = normalized(x[here].astype(F32))
        h_scr[pl.ds(at + 8, TILE)] = hat * gain1 + bias1

    row_tiles(norm1_of)
    pl.semaphore_wait(barrier, len(mates))
    hand_x().start()

    def halo1_rows():
        h_scr[0:8] = normalized(xlast[8:16].astype(F32))[0] * gain1 + bias1

    def mixed(at, here, shares):
        keep = spread(keep_scr, here)
        h, p = with_previous(h_scr, at)
        p = p * keep
        for share_ref, out in shares:
            share = share_ref[...]
            out[here] = (h * share + p * (1.0 - share)).astype(BF16)

    mix1 = functools.partial(mixed, shares=((sk_ref, xk), (sv_ref, xv), (sr_ref, xr)))
    row_tiles(mix1, 1)
    hand_x().wait_recv()
    halo1_rows()
    row_tiles(mix1, 0, 1)

    def wkv_at(at, j, at_scr, bt_scr):
        here = (pl.ds(at, TILE), columns(j))
        return wkv_parts(
            at, j, TILE, blocks, k[here].astype(F32), v[here].astype(F32), at_scr, bt_scr, in_scr[0], in_scr[1],
            rate, boost, first_start,
        )

    def forward(at_scr, bt_scr, ev_scr, ek_scr):
        wait("wk")
        for j in range(width // step):
            k[:, col(j)] = dot(xk[...], w_scr[0, :, col(j)]).astype(BF16)
        start("wr", wr_h, view(w_scr, 0))
        wait("wv")
        for j in range(width // step):
            v[:, col(j)] = dot(xv[...], w_scr[1, :, col(j)]).astype(BF16)
        start("wo", wo_h, view(w_scr, 1))

        def weights_tile(at, here):
            real = real_scr[here]
            for j in range(blocks):
                there = pl.ds(at * blocks + j, TILE, stride=blocks)
                ek = jnp.exp(k[here, columns(j)].astype(F32)) * real
                ek_scr[there] = ek
                ev_scr[there] = ek * v[here, columns(j)].astype(F32)

        row_tiles(weights_tile)

        def scan(t8, carry):
            a, b = carry
            for u in range(8):
                t = t8 * 8 + u
                keep = keep_scr[pl.ds(t, 1)]
                here = pl.ds(pl.multiple_of(t * blocks, blocks), blocks)
                a = a * keep
                b = b * keep
                at_scr[here] = a
                bt_scr[here] = b
                a = a * decay + ev_scr[here]
                b = b * decay + ek_scr[here]
            return a, b

        zero = jnp.zeros((blocks, LANES), F32)
        st_mine[0], st_mine[1] = lax.fori_loop(0, rows // 8, scan, (zero, zero))
        for copy in hand_st:
            copy().start()
        start("xk out", xk, view(spill_b, 0))
        start("xv out", xv, view(spill_b, 1))
        start("xr out", xr, view(spill_b, 2))
        start("at out", at_scr, view(spill_t, 0))
        start("bt out", bt_scr, view(spill_t, 1))
        r = d_scr
        wait("wr")
        for j in range(width // step):
            r[:, col(j)] = dot(xr[...], w_scr[0, :, col(j)])
        start("wfr", wfr_h, view(w_scr, 0))
        start("r out", r, spill_r)
        for copy in hand_st:
            copy().wait_recv()
        a_in, b_in = st_in[0, 0], st_in[0, 1]
        for h in range(1, hops):
            scale = jnp.exp(-rate * float(rows * h)) * jnp.where(before < first - h * rows, 1.0, 0.0)
            a_in, b_in = a_in + scale * st_in[h, 0], b_in + scale * st_in[h, 1]
        in_scr[0], in_scr[1] = a_in, b_in
        wkv, gated = b6, b7

        def outputs_tile(at, here):
            for j in range(blocks):
                out = wkv_at(at, j, at_scr, bt_scr)[-1].astype(BF16)
                wkv[here, columns(j)] = out
                gated[here, columns(j)] = (jax.nn.sigmoid(r[here, columns(j)]) * out.astype(F32)).astype(BF16)

        row_tiles(outputs_tile)
        start("k out", k, view(spill_b, 3))
        start("v out", v, view(spill_b, 4))
        start("wkv out", wkv, view(spill_b, 5))
        start("gated out", gated, view(spill_b, 6))
        wait("at out", "bt out")
        pump(11.0)

    tall = pltpu.VMEM((rows * blocks, LANES), F32)
    pl.run_scoped(forward, tall, tall, tall, tall)

    def ffn(wk_scr, wv_scr, ckt_scr, fv_tile, fk_tile):
        def load_unit(index):
            unit, slot = UNITS[index], index % 2
            for s in range(4):
                at = s * (wfk_h.shape[1] // 4) + unit * LANES
                start(f"wfk{index} {s}", view(wfk_h, slice(None), pl.ds(at, LANES)), view(wk_scr, slot, slice(None), columns(s)))
                start(f"wfv{index} {s}", view(wfv_h, pl.ds(at, LANES)), view(wv_scr, slot, columns(s)))

        load_unit(0)
        load_unit(1)
        gated, g, ck, cr, dvo = b7, b0, b1, b2, b3
        wait("wo")
        for j in range(width // step):
            mid[:, col(j)] = x[:, col(j)].astype(F32) + dot(gated[...], w_scr[1, :, col(j)])
        start("g", g_h, g)
        mine2[...] = normalized(mid[rows - 8 : rows])[0] * gain2 + bias2
        hand_h2().start()

        def norm2_of(at, here):
            hat, _ = normalized(mid[here])
            h_scr[pl.ds(at + 8, TILE)] = hat * gain2 + bias2

        row_tiles(norm2_of)
        wait("xk out", "xv out", "xr out")
        mix2 = functools.partial(mixed, shares=((fk_ref, ck), (fr_ref, cr)))
        row_tiles(mix2, 1)
        hand_h2().wait_recv()
        h_scr[0:8] = halo2[...]
        row_tiles(mix2, 0, 1)
        ckt_scr[...] = ck[...].T
        sig, dck = d_scr, dh
        wait("wfr", "r out", "g")
        real = spread(real_scr, slice(None), step)
        for j in range(width // step):
            s = jax.nn.sigmoid(dot(cr[...], w_scr[0, :, col(j)]))
            sig[:, col(j)] = s
            dvo[:, col(j)] = (g[:, col(j)].astype(F32) * real * s).astype(BF16)
        pump(7.0)
        for index, unit in enumerate(UNITS):
            slot = index % 2
            for s in range(4):
                wait(f"wfk{index} {s}", f"wfv{index} {s}")
            act = jnp.maximum(dot(ck[...], wk_scr[slot]), 0.0)
            hidden = (act * act).astype(BF16)
            fv = t_dot(hidden, dvo[...]).astype(BF16)
            if index:
                for s in range(4):
                    wait(f"fv{index - 1} {s}")
            fv_tile[...] = fv.reshape(4, LANES, width)
            for s in range(4):
                start(f"fv{index} {s}", view(fv_tile, s), view(gfv_h, s // 2, s % 2, pl.ds(unit * LANES, LANES)))
            pump(1.6)
            d_pre = (dot_t(dvo[...], wv_scr[slot]) * (2.0 * act)).astype(BF16)
            fk = dot(ckt_scr[...], d_pre).astype(BF16)
            for s in range(4):
                wait(f"fv{index} {s}")
            summing.complete(f"fv{unit}")
            if index:
                for s in range(4):
                    wait(f"fk{index - 1} {s}")
            fk_tile[...] = fk.reshape(2, 2, quarter, 4 * LANES)
            for s in range(4):
                at = columns(2 * s + unit // 4)
                start(f"fk{index} {s}", view(fk_tile, slice(None), slice(None), slice(None), columns(s)), view(gfk_h, unit % 4, slice(None), slice(None), slice(None), at))
            pump(1.3)
            if index:
                pass_scr[0:rows] += dot(hidden, wv_scr[slot])
                dck[...] += dot_t(d_pre, wk_scr[slot])
            else:
                pass_scr[0:rows] = dot(hidden, wv_scr[slot])
                dck[...] = dot_t(d_pre, wk_scr[slot])
            if index + 2 < len(UNITS):
                load_unit(index + 2)
            if index % 2:
                for s in range(4):
                    wait(f"fk{index} {s}")
                summing.complete(f"fk{unit % 4}")
            pump(1.2)
        dgp = dvo
        wait("k out")
        block_out = b4
        for j in range(width // step):
            s, value = sig[:, col(j)], pass_scr[0:rows, col(j)]
            block_out[:, col(j)] = (mid[:, col(j)] + s * value).astype(BF16)
            top = g[:, col(j)].astype(F32) * real
            dgp[:, col(j)] = (top * value * s * (1.0 - s)).astype(BF16)
        start("block out", block_out, out_h)
        pump(1.3)
        write_grad(0, "fr", cr, dgp)
        dcr = pass_scr
        for j in range(width // step):
            dcr[0:rows, col(j)] = dot_t(dgp[...], w_scr[0, col(j)])
        start("wo again", wo_h, view(w_scr, 0))
        pump(1.4)

    written = []

    def write_grad(index, name, left, right):
        for j in range(width // step):
            slot = j % 2
            if j >= 2:
                wait(*written[-2])
            tile_scr[slot] = t_dot(left[...], right[:, col(j)]).astype(BF16).reshape(2, 2, quarter, step)
            written.append((f"{name} tile {j}",))
            start(written[-1][0], view(tile_scr, slot), view(gw_h, index, slice(None), slice(None), slice(None), col(j)))
            pump(0.4)
        wait(*written[-1], *written[-2])
        summing.complete(name)

    half = pltpu.VMEM((rows, width), BF16)
    pl.run_scoped(
        ffn,
        pltpu.VMEM((2, width, 4 * LANES), BF16),
        pltpu.VMEM((2, 4 * LANES, width), BF16),
        pltpu.VMEM((width, rows), BF16),
        pltpu.VMEM((4, LANES, width), BF16),
        pltpu.VMEM((2, 2, quarter, 4 * LANES), BF16),
    )

    def last_row(halo):
        row = lax.broadcasted_iota(jnp.int32, halo.shape, 0)
        return jnp.where(row == 7, pltpu.roll(halo[...], 7, axis=0), 0.0)

    def attention_back(at_scr, bt_scr, dn_scr, dd_scr):
        g, gated, wkv, datt, dwkv, dr = b0, b1, b2, b5, b6, b7
        wait("block out", "v out", "gated out", "wkv out")
        start("at", view(spill_t, 0), at_scr)
        start("bt", view(spill_t, 1), bt_scr)
        start("gated", view(spill_b, 6), gated)
        start("wkv", view(spill_b, 5), wkv)
        start("k", view(spill_b, 3), b3)
        start("wr again", wr_h, view(w_scr, 1))
        start("v", view(spill_b, 4), b4)
        k, v = b3, b4
        share_k, share_r = fk_ref[...], fr_ref[...]

        def mix2_back(at, here):
            keep = spread(keep_scr, here)
            h, p = with_previous(h_scr, at)
            diff = h - p * keep
            dck, dcr = dh[here], pass_scr[here]
            sums[7] += fold8(diff * dck)
            sums[8] += fold8(diff * dcr)
            pass_scr[here] = (dck * (1.0 - share_k) + dcr * (1.0 - share_r)) * keep
            dh[here] = dck * share_k + dcr * share_r

        row_tiles(mix2_back, 0, 1)
        mineb2[...] = pass_scr[0:8]
        hand_b2().start()
        row_tiles(mix2_back, 1)
        pass_scr[rows : rows + 8] = jnp.zeros((8, width), F32)
        start("r", spill_r, view(h_scr, slice(0, rows)))
        pump(1.6)

        def norm2_back(at, here, extra=None):
            hat, inv = normalized(mid[here])
            d = dh[here] + pass_scr[pl.ds(at, TILE + 8)][1 : TILE + 1]
            if extra is not None:
                d = d + extra
            sums[0] += fold8(d * hat)
            sums[1] += fold8(d)
            d_mid = norm_back(d * gain2, hat, inv) + g[here].astype(F32) * spread(real_scr, here)
            mid[here] = d_mid
            datt[here] = d_mid.astype(BF16)

        def tail_of(halo):
            return jnp.concatenate([jnp.zeros((TILE - 8, width), F32), last_row(halo)], axis=0)

        row_tiles(norm2_back, 0, tiles - 1)
        pump(2.6)
        hand_b2().wait_recv()
        norm2_back(rows - TILE, slice(rows - TILE, rows), tail_of(halob2))
        dmid = mid
        start("x again", x_h, b0)

        wait("wo again")
        for j in range(width // step):
            d_scr[:, col(j)] = dot_t(datt[...], w_scr[0, col(j)])
        start("wv again", wv_h, view(w_scr, 0))
        pump(1.6)
        wait("r", "wkv", "k", "v", "at", "bt")

        def wkv_at(at, j):
            here = (pl.ds(at, TILE), columns(j))
            kk, vv = k[here].astype(F32), v[here].astype(F32)
            return kk, vv, *wkv_parts(
                at, j, TILE, blocks, kk, vv, at_scr, bt_scr, in_scr[0], in_scr[1], rate, boost, first_start
            )

        def gate_tile(at, rows_here):
            for j in range(blocks):
                here = (rows_here, columns(j))
                sig = jax.nn.sigmoid(h_scr[here])
                dg = d_scr[here]
                dw = (dg * sig).astype(BF16)
                dwkv[here] = dw
                dr[here] = (dg * wkv[here].astype(F32) * sig * (1.0 - sig)).astype(BF16)
                *_, inv, out = wkv_at(at, j)
                dn = dw.astype(F32) * inv
                there = pl.ds(at * blocks + j, TILE, stride=blocks)
                dn_scr[there] = dn
                dd_scr[there] = -dn * out

        for part in range(4):
            row_tiles(gate_tile, part * tiles // 4, (part + 1) * tiles // 4)
            pump(0.5)
        start("xv", view(spill_b, 1), wkv)

        def scan(t8, carry):
            a, b = carry
            for u in range(8):
                t = rows - 1 - (t8 * 8 + u)
                keep = keep_scr[pl.ds(t, 1)]
                here = pl.ds(pl.multiple_of(t * blocks, blocks), blocks)
                dn, dd = dn_scr[here], dd_scr[here]
                dn_scr[here] = a
                dd_scr[here] = b
                a = (a * decay + dn) * keep
                b = (b * decay + dd) * keep
            return a, b

        zero = jnp.zeros((blocks, LANES), F32)
        carry = lax.fori_loop(0, rows // 16, scan, (zero, zero))
        pump(1.2)
        adj_mine[0], adj_mine[1] = lax.fori_loop(rows // 16, rows // 8, scan, carry)
        for copy in hand_adj:
            copy().start()
        pump(1.2)

        wait("gated")
        write_grad(1, "wo", gated, datt)
        start("xk", view(spill_b, 0), gated)
        start("xr", view(spill_b, 2), datt)
        xk, xv, xr = gated, wkv, datt

        halo1_rows()
        wait("x again")
        row_tiles(norm1_of)
        pump(1.8)
        wait("xr")
        write_grad(2, "wr", xr, dr)

        for copy in hand_adj:
            copy().wait_recv()
        adj_a, adj_b = adj_in[0, 0], adj_in[0, 1]
        for h in range(1, hops):
            scale = jnp.exp(-rate * float(rows * h)) * jnp.where(after >= first + (h + 1) * rows, 1.0, 0.0)
            adj_a, adj_b = adj_a + scale * adj_in[h, 0], adj_b + scale * adj_in[h, 1]

        def recur_tile(at, rows_here):
            real = real_scr[rows_here]
            pos = at + lax.broadcasted_iota(jnp.int32, (TILE, LANES), 0)
            for j in range(blocks):
                here = (rows_here, columns(j))
                kk, vv, a, b, eu, inv, out = wkv_at(at, j)
                there = pl.ds(at * blocks + j, TILE, stride=blocks)
                lift = jnp.where(pos >= last_start, jnp.exp(-rate[j : j + 1] * (rows - 1 - pos).astype(F32)), 0.0)
                post_a = dn_scr[there] + lift * adj_a[j : j + 1]
                post_b = dd_scr[there] + lift * adj_b[j : j + 1]
                dn = dwkv[here].astype(F32) * inv
                own = eu * dn
                weight = jnp.exp(kk) * real
                v[here] = (own + weight * post_a).astype(BF16)
                first_term = own * (vv - out)
                k[here] = (first_term + weight * (vv * post_a + post_b)).astype(BF16)
                wsums[0, :, columns(j)] += fold8(a * post_a + b * post_b)
                wsums[1, :, columns(j)] += fold8(first_term)

        for part in range(4):
            row_tiles(recur_tile, part * tiles // 4, (part + 1) * tiles // 4)
            pump(1.05)
        for j in range(blocks):
            rr = rate[j : j + 1]
            wsums[0, :, columns(j)] *= -rr * jnp.exp(-rr)
        dk, dv = k, v
        wait("xv")
        write_grad(3, "wv", xv, dv)
        wait("xk")
        write_grad(4, "wk", xk, dk)

        def mix1_back(grad, weight, share_ref, index, fresh):
            for j in range(width // step):
                d_scr[:, col(j)] = dot_t(grad[...], weight[col(j)])
            pump(1.4)
            share = share_ref[...]

            def tile(at, here):
                h, p = with_previous(h_scr, at)
                d = d_scr[here]
                keep = spread(keep_scr, here)
                sums[index] += fold8((h - p * keep) * d)
                passed = d * (1.0 - share) * keep
                if fresh:
                    pass_scr[here] = passed
                    dh[here] = d * share
                else:
                    pass_scr[here] += passed
                    dh[here] += d * share

            row_tiles(tile)
            pump(1.0)

        wait("wr again")
        mix1_back(dr, w_scr.at[1], sr_ref, 4, True)
        start("wk again", wk_h, view(w_scr, 1))
        wait("wv again")
        mix1_back(dv, w_scr.at[0], sv_ref, 3, False)
        wait("wk again")
        mix1_back(dk, w_scr.at[1], sk_ref, 2, False)
        mine1[...] = pass_scr[0:8]
        hand_b1().start()
        x, grad_in = b0, dwkv

        def norm1_back(at, here, extra=None):
            d = dh[here] + pass_scr[pl.ds(at, TILE + 8)][1 : TILE + 1]
            if extra is not None:
                d = d + extra
            hat, inv = normalized(x[here].astype(F32))
            sums[5] += fold8(d * hat)
            sums[6] += fold8(d)
            grad_in[here] = (norm_back(d * gain1, hat, inv) + dmid[here]).astype(BF16)

        row_tiles(norm1_back, 0, tiles - 1)
        pump(2.6)
        hand_b1().wait_recv()
        norm1_back(rows - TILE, slice(rows - TILE, rows), tail_of(halo1))
        start("grad in", grad_in, gin_h)

    pl.run_scoped(attention_back, tall, tall, tall, tall)
    parts = [sums[i] for i in (5, 6, 2, 3, 4)] + [wsums[0], wsums[1]] + [sums[i] for i in (0, 1, 7, 8)]
    lines = [jnp.sum(p, axis=0, keepdims=True) for p in parts]
    lines.append(jnp.zeros((16 - len(lines), width), F32))
    vec_scr[...] = jnp.concatenate(lines, axis=0).astype(BF16)
    for s in range(4):
        start(f"vec {s}", vec_scr, view(gvec_h, s // 2, s % 2))
    for s in range(4):
        wait(f"vec {s}")
    pump(2.0)
    summing.complete("vec")
    summing.drain()
    results = ((ofv, ofv_h), (ofk, ofk_h), (ofr, ofr_h), (owo, owo_h), (owr, owr_h), (owv, owv_h), (owk, owk_h), (ovec, ovec_h))
    for i, (source, target) in enumerate(results):
        start(f"result {i}", source, target)
    summing.finish()
    copies.finish()
    for copy in (hand_x, hand_h2, hand_b2, hand_b1, *hand_st, *hand_adj):
        copy().wait_send()


def block(x, g, weights, vectors, rates, spans, pads, hops):
    rows, width = x.shape
    blocks = width // LANES
    quarter = width // 4
    hid = weights[4].shape[1]
    fv_rows = hid // 4
    block_rows = fv_rows + 4 * quarter + 5 * quarter + 16
    half = pltpu.VMEM((rows, width), BF16)
    flat, flat8 = pltpu.VMEM((rows, width), F32), pltpu.VMEM((rows + 8, width), F32)
    eight = pltpu.VMEM((8, width), F32)
    state = pltpu.VMEM((2, blocks, LANES), F32)
    states = pltpu.VMEM((hops, 2, blocks, LANES), F32)
    lanes = [MOST[lane] for lane in LANES_OF]
    outs = [(fv_rows, LANES), (quarter, 4 * LANES)] + [(quarter, LANES)] * 5 + [(16, LANES)]
    result = pl.pallas_call(
        block_kernel,
        out_shape=[sds((rows, width), BF16)] * 2
        + [sds(shape, F32) for shape in outs]
        + [
            sds((2, block_rows, width), BF16),
            sds((5, 2, 2, quarter, width), BF16),
            sds((2, 2, fv_rows, width), BF16),
            sds((4, 2, 2, quarter, width), BF16),
            sds((2, 2, 16, width), BF16),
            sds((7, rows, width), BF16),
            sds((rows, width), F32),
            sds((2, rows * blocks, LANES), F32),
        ],
        in_specs=[ANY] * 20 + [SMEM] * 2,
        out_specs=[ANY] * 18,
        scratch_shapes=[flat, flat, flat8, flat, flat8]
        + [half] * 8
        + [
            pltpu.VMEM((2, width, width), BF16),
            pltpu.VMEM((2, 2, 2, quarter, 256), BF16),
            pltpu.VMEM((16, width), BF16),
            pltpu.VMEM((rows, LANES), F32),
            pltpu.VMEM((rows, LANES), F32),
            pltpu.VMEM((16, width), BF16),
        ]
        + [eight] * 6
        + [state, states, state, states, state]
        + [pltpu.VMEM((9, 1, width), F32), pltpu.VMEM((2, blocks, LANES), F32)]
        + [pltpu.VMEM(shape, F32) for shape in outs]
        + [pltpu.VMEM((9, 8, width), F32), pltpu.VMEM((2, 8, width), F32)]
        + [pltpu.VMEM((2, 2, most, width), BF16) for most in lanes]
        + [pltpu.VMEM((RING, 2, 2, 2, 2, most, LANES), BF16) for most in lanes]
        + [pltpu.VMEM((2,) * (3 - d) + (block_rows, LANES), BF16) for d in range(4)]
        + [
            pltpu.SemaphoreType.DMA((48,)),
            pltpu.SemaphoreType.DMA((4 + 2 * hops,)),
            pltpu.SemaphoreType.DMA((4 + 2 * hops,)),
            pltpu.SemaphoreType.DMA(()),
            pltpu.SemaphoreType.DMA((len(lanes), RING)),
            pltpu.SemaphoreType.DMA((3,)),
            pltpu.SemaphoreType.DMA((len(CHUNKS),)),
            pltpu.SemaphoreType.DMA((len(lanes), TURNS, STEPS - 1)),
            pltpu.SemaphoreType.DMA((len(lanes), 2)),
        ],
        compiler_params=pltpu.CompilerParams(
            vmem_limit_bytes=63 * MIB, collective_id=0, has_side_effects=True
        ),
        name="block",
    )(x, g, *weights, *vectors, *rates, spans, pads)
    return result[:10]


def finish_kernel(*refs):
    count = (len(refs) - 2) // 3
    sems = refs[-2:]
    sources, targets, held = refs[:count], refs[count : 2 * count], refs[2 * count : 3 * count]
    arrive = [pltpu.make_async_copy(s, h, sems[0].at[i]) for i, (s, h) in enumerate(zip(sources, held))]
    leave = [pltpu.make_async_copy(h, t, sems[1].at[i]) for i, (h, t) in enumerate(zip(held, targets))]
    for copy in arrive:
        copy.start()
    for there, back in zip(arrive, leave):
        there.wait()
        back.start()
    for copy in leave:
        copy.wait()


def finish(arrays):
    return pl.pallas_call(
        finish_kernel,
        out_shape=[sds(a.shape, a.dtype) for a in arrays],
        in_specs=[ANY] * len(arrays),
        out_specs=[ANY] * len(arrays),
        scratch_shapes=[pltpu.VMEM(a.shape, a.dtype) for a in arrays]
        + [pltpu.SemaphoreType.DMA((len(arrays),))] * 2,
        compiler_params=params(62),
        name="finish",
    )(*arrays)


def shift(value, steps):
    count = lax.axis_size("chan")
    pairs = [(i, i + steps) for i in range(count) if 0 <= i + steps < count]
    return lax.ppermute(value, "chan", pairs)


def scatter_sums(mats, vecs):
    def both(m):
        m = lax.psum_scatter(m, "chan", scatter_dimension=1, tiled=True)
        return lax.psum_scatter(m, "seq", scatter_dimension=0, tiled=True).astype(F32)

    v = lax.psum_scatter(vecs.astype(BF16), "chan", scatter_dimension=1, tiled=True).astype(F32)
    return [both(m) for m in mats], lax.psum(v, "seq")


def per_device(
    x, g, gain1, bias1, share_k, share_v, share_r, log_rate, boost, wk, wv, wr, wo, gain2, bias2, share_fk, share_fr,
    wfk, wfv, wfr, spans, pads,
):
    rows, width = x.shape
    chans = lax.axis_size("chan")
    total = rows * chans
    hops = max(1, min(chans - 1, total // 4 // rows))
    if (lax.axis_size("seq"), chans, wfk.shape[1] // chans, width) == (4, 8, 4 * LANES, 8 * LANES):
        line = lambda v: v.reshape(1, width)
        tall = lambda v: v.reshape(width // LANES, LANES)
        vectors = [line(v) for v in (gain1, bias1, share_k, share_v, share_r, gain2, bias2, share_fk, share_fr)]
        weights = (wk, wv, wr, wo, wfk, wfv, wfr)
        results = block(x, g, weights, vectors, (tall(log_rate), tall(boost)), spans, pads, hops)
        vec = results[-1]
        block_out, grad_in, gfv, gfk, gfr, gwo, gwr, gwv, gwk = finish(results[:-1])
        return (block_out, grad_in, *[vec[i] for i in range(7)], gwk, gwv, gwr, gwo, *[vec[i] for i in range(7, 11)], gfk, gfv, gfr)
    base = lambda: lax.axis_index("chan") * rows
    vecs = jnp.stack([gain1, bias1, share_k, share_v, share_r, gain2, bias2, share_fk, share_fr])
    rates = jnp.stack([log_rate, boost]).reshape(2 * width // LANES, LANES)
    begins = jnp.cumsum(spans[0]) - spans[0]
    pos = base() + jnp.arange(rows, dtype=jnp.int32)
    keep = 1.0 - jnp.any(pos[:, None] == begins[None, :], axis=1).astype(F32)

    xprev = shift(jnp.broadcast_to(x[rows - 1 :], (16, width)), 1)[:8]
    xk, xv, xr, k, v, r, at, bt, end = project(base, x, xprev, vecs, rates, spans, pads, keep, wk, wv, wr)
    carry = jnp.concatenate([shift(end, h + 1) for h in range(hops)], axis=0)
    wkv, gated, middle, last, carried = exit_call(base, hops, x, k, v, r, at, bt, carry, rates, vecs, spans, wo)
    hprev = jnp.broadcast_to(shift(last[7:], 1), (8, width))
    block_out, gfk, gfv, gfr, dh2, back2, sums2 = ffn(base, middle, g, hprev, vecs, spans, pads, wfr, wfk, wfv)
    dh2next = shift(back2, -1)
    dmid, gwo, dwkv, dr, sumsn2, adja, adjb, adjend = exit_back(
        base, middle, g, dh2, dh2next, vecs, rates, gated, wkv, r, k, v, at, bt, carried, spans, pads, keep, wo
    )
    adj = jnp.concatenate([shift(adjend, -h - 1) for h in range(hops)], axis=0)
    gwk, gwv, gwr, dh1, back1, sums1, wsums = project_back(
        base, hops, total, x, xprev, vecs, rates, k, v, dwkv, dr, at, bt, carried, adja, adjb, adj, xk, xv, xr, spans,
        pads, wk, wv, wr,
    )
    grad_in, sumsn1 = entry_back(x, dh1, shift(back1, -1), dmid, vecs)
    vec_parts = jnp.concatenate([sumsn1, sums1, wsums, sumsn2, sums2], axis=0).sum(axis=1)
    (gwk, gwv, gwr, gwo, gfk, gfv, gfr), vec = scatter_sums((gwk, gwv, gwr, gwo, gfk, gfv, gfr), vec_parts)
    return (block_out, grad_in, *[vec[i] for i in range(7)], gwk, gwv, gwr, gwo, *[vec[i] for i in range(7, 11)], gfk, gfv, gfr)


def solution(mesh):
    tokens, chan, both = P(("seq", "chan"), None), P("chan"), P("seq", "chan")
    placed = (tokens, tokens) + (P(),) * 18 + (P("seq", None),) * 2
    return jax.shard_map(
        per_device,
        mesh=mesh,
        in_specs=placed,
        out_specs=(tokens, tokens) + (chan,) * 7 + (both,) * 4 + (chan,) * 4 + (both,) * 3,
        check_vma=False,
    )
```

```python
import functools

import jax
import jax.numpy as jnp
from jax import lax
from jax.experimental import pallas as pl
from jax.experimental.pallas import tpu as pltpu
from jax.sharding import PartitionSpec as P

F32, BF16 = jnp.float32, jnp.bfloat16
LANES = 128
TILE = 64
MIB = 1 << 20
VMEM = pl.BlockSpec(memory_space=pltpu.VMEM)
SMEM = pl.BlockSpec(memory_space=pltpu.SMEM)
ANY = pl.BlockSpec(memory_space=pl.ANY)
G1, B1, SK, SV, SR, G2, B2, FK, FR = range(9)


def sds(shape, dtype):
    return jax.ShapeDtypeStruct(shape, dtype)


def params(limit_mib):
    return pltpu.CompilerParams(vmem_limit_bytes=limit_mib * MIB)


def dot(a, b):
    return jnp.dot(a, b, preferred_element_type=F32)


def dot_t(a, b):
    return lax.dot_general(a, b, (((1,), (1,)), ((), ())), preferred_element_type=F32)


def t_dot(a, b):
    return lax.dot_general(a, b, (((0,), (0,)), ((), ())), preferred_element_type=F32)


def fold8(v):
    return jnp.sum(v.reshape(v.shape[0] // 8, 8, v.shape[1]), axis=0)


def normalized(v):
    center = v - jnp.mean(v, axis=-1, keepdims=True)
    inv = lax.rsqrt(jnp.mean(center * center, axis=-1, keepdims=True) + 1e-05)
    return center * inv, inv


def norm_back(d_hat, hat, inv):
    return inv * (
        d_hat
        - jnp.mean(d_hat, axis=-1, keepdims=True)
        - hat * jnp.mean(d_hat * hat, axis=-1, keepdims=True)
    )


def marks(first, rows, spans, pads):
    pos = first + lax.broadcasted_iota(jnp.int32, (rows, LANES), 0)
    begin = 0
    start, real = pos < 0, pos < 0
    for i in range(spans.shape[1]):
        length = spans[0, i]
        start = start | (pos == begin)
        real = real | ((pos >= begin) & (pos < begin + length - pads[0, i]))
        begin = begin + length
    return start, real


def first_start_from(spans, at, otherwise):
    begin, best = 0, otherwise
    for i in range(spans.shape[1]):
        best = jnp.where((begin >= at) & (begin < best), begin, best)
        begin = begin + spans[0, i]
    return best


def last_start_before(spans, at):
    begin, best = 0, -(1 << 20)
    for i in range(spans.shape[1]):
        best = jnp.where(begin < at, begin, best)
        begin = begin + spans[0, i]
    return best


def wide(flag, width):
    return jnp.concatenate([flag] * (width // LANES), axis=1)


def with_previous(ref, at):
    block = ref[pl.ds(at, TILE + 8)]
    return block[8:], block[7 : TILE + 7]


def columns(j):
    return slice(j * LANES, (j + 1) * LANES)


def gather_carry(hops, rows, carry_ref, counts, rate):
    a, b = carry_ref[0], carry_ref[1]
    for h in range(1, hops):
        scale = jnp.exp(-rate * float(rows * h)) * counts[h]
        a, b = a + scale * carry_ref[2 * h], b + scale * carry_ref[2 * h + 1]
    return a, b


def project_kernel(
    base, x_ref, xprev_ref, vec_ref, rate_ref, spans, pads, keep_s, wk_hbm, wv_hbm, wr_hbm,
    xk_ref, xv_ref, xr_ref, k_ref, v_ref, r_ref, at_ref, bt_ref, end_ref,
    h_scr, ek_scr, ev_scr, w_scr, sems,
):
    rows, width = x_ref.shape
    blocks = width // LANES
    copies = [
        pltpu.make_async_copy(hbm, w_scr.at[i], sems.at[i])
        for i, hbm in enumerate((wk_hbm, wv_hbm, wr_hbm))
    ]
    for copy in copies:
        copy.start()
    first = base()
    gain, bias = vec_ref[G1 : G1 + 1], vec_ref[B1 : B1 + 1]
    prev = xprev_ref[...].astype(F32)
    h_scr[0:8] = normalized(prev)[0] * gain + bias

    @pl.loop(0, rows // TILE)
    def _(i):
        at = pl.multiple_of(i * TILE, TILE)
        hat, _ = normalized(x_ref[pl.ds(at, TILE)].astype(F32))
        h_scr[pl.ds(at + 8, TILE)] = hat * gain + bias

    @pl.loop(0, rows // TILE)
    def _(i):
        at = pl.multiple_of(i * TILE, TILE)
        start, _ = marks(first + at, TILE, spans, pads)
        keep = wide(1.0 - start.astype(F32), width)
        h, p = with_previous(h_scr, at)
        p = p * keep
        for row, out in ((SK, xk_ref), (SV, xv_ref), (SR, xr_ref)):
            share = vec_ref[row : row + 1]
            out[pl.ds(at, TILE)] = (h * share + p * (1.0 - share)).astype(BF16)

    _, real = marks(first, rows, spans, pads)
    real = real.astype(F32)
    step = 256
    for i, (src, out) in enumerate(((xk_ref, k_ref), (xv_ref, v_ref), (xr_ref, r_ref))):
        copies[i].wait()
        for j in range(width // step):
            tile = dot(src[...], w_scr[i, :, j * step : (j + 1) * step])
            out[:, j * step : (j + 1) * step] = tile.astype(out.dtype)
    for j in range(blocks):
        ek = jnp.exp(k_ref[:, columns(j)].astype(F32)) * real
        ek_scr[pl.ds(j, rows, stride=blocks)] = ek
        ev_scr[pl.ds(j, rows, stride=blocks)] = ek * v_ref[:, columns(j)].astype(F32)
    decay = jnp.exp(-jnp.exp(rate_ref[0:blocks]))

    def scan(t8, carry):
        a, b = carry
        for u in range(8):
            t = t8 * 8 + u
            keep = keep_s[t]
            here = pl.ds(pl.multiple_of(t * blocks, blocks), blocks)
            at_ref[here] = a * keep
            bt_ref[here] = b * keep
            fade = decay * keep
            a = a * fade + ev_scr[here]
            b = b * fade + ek_scr[here]
        return a, b

    zero = jnp.zeros((blocks, LANES), F32)
    a, b = lax.fori_loop(0, rows // 8, scan, (zero, zero))
    end_ref[0] = a
    end_ref[1] = b


def project(base, x, xprev, vecs, rates, spans, pads, keep, wk, wv, wr):
    rows, width = x.shape
    shape = (rows, width)
    tall = (rows * (width // LANES), LANES)
    return pl.pallas_call(
        functools.partial(project_kernel, base),
        out_shape=(
            [sds(shape, BF16)] * 5 + [sds(shape, F32)] + [sds(tall, F32)] * 2 + [sds((2, width // LANES, LANES), F32)]
        ),
        in_specs=[VMEM] * 4 + [SMEM] * 3 + [ANY] * 3,
        out_specs=[VMEM] * 9,
        scratch_shapes=[
            pltpu.VMEM((rows + 8, width), F32),
            pltpu.VMEM(tall, F32),
            pltpu.VMEM(tall, F32),
            pltpu.VMEM((3, width, width), BF16),
            pltpu.SemaphoreType.DMA((3,)),
        ],
        compiler_params=params(56),
        name="project",
    )(x, xprev, vecs, rates, spans, pads, keep, wk, wv, wr)


def wkv_parts(at, j, rows, blocks, k, v, at_ref, bt_ref, a_in, b_in, rate, boost, first_start):
    here = pl.ds(at * blocks + j, rows, stride=blocks)
    pos = at + lax.broadcasted_iota(jnp.int32, (rows, LANES), 0)
    lift = jnp.where(pos < first_start, jnp.exp(-rate[j : j + 1] * pos.astype(F32)), 0.0)
    a = at_ref[here] + lift * a_in[j : j + 1]
    b = bt_ref[here] + lift * b_in[j : j + 1]
    eu = jnp.exp(boost[j : j + 1] + k)
    inv = 1.0 / (b + eu)
    return a, b, eu, inv, (a + eu * v) * inv


def carry_counts(hops, rows, first, spans):
    last = last_start_before(spans, first)
    return [jnp.where(last < first - h * rows, 1.0, 0.0) for h in range(hops)]


def exit_kernel(
    base, hops, x_ref, k_ref, v_ref, r_ref, at_ref, bt_ref, carry_ref, rate_ref, vec_ref, spans, wo_hbm,
    wkv_ref, gated_ref, middle_ref, last_ref, in_ref, wo_scr, sem,
):
    rows, width = x_ref.shape
    blocks = width // LANES
    copy = pltpu.make_async_copy(wo_hbm, wo_scr, sem)
    copy.start()
    first = base()
    rate = jnp.exp(rate_ref[0:blocks])
    boost = rate_ref[blocks : 2 * blocks]
    a_in, b_in = gather_carry(hops, rows, carry_ref, carry_counts(hops, rows, first, spans), rate)
    in_ref[0] = a_in
    in_ref[1] = b_in
    first_start = first_start_from(spans, first, 1 << 20) - first

    @pl.loop(0, rows // TILE)
    def _(i):
        at = pl.multiple_of(i * TILE, TILE)
        for j in range(blocks):
            here = (pl.ds(at, TILE), columns(j))
            k, v = k_ref[here].astype(F32), v_ref[here].astype(F32)
            wkv = wkv_parts(at, j, TILE, blocks, k, v, at_ref, bt_ref, a_in, b_in, rate, boost, first_start)[-1]
            wkv = wkv.astype(BF16)
            wkv_ref[here] = wkv
            gated_ref[here] = (jax.nn.sigmoid(r_ref[here]) * wkv.astype(F32)).astype(BF16)

    copy.wait()
    step = 256
    for j in range(width // step):
        here = (slice(None), slice(j * step, (j + 1) * step))
        middle_ref[here] = x_ref[here].astype(F32) + dot(gated_ref[...], wo_scr[here])
    hat, _ = normalized(middle_ref[rows - 8 : rows])
    last_ref[...] = hat * vec_ref[G2 : G2 + 1] + vec_ref[B2 : B2 + 1]


def exit_call(base, hops, x, k, v, r, at, bt, carry, rates, vecs, spans, wo):
    rows, width = x.shape
    blocks = width // LANES
    return pl.pallas_call(
        functools.partial(exit_kernel, base, hops),
        out_shape=[
            sds((rows, width), BF16),
            sds((rows, width), BF16),
            sds((rows, width), F32),
            sds((8, width), F32),
            sds((2, blocks, LANES), F32),
        ],
        in_specs=[VMEM] * 9 + [SMEM, ANY],
        out_specs=[VMEM] * 5,
        scratch_shapes=[pltpu.VMEM((width, width), BF16), pltpu.SemaphoreType.DMA(())],
        compiler_params=params(56),
        name="exit",
    )(x, k, v, r, at, bt, carry, rates, vecs, spans, wo)


def ffn_kernel(
    base, mid_ref, g_ref, hprev_ref, vec_ref, spans, pads, wg_ref, wk_ref, wv_ref,
    out_ref, gfk_ref, gfv_ref, gfr_ref, dh_ref, back_ref, sums_ref,
    h_scr, ck_scr, cr_scr, ckt_scr, sig_scr, dvo_scr, val_scr, dck_scr, pass_scr,
):
    rows, width = mid_ref.shape
    step = pl.program_id(0)
    first = base()
    tiles = rows // TILE

    @pl.when(step == 0)
    def _():
        gain, bias = vec_ref[G2 : G2 + 1], vec_ref[B2 : B2 + 1]
        h_scr[0:8] = hprev_ref[...]

        @pl.loop(0, tiles)
        def _(i):
            at = pl.multiple_of(i * TILE, TILE)
            hat, _ = normalized(mid_ref[pl.ds(at, TILE)])
            h_scr[pl.ds(at + 8, TILE)] = hat * gain + bias

        @pl.loop(0, tiles)
        def _(i):
            at = pl.multiple_of(i * TILE, TILE)
            start, _ = marks(first + at, TILE, spans, pads)
            keep = wide(1.0 - start.astype(F32), width)
            h, p = with_previous(h_scr, at)
            p = p * keep
            for row, out in ((FK, ck_scr), (FR, cr_scr)):
                share = vec_ref[row : row + 1]
                out[pl.ds(at, TILE)] = (h * share + p * (1.0 - share)).astype(BF16)

        ckt_scr[...] = ck_scr[...].T
        _, real = marks(first, rows, spans, pads)
        real = wide(real.astype(F32), 256)
        for j in range(width // 256):
            here = (slice(None), slice(j * 256, (j + 1) * 256))
            sig = jax.nn.sigmoid(dot(cr_scr[...], wg_ref[here]))
            sig_scr[here] = sig
            dvo_scr[here] = (g_ref[here].astype(F32) * real * sig).astype(BF16)
        val_scr[...] = jnp.zeros_like(val_scr)
        dck_scr[...] = jnp.zeros_like(dck_scr)

    act = jnp.maximum(dot(ck_scr[...], wk_ref[...]), 0.0)
    hidden = (act * act).astype(BF16)
    val_scr[...] += dot(hidden, wv_ref[...])
    gfv_ref[...] = t_dot(hidden, dvo_scr[...]).astype(BF16)
    d_pre = (dot_t(dvo_scr[...], wv_ref[...]) * (2.0 * act)).astype(BF16)
    gfk_ref[...] = dot(ckt_scr[...], d_pre).astype(BF16)
    dck_scr[...] += dot_t(d_pre, wk_ref[...])

    @pl.when(step == pl.num_programs(0) - 1)
    def _():
        dgp_scr = dvo_scr
        _, real = marks(first, rows, spans, pads)
        real = wide(real.astype(F32), 256)
        for j in range(width // 256):
            here = (slice(None), slice(j * 256, (j + 1) * 256))
            sig, value = sig_scr[here], val_scr[here]
            out_ref[here] = (mid_ref[here] + sig * value).astype(BF16)
            top = g_ref[here].astype(F32) * real
            dgp_scr[here] = (top * value * sig * (1.0 - sig)).astype(BF16)
        for j in range(width // 256):
            here = (slice(None), slice(j * 256, (j + 1) * 256))
            gfr_ref[here] = t_dot(cr_scr[...], dgp_scr[here]).astype(BF16)
        dcr_scr = val_scr
        for j in range(width // 256):
            dcr_scr[:, j * 256 : (j + 1) * 256] = dot_t(dgp_scr[...], wg_ref[j * 256 : (j + 1) * 256])
        sums_ref[...] = jnp.zeros_like(sums_ref)
        share_k, share_r = vec_ref[FK : FK + 1], vec_ref[FR : FR + 1]

        @pl.loop(0, tiles)
        def _(i):
            at = pl.multiple_of(i * TILE, TILE)
            here = pl.ds(at, TILE)
            start, _ = marks(first + at, TILE, spans, pads)
            keep = wide(1.0 - start.astype(F32), width)
            h, p = with_previous(h_scr, at)
            diff = h - p * keep
            dck, dcr = dck_scr[here], dcr_scr[here]
            sums_ref[0] += fold8(diff * dck)
            sums_ref[1] += fold8(diff * dcr)
            pass_scr[here] = (dck * (1.0 - share_k) + dcr * (1.0 - share_r)) * keep
            dh_ref[here] = dck * share_k + dcr * share_r

        back_ref[...] = pass_scr[0:8]

        pass_scr[rows : rows + 8] = jnp.zeros((8, width), F32)

        @pl.loop(0, tiles)
        def _(i):
            at = pl.multiple_of(i * TILE, TILE)
            dh_ref[pl.ds(at, TILE)] += pass_scr[pl.ds(at, TILE + 8)][1 : TILE + 1]


def ffn(base, middle, g, hprev, vecs, spans, pads, wg, wk, wv):
    rows, width = middle.shape
    hid = wk.shape[1]
    unit = 512
    full = lambda shape: pl.BlockSpec(shape, lambda j: (0,) * len(shape))
    return pl.pallas_call(
        functools.partial(ffn_kernel, base),
        grid=(hid // unit,),
        out_shape=[
            sds((rows, width), BF16),
            sds((width, hid), BF16),
            sds((hid, width), BF16),
            sds((width, width), BF16),
            sds((rows, width), F32),
            sds((8, width), F32),
            sds((2, 8, width), F32),
        ],
        in_specs=[
            full((rows, width)),
            full((rows, width)),
            full((8, width)),
            full(vecs.shape),
            SMEM,
            SMEM,
            full((width, width)),
            pl.BlockSpec((width, unit), lambda j: (0, j)),
            pl.BlockSpec((unit, width), lambda j: (j, 0)),
        ],
        out_specs=[
            full((rows, width)),
            pl.BlockSpec((width, unit), lambda j: (0, j)),
            pl.BlockSpec((unit, width), lambda j: (j, 0)),
            full((width, width)),
            full((rows, width)),
            full((8, width)),
            full((2, 8, width)),
        ],
        scratch_shapes=[
            pltpu.VMEM((rows + 8, width), F32),
            pltpu.VMEM((rows, width), BF16),
            pltpu.VMEM((rows, width), BF16),
            pltpu.VMEM((width, rows), BF16),
            pltpu.VMEM((rows, width), F32),
            pltpu.VMEM((rows, width), BF16),
            pltpu.VMEM((rows, width), F32),
            pltpu.VMEM((rows, width), F32),
            pltpu.VMEM((rows + 8, width), F32),
        ],
        compiler_params=params(60),
        name="ffn",
    )(middle, g, hprev, vecs, spans, pads, wg, wk, wv)


def exit_back_kernel(
    base, mid_ref, g_ref, dh_ref, dhnext_ref, vec_ref, rate_ref, gated_ref, wkv_ref, r_ref, k_ref, v_ref, at_ref, bt_ref,
    in_ref, spans, pads, keep_s, wo_ref,
    dmid_ref, gwo_ref, dwkv_ref, dr_ref, sums_ref, adja_ref, adjb_ref, adjend_ref,
    datt_scr, dn_scr, dd_scr,
):
    rows, width = mid_ref.shape
    blocks = width // LANES
    first = base()
    gain = vec_ref[G2 : G2 + 1]
    sums_ref[...] = jnp.zeros_like(sums_ref)
    tail = dhnext_ref[...]
    row = lax.broadcasted_iota(jnp.int32, tail.shape, 0)
    dh_ref[rows - 8 : rows] += jnp.where(row == 7, pltpu.roll(tail, 7, axis=0), 0.0)

    @pl.loop(0, rows // TILE)
    def _(i):
        at = pl.multiple_of(i * TILE, TILE)
        here = pl.ds(at, TILE)
        _, real = marks(first + at, TILE, spans, pads)
        hat, inv = normalized(mid_ref[here])
        dh = dh_ref[here]
        sums_ref[0] += fold8(dh * hat)
        sums_ref[1] += fold8(dh)
        d_mid = norm_back(dh * gain, hat, inv) + g_ref[here].astype(F32) * wide(real.astype(F32), width)
        dmid_ref[here] = d_mid
        datt_scr[here] = d_mid.astype(BF16)

    step = 256
    rate = jnp.exp(rate_ref[0:blocks])
    boost = rate_ref[blocks : 2 * blocks]
    a_in, b_in = in_ref[0], in_ref[1]
    first_start = first_start_from(spans, first, 1 << 20) - first
    for j in range(width // step):
        here = (slice(None), slice(j * step, (j + 1) * step))
        dr_ref[here] = dot_t(datt_scr[...], wo_ref[j * step : (j + 1) * step]).astype(BF16)
    d_gated = dr_ref

    @pl.loop(0, rows // TILE)
    def _(i):
        at = pl.multiple_of(i * TILE, TILE)
        for j in range(blocks):
            here = (pl.ds(at, TILE), columns(j))
            sig = jax.nn.sigmoid(r_ref[here])
            dg = d_gated[here].astype(F32)
            dwkv = (dg * sig).astype(BF16)
            dwkv_ref[here] = dwkv
            dr_ref[here] = (dg * wkv_ref[here].astype(F32) * sig * (1.0 - sig)).astype(BF16)
            k, v = k_ref[here].astype(F32), v_ref[here].astype(F32)
            _, _, _, inv, wkv = wkv_parts(
                at, j, TILE, blocks, k, v, at_ref, bt_ref, a_in, b_in, rate, boost, first_start
            )
            dn = dwkv.astype(F32) * inv
            there = pl.ds(at * blocks + j, TILE, stride=blocks)
            dn_scr[there] = dn
            dd_scr[there] = -dn * wkv

    decay = jnp.exp(-rate)

    def scan(t8, carry):
        a, b = carry
        for u in range(8):
            t = rows - 1 - (t8 * 8 + u)
            keep = keep_s[t]
            here = pl.ds(pl.multiple_of(t * blocks, blocks), blocks)
            adja_ref[here] = a
            adjb_ref[here] = b
            fade = decay * keep
            a = a * fade + dn_scr[here] * keep
            b = b * fade + dd_scr[here] * keep
        return a, b

    zero = jnp.zeros((blocks, LANES), F32)
    a, b = lax.fori_loop(0, rows // 8, scan, (zero, zero))
    adjend_ref[0] = a
    adjend_ref[1] = b
    for j in range(width // step):
        here = (slice(None), slice(j * step, (j + 1) * step))
        gwo_ref[here] = t_dot(gated_ref[...], datt_scr[here]).astype(BF16)


def exit_back(base, middle, g, dh, dhnext, vecs, rates, gated, wkv, r, k, v, at, bt, carry, spans, pads, keep, wo):
    rows, width = middle.shape
    blocks = width // LANES
    tall = (rows * blocks, LANES)
    return pl.pallas_call(
        functools.partial(exit_back_kernel, base),
        out_shape=[
            sds((rows, width), F32),
            sds((width, width), BF16),
            sds((rows, width), BF16),
            sds((rows, width), BF16),
            sds((2, 8, width), F32),
            sds(tall, F32),
            sds(tall, F32),
            sds((2, blocks, LANES), F32),
        ],
        in_specs=[VMEM] * 14 + [SMEM] * 3 + [VMEM],
        out_specs=[VMEM] * 8,
        scratch_shapes=[
            pltpu.VMEM((rows, width), BF16),
            pltpu.VMEM(tall, F32),
            pltpu.VMEM(tall, F32),
        ],
        compiler_params=params(60),
        name="exit_back",
    )(middle, g, dh, dhnext, vecs, rates, gated, wkv, r, k, v, at, bt, carry, spans, pads, keep, wo)


def project_back_kernel(
    base, hops, total, x_ref, xprev_ref, vec_ref, rate_ref, k_ref, v_ref, dwkv_ref, dr_ref, at_ref, bt_ref, in_ref,
    adja_ref, adjb_ref, adj_ref, xk_ref, xv_ref, xr_ref, spans, pads, wk_hbm, wv_hbm, wr_hbm,
    gwk_ref, gwv_ref, gwr_ref, dh_ref, back_ref, sums_ref, wsums_ref,
    h_scr, dk_scr, dv_scr, d_scr, pass_scr, w_scr, sems,
):
    rows, width = x_ref.shape
    blocks = width // LANES
    copies = [
        pltpu.make_async_copy(hbm, w_scr.at[i], sems.at[i])
        for i, hbm in enumerate((wk_hbm, wv_hbm, wr_hbm))
    ]
    for copy in copies:
        copy.start()
    first = base()
    rate = jnp.exp(rate_ref[0:blocks])
    boost = rate_ref[blocks : 2 * blocks]
    a_in, b_in = in_ref[0], in_ref[1]
    first_start = first_start_from(spans, first, 1 << 20) - first
    last_start = last_start_before(spans, first + rows) - first
    after = first_start_from(spans, first + rows, total)
    counts = [jnp.where(after >= first + (h + 1) * rows, 1.0, 0.0) for h in range(hops)]
    adj_a, adj_b = gather_carry(hops, rows, adj_ref, counts, rate)
    wsums_ref[...] = jnp.zeros_like(wsums_ref)
    sums_ref[...] = jnp.zeros_like(sums_ref)

    @pl.loop(0, rows // TILE)
    def _(i):
        at = pl.multiple_of(i * TILE, TILE)
        _, real = marks(first + at, TILE, spans, pads)
        real = real.astype(F32)
        pos = at + lax.broadcasted_iota(jnp.int32, (TILE, LANES), 0)
        for j in range(blocks):
            here = (pl.ds(at, TILE), columns(j))
            k, v = k_ref[here].astype(F32), v_ref[here].astype(F32)
            a, b, eu, inv, wkv = wkv_parts(
                at, j, TILE, blocks, k, v, at_ref, bt_ref, a_in, b_in, rate, boost, first_start
            )
            there = pl.ds(at * blocks + j, TILE, stride=blocks)
            lift = jnp.where(
                pos >= last_start, jnp.exp(-rate[j : j + 1] * (rows - 1 - pos).astype(F32)), 0.0
            )
            post_a = adja_ref[there] + lift * adj_a[j : j + 1]
            post_b = adjb_ref[there] + lift * adj_b[j : j + 1]
            dn = dwkv_ref[here].astype(F32) * inv
            own = eu * dn
            weight = jnp.exp(k) * real
            dv_scr[here] = (own + weight * post_a).astype(BF16)
            first_term = own * (v - wkv)
            dk_scr[here] = (first_term + weight * (v * post_a + post_b)).astype(BF16)
            wsums_ref[0, :, columns(j)] += fold8(a * post_a + b * post_b)
            wsums_ref[1, :, columns(j)] += fold8(first_term)

    for j in range(blocks):
        r = rate[j : j + 1]
        wsums_ref[0, :, columns(j)] *= -r * jnp.exp(-r)
    gain, bias = vec_ref[G1 : G1 + 1], vec_ref[B1 : B1 + 1]
    h_scr[0:8] = normalized(xprev_ref[...].astype(F32))[0] * gain + bias

    @pl.loop(0, rows // TILE)
    def _(i):
        at = pl.multiple_of(i * TILE, TILE)
        hat, _ = normalized(x_ref[pl.ds(at, TILE)].astype(F32))
        h_scr[pl.ds(at + 8, TILE)] = hat * gain + bias

    step = 256
    dh_ref[...] = jnp.zeros_like(dh_ref)
    groups = ((dk_scr, xk_ref, gwk_ref, SK), (dv_scr, xv_ref, gwv_ref, SV), (dr_ref, xr_ref, gwr_ref, SR))
    pass_scr[...] = jnp.zeros_like(pass_scr)
    for i, (grad, mixed, out, row) in enumerate(groups):
        copies[i].wait()
        for j in range(width // step):
            here = (slice(None), slice(j * step, (j + 1) * step))
            d_scr[:, j * step : (j + 1) * step] = dot_t(grad[...], w_scr[i, j * step : (j + 1) * step])
            out[here] = t_dot(mixed[...], grad[here]).astype(BF16)
        share = vec_ref[row : row + 1]

        @pl.loop(0, rows // TILE)
        def _(t):
            at = pl.multiple_of(t * TILE, TILE)
            here = pl.ds(at, TILE)
            start, _ = marks(first + at, TILE, spans, pads)
            keep = wide(1.0 - start.astype(F32), width)
            h, p = with_previous(h_scr, at)
            d = d_scr[here]
            sums_ref[i] += fold8((h - p * keep) * d)
            pass_scr[here] += d * (1.0 - share) * keep
            dh_ref[here] += d * share

    back_ref[...] = pass_scr[0:8]

    @pl.loop(0, rows // TILE)
    def _(i):
        at = pl.multiple_of(i * TILE, TILE)
        dh_ref[pl.ds(at, TILE)] += pass_scr[pl.ds(at, TILE + 8)][1 : TILE + 1]


def project_back(base, hops, total, x, xprev, vecs, rates, k, v, dwkv, dr, at, bt, carry, adja, adjb, adj, xk, xv, xr, spans, pads, wk, wv, wr):
    rows, width = x.shape
    return pl.pallas_call(
        functools.partial(project_back_kernel, base, hops, total),
        out_shape=[sds((width, width), BF16)] * 3
        + [
            sds((rows, width), F32),
            sds((8, width), F32),
            sds((3, 8, width), F32),
            sds((2, 8, width), F32),
        ],
        in_specs=[VMEM] * 17 + [SMEM] * 2 + [ANY] * 3,
        out_specs=[VMEM] * 7,
        scratch_shapes=[
            pltpu.VMEM((rows + 8, width), F32),
            pltpu.VMEM((rows, width), BF16),
            pltpu.VMEM((rows, width), BF16),
            pltpu.VMEM((rows, width), F32),
            pltpu.VMEM((rows + 8, width), F32),
            pltpu.VMEM((3, width, width), BF16),
            pltpu.SemaphoreType.DMA((3,)),
        ],
        compiler_params=params(60),
        name="project_back",
    )(x, xprev, vecs, rates, k, v, dwkv, dr, at, bt, carry, adja, adjb, adj, xk, xv, xr, spans, pads, wk, wv, wr)


def entry_back_kernel(x_ref, dh_ref, dhnext_ref, dmid_ref, vec_ref, out_ref, sums_ref):
    rows = x_ref.shape[0]
    gain = vec_ref[G1 : G1 + 1]
    sums_ref[...] = jnp.zeros_like(sums_ref)
    tail = dhnext_ref[...]
    row = lax.broadcasted_iota(jnp.int32, tail.shape, 0)
    dh_ref[rows - 8 : rows] += jnp.where(row == 7, pltpu.roll(tail, 7, axis=0), 0.0)

    @pl.loop(0, rows // TILE)
    def _(i):
        here = pl.ds(pl.multiple_of(i * TILE, TILE), TILE)
        hat, inv = normalized(x_ref[here].astype(F32))
        dh = dh_ref[here]
        sums_ref[0] += fold8(dh * hat)
        sums_ref[1] += fold8(dh)
        out_ref[here] = (norm_back(dh * gain, hat, inv) + dmid_ref[here]).astype(BF16)


def entry_back(x, dh, dhnext, dmid, vecs):
    rows, width = x.shape
    return pl.pallas_call(
        entry_back_kernel,
        out_shape=[sds((rows, width), BF16), sds((2, 8, width), F32)],
        in_specs=[VMEM] * 5,
        out_specs=[VMEM] * 2,
        compiler_params=params(40),
        name="entry_back",
    )(x, dh, dhnext, dmid, vecs)


X, Y, Z = "x", "y", "z"
ORDERS = {
    X: ("x", "y", "low", "high"),
    Y: ("y", "x", "low", "high"),
    Z: ("low", "high", "x", "y"),
}
AXIS_BIT = {"core": ("seq", 1), "x": ("seq", 2), "y": ("chan", 1), "low": ("chan", 2), "high": ("chan", 4)}
STEPS = 5
SEQ, CHAN = 4, 8
RING = 3
BIG = 256
MESH = pl.DeviceIdType.MESH
ARRAYS = ("fv", "fk0", "fk1", "fk2", "fk3", "fr", "wo", "wr", "wv", "wk")
UNITS = (0, 4, 1, 5, 2, 6, 3, 7)


def third(name):
    return ((name, 0, 96, X), (name, 96, 96, Y), (name, 192, 64, Z))


CHUNKS = (
    tuple(
        chunk
        for q in range(4)
        for chunk in (
            ("fv", q * 128, 128, X),
            ("fv", (q + 4) * 128, 128, Y),
            (f"fk{q}", 128, 128, Z),
            (f"fk{q}", 0, 128, Y if q % 2 else X),
        )
    )
    + (("fr", 0, 128, X), ("fr", 128, 128, Y), ("wo", 0, 128, X), ("wo", 128, 128, Y))
    + (("wr", 0, 64, X), ("wr", 64, 64, Y), ("wr", 128, 128, Z))
    + third("wv")
    + third("wk")
)
MOST = {X: 128, Y: 128, Z: 128}
LANES_OF = (X, Y, Z)
TURNS = 6
LINK, CORE, HOP, FETCH, ACTION, ADD = 46000.0, 570000.0, 4.0, 1.6, 0.06, 0.0012
BACKLOG, PACE = 3.0, 1.12


def bit_of(index, weight):
    return index // weight % 2


def partner(axis):
    name, weight = AXIS_BIT[axis]
    where = {"seq": lax.axis_index("seq"), "chan": lax.axis_index("chan")}
    bit = bit_of(where[name], weight)
    where[name] = where[name] + weight * (1 - 2 * bit)
    return bit, (where["seq"], where["chan"])


class Summing:
    def __init__(self, grads, received, outs, stages, rings, levels, sems):
        self.grads, self.received, self.outs = grads, received, outs
        self.stages, self.rings, self.levels = stages, rings, levels
        self.across_sem, self.ring_sems, self.level_sems, self.across_recv, self.recv_sems, self.stage_sems = sems
        self.sides = {axis: partner(axis) for axis in AXIS_BIT}
        self.bases, filled = {}, 0
        for name in ARRAYS:
            self.bases[name] = filled
            filled += grads[name]().shape[2]
        count = len(CHUNKS)
        self.queue = {lane: [n for n in range(count) if CHUNKS[n][3] == lane] for lane in LANES_OF}
        self.turn = {n: i for queue in self.queue.values() for i, n in enumerate(queue)}
        self.now, self.waited = 0.0, 0.0
        self.free = dict.fromkeys(("core", "x", "y", "end", "middle"), 0.0)
        self.ready = {}
        self.did = set()


    def place(self, number):
        array, first, rows, stream = CHUNKS[number]
        return array, first, rows, stream, LANES_OF.index(stream), self.bases[array] + first

    def key(self, number):
        array, first, _, _ = CHUNKS[number]
        return f"fv{first // 128}" if array == "fv" else array

    def across(self, number):
        array, first, rows, _, _, base = self.place(number)
        core, mate = self.sides["core"]
        return pltpu.make_async_remote_copy(
            src_ref=self.grads[array]().at[:, 1 - core, pl.ds(first, rows)],
            dst_ref=self.received.at[:, pl.ds(base, rows)],
            send_sem=self.across_sem,
            recv_sem=self.across_recv.at[number],
            device_id=mate,
            device_id_type=MESH,
        )

    def staged(self, number):
        array, first, rows, _, lane, base = self.place(number)
        core, _ = self.sides["core"]
        stage = self.stages[lane]
        return (
            pltpu.make_async_copy(
                self.grads[array]().at[:, core, pl.ds(first, rows)], stage.at[0, :, 0:rows], self.stage_sems.at[lane, 0]
            ),
            pltpu.make_async_copy(self.received.at[:, pl.ds(base, rows)], stage.at[1, :, 0:rows], self.stage_sems.at[lane, 1]),
        )

    def half(self, number, step, other):
        _, _, rows, stream, lane, base = self.place(number)
        bit, _ = self.sides[ORDERS[stream][step - 1]]
        size = (16 >> step) * rows
        at = pl.ds(pl.multiple_of((1 - bit if other else bit) * size + (step > 1) * base * (32 >> step), 16), size)
        if step == 1:
            return self.rings[lane], (self.turn[number] % RING, at)
        return self.levels[step - 2], (at,)

    def target(self, number, step):
        _, _, rows, _, _, base = self.place(number)
        return self.levels[step - 1], pl.ds(base * (16 >> step), rows * (16 >> step))

    def send(self, number, step):
        _, _, _, stream, lane, _ = self.place(number)
        _, mate = self.sides[ORDERS[stream][step - 1]]
        source, there = self.half(number, step, True)
        target, here = self.target(number, step)
        return pltpu.make_async_remote_copy(
            src_ref=source.at[there],
            dst_ref=target.at[here],
            send_sem=self.ring_sems.at[lane, self.turn[number] % RING] if step == 1 else self.level_sems.at[step - 2],
            recv_sem=self.recv_sems.at[lane, self.turn[number] % TURNS, step - 1],
            device_id=mate,
            device_id_type=MESH,
        )


    def transfer(self, number, step):
        rows = CHUNKS[number][2]
        if step == 0:
            hops = (("core", rows * 4096 / CORE),)
        else:
            took = rows * (16 >> step) * 256 / LINK
            axis = ORDERS[CHUNKS[number][3]][step - 1]
            hops = {"low": (("end", took),), "high": (("end", took), ("middle", 2 * took))}.get(axis, ((axis, took),))
        arrived = 0.0
        for link, took in hops:
            self.free[link] = max(self.now, self.free[link]) + took
            arrived = max(arrived, self.free[link])
        self.ready[number, step] = arrived + HOP

    def link_of(self, number, step):
        axis = ORDERS[CHUNKS[number][3]][step - 1]
        return {"low": "end", "high": "end"}.get(axis, axis)

    def possible(self):
        found = []
        for queue in self.queue.values():
            for n in queue:
                if (n, 0) not in self.ready:
                    break
                turn = self.turn[n]
                if (n, "fetch") not in self.did:
                    if turn == 0 or (queue[turn - 1], 0) in self.did:
                        found.append((self.ready[n, 0], None, n, "fetch"))
                    break
                if (n, 0) not in self.did:
                    old = queue[turn - RING] if turn >= RING else None
                    if old is None or (old, 1) in self.did:
                        when = max(self.ready[n, "fetch"], 0.0 if old is None else self.ready[old, 1])
                        found.append((when, self.link_of(n, 1), n, 0))
                    continue
                step = next((s for s in range(1, STEPS) if (n, s) not in self.did), None)
                if step:
                    found.append((self.ready[n, step], self.link_of(n, step + 1) if step < 4 else None, n, step))
        return found

    def act(self, when, number, step):
        self.waited += max(0.0, when - self.now)
        self.now = max(self.now, when) + ACTION
        rows = CHUNKS[number][2]
        self.did.add((number, step))
        if step == "fetch":
            self.start_stage(number)
            self.ready[number, "fetch"] = self.now + FETCH
        elif step == 0:
            self.now += rows * ADD
            self.first_sum(number)
            self.transfer(number, 1)
        else:
            self.now += rows * 2 * ADD / (1 << step)
            self.later_sum(number, step)
            if step < 4:
                self.transfer(number, step + 1)

    def pump(self, took):
        self.now += took * PACE
        while True:
            able = [
                (self.free.get(link, 0.0), n, step, when)
                for when, link, n, step in self.possible()
                if when <= self.now and self.free.get(link, 0.0) < self.now + BACKLOG
            ]
            if not able:
                return
            _, number, step, when = min(able, key=lambda a: a[:2])
            self.act(when, number, step)

    def drain(self):
        while found := self.possible():
            when, _, number, step = min(found, key=lambda a: (max(a[0], self.now), a[2]))
            self.act(when, number, step)

    def complete(self, key):
        for n in range(len(CHUNKS)):
            if self.key(n) == key:
                self.across(n).start()
                self.now += 0.05
                self.transfer(n, 0)


    def start_stage(self, number):
        self.across(number).wait_recv()
        for copy in self.staged(number):
            copy.start()

    def first_sum(self, number):
        _, _, rows, stream, lane, _ = self.place(number)
        turn = self.turn[number]
        stage, ring = self.stages[lane], self.rings[lane]
        if turn >= RING:
            self.send(self.queue[stream][turn - RING], 1).wait_send()
        for copy in self.staged(number):
            copy.wait()
        for i in range(16):
            c = i % 8
            bits = {"x": i // 8, "y": c % 2, "low": c // 2 % 2, "high": c // 4}
            at = sum(bits[axis] << (3 - d) for d, axis in enumerate(ORDERS[stream])) * rows
            ring[turn % RING, at : at + rows] = stage[0, i // 8, 0:rows, columns(c)] + stage[1, i // 8, 0:rows, columns(c)]
        self.send(number, 1).start()

    def later_sum(self, number, step):
        array, first, rows, _, _, _ = self.place(number)
        source, own = self.half(number, step, False)
        target, here = self.target(number, step)
        self.send(number, step).wait_recv()
        if step == 4:
            out, cols = self.outs[array]
            out[first : first + rows, cols] = source[own].astype(F32) + target[here].astype(F32)
            return
        target[here] = source[own] + target[here]
        self.send(number, step + 1).start()

    def finish(self):
        pltpu.make_async_copy(self.received, self.received, self.across_sem).wait()
        for i, level in enumerate(self.levels[1:]):
            pltpu.make_async_copy(level, level, self.level_sems.at[i]).wait()
        for queue in self.queue.values():
            for n in queue[-RING:]:
                self.send(n, 1).wait_send()


def view(ref, *index):
    return lambda: ref.at[index]


class Copies:
    def __init__(self, sems):
        self.sems, self.all, self.waited = sems, {}, set()
        self.idle = list(range(sems.shape[0]))

    def start(self, name, source, target):
        assert name not in self.all
        self.all[name] = (source, target, self.idle.pop(0))
        self.copy(name).start()

    def copy(self, name):
        source, target, number = self.all[name]
        source, target = (r() if callable(r) else r for r in (source, target))
        return pltpu.make_async_copy(source, target, self.sems.at[number])

    def wait(self, *names):
        for name in names:
            if name not in self.waited:
                self.copy(name).wait()
                self.waited.add(name)
                self.idle.append(self.all[name][2])

    def finish(self):
        self.wait(*self.all)


def block_kernel(*refs):
    (
        spans, pads,
        out_h, gin_h, ofv_h, ofk_h, ofr_h, owo_h, owr_h, owv_h, owk_h, ovec_h,
        received, gw_h, gfv_h, gfk_h, spill_b, spill_r, spill_t,
        mid, dh, h_scr, d_scr, pass_scr, b0, b1, b2, b3, b4, b5, b6, b7, w_scr, tile_scr, vec_scr, vec_chan, vec_mine, vec_seq,
        keep_scr, real_scr, xlast, halo2, halob2, halo1, mine2, mine1, mineb2, st_mine, st_in, adj_mine, adj_in, in_scr,
        line, tall_line, ofv, ofk, ofr, owo, owr, owv, owk, ovec,
        sums, wsums, s0, s1, s2, g0, g1, g2, l1, l2, l3, l4,
        copy_sems, halo_send, halo_recv, chan_send, chan_recv, seq_send, seq_recv, *sum_sems,
    ) = refs[9 + 11 :]
    small_h, refs = refs[9 : 9 + 11], refs[:9]
    x_h, g_h, wk_h, wv_h, wr_h, wo_h, wfk_h, wfv_h, wfr_h = refs
    gain1_ref, bias1_ref, sk_ref, sv_ref, sr_ref, gain2_ref, bias2_ref, fk_ref, fr_ref = [line.at[i] for i in range(9)]
    rows, width = x_h.shape
    blocks = width // LANES
    chans = lax.axis_size("chan")
    seq, chan = lax.axis_index("seq"), lax.axis_index("chan")
    first = chan * rows
    total = rows * chans
    hops = adj_in.shape[0]
    tiles = rows // TILE
    step = 256
    quarter = width // 4

    grads = {"fv": lambda: gfv_h}
    outs = {"fv": (ofv, slice(None))}
    for i in range(4):
        grads[f"fk{i}"], outs[f"fk{i}"] = view(gfk_h, i), (ofk, columns(i))
    names = ("fr", "wo", "wr", "wv", "wk")
    for i, (name, out) in enumerate(zip(names, (ofr, owo, owr, owv, owk))):
        grads[name], outs[name] = view(gw_h, i), (out, slice(None))
    summing = Summing(
        grads, received, outs, (s0, s1, s2), (g0, g1, g2), (l1, l2, l3, l4), sum_sems
    )
    pump = summing.pump
    copies = Copies(copy_sems)
    start, wait = copies.start, copies.wait

    def row_tiles(body, lo=0, hi=tiles, size=TILE):
        @pl.loop(lo, hi)
        def _(i):
            at = pl.multiple_of(i * size, size)
            body(at, pl.ds(at, size))

    def col(j):
        return slice(j * step, (j + 1) * step)

    def spread(ref, here, to=width):
        return wide(ref[here], to)

    def hand(source, target, number, offset):
        return lambda: pltpu.make_async_remote_copy(
            src_ref=source() if callable(source) else source,
            dst_ref=target() if callable(target) else target,
            send_sem=halo_send.at[number],
            recv_sem=halo_recv.at[number],
            device_id=(seq, (chan + chans + offset) % chans),
            device_id_type=MESH,
        )

    hand_x = hand(view(x_h, pl.ds(rows - 16, 16)), xlast, 0, 1)
    hand_h2 = hand(mine2, halo2, 1, 1)
    hand_b2 = hand(mineb2, halob2, 2, -1)
    hand_b1 = hand(mine1, halo1, 3, -1)
    hand_st = [hand(st_mine, view(st_in, h), 4 + h, h + 1) for h in range(hops)]
    hand_adj = [hand(adj_mine, view(adj_in, h), 4 + hops + h, -h - 1) for h in range(hops)]

    x, xk, xv, xr, k, v = b0, b1, b2, b3, b4, b5
    start("x", x_h, x)
    for i, small in enumerate(small_h):
        start(f"small {i}", small, view(line, i) if i < 9 else view(tall_line, i - 9))
    start("wk", wk_h, view(w_scr, 0))
    start("wv", wv_h, view(w_scr, 1))
    barrier = pltpu.get_barrier_semaphore()
    seqs = SEQ
    mates = [(seq, (chan + d) % chans) for d in range(1, chans)] + [((seq + d) % seqs, chan) for d in range(1, seqs)]
    for mate in mates:
        pl.semaphore_signal(barrier, inc=1, device_id=mate, device_id_type=MESH)

    wait(*(f"small {i}" for i in range(len(small_h))))
    rate = jnp.exp(tall_line[0])
    decay = jnp.exp(-rate)
    boost = tall_line[1]
    gain1, bias1, gain2, bias2 = gain1_ref[...], bias1_ref[...], gain2_ref[...], bias2_ref[...]
    sums[...] = jnp.zeros_like(sums)
    wsums[...] = jnp.zeros_like(wsums)
    first_start = first_start_from(spans, first, 1 << 20) - first
    last_start = last_start_before(spans, first + rows) - first
    before = last_start_before(spans, first)
    after = first_start_from(spans, first + rows, total)

    def marks_tile(at, here):
        begins, real = marks(first + at, TILE, spans, pads)
        keep_scr[here] = 1.0 - begins.astype(F32)
        real_scr[here] = real.astype(F32)

    row_tiles(marks_tile)
    pl.semaphore_wait(barrier, len(mates))
    hand_x().start()
    wait("x")

    def norm1_of(at, here):
        hat, _ = normalized(x[here].astype(F32))
        h_scr[pl.ds(at + 8, BIG)] = hat * gain1 + bias1

    row_tiles(norm1_of, 0, rows // BIG, BIG)

    def halo1_rows():
        h_scr[0:8] = normalized(xlast[8:16].astype(F32))[0] * gain1 + bias1

    def mixed(at, here, shares):
        keep = spread(keep_scr, here)
        h, p = with_previous(h_scr, at)
        p = p * keep
        for share_ref, out in shares:
            share = share_ref[...]
            out[here] = (h * share + p * (1.0 - share)).astype(BF16)

    mix1 = functools.partial(mixed, shares=((sk_ref, xk), (sv_ref, xv), (sr_ref, xr)))
    row_tiles(mix1, 1)
    hand_x().wait_recv()
    halo1_rows()
    row_tiles(mix1, 0, 1)

    def wkv_at(at, j, at_scr, bt_scr):
        here = (pl.ds(at, TILE), columns(j))
        return wkv_parts(
            at, j, TILE, blocks, k[here].astype(F32), v[here].astype(F32), at_scr, bt_scr, in_scr[0], in_scr[1],
            rate, boost, first_start,
        )

    def forward(at_scr, bt_scr, ev_scr, ek_scr):
        wait("wk")
        for j in range(width // step):
            k[:, col(j)] = dot(xk[...], w_scr[0, :, col(j)]).astype(BF16)
        start("wr", wr_h, view(w_scr, 0))
        wait("wv")
        for j in range(width // step):
            v[:, col(j)] = dot(xv[...], w_scr[1, :, col(j)]).astype(BF16)
        start("wo", wo_h, view(w_scr, 1))

        def weights_tile(at, here):
            real = real_scr[here]
            for j in range(blocks):
                there = pl.ds(at * blocks + j, TILE, stride=blocks)
                ek = jnp.exp(k[here, columns(j)].astype(F32)) * real
                ek_scr[there] = ek
                ev_scr[there] = ek * v[here, columns(j)].astype(F32)

        row_tiles(weights_tile)

        def scan(t8, carry):
            a, b = carry
            for u in range(8):
                t = t8 * 8 + u
                keep = keep_scr[pl.ds(t, 1)]
                here = pl.ds(pl.multiple_of(t * blocks, blocks), blocks)
                fade = decay * keep
                at_scr[here] = a * keep
                bt_scr[here] = b * keep
                a = a * fade + ev_scr[here]
                b = b * fade + ek_scr[here]
            return a, b

        zero = jnp.zeros((blocks, LANES), F32)
        st_mine[0], st_mine[1] = lax.fori_loop(0, rows // 8, scan, (zero, zero))
        for copy in hand_st:
            copy().start()
        start("xk out", xk, view(spill_b, 0))
        start("xv out", xv, view(spill_b, 1))
        start("xr out", xr, view(spill_b, 2))
        r = d_scr
        wait("wr")
        for j in range(width // step):
            r[:, col(j)] = dot(xr[...], w_scr[0, :, col(j)])
        start("wfr", wfr_h, view(w_scr, 0))
        start("r out", r, spill_r)
        for copy in hand_st:
            copy().wait_recv()
        a_in, b_in = st_in[0, 0], st_in[0, 1]
        for h in range(1, hops):
            scale = jnp.exp(-rate * float(rows * h)) * jnp.where(before < first - h * rows, 1.0, 0.0)
            a_in, b_in = a_in + scale * st_in[h, 0], b_in + scale * st_in[h, 1]
        in_scr[0], in_scr[1] = a_in, b_in
        wkv, gated = b6, b7

        def outputs_tile(at, here):
            for j in range(blocks):
                a, b, _, _, out = wkv_at(at, j, at_scr, bt_scr)
                there = pl.ds(at * blocks + j, TILE, stride=blocks)
                at_scr[there] = a
                bt_scr[there] = b
                out = out.astype(BF16)
                wkv[here, columns(j)] = out
                gated[here, columns(j)] = (jax.nn.sigmoid(r[here, columns(j)]) * out.astype(F32)).astype(BF16)

        row_tiles(outputs_tile)
        start("at out", at_scr, view(spill_t, 0))
        start("bt out", bt_scr, view(spill_t, 1))
        start("k out", k, view(spill_b, 3))
        start("v out", v, view(spill_b, 4))
        start("wkv out", wkv, view(spill_b, 5))
        start("gated out", gated, view(spill_b, 6))
        wait("wo")
        for tail in (pl.ds(rows - 16, 16), pl.ds(0, rows)):
            for j in range(width // step):
                mid[tail, col(j)] = x[tail, col(j)].astype(F32) + dot(gated[tail], w_scr[1, :, col(j)])
            if tail.size == 16:
                mine2[...] = normalized(mid[rows - 8 : rows])[0] * gain2 + bias2
                hand_h2().start()
        wait("at out", "bt out")
        pump(11.0)

    tall = pltpu.VMEM((rows * blocks, LANES), F32)
    pl.run_scoped(forward, tall, tall, tall, tall)

    def ffn(wk_scr, wv_scr, ckt_scr, fv_tile, fk_tile):
        def load_unit(index):
            unit, slot = UNITS[index], index % 2
            for s in range(4):
                at = s * (wfk_h.shape[1] // 4) + unit * LANES
                start(f"wfk{index} {s}", view(wfk_h, slice(None), pl.ds(at, LANES)), view(wk_scr, slot, slice(None), columns(s)))
                start(f"wfv{index} {s}", view(wfv_h, pl.ds(at, LANES)), view(wv_scr, slot, columns(s)))

        load_unit(0)
        load_unit(1)
        g, ck, cr, dvo = b0, b1, b2, b3
        start("g", g_h, g)

        def norm2_of(at, here):
            hat, _ = normalized(mid[here])
            h_scr[pl.ds(at + 8, BIG)] = hat * gain2 + bias2

        row_tiles(norm2_of, 0, rows // BIG, BIG)
        wait("xk out", "xv out", "xr out")
        mix2 = functools.partial(mixed, shares=((fk_ref, ck), (fr_ref, cr)))
        row_tiles(mix2, 1)
        hand_h2().wait_recv()
        h_scr[0:8] = halo2[...]
        row_tiles(mix2, 0, 1)
        ckt_scr[...] = ck[...].T
        sig, dck = d_scr, dh
        wait("wfr", "r out", "g")
        real = spread(real_scr, slice(None), step)
        for j in range(width // step):
            s = jax.nn.sigmoid(dot(cr[...], w_scr[0, :, col(j)]))
            sig[:, col(j)] = s
            dvo[:, col(j)] = (g[:, col(j)].astype(F32) * real * s).astype(BF16)
        pump(7.0)
        for index, unit in enumerate(UNITS):
            slot = index % 2
            for s in range(4):
                wait(f"wfk{index} {s}", f"wfv{index} {s}")
            act = jnp.maximum(dot(ck[...], wk_scr[slot]), 0.0)
            hidden = (act * act).astype(BF16)
            fv = t_dot(hidden, dvo[...]).astype(BF16)
            if index:
                for s in range(4):
                    wait(f"fv{index - 1} {s}")
            fv_tile[...] = fv.reshape(4, LANES, width)
            for s in range(4):
                start(f"fv{index} {s}", view(fv_tile, s), view(gfv_h, s // 2, s % 2, pl.ds(unit * LANES, LANES)))
            pump(1.6)
            d_pre = (dot_t(dvo[...], wv_scr[slot]) * (2.0 * act)).astype(BF16)
            fk = dot(ckt_scr[...], d_pre).astype(BF16)
            for s in range(4):
                wait(f"fv{index} {s}")
            summing.complete(f"fv{unit}")
            if index:
                for s in range(4):
                    wait(f"fk{index - 1} {s}")
            fk_tile[...] = fk.reshape(2, 2, quarter, 4 * LANES)
            for s in range(4):
                at = columns(2 * s + unit // 4)
                start(f"fk{index} {s}", view(fk_tile, slice(None), slice(None), slice(None), columns(s)), view(gfk_h, unit % 4, slice(None), slice(None), slice(None), at))
            pump(1.3)
            if index:
                pass_scr[0:rows] += dot(hidden, wv_scr[slot])
                dck[...] += dot_t(d_pre, wk_scr[slot])
            else:
                pass_scr[0:rows] = dot(hidden, wv_scr[slot])
                dck[...] = dot_t(d_pre, wk_scr[slot])
            if index + 2 < len(UNITS):
                load_unit(index + 2)
            if index % 2:
                for s in range(4):
                    wait(f"fk{index} {s}")
                summing.complete(f"fk{unit % 4}")
            pump(1.2)
        dgp = dvo
        wait("k out")
        block_out = b4
        for j in range(width // step):
            s, value = sig[:, col(j)], pass_scr[0:rows, col(j)]
            block_out[:, col(j)] = (mid[:, col(j)] + s * value).astype(BF16)
            top = g[:, col(j)].astype(F32) * real
            dgp[:, col(j)] = (top * value * s * (1.0 - s)).astype(BF16)
        start("block out", block_out, out_h)
        pump(1.3)
        write_grad(0, "fr", cr, dgp)
        dcr = pass_scr
        for j in range(width // step):
            dcr[0:rows, col(j)] = dot_t(dgp[...], w_scr[0, col(j)])
        start("wo again", wo_h, view(w_scr, 0))
        pump(1.4)

    written = []

    def write_grad(index, name, left, right):
        for j in range(width // step):
            slot = j % 2
            if j >= 2:
                wait(*written[-2])
            tile_scr[slot] = t_dot(left[...], right[:, col(j)]).astype(BF16).reshape(2, 2, quarter, step)
            written.append((f"{name} tile {j}",))
            start(written[-1][0], view(tile_scr, slot), view(gw_h, index, slice(None), slice(None), slice(None), col(j)))
            pump(0.4)
        wait(*written[-1], *written[-2])
        summing.complete(name)

    half = pltpu.VMEM((rows, width), BF16)
    pl.run_scoped(
        ffn,
        pltpu.VMEM((2, width, 4 * LANES), BF16),
        pltpu.VMEM((2, 4 * LANES, width), BF16),
        pltpu.VMEM((width, rows), BF16),
        pltpu.VMEM((4, LANES, width), BF16),
        pltpu.VMEM((2, 2, quarter, 4 * LANES), BF16),
    )

    def last_row(halo):
        row = lax.broadcasted_iota(jnp.int32, halo.shape, 0)
        return jnp.where(row == 7, pltpu.roll(halo[...], 7, axis=0), 0.0)

    def attention_back(at_scr, bt_scr, dn_scr, dd_scr):
        g, gated, wkv, datt, dr = b0, b1, b2, b5, b7
        wait("block out", "v out", "gated out", "wkv out")
        start("at", view(spill_t, 0), at_scr)
        start("bt", view(spill_t, 1), bt_scr)
        start("gated", view(spill_b, 6), gated)
        start("wkv", view(spill_b, 5), wkv)
        start("k", view(spill_b, 3), b3)
        start("wr again", wr_h, view(w_scr, 1))
        start("v", view(spill_b, 4), b4)
        k, v = b3, b4
        share_k, share_r = fk_ref[...], fr_ref[...]

        def mix2_back(at, here):
            keep = spread(keep_scr, here)
            h, p = with_previous(h_scr, at)
            diff = h - p * keep
            dck, dcr = dh[here], pass_scr[here]
            sums[7] += fold8(diff * dck)
            sums[8] += fold8(diff * dcr)
            pass_scr[here] = (dck * (1.0 - share_k) + dcr * (1.0 - share_r)) * keep
            dh[here] = dck * share_k + dcr * share_r

        row_tiles(mix2_back, 0, 1)
        mineb2[...] = pass_scr[0:8]
        hand_b2().start()
        row_tiles(mix2_back, 1)
        pass_scr[rows : rows + 8] = jnp.zeros((8, width), F32)
        start("r", spill_r, view(h_scr, slice(0, rows)))
        pump(1.6)

        def norm2_back(at, here, extra=None):
            hat, inv = normalized(mid[here])
            d = dh[here] + pass_scr[pl.ds(at, BIG + 8)][1 : BIG + 1]
            if extra is not None:
                d = d + extra
            sums[0] += fold8(d * hat)
            sums[1] += fold8(d)
            d_mid = norm_back(d * gain2, hat, inv) + g[here].astype(F32) * spread(real_scr, here)
            mid[here] = d_mid
            datt[here] = d_mid.astype(BF16)

        def tail_of(halo):
            return jnp.concatenate([jnp.zeros((BIG - 8, width), F32), last_row(halo)], axis=0)

        row_tiles(norm2_back, 0, rows // BIG - 1, BIG)
        pump(1.0)
        hand_b2().wait_recv()
        norm2_back(rows - BIG, slice(rows - BIG, rows), tail_of(halob2))
        dmid = mid
        start("x again", x_h, b0)

        wait("wo again")
        for j in range(width // step):
            d_scr[:, col(j)] = dot_t(datt[...], w_scr[0, col(j)])
        start("wv again", wv_h, view(w_scr, 0))
        pump(2.4)
        wait("r", "wkv", "k", "v", "at", "bt")

        def gate_tile(at, rows_here):
            for j in range(blocks):
                here = (rows_here, columns(j))
                there = pl.ds(at * blocks + j, TILE, stride=blocks)
                sig = jax.nn.sigmoid(h_scr[here])
                dg = d_scr[here]
                dw = (dg * sig).astype(BF16)
                dr[here] = (dg * wkv[here].astype(F32) * sig * (1.0 - sig)).astype(BF16)
                vv = v[here].astype(F32)
                eu = jnp.exp(boost[j : j + 1] + k[here].astype(F32))
                inv = 1.0 / (bt_scr[there] + eu)
                out = (at_scr[there] + eu * vv) * inv
                dn = dw.astype(F32) * inv
                dn_scr[there] = dn
                dd_scr[there] = -dn * out
                own = eu * dn
                d_scr[here] = own
                h_scr[here] = own * (vv - out)

        for part in range(4):
            row_tiles(gate_tile, part * tiles // 4, (part + 1) * tiles // 4)
            pump(0.5)
        start("xv", view(spill_b, 1), wkv)

        def scan(t8, carry):
            a, b = carry
            for u in range(8):
                t = rows - 1 - (t8 * 8 + u)
                keep = keep_scr[pl.ds(t, 1)]
                here = pl.ds(pl.multiple_of(t * blocks, blocks), blocks)
                dn, dd = dn_scr[here], dd_scr[here]
                dn_scr[here] = a
                dd_scr[here] = b
                fade = decay * keep
                a = a * fade + dn * keep
                b = b * fade + dd * keep
            return a, b

        zero = jnp.zeros((blocks, LANES), F32)
        carry = lax.fori_loop(0, rows // 16, scan, (zero, zero))
        pump(1.2)
        adj_mine[0], adj_mine[1] = lax.fori_loop(rows // 16, rows // 8, scan, carry)
        for copy in hand_adj:
            copy().start()
        pump(1.2)

        wait("gated")
        write_grad(1, "wo", gated, datt)
        start("xk", view(spill_b, 0), gated)
        start("xr", view(spill_b, 2), datt)
        xk, xv, xr = gated, wkv, datt

        wait("xr")
        write_grad(2, "wr", xr, dr)

        for copy in hand_adj:
            copy().wait_recv()
        adj_a, adj_b = adj_in[0, 0], adj_in[0, 1]
        for h in range(1, hops):
            scale = jnp.exp(-rate * float(rows * h)) * jnp.where(after >= first + (h + 1) * rows, 1.0, 0.0)
            adj_a, adj_b = adj_a + scale * adj_in[h, 0], adj_b + scale * adj_in[h, 1]

        def recur_tile(at, rows_here):
            real = real_scr[rows_here]
            pos = at + lax.broadcasted_iota(jnp.int32, (TILE, LANES), 0)
            for j in range(blocks):
                here = (rows_here, columns(j))
                there = pl.ds(at * blocks + j, TILE, stride=blocks)
                lift = jnp.where(pos >= last_start, jnp.exp(-rate[j : j + 1] * (rows - 1 - pos).astype(F32)), 0.0)
                post_a = dn_scr[there] + lift * adj_a[j : j + 1]
                post_b = dd_scr[there] + lift * adj_b[j : j + 1]
                own_k = h_scr[here]
                weight = jnp.exp(k[here].astype(F32)) * real
                vv = v[here].astype(F32)
                v[here] = (d_scr[here] + weight * post_a).astype(BF16)
                k[here] = (own_k + weight * (vv * post_a + post_b)).astype(BF16)
                wsums[0, :, columns(j)] += fold8(at_scr[there] * post_a + bt_scr[there] * post_b)
                wsums[1, :, columns(j)] += fold8(own_k)

        for part in range(4):
            row_tiles(recur_tile, part * tiles // 4, (part + 1) * tiles // 4)
            pump(1.05)
        for j in range(blocks):
            rr = rate[j : j + 1]
            wsums[0, :, columns(j)] *= -rr * jnp.exp(-rr)
        dk, dv = k, v
        halo1_rows()
        wait("x again")
        row_tiles(norm1_of, 0, rows // BIG, BIG)
        pump(0.8)
        wait("xv")
        write_grad(3, "wv", xv, dv)
        wait("xk")
        write_grad(4, "wk", xk, dk)

        def mix1_back(grad, weight, share_ref, index, fresh):
            for j in range(width // step):
                d_scr[:, col(j)] = dot_t(grad[...], weight[col(j)])
            pump(1.4)
            share = share_ref[...]

            def tile(at, here):
                h, p = with_previous(h_scr, at)
                d = d_scr[here]
                keep = spread(keep_scr, here)
                sums[index] += fold8((h - p * keep) * d)
                passed = d * (1.0 - share) * keep
                if fresh:
                    pass_scr[here] = passed
                    dh[here] = d * share
                else:
                    pass_scr[here] += passed
                    dh[here] += d * share

            row_tiles(tile)
            pump(1.0)

        wait("wr again")
        mix1_back(dr, w_scr.at[1], sr_ref, 4, True)
        start("wk again", wk_h, view(w_scr, 1))
        wait("wv again")
        mix1_back(dv, w_scr.at[0], sv_ref, 3, False)
        wait("wk again")
        mix1_back(dk, w_scr.at[1], sk_ref, 2, False)
        mine1[...] = pass_scr[0:8]
        hand_b1().start()
        x, grad_in = b0, b6

        def norm1_back(at, here, extra=None):
            d = dh[here] + pass_scr[pl.ds(at, BIG + 8)][1 : BIG + 1]
            if extra is not None:
                d = d + extra
            hat, inv = normalized(x[here].astype(F32))
            sums[5] += fold8(d * hat)
            sums[6] += fold8(d)
            grad_in[here] = (norm_back(d * gain1, hat, inv) + dmid[here]).astype(BF16)

        row_tiles(norm1_back, 0, rows // BIG - 1, BIG)
        pump(1.0)
        hand_b1().wait_recv()
        norm1_back(rows - BIG, slice(rows - BIG, rows), tail_of(halo1))
        start("grad in", grad_in, gin_h)

    pl.run_scoped(attention_back, tall, tall, tall, tall)
    parts = [sums[i] for i in (5, 6, 2, 3, 4)] + [wsums[0], wsums[1]] + [sums[i] for i in (0, 1, 7, 8)]
    lines = [jnp.sum(p, axis=0, keepdims=True) for p in parts]
    lines.append(jnp.zeros((16 - len(lines), width), F32))
    vec_scr[...] = jnp.concatenate(lines, axis=0)

    def to_chan(d):
        return pltpu.make_async_remote_copy(
            src_ref=vec_scr.at[:, pl.ds(pl.multiple_of((chan + d) % chans * LANES, LANES), LANES)],
            dst_ref=vec_chan.at[d],
            send_sem=chan_send.at[d],
            recv_sem=chan_recv.at[d],
            device_id=(seq, (chan + d) % chans),
            device_id_type=MESH,
        )

    def to_seq(d):
        return pltpu.make_async_remote_copy(
            src_ref=vec_mine,
            dst_ref=vec_seq.at[d],
            send_sem=seq_send.at[d],
            recv_sem=seq_recv.at[d],
            device_id=((seq + d) % seqs, chan),
            device_id_type=MESH,
        )

    for d in range(1, chans):
        to_chan(d).start()
    pump(4.0)
    vec = vec_scr[:, pl.ds(pl.multiple_of(chan * LANES, LANES), LANES)]
    for d in range(1, chans):
        to_chan(d).wait_recv()
        vec = vec + vec_chan[d]
    vec_mine[...] = vec
    for d in range(1, seqs):
        to_seq(d).start()
    pump(3.0)
    for d in range(1, seqs):
        to_seq(d).wait_recv()
        vec = vec + vec_seq[d]
    ovec[...] = vec
    start("vec", ovec, ovec_h)
    for d in range(1, chans):
        to_chan(d).wait_send()
    for d in range(1, seqs):
        to_seq(d).wait_send()
    summing.drain()
    results = ((ofv, ofv_h), (ofk, ofk_h), (ofr, ofr_h), (owo, owo_h), (owr, owr_h), (owv, owv_h), (owk, owk_h))
    for i, (source, target) in enumerate(results):
        start(f"result {i}", source, target)
    summing.finish()
    copies.finish()
    for copy in (hand_x, hand_h2, hand_b2, hand_b1, *hand_st, *hand_adj):
        copy().wait_send()


def block(x, g, weights, vectors, rates, spans, pads, hops):
    rows, width = x.shape
    blocks = width // LANES
    quarter = width // 4
    hid = weights[4].shape[1]
    fv_rows = hid // 4
    block_rows = fv_rows + 4 * quarter + 5 * quarter
    half = pltpu.VMEM((rows, width), BF16)
    flat, flat8 = pltpu.VMEM((rows, width), F32), pltpu.VMEM((rows + 8, width), F32)
    eight = pltpu.VMEM((8, width), F32)
    state = pltpu.VMEM((2, blocks, LANES), F32)
    states = pltpu.VMEM((hops, 2, blocks, LANES), F32)
    lanes = [MOST[lane] for lane in LANES_OF]
    outs = [(fv_rows, LANES), (quarter, 4 * LANES)] + [(quarter, LANES)] * 5 + [(16, LANES)]
    result = pl.pallas_call(
        block_kernel,
        out_shape=[sds((rows, width), BF16)] * 2
        + [sds(shape, F32) for shape in outs]
        + [
            sds((2, block_rows, width), BF16),
            sds((5, 2, 2, quarter, width), BF16),
            sds((2, 2, fv_rows, width), BF16),
            sds((4, 2, 2, quarter, width), BF16),
            sds((7, rows, width), BF16),
            sds((rows, width), F32),
            sds((2, rows * blocks, LANES), F32),
        ],
        in_specs=[ANY] * 20 + [SMEM] * 2,
        out_specs=[ANY] * 17,
        scratch_shapes=[flat, flat, flat8, flat, flat8]
        + [half] * 8
        + [
            pltpu.VMEM((2, width, width), BF16),
            pltpu.VMEM((2, 2, 2, quarter, 256), BF16),
            pltpu.VMEM((16, width), F32),
            pltpu.VMEM((CHAN, 16, LANES), F32),
            pltpu.VMEM((16, LANES), F32),
            pltpu.VMEM((SEQ, 16, LANES), F32),
            pltpu.VMEM((rows, LANES), F32),
            pltpu.VMEM((rows, LANES), F32),
            pltpu.VMEM((16, width), BF16),
        ]
        + [eight] * 6
        + [state, states, state, states, state]
        + [pltpu.VMEM((9, 1, width), F32), pltpu.VMEM((2, blocks, LANES), F32)]
        + [pltpu.VMEM(shape, F32) for shape in outs]
        + [pltpu.VMEM((9, 8, width), F32), pltpu.VMEM((2, 8, width), F32)]
        + [pltpu.VMEM((2, 2, most, width), BF16) for most in lanes]
        + [pltpu.VMEM((RING, 16 * most, LANES), BF16) for most in lanes]
        + [pltpu.VMEM((block_rows << (3 - d), LANES), BF16) for d in range(4)]
        + [
            pltpu.SemaphoreType.DMA((48,)),
            pltpu.SemaphoreType.DMA((4 + 2 * hops,)),
            pltpu.SemaphoreType.DMA((4 + 2 * hops,)),
            pltpu.SemaphoreType.DMA((CHAN,)),
            pltpu.SemaphoreType.DMA((CHAN,)),
            pltpu.SemaphoreType.DMA((SEQ,)),
            pltpu.SemaphoreType.DMA((SEQ,)),
            pltpu.SemaphoreType.DMA(()),
            pltpu.SemaphoreType.DMA((len(lanes), RING)),
            pltpu.SemaphoreType.DMA((3,)),
            pltpu.SemaphoreType.DMA((len(CHUNKS),)),
            pltpu.SemaphoreType.DMA((len(lanes), TURNS, STEPS - 1)),
            pltpu.SemaphoreType.DMA((len(lanes), 2)),
        ],
        compiler_params=pltpu.CompilerParams(
            vmem_limit_bytes=63 * MIB, collective_id=0, has_side_effects=True
        ),
        name="block",
    )(x, g, *weights, *vectors, *rates, spans, pads)
    return result[:10]


def finish_kernel(count, lines, *refs):
    sources, targets, held = refs[: count + 1], refs[count + 1 : 2 * count + 1 + lines], refs[2 * count + 1 + lines : -2]
    sems = refs[-2:]
    arrive = [pltpu.make_async_copy(s, h, sems[0].at[i]) for i, (s, h) in enumerate(zip(sources, held))]
    leave = [pltpu.make_async_copy(h, t, sems[1].at[i]) for i, (h, t) in enumerate(zip(held[:count], targets))]
    for copy in arrive[::-1]:
        copy.start()
    arrive[count].wait()
    for i in range(lines):
        targets[count + i][...] = held[count][i]
    for there, back in zip(arrive, leave):
        there.wait()
        back.start()
    for copy in leave:
        copy.wait()


def finish(arrays, vec, lines):
    count = len(arrays)
    return pl.pallas_call(
        functools.partial(finish_kernel, count, lines),
        out_shape=[sds(a.shape, a.dtype) for a in arrays] + [sds(vec.shape[1:], vec.dtype)] * lines,
        in_specs=[ANY] * (count + 1),
        out_specs=[ANY] * count + [VMEM] * lines,
        scratch_shapes=[pltpu.VMEM(a.shape, a.dtype) for a in (*arrays, vec)]
        + [pltpu.SemaphoreType.DMA((count + 1,))] * 2,
        compiler_params=params(62),
        name="finish",
    )(*arrays, vec)


def shift(value, steps):
    count = lax.axis_size("chan")
    pairs = [(i, i + steps) for i in range(count) if 0 <= i + steps < count]
    return lax.ppermute(value, "chan", pairs)


def scatter_sums(mats, vecs):
    def both(m):
        m = lax.psum_scatter(m, "chan", scatter_dimension=1, tiled=True)
        return lax.psum_scatter(m, "seq", scatter_dimension=0, tiled=True).astype(F32)

    v = lax.psum_scatter(vecs.astype(BF16), "chan", scatter_dimension=1, tiled=True).astype(F32)
    return [both(m) for m in mats], lax.psum(v, "seq")


def per_device(
    x, g, gain1, bias1, share_k, share_v, share_r, log_rate, boost, wk, wv, wr, wo, gain2, bias2, share_fk, share_fr,
    wfk, wfv, wfr, spans, pads,
):
    rows, width = x.shape
    chans = lax.axis_size("chan")
    total = rows * chans
    hops = max(1, min(chans - 1, total // 4 // rows))
    if (lax.axis_size("seq"), chans, wfk.shape[1] // chans, width) == (4, 8, 4 * LANES, 8 * LANES):
        line = lambda v: v.reshape(1, width)
        tall = lambda v: v.reshape(width // LANES, LANES)
        vectors = [line(v) for v in (gain1, bias1, share_k, share_v, share_r, gain2, bias2, share_fk, share_fr)]
        weights = (wk, wv, wr, wo, wfk, wfv, wfr)
        results = block(x, g, weights, vectors, (tall(log_rate), tall(boost)), spans, pads, hops)
        block_out, grad_in, gfv, gfk, gfr, gwo, gwr, gwv, gwk, *vec = finish(results[:-1], results[-1], 11)
        return (block_out, grad_in, *[vec[i] for i in range(7)], gwk, gwv, gwr, gwo, *[vec[i] for i in range(7, 11)], gfk, gfv, gfr)
    base = lambda: lax.axis_index("chan") * rows
    vecs = jnp.stack([gain1, bias1, share_k, share_v, share_r, gain2, bias2, share_fk, share_fr])
    rates = jnp.stack([log_rate, boost]).reshape(2 * width // LANES, LANES)
    begins = jnp.cumsum(spans[0]) - spans[0]
    pos = base() + jnp.arange(rows, dtype=jnp.int32)
    keep = 1.0 - jnp.any(pos[:, None] == begins[None, :], axis=1).astype(F32)

    xprev = shift(jnp.broadcast_to(x[rows - 1 :], (16, width)), 1)[:8]
    xk, xv, xr, k, v, r, at, bt, end = project(base, x, xprev, vecs, rates, spans, pads, keep, wk, wv, wr)
    carry = jnp.concatenate([shift(end, h + 1) for h in range(hops)], axis=0)
    wkv, gated, middle, last, carried = exit_call(base, hops, x, k, v, r, at, bt, carry, rates, vecs, spans, wo)
    hprev = jnp.broadcast_to(shift(last[7:], 1), (8, width))
    block_out, gfk, gfv, gfr, dh2, back2, sums2 = ffn(base, middle, g, hprev, vecs, spans, pads, wfr, wfk, wfv)
    dh2next = shift(back2, -1)
    dmid, gwo, dwkv, dr, sumsn2, adja, adjb, adjend = exit_back(
        base, middle, g, dh2, dh2next, vecs, rates, gated, wkv, r, k, v, at, bt, carried, spans, pads, keep, wo
    )
    adj = jnp.concatenate([shift(adjend, -h - 1) for h in range(hops)], axis=0)
    gwk, gwv, gwr, dh1, back1, sums1, wsums = project_back(
        base, hops, total, x, xprev, vecs, rates, k, v, dwkv, dr, at, bt, carried, adja, adjb, adj, xk, xv, xr, spans,
        pads, wk, wv, wr,
    )
    grad_in, sumsn1 = entry_back(x, dh1, shift(back1, -1), dmid, vecs)
    vec_parts = jnp.concatenate([sumsn1, sums1, wsums, sumsn2, sums2], axis=0).sum(axis=1)
    (gwk, gwv, gwr, gwo, gfk, gfv, gfr), vec = scatter_sums((gwk, gwv, gwr, gwo, gfk, gfv, gfr), vec_parts)
    return (block_out, grad_in, *[vec[i] for i in range(7)], gwk, gwv, gwr, gwo, *[vec[i] for i in range(7, 11)], gfk, gfv, gfr)


def solution(mesh):
    tokens, chan, both = P(("seq", "chan"), None), P("chan"), P("seq", "chan")
    placed = (tokens, tokens) + (P(),) * 18 + (P("seq", None),) * 2
    return jax.shard_map(
        per_device,
        mesh=mesh,
        in_specs=placed,
        out_specs=(tokens, tokens) + (chan,) * 7 + (both,) * 4 + (chan,) * 4 + (both,) * 3,
        check_vma=False,
    )
```

```python
import functools

import jax
import jax.numpy as jnp
from jax import lax
from jax.experimental import pallas as pl
from jax.experimental.pallas import tpu as pltpu
from jax.sharding import PartitionSpec as P

F32, BF16 = jnp.float32, jnp.bfloat16
LANES = 128
TILE = 64
MIB = 1 << 20
VMEM = pl.BlockSpec(memory_space=pltpu.VMEM)
SMEM = pl.BlockSpec(memory_space=pltpu.SMEM)
ANY = pl.BlockSpec(memory_space=pl.ANY)
G1, B1, SK, SV, SR, G2, B2, FK, FR = range(9)


def sds(shape, dtype):
    return jax.ShapeDtypeStruct(shape, dtype)


def params(limit_mib):
    return pltpu.CompilerParams(vmem_limit_bytes=limit_mib * MIB)


def dot(a, b):
    return jnp.dot(a, b, preferred_element_type=F32)


def dot_t(a, b):
    return lax.dot_general(a, b, (((1,), (1,)), ((), ())), preferred_element_type=F32)


def t_dot(a, b):
    return lax.dot_general(a, b, (((0,), (0,)), ((), ())), preferred_element_type=F32)


def fold8(v):
    return jnp.sum(v.reshape(v.shape[0] // 8, 8, v.shape[1]), axis=0)


def normalized(v):
    center = v - jnp.mean(v, axis=-1, keepdims=True)
    inv = lax.rsqrt(jnp.mean(center * center, axis=-1, keepdims=True) + 1e-05)
    return center * inv, inv


def norm_back(d_hat, hat, inv):
    return inv * (
        d_hat
        - jnp.mean(d_hat, axis=-1, keepdims=True)
        - hat * jnp.mean(d_hat * hat, axis=-1, keepdims=True)
    )


def marks(first, rows, spans, pads):
    pos = first + lax.broadcasted_iota(jnp.int32, (rows, LANES), 0)
    begin = 0
    start, real = pos < 0, pos < 0
    for i in range(spans.shape[1]):
        length = spans[0, i]
        start = start | (pos == begin)
        real = real | ((pos >= begin) & (pos < begin + length - pads[0, i]))
        begin = begin + length
    return start, real


def first_start_from(spans, at, otherwise):
    begin, best = 0, otherwise
    for i in range(spans.shape[1]):
        best = jnp.where((begin >= at) & (begin < best), begin, best)
        begin = begin + spans[0, i]
    return best


def last_start_before(spans, at):
    begin, best = 0, -(1 << 20)
    for i in range(spans.shape[1]):
        best = jnp.where(begin < at, begin, best)
        begin = begin + spans[0, i]
    return best


def wide(flag, width):
    return jnp.concatenate([flag] * (width // LANES), axis=1)


def with_previous(ref, at):
    block = ref[pl.ds(at, TILE + 8)]
    return block[8:], block[7 : TILE + 7]


def columns(j):
    return slice(j * LANES, (j + 1) * LANES)


def gather_carry(hops, rows, carry_ref, counts, rate):
    a, b = carry_ref[0], carry_ref[1]
    for h in range(1, hops):
        scale = jnp.exp(-rate * float(rows * h)) * counts[h]
        a, b = a + scale * carry_ref[2 * h], b + scale * carry_ref[2 * h + 1]
    return a, b


def project_kernel(
    base, x_ref, xprev_ref, vec_ref, rate_ref, spans, pads, keep_s, wk_hbm, wv_hbm, wr_hbm,
    xk_ref, xv_ref, xr_ref, k_ref, v_ref, r_ref, at_ref, bt_ref, end_ref,
    h_scr, ek_scr, ev_scr, w_scr, sems,
):
    rows, width = x_ref.shape
    blocks = width // LANES
    copies = [
        pltpu.make_async_copy(hbm, w_scr.at[i], sems.at[i])
        for i, hbm in enumerate((wk_hbm, wv_hbm, wr_hbm))
    ]
    for copy in copies:
        copy.start()
    first = base()
    gain, bias = vec_ref[G1 : G1 + 1], vec_ref[B1 : B1 + 1]
    prev = xprev_ref[...].astype(F32)
    h_scr[0:8] = normalized(prev)[0] * gain + bias

    @pl.loop(0, rows // TILE)
    def _(i):
        at = pl.multiple_of(i * TILE, TILE)
        hat, _ = normalized(x_ref[pl.ds(at, TILE)].astype(F32))
        h_scr[pl.ds(at + 8, TILE)] = hat * gain + bias

    @pl.loop(0, rows // TILE)
    def _(i):
        at = pl.multiple_of(i * TILE, TILE)
        start, _ = marks(first + at, TILE, spans, pads)
        keep = wide(1.0 - start.astype(F32), width)
        h, p = with_previous(h_scr, at)
        p = p * keep
        for row, out in ((SK, xk_ref), (SV, xv_ref), (SR, xr_ref)):
            share = vec_ref[row : row + 1]
            out[pl.ds(at, TILE)] = (h * share + p * (1.0 - share)).astype(BF16)

    _, real = marks(first, rows, spans, pads)
    real = real.astype(F32)
    step = 256
    for i, (src, out) in enumerate(((xk_ref, k_ref), (xv_ref, v_ref), (xr_ref, r_ref))):
        copies[i].wait()
        for j in range(width // step):
            tile = dot(src[...], w_scr[i, :, j * step : (j + 1) * step])
            out[:, j * step : (j + 1) * step] = tile.astype(out.dtype)
    for j in range(blocks):
        ek = jnp.exp(k_ref[:, columns(j)].astype(F32)) * real
        ek_scr[pl.ds(j, rows, stride=blocks)] = ek
        ev_scr[pl.ds(j, rows, stride=blocks)] = ek * v_ref[:, columns(j)].astype(F32)
    decay = jnp.exp(-jnp.exp(rate_ref[0:blocks]))

    def scan(t8, carry):
        a, b = carry
        for u in range(8):
            t = t8 * 8 + u
            keep = keep_s[t]
            here = pl.ds(pl.multiple_of(t * blocks, blocks), blocks)
            at_ref[here] = a * keep
            bt_ref[here] = b * keep
            fade = decay * keep
            a = a * fade + ev_scr[here]
            b = b * fade + ek_scr[here]
        return a, b

    zero = jnp.zeros((blocks, LANES), F32)
    a, b = lax.fori_loop(0, rows // 8, scan, (zero, zero))
    end_ref[0] = a
    end_ref[1] = b


def project(base, x, xprev, vecs, rates, spans, pads, keep, wk, wv, wr):
    rows, width = x.shape
    shape = (rows, width)
    tall = (rows * (width // LANES), LANES)
    return pl.pallas_call(
        functools.partial(project_kernel, base),
        out_shape=(
            [sds(shape, BF16)] * 5 + [sds(shape, F32)] + [sds(tall, F32)] * 2 + [sds((2, width // LANES, LANES), F32)]
        ),
        in_specs=[VMEM] * 4 + [SMEM] * 3 + [ANY] * 3,
        out_specs=[VMEM] * 9,
        scratch_shapes=[
            pltpu.VMEM((rows + 8, width), F32),
            pltpu.VMEM(tall, F32),
            pltpu.VMEM(tall, F32),
            pltpu.VMEM((3, width, width), BF16),
            pltpu.SemaphoreType.DMA((3,)),
        ],
        compiler_params=params(56),
        name="project",
    )(x, xprev, vecs, rates, spans, pads, keep, wk, wv, wr)


def wkv_parts(at, j, rows, blocks, k, v, at_ref, bt_ref, a_in, b_in, rate, boost, first_start):
    here = pl.ds(at * blocks + j, rows, stride=blocks)
    pos = at + lax.broadcasted_iota(jnp.int32, (rows, LANES), 0)
    lift = jnp.where(pos < first_start, jnp.exp(-rate[j : j + 1] * pos.astype(F32)), 0.0)
    a = at_ref[here] + lift * a_in[j : j + 1]
    b = bt_ref[here] + lift * b_in[j : j + 1]
    eu = jnp.exp(boost[j : j + 1] + k)
    inv = 1.0 / (b + eu)
    return a, b, eu, inv, (a + eu * v) * inv


def carry_counts(hops, rows, first, spans):
    last = last_start_before(spans, first)
    return [jnp.where(last < first - h * rows, 1.0, 0.0) for h in range(hops)]


def exit_kernel(
    base, hops, x_ref, k_ref, v_ref, r_ref, at_ref, bt_ref, carry_ref, rate_ref, vec_ref, spans, wo_hbm,
    wkv_ref, gated_ref, middle_ref, last_ref, in_ref, wo_scr, sem,
):
    rows, width = x_ref.shape
    blocks = width // LANES
    copy = pltpu.make_async_copy(wo_hbm, wo_scr, sem)
    copy.start()
    first = base()
    rate = jnp.exp(rate_ref[0:blocks])
    boost = rate_ref[blocks : 2 * blocks]
    a_in, b_in = gather_carry(hops, rows, carry_ref, carry_counts(hops, rows, first, spans), rate)
    in_ref[0] = a_in
    in_ref[1] = b_in
    first_start = first_start_from(spans, first, 1 << 20) - first

    @pl.loop(0, rows // TILE)
    def _(i):
        at = pl.multiple_of(i * TILE, TILE)
        for j in range(blocks):
            here = (pl.ds(at, TILE), columns(j))
            k, v = k_ref[here].astype(F32), v_ref[here].astype(F32)
            wkv = wkv_parts(at, j, TILE, blocks, k, v, at_ref, bt_ref, a_in, b_in, rate, boost, first_start)[-1]
            wkv = wkv.astype(BF16)
            wkv_ref[here] = wkv
            gated_ref[here] = (jax.nn.sigmoid(r_ref[here]) * wkv.astype(F32)).astype(BF16)

    copy.wait()
    step = 256
    for j in range(width // step):
        here = (slice(None), slice(j * step, (j + 1) * step))
        middle_ref[here] = x_ref[here].astype(F32) + dot(gated_ref[...], wo_scr[here])
    hat, _ = normalized(middle_ref[rows - 8 : rows])
    last_ref[...] = hat * vec_ref[G2 : G2 + 1] + vec_ref[B2 : B2 + 1]


def exit_call(base, hops, x, k, v, r, at, bt, carry, rates, vecs, spans, wo):
    rows, width = x.shape
    blocks = width // LANES
    return pl.pallas_call(
        functools.partial(exit_kernel, base, hops),
        out_shape=[
            sds((rows, width), BF16),
            sds((rows, width), BF16),
            sds((rows, width), F32),
            sds((8, width), F32),
            sds((2, blocks, LANES), F32),
        ],
        in_specs=[VMEM] * 9 + [SMEM, ANY],
        out_specs=[VMEM] * 5,
        scratch_shapes=[pltpu.VMEM((width, width), BF16), pltpu.SemaphoreType.DMA(())],
        compiler_params=params(56),
        name="exit",
    )(x, k, v, r, at, bt, carry, rates, vecs, spans, wo)


def ffn_kernel(
    base, mid_ref, g_ref, hprev_ref, vec_ref, spans, pads, wg_ref, wk_ref, wv_ref,
    out_ref, gfk_ref, gfv_ref, gfr_ref, dh_ref, back_ref, sums_ref,
    h_scr, ck_scr, cr_scr, ckt_scr, sig_scr, dvo_scr, val_scr, dck_scr, pass_scr,
):
    rows, width = mid_ref.shape
    step = pl.program_id(0)
    first = base()
    tiles = rows // TILE

    @pl.when(step == 0)
    def _():
        gain, bias = vec_ref[G2 : G2 + 1], vec_ref[B2 : B2 + 1]
        h_scr[0:8] = hprev_ref[...]

        @pl.loop(0, tiles)
        def _(i):
            at = pl.multiple_of(i * TILE, TILE)
            hat, _ = normalized(mid_ref[pl.ds(at, TILE)])
            h_scr[pl.ds(at + 8, TILE)] = hat * gain + bias

        @pl.loop(0, tiles)
        def _(i):
            at = pl.multiple_of(i * TILE, TILE)
            start, _ = marks(first + at, TILE, spans, pads)
            keep = wide(1.0 - start.astype(F32), width)
            h, p = with_previous(h_scr, at)
            p = p * keep
            for row, out in ((FK, ck_scr), (FR, cr_scr)):
                share = vec_ref[row : row + 1]
                out[pl.ds(at, TILE)] = (h * share + p * (1.0 - share)).astype(BF16)

        ckt_scr[...] = ck_scr[...].T
        _, real = marks(first, rows, spans, pads)
        real = wide(real.astype(F32), 256)
        for j in range(width // 256):
            here = (slice(None), slice(j * 256, (j + 1) * 256))
            sig = jax.nn.sigmoid(dot(cr_scr[...], wg_ref[here]))
            sig_scr[here] = sig
            dvo_scr[here] = (g_ref[here].astype(F32) * real * sig).astype(BF16)
        val_scr[...] = jnp.zeros_like(val_scr)
        dck_scr[...] = jnp.zeros_like(dck_scr)

    act = jnp.maximum(dot(ck_scr[...], wk_ref[...]), 0.0)
    hidden = (act * act).astype(BF16)
    val_scr[...] += dot(hidden, wv_ref[...])
    gfv_ref[...] = t_dot(hidden, dvo_scr[...]).astype(BF16)
    d_pre = (dot_t(dvo_scr[...], wv_ref[...]) * (2.0 * act)).astype(BF16)
    gfk_ref[...] = dot(ckt_scr[...], d_pre).astype(BF16)
    dck_scr[...] += dot_t(d_pre, wk_ref[...])

    @pl.when(step == pl.num_programs(0) - 1)
    def _():
        dgp_scr = dvo_scr
        _, real = marks(first, rows, spans, pads)
        real = wide(real.astype(F32), 256)
        for j in range(width // 256):
            here = (slice(None), slice(j * 256, (j + 1) * 256))
            sig, value = sig_scr[here], val_scr[here]
            out_ref[here] = (mid_ref[here] + sig * value).astype(BF16)
            top = g_ref[here].astype(F32) * real
            dgp_scr[here] = (top * value * sig * (1.0 - sig)).astype(BF16)
        for j in range(width // 256):
            here = (slice(None), slice(j * 256, (j + 1) * 256))
            gfr_ref[here] = t_dot(cr_scr[...], dgp_scr[here]).astype(BF16)
        dcr_scr = val_scr
        for j in range(width // 256):
            dcr_scr[:, j * 256 : (j + 1) * 256] = dot_t(dgp_scr[...], wg_ref[j * 256 : (j + 1) * 256])
        sums_ref[...] = jnp.zeros_like(sums_ref)
        share_k, share_r = vec_ref[FK : FK + 1], vec_ref[FR : FR + 1]

        @pl.loop(0, tiles)
        def _(i):
            at = pl.multiple_of(i * TILE, TILE)
            here = pl.ds(at, TILE)
            start, _ = marks(first + at, TILE, spans, pads)
            keep = wide(1.0 - start.astype(F32), width)
            h, p = with_previous(h_scr, at)
            diff = h - p * keep
            dck, dcr = dck_scr[here], dcr_scr[here]
            sums_ref[0] += fold8(diff * dck)
            sums_ref[1] += fold8(diff * dcr)
            pass_scr[here] = (dck * (1.0 - share_k) + dcr * (1.0 - share_r)) * keep
            dh_ref[here] = dck * share_k + dcr * share_r

        back_ref[...] = pass_scr[0:8]

        pass_scr[rows : rows + 8] = jnp.zeros((8, width), F32)

        @pl.loop(0, tiles)
        def _(i):
            at = pl.multiple_of(i * TILE, TILE)
            dh_ref[pl.ds(at, TILE)] += pass_scr[pl.ds(at, TILE + 8)][1 : TILE + 1]


def ffn(base, middle, g, hprev, vecs, spans, pads, wg, wk, wv):
    rows, width = middle.shape
    hid = wk.shape[1]
    unit = 512
    full = lambda shape: pl.BlockSpec(shape, lambda j: (0,) * len(shape))
    return pl.pallas_call(
        functools.partial(ffn_kernel, base),
        grid=(hid // unit,),
        out_shape=[
            sds((rows, width), BF16),
            sds((width, hid), BF16),
            sds((hid, width), BF16),
            sds((width, width), BF16),
            sds((rows, width), F32),
            sds((8, width), F32),
            sds((2, 8, width), F32),
        ],
        in_specs=[
            full((rows, width)),
            full((rows, width)),
            full((8, width)),
            full(vecs.shape),
            SMEM,
            SMEM,
            full((width, width)),
            pl.BlockSpec((width, unit), lambda j: (0, j)),
            pl.BlockSpec((unit, width), lambda j: (j, 0)),
        ],
        out_specs=[
            full((rows, width)),
            pl.BlockSpec((width, unit), lambda j: (0, j)),
            pl.BlockSpec((unit, width), lambda j: (j, 0)),
            full((width, width)),
            full((rows, width)),
            full((8, width)),
            full((2, 8, width)),
        ],
        scratch_shapes=[
            pltpu.VMEM((rows + 8, width), F32),
            pltpu.VMEM((rows, width), BF16),
            pltpu.VMEM((rows, width), BF16),
            pltpu.VMEM((width, rows), BF16),
            pltpu.VMEM((rows, width), F32),
            pltpu.VMEM((rows, width), BF16),
            pltpu.VMEM((rows, width), F32),
            pltpu.VMEM((rows, width), F32),
            pltpu.VMEM((rows + 8, width), F32),
        ],
        compiler_params=params(60),
        name="ffn",
    )(middle, g, hprev, vecs, spans, pads, wg, wk, wv)


def exit_back_kernel(
    base, mid_ref, g_ref, dh_ref, dhnext_ref, vec_ref, rate_ref, gated_ref, wkv_ref, r_ref, k_ref, v_ref, at_ref, bt_ref,
    in_ref, spans, pads, keep_s, wo_ref,
    dmid_ref, gwo_ref, dwkv_ref, dr_ref, sums_ref, adja_ref, adjb_ref, adjend_ref,
    datt_scr, dn_scr, dd_scr,
):
    rows, width = mid_ref.shape
    blocks = width // LANES
    first = base()
    gain = vec_ref[G2 : G2 + 1]
    sums_ref[...] = jnp.zeros_like(sums_ref)
    tail = dhnext_ref[...]
    row = lax.broadcasted_iota(jnp.int32, tail.shape, 0)
    dh_ref[rows - 8 : rows] += jnp.where(row == 7, pltpu.roll(tail, 7, axis=0), 0.0)

    @pl.loop(0, rows // TILE)
    def _(i):
        at = pl.multiple_of(i * TILE, TILE)
        here = pl.ds(at, TILE)
        _, real = marks(first + at, TILE, spans, pads)
        hat, inv = normalized(mid_ref[here])
        dh = dh_ref[here]
        sums_ref[0] += fold8(dh * hat)
        sums_ref[1] += fold8(dh)
        d_mid = norm_back(dh * gain, hat, inv) + g_ref[here].astype(F32) * wide(real.astype(F32), width)
        dmid_ref[here] = d_mid
        datt_scr[here] = d_mid.astype(BF16)

    step = 256
    rate = jnp.exp(rate_ref[0:blocks])
    boost = rate_ref[blocks : 2 * blocks]
    a_in, b_in = in_ref[0], in_ref[1]
    first_start = first_start_from(spans, first, 1 << 20) - first
    for j in range(width // step):
        here = (slice(None), slice(j * step, (j + 1) * step))
        dr_ref[here] = dot_t(datt_scr[...], wo_ref[j * step : (j + 1) * step]).astype(BF16)
    d_gated = dr_ref

    @pl.loop(0, rows // TILE)
    def _(i):
        at = pl.multiple_of(i * TILE, TILE)
        for j in range(blocks):
            here = (pl.ds(at, TILE), columns(j))
            sig = jax.nn.sigmoid(r_ref[here])
            dg = d_gated[here].astype(F32)
            dwkv = (dg * sig).astype(BF16)
            dwkv_ref[here] = dwkv
            dr_ref[here] = (dg * wkv_ref[here].astype(F32) * sig * (1.0 - sig)).astype(BF16)
            k, v = k_ref[here].astype(F32), v_ref[here].astype(F32)
            _, _, _, inv, wkv = wkv_parts(
                at, j, TILE, blocks, k, v, at_ref, bt_ref, a_in, b_in, rate, boost, first_start
            )
            dn = dwkv.astype(F32) * inv
            there = pl.ds(at * blocks + j, TILE, stride=blocks)
            dn_scr[there] = dn
            dd_scr[there] = -dn * wkv

    decay = jnp.exp(-rate)

    def scan(t8, carry):
        a, b = carry
        for u in range(8):
            t = rows - 1 - (t8 * 8 + u)
            keep = keep_s[t]
            here = pl.ds(pl.multiple_of(t * blocks, blocks), blocks)
            adja_ref[here] = a
            adjb_ref[here] = b
            fade = decay * keep
            a = a * fade + dn_scr[here] * keep
            b = b * fade + dd_scr[here] * keep
        return a, b

    zero = jnp.zeros((blocks, LANES), F32)
    a, b = lax.fori_loop(0, rows // 8, scan, (zero, zero))
    adjend_ref[0] = a
    adjend_ref[1] = b
    for j in range(width // step):
        here = (slice(None), slice(j * step, (j + 1) * step))
        gwo_ref[here] = t_dot(gated_ref[...], datt_scr[here]).astype(BF16)


def exit_back(base, middle, g, dh, dhnext, vecs, rates, gated, wkv, r, k, v, at, bt, carry, spans, pads, keep, wo):
    rows, width = middle.shape
    blocks = width // LANES
    tall = (rows * blocks, LANES)
    return pl.pallas_call(
        functools.partial(exit_back_kernel, base),
        out_shape=[
            sds((rows, width), F32),
            sds((width, width), BF16),
            sds((rows, width), BF16),
            sds((rows, width), BF16),
            sds((2, 8, width), F32),
            sds(tall, F32),
            sds(tall, F32),
            sds((2, blocks, LANES), F32),
        ],
        in_specs=[VMEM] * 14 + [SMEM] * 3 + [VMEM],
        out_specs=[VMEM] * 8,
        scratch_shapes=[
            pltpu.VMEM((rows, width), BF16),
            pltpu.VMEM(tall, F32),
            pltpu.VMEM(tall, F32),
        ],
        compiler_params=params(60),
        name="exit_back",
    )(middle, g, dh, dhnext, vecs, rates, gated, wkv, r, k, v, at, bt, carry, spans, pads, keep, wo)


def project_back_kernel(
    base, hops, total, x_ref, xprev_ref, vec_ref, rate_ref, k_ref, v_ref, dwkv_ref, dr_ref, at_ref, bt_ref, in_ref,
    adja_ref, adjb_ref, adj_ref, xk_ref, xv_ref, xr_ref, spans, pads, wk_hbm, wv_hbm, wr_hbm,
    gwk_ref, gwv_ref, gwr_ref, dh_ref, back_ref, sums_ref, wsums_ref,
    h_scr, dk_scr, dv_scr, d_scr, pass_scr, w_scr, sems,
):
    rows, width = x_ref.shape
    blocks = width // LANES
    copies = [
        pltpu.make_async_copy(hbm, w_scr.at[i], sems.at[i])
        for i, hbm in enumerate((wk_hbm, wv_hbm, wr_hbm))
    ]
    for copy in copies:
        copy.start()
    first = base()
    rate = jnp.exp(rate_ref[0:blocks])
    boost = rate_ref[blocks : 2 * blocks]
    a_in, b_in = in_ref[0], in_ref[1]
    first_start = first_start_from(spans, first, 1 << 20) - first
    last_start = last_start_before(spans, first + rows) - first
    after = first_start_from(spans, first + rows, total)
    counts = [jnp.where(after >= first + (h + 1) * rows, 1.0, 0.0) for h in range(hops)]
    adj_a, adj_b = gather_carry(hops, rows, adj_ref, counts, rate)
    wsums_ref[...] = jnp.zeros_like(wsums_ref)
    sums_ref[...] = jnp.zeros_like(sums_ref)

    @pl.loop(0, rows // TILE)
    def _(i):
        at = pl.multiple_of(i * TILE, TILE)
        _, real = marks(first + at, TILE, spans, pads)
        real = real.astype(F32)
        pos = at + lax.broadcasted_iota(jnp.int32, (TILE, LANES), 0)
        for j in range(blocks):
            here = (pl.ds(at, TILE), columns(j))
            k, v = k_ref[here].astype(F32), v_ref[here].astype(F32)
            a, b, eu, inv, wkv = wkv_parts(
                at, j, TILE, blocks, k, v, at_ref, bt_ref, a_in, b_in, rate, boost, first_start
            )
            there = pl.ds(at * blocks + j, TILE, stride=blocks)
            lift = jnp.where(
                pos >= last_start, jnp.exp(-rate[j : j + 1] * (rows - 1 - pos).astype(F32)), 0.0
            )
            post_a = adja_ref[there] + lift * adj_a[j : j + 1]
            post_b = adjb_ref[there] + lift * adj_b[j : j + 1]
            dn = dwkv_ref[here].astype(F32) * inv
            own = eu * dn
            weight = jnp.exp(k) * real
            dv_scr[here] = (own + weight * post_a).astype(BF16)
            first_term = own * (v - wkv)
            dk_scr[here] = (first_term + weight * (v * post_a + post_b)).astype(BF16)
            wsums_ref[0, :, columns(j)] += fold8(a * post_a + b * post_b)
            wsums_ref[1, :, columns(j)] += fold8(first_term)

    for j in range(blocks):
        r = rate[j : j + 1]
        wsums_ref[0, :, columns(j)] *= -r * jnp.exp(-r)
    gain, bias = vec_ref[G1 : G1 + 1], vec_ref[B1 : B1 + 1]
    h_scr[0:8] = normalized(xprev_ref[...].astype(F32))[0] * gain + bias

    @pl.loop(0, rows // TILE)
    def _(i):
        at = pl.multiple_of(i * TILE, TILE)
        hat, _ = normalized(x_ref[pl.ds(at, TILE)].astype(F32))
        h_scr[pl.ds(at + 8, TILE)] = hat * gain + bias

    step = 256
    dh_ref[...] = jnp.zeros_like(dh_ref)
    groups = ((dk_scr, xk_ref, gwk_ref, SK), (dv_scr, xv_ref, gwv_ref, SV), (dr_ref, xr_ref, gwr_ref, SR))
    pass_scr[...] = jnp.zeros_like(pass_scr)
    for i, (grad, mixed, out, row) in enumerate(groups):
        copies[i].wait()
        for j in range(width // step):
            here = (slice(None), slice(j * step, (j + 1) * step))
            d_scr[:, j * step : (j + 1) * step] = dot_t(grad[...], w_scr[i, j * step : (j + 1) * step])
            out[here] = t_dot(mixed[...], grad[here]).astype(BF16)
        share = vec_ref[row : row + 1]

        @pl.loop(0, rows // TILE)
        def _(t):
            at = pl.multiple_of(t * TILE, TILE)
            here = pl.ds(at, TILE)
            start, _ = marks(first + at, TILE, spans, pads)
            keep = wide(1.0 - start.astype(F32), width)
            h, p = with_previous(h_scr, at)
            d = d_scr[here]
            sums_ref[i] += fold8((h - p * keep) * d)
            pass_scr[here] += d * (1.0 - share) * keep
            dh_ref[here] += d * share

    back_ref[...] = pass_scr[0:8]

    @pl.loop(0, rows // TILE)
    def _(i):
        at = pl.multiple_of(i * TILE, TILE)
        dh_ref[pl.ds(at, TILE)] += pass_scr[pl.ds(at, TILE + 8)][1 : TILE + 1]


def project_back(base, hops, total, x, xprev, vecs, rates, k, v, dwkv, dr, at, bt, carry, adja, adjb, adj, xk, xv, xr, spans, pads, wk, wv, wr):
    rows, width = x.shape
    return pl.pallas_call(
        functools.partial(project_back_kernel, base, hops, total),
        out_shape=[sds((width, width), BF16)] * 3
        + [
            sds((rows, width), F32),
            sds((8, width), F32),
            sds((3, 8, width), F32),
            sds((2, 8, width), F32),
        ],
        in_specs=[VMEM] * 17 + [SMEM] * 2 + [ANY] * 3,
        out_specs=[VMEM] * 7,
        scratch_shapes=[
            pltpu.VMEM((rows + 8, width), F32),
            pltpu.VMEM((rows, width), BF16),
            pltpu.VMEM((rows, width), BF16),
            pltpu.VMEM((rows, width), F32),
            pltpu.VMEM((rows + 8, width), F32),
            pltpu.VMEM((3, width, width), BF16),
            pltpu.SemaphoreType.DMA((3,)),
        ],
        compiler_params=params(60),
        name="project_back",
    )(x, xprev, vecs, rates, k, v, dwkv, dr, at, bt, carry, adja, adjb, adj, xk, xv, xr, spans, pads, wk, wv, wr)


def entry_back_kernel(x_ref, dh_ref, dhnext_ref, dmid_ref, vec_ref, out_ref, sums_ref):
    rows = x_ref.shape[0]
    gain = vec_ref[G1 : G1 + 1]
    sums_ref[...] = jnp.zeros_like(sums_ref)
    tail = dhnext_ref[...]
    row = lax.broadcasted_iota(jnp.int32, tail.shape, 0)
    dh_ref[rows - 8 : rows] += jnp.where(row == 7, pltpu.roll(tail, 7, axis=0), 0.0)

    @pl.loop(0, rows // TILE)
    def _(i):
        here = pl.ds(pl.multiple_of(i * TILE, TILE), TILE)
        hat, inv = normalized(x_ref[here].astype(F32))
        dh = dh_ref[here]
        sums_ref[0] += fold8(dh * hat)
        sums_ref[1] += fold8(dh)
        out_ref[here] = (norm_back(dh * gain, hat, inv) + dmid_ref[here]).astype(BF16)


def entry_back(x, dh, dhnext, dmid, vecs):
    rows, width = x.shape
    return pl.pallas_call(
        entry_back_kernel,
        out_shape=[sds((rows, width), BF16), sds((2, 8, width), F32)],
        in_specs=[VMEM] * 5,
        out_specs=[VMEM] * 2,
        compiler_params=params(40),
        name="entry_back",
    )(x, dh, dhnext, dmid, vecs)


X, Y, Z = "x", "y", "z"
ORDERS = {
    X: ("x", "y", "low", "high"),
    Y: ("y", "x", "low", "high"),
    Z: ("low", "high", "x", "y"),
}
AXIS_BIT = {"core": ("seq", 1), "x": ("seq", 2), "y": ("chan", 1), "low": ("chan", 2), "high": ("chan", 4)}
STEPS = 5
SEQ, CHAN = 4, 8
RING = 3
BIG = 256
MESH = pl.DeviceIdType.MESH
ARRAYS = ("fv", "fk0", "fk1", "fk2", "fk3", "fr", "wo", "wr", "wv", "wk")
UNITS = (0, 4, 1, 5, 2, 6, 3, 7)


def third(name):
    return ((name, 0, 96, X), (name, 96, 96, Y), (name, 192, 64, Z))


CHUNKS = (
    tuple(
        chunk
        for q in range(4)
        for chunk in (
            ("fv", q * 128, 128, X),
            ("fv", (q + 4) * 128, 128, Y),
            (f"fk{q}", 128, 128, Z),
            (f"fk{q}", 0, 128, Y if q % 2 else X),
        )
    )
    + (("fr", 0, 128, X), ("fr", 128, 128, Y), ("wo", 0, 128, X), ("wo", 128, 128, Y))
    + (("wr", 0, 64, X), ("wr", 64, 64, Y), ("wr", 128, 128, Z))
    + third("wv")
    + third("wk")
)
MOST = {X: 128, Y: 128, Z: 128}
LANES_OF = (X, Y, Z)
TURNS = 6
LINK, CORE, HOP, FETCH, ACTION, ADD = 46000.0, 570000.0, 4.0, 1.6, 0.06, 0.0012
BACKLOG, PACE = 3.0, 1.0


def bit_of(index, weight):
    return index // weight % 2


def partner(axis):
    name, weight = AXIS_BIT[axis]
    where = {"seq": lax.axis_index("seq"), "chan": lax.axis_index("chan")}
    bit = bit_of(where[name], weight)
    where[name] = where[name] + weight * (1 - 2 * bit)
    return bit, (where["seq"], where["chan"])


class Summing:
    def __init__(self, grads, received, outs, stages, rings, levels, sems):
        self.grads, self.received, self.outs = grads, received, outs
        self.stages, self.rings, self.levels = stages, rings, levels
        self.across_sem, self.ring_sems, self.level_sems, self.across_recv, self.recv_sems, self.stage_sems = sems
        self.sides = {axis: partner(axis) for axis in AXIS_BIT}
        self.bases, filled = {}, 0
        for name in ARRAYS:
            self.bases[name] = filled
            filled += grads[name]().shape[2]
        count = len(CHUNKS)
        self.queue = {lane: [n for n in range(count) if CHUNKS[n][3] == lane] for lane in LANES_OF}
        self.turn = {n: i for queue in self.queue.values() for i, n in enumerate(queue)}
        self.now, self.waited = 0.0, 0.0
        self.free = dict.fromkeys(("core", "x", "y", "end", "middle"), 0.0)
        self.ready = {}
        self.did = set()


    def place(self, number):
        array, first, rows, stream = CHUNKS[number]
        return array, first, rows, stream, LANES_OF.index(stream), self.bases[array] + first

    def key(self, number):
        array, first, _, _ = CHUNKS[number]
        return f"fv{first // 128}" if array == "fv" else array

    def across(self, number):
        array, first, rows, _, _, base = self.place(number)
        core, mate = self.sides["core"]
        return pltpu.make_async_remote_copy(
            src_ref=self.grads[array]().at[:, 1 - core, pl.ds(first, rows)],
            dst_ref=self.received.at[:, pl.ds(base, rows)],
            send_sem=self.across_sem,
            recv_sem=self.across_recv.at[number],
            device_id=mate,
            device_id_type=MESH,
        )

    def staged(self, number):
        array, first, rows, _, lane, base = self.place(number)
        core, _ = self.sides["core"]
        stage = self.stages[lane]
        return (
            pltpu.make_async_copy(
                self.grads[array]().at[:, core, pl.ds(first, rows)], stage.at[0, :, 0:rows], self.stage_sems.at[lane, 0]
            ),
            pltpu.make_async_copy(self.received.at[:, pl.ds(base, rows)], stage.at[1, :, 0:rows], self.stage_sems.at[lane, 1]),
        )

    def half(self, number, step, other):
        _, _, rows, stream, lane, base = self.place(number)
        bit, _ = self.sides[ORDERS[stream][step - 1]]
        size = (16 >> step) * rows
        at = pl.ds(pl.multiple_of((1 - bit if other else bit) * size + (step > 1) * base * (32 >> step), 16), size)
        if step == 1:
            return self.rings[lane], (self.turn[number] % RING, at)
        return self.levels[step - 2], (at,)

    def target(self, number, step):
        _, _, rows, _, _, base = self.place(number)
        return self.levels[step - 1], pl.ds(base * (16 >> step), rows * (16 >> step))

    def send(self, number, step):
        _, _, _, stream, lane, _ = self.place(number)
        _, mate = self.sides[ORDERS[stream][step - 1]]
        source, there = self.half(number, step, True)
        target, here = self.target(number, step)
        return pltpu.make_async_remote_copy(
            src_ref=source.at[there],
            dst_ref=target.at[here],
            send_sem=self.ring_sems.at[lane, self.turn[number] % RING] if step == 1 else self.level_sems.at[step - 2],
            recv_sem=self.recv_sems.at[lane, self.turn[number] % TURNS, step - 1],
            device_id=mate,
            device_id_type=MESH,
        )


    def transfer(self, number, step):
        rows = CHUNKS[number][2]
        if step == 0:
            hops = (("core", rows * 4096 / CORE),)
        else:
            took = rows * (16 >> step) * 256 / LINK
            axis = ORDERS[CHUNKS[number][3]][step - 1]
            hops = {"low": (("end", took),), "high": (("end", took), ("middle", 2 * took))}.get(axis, ((axis, took),))
        arrived = 0.0
        for link, took in hops:
            self.free[link] = max(self.now, self.free[link]) + took
            arrived = max(arrived, self.free[link])
        self.ready[number, step] = arrived + HOP

    def link_of(self, number, step):
        axis = ORDERS[CHUNKS[number][3]][step - 1]
        return {"low": "end", "high": "end"}.get(axis, axis)

    def possible(self):
        found = []
        for queue in self.queue.values():
            for n in queue:
                if (n, 0) not in self.ready:
                    break
                turn = self.turn[n]
                if (n, "fetch") not in self.did:
                    if turn == 0 or (queue[turn - 1], 0) in self.did:
                        found.append((self.ready[n, 0], None, n, "fetch"))
                    break
                if (n, 0) not in self.did:
                    old = queue[turn - RING] if turn >= RING else None
                    if old is None or (old, 1) in self.did:
                        when = max(self.ready[n, "fetch"], 0.0 if old is None else self.ready[old, 1])
                        found.append((when, self.link_of(n, 1), n, 0))
                    continue
                step = next((s for s in range(1, STEPS) if (n, s) not in self.did), None)
                if step:
                    found.append((self.ready[n, step], self.link_of(n, step + 1) if step < 4 else None, n, step))
        return found

    def act(self, when, number, step):
        self.waited += max(0.0, when - self.now)
        self.now = max(self.now, when) + ACTION
        rows = CHUNKS[number][2]
        self.did.add((number, step))
        if step == "fetch":
            self.start_stage(number)
            self.ready[number, "fetch"] = self.now + FETCH
        elif step == 0:
            self.now += rows * ADD
            self.first_sum(number)
            self.transfer(number, 1)
        else:
            self.now += rows * 2 * ADD / (1 << step)
            self.later_sum(number, step)
            if step < 4:
                self.transfer(number, step + 1)

    def pump(self, took):
        self.now += took * PACE
        while True:
            able = [
                (self.free.get(link, 0.0), n, step, when)
                for when, link, n, step in self.possible()
                if when <= self.now and self.free.get(link, 0.0) < self.now + BACKLOG
            ]
            if not able:
                return
            _, number, step, when = min(able, key=lambda a: a[:2])
            self.act(when, number, step)

    def drain(self):
        while found := self.possible():
            when, _, number, step = min(found, key=lambda a: (max(a[0], self.now), a[2]))
            self.act(when, number, step)

    def complete(self, key):
        for n in range(len(CHUNKS)):
            if self.key(n) == key:
                self.across(n).start()
                self.now += 0.05
                self.transfer(n, 0)


    def start_stage(self, number):
        self.across(number).wait_recv()
        for copy in self.staged(number):
            copy.start()

    def first_sum(self, number):
        _, _, rows, stream, lane, _ = self.place(number)
        turn = self.turn[number]
        stage, ring = self.stages[lane], self.rings[lane]
        if turn >= RING:
            self.send(self.queue[stream][turn - RING], 1).wait_send()
        for copy in self.staged(number):
            copy.wait()
        for i in range(16):
            c = i % 8
            bits = {"x": i // 8, "y": c % 2, "low": c // 2 % 2, "high": c // 4}
            at = sum(bits[axis] << (3 - d) for d, axis in enumerate(ORDERS[stream])) * rows
            ring[turn % RING, at : at + rows] = stage[0, i // 8, 0:rows, columns(c)] + stage[1, i // 8, 0:rows, columns(c)]
        self.send(number, 1).start()

    def later_sum(self, number, step):
        array, first, rows, _, _, _ = self.place(number)
        source, own = self.half(number, step, False)
        target, here = self.target(number, step)
        self.send(number, step).wait_recv()
        if step == 4:
            out, cols = self.outs[array]
            out[first : first + rows, cols] = source[own].astype(F32) + target[here].astype(F32)
            return
        target[here] = source[own] + target[here]
        self.send(number, step + 1).start()

    def finish(self):
        pltpu.make_async_copy(self.received, self.received, self.across_sem).wait()
        for i, level in enumerate(self.levels[1:]):
            pltpu.make_async_copy(level, level, self.level_sems.at[i]).wait()
        for queue in self.queue.values():
            for n in queue[-RING:]:
                self.send(n, 1).wait_send()


def view(ref, *index):
    return lambda: ref.at[index]


class Copies:
    def __init__(self, sems):
        self.sems, self.all, self.waited = sems, {}, set()
        self.idle = list(range(sems.shape[0]))

    def start(self, name, source, target):
        assert name not in self.all
        self.all[name] = (source, target, self.idle.pop(0))
        self.copy(name).start()

    def copy(self, name):
        source, target, number = self.all[name]
        source, target = (r() if callable(r) else r for r in (source, target))
        return pltpu.make_async_copy(source, target, self.sems.at[number])

    def wait(self, *names):
        for name in names:
            if name not in self.waited:
                self.copy(name).wait()
                self.waited.add(name)
                self.idle.append(self.all[name][2])

    def finish(self):
        self.wait(*self.all)


def block_kernel(*refs):
    (
        spans, pads,
        out_h, gin_h, ofv_h, ofk_h, ofr_h, owo_h, owr_h, owv_h, owk_h, ovec_h,
        received, gw_h, gfv_h, gfk_h, spill_b, spill_r, spill_t,
        mid, dh, h_scr, d_scr, pass_scr, b0, b1, b2, b3, b4, b5, b6, b7, w_scr, tile_scr, vec_scr, vec_chan, vec_mine, vec_seq,
        keep_scr, real_scr, xlast, halo2, halob2, halo1, mine2, mine1, mineb2, st_mine, st_in, adj_mine, adj_in, in_scr,
        line, tall_line, ofv, ofk, ofr, owo, owr, owv, owk, ovec,
        sums, wsums, s0, s1, s2, g0, g1, g2, l1, l2, l3, l4,
        copy_sems, halo_send, halo_recv, chan_send, chan_recv, seq_send, seq_recv, *sum_sems,
    ) = refs[9 + 11 :]
    small_h, refs = refs[9 : 9 + 11], refs[:9]
    x_h, g_h, wk_h, wv_h, wr_h, wo_h, wfk_h, wfv_h, wfr_h = refs
    gain1_ref, bias1_ref, sk_ref, sv_ref, sr_ref, gain2_ref, bias2_ref, fk_ref, fr_ref = [line.at[i] for i in range(9)]
    rows, width = x_h.shape
    blocks = width // LANES
    chans = lax.axis_size("chan")
    seq, chan = lax.axis_index("seq"), lax.axis_index("chan")
    first = chan * rows
    total = rows * chans
    hops = adj_in.shape[0]
    tiles = rows // TILE
    step = 256
    quarter = width // 4

    grads = {"fv": lambda: gfv_h}
    outs = {"fv": (ofv, slice(None))}
    for i in range(4):
        grads[f"fk{i}"], outs[f"fk{i}"] = view(gfk_h, i), (ofk, columns(i))
    names = ("fr", "wo", "wr", "wv", "wk")
    for i, (name, out) in enumerate(zip(names, (ofr, owo, owr, owv, owk))):
        grads[name], outs[name] = view(gw_h, i), (out, slice(None))
    summing = Summing(
        grads, received, outs, (s0, s1, s2), (g0, g1, g2), (l1, l2, l3, l4), sum_sems
    )
    pump = summing.pump
    copies = Copies(copy_sems)
    start, wait = copies.start, copies.wait

    def row_tiles(body, lo=0, hi=tiles, size=TILE):
        @pl.loop(lo, hi)
        def _(i):
            at = pl.multiple_of(i * size, size)
            body(at, pl.ds(at, size))

    def col(j):
        return slice(j * step, (j + 1) * step)

    def spread(ref, here, to=width):
        return wide(ref[here], to)

    def hand(source, target, number, offset):
        return lambda: pltpu.make_async_remote_copy(
            src_ref=source() if callable(source) else source,
            dst_ref=target() if callable(target) else target,
            send_sem=halo_send.at[number],
            recv_sem=halo_recv.at[number],
            device_id=(seq, (chan + chans + offset) % chans),
            device_id_type=MESH,
        )

    hand_x = hand(view(x_h, pl.ds(rows - 16, 16)), xlast, 0, 1)
    hand_h2 = hand(mine2, halo2, 1, 1)
    hand_b2 = hand(mineb2, halob2, 2, -1)
    hand_b1 = hand(mine1, halo1, 3, -1)
    hand_st = [hand(st_mine, view(st_in, h), 4 + h, h + 1) for h in range(hops)]
    hand_adj = [hand(adj_mine, view(adj_in, h), 4 + hops + h, -h - 1) for h in range(hops)]

    x, xk, xv, xr, k, v = b0, b1, b2, b3, b4, b5
    start("x", x_h, x)
    for i, small in enumerate(small_h):
        start(f"small {i}", small, view(line, i) if i < 9 else view(tall_line, i - 9))
    start("wk", wk_h, view(w_scr, 0))
    start("wv", wv_h, view(w_scr, 1))
    barrier = pltpu.get_barrier_semaphore()
    seqs = SEQ
    mates = [(seq, (chan + d) % chans) for d in range(1, chans)] + [((seq + d) % seqs, chan) for d in range(1, seqs)]
    for mate in mates:
        pl.semaphore_signal(barrier, inc=1, device_id=mate, device_id_type=MESH)

    wait(*(f"small {i}" for i in range(len(small_h))))
    rate = jnp.exp(tall_line[0])
    decay = jnp.exp(-rate)
    boost = tall_line[1]
    gain1, bias1, gain2, bias2 = gain1_ref[...], bias1_ref[...], gain2_ref[...], bias2_ref[...]
    sums[...] = jnp.zeros_like(sums)
    wsums[...] = jnp.zeros_like(wsums)
    first_start = first_start_from(spans, first, 1 << 20) - first
    last_start = last_start_before(spans, first + rows) - first
    before = last_start_before(spans, first)
    after = first_start_from(spans, first + rows, total)

    def marks_tile(at, here):
        begins, real = marks(first + at, TILE, spans, pads)
        keep_scr[here] = 1.0 - begins.astype(F32)
        real_scr[here] = real.astype(F32)

    row_tiles(marks_tile)
    pl.semaphore_wait(barrier, len(mates))
    hand_x().start()
    wait("x")

    def norm1_of(at, here):
        hat, _ = normalized(x[here].astype(F32))
        h_scr[pl.ds(at + 8, BIG)] = hat * gain1 + bias1

    row_tiles(norm1_of, 0, rows // BIG, BIG)

    def halo1_rows():
        h_scr[0:8] = normalized(xlast[8:16].astype(F32))[0] * gain1 + bias1

    def mixed(at, here, shares):
        keep = spread(keep_scr, here)
        h, p = with_previous(h_scr, at)
        p = p * keep
        for share_ref, out in shares:
            share = share_ref[...]
            out[here] = (h * share + p * (1.0 - share)).astype(BF16)

    mix1 = functools.partial(mixed, shares=((sk_ref, xk), (sv_ref, xv), (sr_ref, xr)))
    row_tiles(mix1, 1)
    hand_x().wait_recv()
    halo1_rows()
    row_tiles(mix1, 0, 1)

    def wkv_at(at, j, at_scr, bt_scr):
        here = (pl.ds(at, TILE), columns(j))
        return wkv_parts(
            at, j, TILE, blocks, k[here].astype(F32), v[here].astype(F32), at_scr, bt_scr, in_scr[0], in_scr[1],
            rate, boost, first_start,
        )

    def forward(at_scr, bt_scr, ev_scr, ek_scr):
        wait("wk")
        for j in range(width // step):
            k[:, col(j)] = dot(xk[...], w_scr[0, :, col(j)]).astype(BF16)
        start("wr", wr_h, view(w_scr, 0))
        wait("wv")
        for j in range(width // step):
            v[:, col(j)] = dot(xv[...], w_scr[1, :, col(j)]).astype(BF16)
        start("wo", wo_h, view(w_scr, 1))

        def weights_tile(at, here):
            real = real_scr[here]
            for j in range(blocks):
                there = pl.ds(at * blocks + j, TILE, stride=blocks)
                ek = jnp.exp(k[here, columns(j)].astype(F32)) * real
                ek_scr[there] = ek
                ev_scr[there] = ek * v[here, columns(j)].astype(F32)

        row_tiles(weights_tile)

        def scan(t8, carry):
            a, b = carry
            for u in range(8):
                t = t8 * 8 + u
                keep = keep_scr[pl.ds(t, 1)]
                here = pl.ds(pl.multiple_of(t * blocks, blocks), blocks)
                fade = decay * keep
                at_scr[here] = a * keep
                bt_scr[here] = b * keep
                a = a * fade + ev_scr[here]
                b = b * fade + ek_scr[here]
            return a, b

        zero = jnp.zeros((blocks, LANES), F32)
        st_mine[0], st_mine[1] = lax.fori_loop(0, rows // 8, scan, (zero, zero))
        for copy in hand_st:
            copy().start()
        start("xk out", xk, view(spill_b, 0))
        start("xv out", xv, view(spill_b, 1))
        start("xr out", xr, view(spill_b, 2))
        r = d_scr
        wait("wr")
        for j in range(width // step):
            r[:, col(j)] = dot(xr[...], w_scr[0, :, col(j)])
        start("wfr", wfr_h, view(w_scr, 0))
        start("r out", r, spill_r)
        for copy in hand_st:
            copy().wait_recv()
        a_in, b_in = st_in[0, 0], st_in[0, 1]
        for h in range(1, hops):
            scale = jnp.exp(-rate * float(rows * h)) * jnp.where(before < first - h * rows, 1.0, 0.0)
            a_in, b_in = a_in + scale * st_in[h, 0], b_in + scale * st_in[h, 1]
        in_scr[0], in_scr[1] = a_in, b_in
        wkv, gated = b6, b7

        def outputs_tile(at, here):
            for j in range(blocks):
                a, b, _, _, out = wkv_at(at, j, at_scr, bt_scr)
                there = pl.ds(at * blocks + j, TILE, stride=blocks)
                at_scr[there] = a
                bt_scr[there] = b
                out = out.astype(BF16)
                wkv[here, columns(j)] = out
                gated[here, columns(j)] = (jax.nn.sigmoid(r[here, columns(j)]) * out.astype(F32)).astype(BF16)

        row_tiles(outputs_tile)
        start("at out", at_scr, view(spill_t, 0))
        start("bt out", bt_scr, view(spill_t, 1))
        start("k out", k, view(spill_b, 3))
        start("v out", v, view(spill_b, 4))
        start("wkv out", wkv, view(spill_b, 5))
        start("gated out", gated, view(spill_b, 6))
        wait("wo")
        for tail in (pl.ds(rows - 16, 16), pl.ds(0, rows)):
            for j in range(width // step):
                mid[tail, col(j)] = x[tail, col(j)].astype(F32) + dot(gated[tail], w_scr[1, :, col(j)])
            if tail.size == 16:
                mine2[...] = normalized(mid[rows - 8 : rows])[0] * gain2 + bias2
                hand_h2().start()
        wait("at out", "bt out")
        pump(11.0)

    tall = pltpu.VMEM((rows * blocks, LANES), F32)
    pl.run_scoped(forward, tall, tall, tall, tall)

    def ffn(wk_scr, wv_scr, ckt_scr, fv_tile, fk_tile):
        def load_unit(index):
            unit, slot = UNITS[index], index % 2
            for s in range(4):
                at = s * (wfk_h.shape[1] // 4) + unit * LANES
                start(f"wfk{index} {s}", view(wfk_h, slice(None), pl.ds(at, LANES)), view(wk_scr, slot, slice(None), columns(s)))
                start(f"wfv{index} {s}", view(wfv_h, pl.ds(at, LANES)), view(wv_scr, slot, columns(s)))

        load_unit(0)
        load_unit(1)
        g, ck, cr, dvo = b0, b1, b2, b3
        start("g", g_h, g)

        def norm2_of(at, here):
            hat, _ = normalized(mid[here])
            h_scr[pl.ds(at + 8, BIG)] = hat * gain2 + bias2

        row_tiles(norm2_of, 0, rows // BIG, BIG)
        wait("xk out", "xv out", "xr out")
        mix2 = functools.partial(mixed, shares=((fk_ref, ck), (fr_ref, cr)))
        row_tiles(mix2, 1)
        hand_h2().wait_recv()
        h_scr[0:8] = halo2[...]
        row_tiles(mix2, 0, 1)
        ckt_scr[...] = ck[...].T
        sig, dck = d_scr, dh
        wait("wfr", "r out", "g")
        real = spread(real_scr, slice(None), step)
        for j in range(width // step):
            s = jax.nn.sigmoid(dot(cr[...], w_scr[0, :, col(j)]))
            sig[:, col(j)] = s
            dvo[:, col(j)] = (g[:, col(j)].astype(F32) * real * s).astype(BF16)
        pump(7.0)
        for index, unit in enumerate(UNITS):
            slot = index % 2
            for s in range(4):
                wait(f"wfk{index} {s}", f"wfv{index} {s}")
            act = jnp.maximum(dot(ck[...], wk_scr[slot]), 0.0)
            hidden = (act * act).astype(BF16)
            fv = t_dot(hidden, dvo[...]).astype(BF16)
            if index:
                for s in range(4):
                    wait(f"fv{index - 1} {s}")
            fv_tile[...] = fv.reshape(4, LANES, width)
            for s in range(4):
                start(f"fv{index} {s}", view(fv_tile, s), view(gfv_h, s // 2, s % 2, pl.ds(unit * LANES, LANES)))
            pump(1.6)
            d_pre = (dot_t(dvo[...], wv_scr[slot]) * (2.0 * act)).astype(BF16)
            fk = dot(ckt_scr[...], d_pre).astype(BF16)
            for s in range(4):
                wait(f"fv{index} {s}")
            summing.complete(f"fv{unit}")
            if index:
                for s in range(4):
                    wait(f"fk{index - 1} {s}")
            fk_tile[...] = fk.reshape(2, 2, quarter, 4 * LANES)
            for s in range(4):
                at = columns(2 * s + unit // 4)
                start(f"fk{index} {s}", view(fk_tile, slice(None), slice(None), slice(None), columns(s)), view(gfk_h, unit % 4, slice(None), slice(None), slice(None), at))
            pump(1.3)
            if index:
                pass_scr[0:rows] += dot(hidden, wv_scr[slot])
                dck[...] += dot_t(d_pre, wk_scr[slot])
            else:
                pass_scr[0:rows] = dot(hidden, wv_scr[slot])
                dck[...] = dot_t(d_pre, wk_scr[slot])
            if index + 2 < len(UNITS):
                load_unit(index + 2)
            if index % 2:
                for s in range(4):
                    wait(f"fk{index} {s}")
                summing.complete(f"fk{unit % 4}")
            pump(1.2)
        dgp = dvo
        wait("k out")
        block_out = b4
        for j in range(width // step):
            s, value = sig[:, col(j)], pass_scr[0:rows, col(j)]
            block_out[:, col(j)] = (mid[:, col(j)] + s * value).astype(BF16)
            top = g[:, col(j)].astype(F32) * real
            dgp[:, col(j)] = (top * value * s * (1.0 - s)).astype(BF16)
        start("block out", block_out, out_h)
        pump(1.3)
        write_grad(0, "fr", cr, dgp)
        dcr = pass_scr
        for j in range(width // step):
            dcr[0:rows, col(j)] = dot_t(dgp[...], w_scr[0, col(j)])
        flush()
        start("wo again", wo_h, view(w_scr, 0))
        pump(1.4)

    written, unsent = [], []

    def write_grad(index, name, left, right):
        flush()
        for j in range(width // step):
            slot = j % 2
            if j >= 2:
                wait(*written[-2])
            tile_scr[slot] = t_dot(left[...], right[:, col(j)]).astype(BF16).reshape(2, 2, quarter, step)
            written.append((f"{name} tile {j}",))
            start(written[-1][0], view(tile_scr, slot), view(gw_h, index, slice(None), slice(None), slice(None), col(j)))
            pump(0.4)
        unsent.append(name)

    def flush():
        if unsent:
            wait(*written[-1], *written[-2])
            summing.complete(unsent.pop())

    half = pltpu.VMEM((rows, width), BF16)
    pl.run_scoped(
        ffn,
        pltpu.VMEM((2, width, 4 * LANES), BF16),
        pltpu.VMEM((2, 4 * LANES, width), BF16),
        pltpu.VMEM((width, rows), BF16),
        pltpu.VMEM((4, LANES, width), BF16),
        pltpu.VMEM((2, 2, quarter, 4 * LANES), BF16),
    )

    def last_row(halo):
        row = lax.broadcasted_iota(jnp.int32, halo.shape, 0)
        return jnp.where(row == 7, pltpu.roll(halo[...], 7, axis=0), 0.0)

    def attention_back(at_scr, bt_scr, dn_scr, dd_scr):
        g, gated, wkv, datt, dr = b0, b1, b2, b5, b7
        wait("block out", "v out", "gated out", "wkv out")
        start("at", view(spill_t, 0), at_scr)
        start("bt", view(spill_t, 1), bt_scr)
        start("gated", view(spill_b, 6), gated)
        start("wkv", view(spill_b, 5), wkv)
        start("k", view(spill_b, 3), b3)
        start("wr again", wr_h, view(w_scr, 1))
        start("v", view(spill_b, 4), b4)
        k, v = b3, b4
        share_k, share_r = fk_ref[...], fr_ref[...]

        def mix2_back(at, here):
            keep = spread(keep_scr, here)
            h, p = with_previous(h_scr, at)
            diff = h - p * keep
            dck, dcr = dh[here], pass_scr[here]
            sums[7] += fold8(diff * dck)
            sums[8] += fold8(diff * dcr)
            pass_scr[here] = (dck * (1.0 - share_k) + dcr * (1.0 - share_r)) * keep
            dh[here] = dck * share_k + dcr * share_r

        row_tiles(mix2_back, 0, 1)
        mineb2[...] = pass_scr[0:8]
        hand_b2().start()
        row_tiles(mix2_back, 1)
        pass_scr[rows : rows + 8] = jnp.zeros((8, width), F32)
        start("r", spill_r, view(h_scr, slice(0, rows)))
        pump(1.6)

        def norm2_back(at, here, extra=None):
            hat, inv = normalized(mid[here])
            d = dh[here] + pass_scr[pl.ds(at, BIG + 8)][1 : BIG + 1]
            if extra is not None:
                d = d + extra
            sums[0] += fold8(d * hat)
            sums[1] += fold8(d)
            d_mid = norm_back(d * gain2, hat, inv) + g[here].astype(F32) * spread(real_scr, here)
            mid[here] = d_mid
            datt[here] = d_mid.astype(BF16)

        def tail_of(halo):
            return jnp.concatenate([jnp.zeros((BIG - 8, width), F32), last_row(halo)], axis=0)

        row_tiles(norm2_back, 0, rows // BIG - 1, BIG)
        pump(1.0)
        hand_b2().wait_recv()
        norm2_back(rows - BIG, slice(rows - BIG, rows), tail_of(halob2))
        dmid = mid
        start("x again", x_h, b0)

        wait("wo again")
        for j in range(width // step):
            d_scr[:, col(j)] = dot_t(datt[...], w_scr[0, col(j)])
        start("wv again", wv_h, view(w_scr, 0))
        pump(2.4)
        wait("r", "wkv", "k", "v", "at", "bt")

        def gate_tile(at, rows_here):
            for j in range(blocks):
                here = (rows_here, columns(j))
                there = pl.ds(at * blocks + j, TILE, stride=blocks)
                sig = jax.nn.sigmoid(h_scr[here])
                dg = d_scr[here]
                dw = (dg * sig).astype(BF16)
                dr[here] = (dg * wkv[here].astype(F32) * sig * (1.0 - sig)).astype(BF16)
                vv = v[here].astype(F32)
                eu = jnp.exp(boost[j : j + 1] + k[here].astype(F32))
                inv = 1.0 / (bt_scr[there] + eu)
                out = (at_scr[there] + eu * vv) * inv
                dn = dw.astype(F32) * inv
                dn_scr[there] = dn
                dd_scr[there] = -dn * out
                own = eu * dn
                d_scr[here] = own
                h_scr[here] = own * (vv - out)

        for part in range(4):
            row_tiles(gate_tile, part * tiles // 4, (part + 1) * tiles // 4)
            pump(0.5)
        start("xv", view(spill_b, 1), wkv)

        def scan(t8, carry):
            a, b = carry
            for u in range(8):
                t = rows - 1 - (t8 * 8 + u)
                keep = keep_scr[pl.ds(t, 1)]
                here = pl.ds(pl.multiple_of(t * blocks, blocks), blocks)
                dn, dd = dn_scr[here], dd_scr[here]
                dn_scr[here] = a
                dd_scr[here] = b
                fade = decay * keep
                a = a * fade + dn * keep
                b = b * fade + dd * keep
            return a, b

        zero = jnp.zeros((blocks, LANES), F32)
        carry = lax.fori_loop(0, rows // 16, scan, (zero, zero))
        pump(1.2)
        adj_mine[0], adj_mine[1] = lax.fori_loop(rows // 16, rows // 8, scan, carry)
        for copy in hand_adj:
            copy().start()
        pump(1.2)

        wait("gated")
        write_grad(1, "wo", gated, datt)
        start("xk", view(spill_b, 0), gated)
        start("xr", view(spill_b, 2), datt)
        xk, xv, xr = gated, wkv, datt

        wait("xr")
        write_grad(2, "wr", xr, dr)

        for copy in hand_adj:
            copy().wait_recv()
        adj_a, adj_b = adj_in[0, 0], adj_in[0, 1]
        for h in range(1, hops):
            scale = jnp.exp(-rate * float(rows * h)) * jnp.where(after >= first + (h + 1) * rows, 1.0, 0.0)
            adj_a, adj_b = adj_a + scale * adj_in[h, 0], adj_b + scale * adj_in[h, 1]

        def recur_tile(at, rows_here):
            real = real_scr[rows_here]
            pos = at + lax.broadcasted_iota(jnp.int32, (TILE, LANES), 0)
            for j in range(blocks):
                here = (rows_here, columns(j))
                there = pl.ds(at * blocks + j, TILE, stride=blocks)
                lift = jnp.where(pos >= last_start, jnp.exp(-rate[j : j + 1] * (rows - 1 - pos).astype(F32)), 0.0)
                post_a = dn_scr[there] + lift * adj_a[j : j + 1]
                post_b = dd_scr[there] + lift * adj_b[j : j + 1]
                own_k = h_scr[here]
                weight = jnp.exp(k[here].astype(F32)) * real
                vv = v[here].astype(F32)
                v[here] = (d_scr[here] + weight * post_a).astype(BF16)
                k[here] = (own_k + weight * (vv * post_a + post_b)).astype(BF16)
                wsums[0, :, columns(j)] += fold8(at_scr[there] * post_a + bt_scr[there] * post_b)
                wsums[1, :, columns(j)] += fold8(own_k)

        for part in range(4):
            row_tiles(recur_tile, part * tiles // 4, (part + 1) * tiles // 4)
            flush()
            pump(1.05)
        for j in range(blocks):
            rr = rate[j : j + 1]
            wsums[0, :, columns(j)] *= -rr * jnp.exp(-rr)
        dk, dv = k, v
        halo1_rows()
        wait("x again")
        row_tiles(norm1_of, 0, rows // BIG, BIG)
        pump(0.8)
        wait("xv")
        write_grad(3, "wv", xv, dv)
        wait("xk")
        write_grad(4, "wk", xk, dk)

        def mix1_back(grad, weight, share_ref, index, fresh):
            for j in range(width // step):
                d_scr[:, col(j)] = dot_t(grad[...], weight[col(j)])
            flush()
            pump(1.4)
            share = share_ref[...]

            def tile(at, here):
                h, p = with_previous(h_scr, at)
                d = d_scr[here]
                keep = spread(keep_scr, here)
                sums[index] += fold8((h - p * keep) * d)
                passed = d * (1.0 - share) * keep
                if fresh:
                    pass_scr[here] = passed
                    dh[here] = d * share
                else:
                    pass_scr[here] += passed
                    dh[here] += d * share

            row_tiles(tile)
            pump(1.0)

        wait("wr again")
        mix1_back(dr, w_scr.at[1], sr_ref, 4, True)
        start("wk again", wk_h, view(w_scr, 1))
        wait("wv again")
        mix1_back(dv, w_scr.at[0], sv_ref, 3, False)
        wait("wk again")
        mix1_back(dk, w_scr.at[1], sk_ref, 2, False)
        mine1[...] = pass_scr[0:8]
        hand_b1().start()
        x, grad_in = b0, b6

        def norm1_back(at, here, extra=None):
            d = dh[here] + pass_scr[pl.ds(at, BIG + 8)][1 : BIG + 1]
            if extra is not None:
                d = d + extra
            hat, inv = normalized(x[here].astype(F32))
            sums[5] += fold8(d * hat)
            sums[6] += fold8(d)
            grad_in[here] = (norm_back(d * gain1, hat, inv) + dmid[here]).astype(BF16)

        row_tiles(norm1_back, 0, rows // BIG - 1, BIG)
        pump(1.0)
        hand_b1().wait_recv()
        norm1_back(rows - BIG, slice(rows - BIG, rows), tail_of(halo1))
        start("grad in", grad_in, gin_h)

    pl.run_scoped(attention_back, tall, tall, tall, tall)
    parts = [sums[i] for i in (5, 6, 2, 3, 4)] + [wsums[0], wsums[1]] + [sums[i] for i in (0, 1, 7, 8)]
    lines = [jnp.sum(p, axis=0, keepdims=True) for p in parts]
    lines.append(jnp.zeros((16 - len(lines), width), F32))
    vec_scr[...] = jnp.concatenate(lines, axis=0)

    def to_chan(d):
        return pltpu.make_async_remote_copy(
            src_ref=vec_scr.at[:, pl.ds(pl.multiple_of((chan + d) % chans * LANES, LANES), LANES)],
            dst_ref=vec_chan.at[d],
            send_sem=chan_send.at[d],
            recv_sem=chan_recv.at[d],
            device_id=(seq, (chan + d) % chans),
            device_id_type=MESH,
        )

    def to_seq(d):
        return pltpu.make_async_remote_copy(
            src_ref=vec_mine,
            dst_ref=vec_seq.at[d],
            send_sem=seq_send.at[d],
            recv_sem=seq_recv.at[d],
            device_id=((seq + d) % seqs, chan),
            device_id_type=MESH,
        )

    for d in range(1, chans):
        to_chan(d).start()
    pump(4.0)
    vec = vec_scr[:, pl.ds(pl.multiple_of(chan * LANES, LANES), LANES)]
    for d in range(1, chans):
        to_chan(d).wait_recv()
        vec = vec + vec_chan[d]
    vec_mine[...] = vec
    for d in range(1, seqs):
        to_seq(d).start()
    pump(3.0)
    for d in range(1, seqs):
        to_seq(d).wait_recv()
        vec = vec + vec_seq[d]
    ovec[...] = vec
    start("vec", ovec, ovec_h)
    for d in range(1, chans):
        to_chan(d).wait_send()
    for d in range(1, seqs):
        to_seq(d).wait_send()
    summing.drain()
    results = ((ofv, ofv_h), (ofk, ofk_h), (ofr, ofr_h), (owo, owo_h), (owr, owr_h), (owv, owv_h), (owk, owk_h))
    for i, (source, target) in enumerate(results):
        start(f"result {i}", source, target)
    summing.finish()
    copies.finish()
    for copy in (hand_x, hand_h2, hand_b2, hand_b1, *hand_st, *hand_adj):
        copy().wait_send()


def block(x, g, weights, vectors, rates, spans, pads, hops):
    rows, width = x.shape
    blocks = width // LANES
    quarter = width // 4
    hid = weights[4].shape[1]
    fv_rows = hid // 4
    block_rows = fv_rows + 4 * quarter + 5 * quarter
    half = pltpu.VMEM((rows, width), BF16)
    flat, flat8 = pltpu.VMEM((rows, width), F32), pltpu.VMEM((rows + 8, width), F32)
    eight = pltpu.VMEM((8, width), F32)
    state = pltpu.VMEM((2, blocks, LANES), F32)
    states = pltpu.VMEM((hops, 2, blocks, LANES), F32)
    lanes = [MOST[lane] for lane in LANES_OF]
    outs = [(fv_rows, LANES), (quarter, 4 * LANES)] + [(quarter, LANES)] * 5 + [(16, LANES)]
    result = pl.pallas_call(
        block_kernel,
        out_shape=[sds((rows, width), BF16)] * 2
        + [sds(shape, F32) for shape in outs]
        + [
            sds((2, block_rows, width), BF16),
            sds((5, 2, 2, quarter, width), BF16),
            sds((2, 2, fv_rows, width), BF16),
            sds((4, 2, 2, quarter, width), BF16),
            sds((7, rows, width), BF16),
            sds((rows, width), F32),
            sds((2, rows * blocks, LANES), F32),
        ],
        in_specs=[ANY] * 20 + [SMEM] * 2,
        out_specs=[ANY] * 17,
        scratch_shapes=[flat, flat, flat8, flat, flat8]
        + [half] * 8
        + [
            pltpu.VMEM((2, width, width), BF16),
            pltpu.VMEM((2, 2, 2, quarter, 256), BF16),
            pltpu.VMEM((16, width), F32),
            pltpu.VMEM((CHAN, 16, LANES), F32),
            pltpu.VMEM((16, LANES), F32),
            pltpu.VMEM((SEQ, 16, LANES), F32),
            pltpu.VMEM((rows, LANES), F32),
            pltpu.VMEM((rows, LANES), F32),
            pltpu.VMEM((16, width), BF16),
        ]
        + [eight] * 6
        + [state, states, state, states, state]
        + [pltpu.VMEM((9, 1, width), F32), pltpu.VMEM((2, blocks, LANES), F32)]
        + [pltpu.VMEM(shape, F32) for shape in outs]
        + [pltpu.VMEM((9, 8, width), F32), pltpu.VMEM((2, 8, width), F32)]
        + [pltpu.VMEM((2, 2, most, width), BF16) for most in lanes]
        + [pltpu.VMEM((RING, 16 * most, LANES), BF16) for most in lanes]
        + [pltpu.VMEM((block_rows << (3 - d), LANES), BF16) for d in range(4)]
        + [
            pltpu.SemaphoreType.DMA((48,)),
            pltpu.SemaphoreType.DMA((4 + 2 * hops,)),
            pltpu.SemaphoreType.DMA((4 + 2 * hops,)),
            pltpu.SemaphoreType.DMA((CHAN,)),
            pltpu.SemaphoreType.DMA((CHAN,)),
            pltpu.SemaphoreType.DMA((SEQ,)),
            pltpu.SemaphoreType.DMA((SEQ,)),
            pltpu.SemaphoreType.DMA(()),
            pltpu.SemaphoreType.DMA((len(lanes), RING)),
            pltpu.SemaphoreType.DMA((3,)),
            pltpu.SemaphoreType.DMA((len(CHUNKS),)),
            pltpu.SemaphoreType.DMA((len(lanes), TURNS, STEPS - 1)),
            pltpu.SemaphoreType.DMA((len(lanes), 2)),
        ],
        compiler_params=pltpu.CompilerParams(
            vmem_limit_bytes=63 * MIB, collective_id=0, has_side_effects=True
        ),
        name="block",
    )(x, g, *weights, *vectors, *rates, spans, pads)
    return result[:10]


def finish_kernel(count, lines, *refs):
    sources, targets, held = refs[: count + 1], refs[count + 1 : 2 * count + 1 + lines], refs[2 * count + 1 + lines : -2]
    sems = refs[-2:]
    arrive = [pltpu.make_async_copy(s, h, sems[0].at[i]) for i, (s, h) in enumerate(zip(sources, held))]
    leave = [pltpu.make_async_copy(h, t, sems[1].at[i]) for i, (h, t) in enumerate(zip(held[:count], targets))]
    for copy in arrive[::-1]:
        copy.start()
    arrive[count].wait()
    for i in range(lines):
        targets[count + i][...] = held[count][i]
    for there, back in zip(arrive, leave):
        there.wait()
        back.start()
    for copy in leave:
        copy.wait()


def finish(arrays, vec, lines):
    count = len(arrays)
    return pl.pallas_call(
        functools.partial(finish_kernel, count, lines),
        out_shape=[sds(a.shape, a.dtype) for a in arrays] + [sds(vec.shape[1:], vec.dtype)] * lines,
        in_specs=[ANY] * (count + 1),
        out_specs=[ANY] * count + [VMEM] * lines,
        scratch_shapes=[pltpu.VMEM(a.shape, a.dtype) for a in (*arrays, vec)]
        + [pltpu.SemaphoreType.DMA((count + 1,))] * 2,
        compiler_params=params(62),
        name="finish",
    )(*arrays, vec)


def shift(value, steps):
    count = lax.axis_size("chan")
    pairs = [(i, i + steps) for i in range(count) if 0 <= i + steps < count]
    return lax.ppermute(value, "chan", pairs)


def scatter_sums(mats, vecs):
    def both(m):
        m = lax.psum_scatter(m, "chan", scatter_dimension=1, tiled=True)
        return lax.psum_scatter(m, "seq", scatter_dimension=0, tiled=True).astype(F32)

    v = lax.psum_scatter(vecs.astype(BF16), "chan", scatter_dimension=1, tiled=True).astype(F32)
    return [both(m) for m in mats], lax.psum(v, "seq")


def per_device(
    x, g, gain1, bias1, share_k, share_v, share_r, log_rate, boost, wk, wv, wr, wo, gain2, bias2, share_fk, share_fr,
    wfk, wfv, wfr, spans, pads,
):
    rows, width = x.shape
    chans = lax.axis_size("chan")
    total = rows * chans
    hops = max(1, min(chans - 1, total // 4 // rows))
    if (lax.axis_size("seq"), chans, wfk.shape[1] // chans, width) == (4, 8, 4 * LANES, 8 * LANES):
        line = lambda v: v.reshape(1, width)
        tall = lambda v: v.reshape(width // LANES, LANES)
        vectors = [line(v) for v in (gain1, bias1, share_k, share_v, share_r, gain2, bias2, share_fk, share_fr)]
        weights = (wk, wv, wr, wo, wfk, wfv, wfr)
        results = block(x, g, weights, vectors, (tall(log_rate), tall(boost)), spans, pads, hops)
        block_out, grad_in, gfv, gfk, gfr, gwo, gwr, gwv, gwk, *vec = finish(results[:-1], results[-1], 11)
        return (block_out, grad_in, *[vec[i] for i in range(7)], gwk, gwv, gwr, gwo, *[vec[i] for i in range(7, 11)], gfk, gfv, gfr)
    base = lambda: lax.axis_index("chan") * rows
    vecs = jnp.stack([gain1, bias1, share_k, share_v, share_r, gain2, bias2, share_fk, share_fr])
    rates = jnp.stack([log_rate, boost]).reshape(2 * width // LANES, LANES)
    begins = jnp.cumsum(spans[0]) - spans[0]
    pos = base() + jnp.arange(rows, dtype=jnp.int32)
    keep = 1.0 - jnp.any(pos[:, None] == begins[None, :], axis=1).astype(F32)

    xprev = shift(jnp.broadcast_to(x[rows - 1 :], (16, width)), 1)[:8]
    xk, xv, xr, k, v, r, at, bt, end = project(base, x, xprev, vecs, rates, spans, pads, keep, wk, wv, wr)
    carry = jnp.concatenate([shift(end, h + 1) for h in range(hops)], axis=0)
    wkv, gated, middle, last, carried = exit_call(base, hops, x, k, v, r, at, bt, carry, rates, vecs, spans, wo)
    hprev = jnp.broadcast_to(shift(last[7:], 1), (8, width))
    block_out, gfk, gfv, gfr, dh2, back2, sums2 = ffn(base, middle, g, hprev, vecs, spans, pads, wfr, wfk, wfv)
    dh2next = shift(back2, -1)
    dmid, gwo, dwkv, dr, sumsn2, adja, adjb, adjend = exit_back(
        base, middle, g, dh2, dh2next, vecs, rates, gated, wkv, r, k, v, at, bt, carried, spans, pads, keep, wo
    )
    adj = jnp.concatenate([shift(adjend, -h - 1) for h in range(hops)], axis=0)
    gwk, gwv, gwr, dh1, back1, sums1, wsums = project_back(
        base, hops, total, x, xprev, vecs, rates, k, v, dwkv, dr, at, bt, carried, adja, adjb, adj, xk, xv, xr, spans,
        pads, wk, wv, wr,
    )
    grad_in, sumsn1 = entry_back(x, dh1, shift(back1, -1), dmid, vecs)
    vec_parts = jnp.concatenate([sumsn1, sums1, wsums, sumsn2, sums2], axis=0).sum(axis=1)
    (gwk, gwv, gwr, gwo, gfk, gfv, gfr), vec = scatter_sums((gwk, gwv, gwr, gwo, gfk, gfv, gfr), vec_parts)
    return (block_out, grad_in, *[vec[i] for i in range(7)], gwk, gwv, gwr, gwo, *[vec[i] for i in range(7, 11)], gfk, gfv, gfr)


def solution(mesh):
    tokens, chan, both = P(("seq", "chan"), None), P("chan"), P("seq", "chan")
    placed = (tokens, tokens) + (P(),) * 18 + (P("seq", None),) * 2
    return jax.shard_map(
        per_device,
        mesh=mesh,
        in_specs=placed,
        out_specs=(tokens, tokens) + (chan,) * 7 + (both,) * 4 + (chan,) * 4 + (both,) * 3,
        check_vma=False,
    )
```
